32 devices in a mesh: shard: 4 (over y, x), ctx: 4 (over z), tp: 2 (over core).
Axes of the slice: x: 2, y: 2, z: 4, core: 2. Of those that a mesh axis runs over, the one named last changes fastest.
Arguments:
- tokens: bfloat16 [8, 2560, 768], P('shard', 'ctx'), may hold values from -6 to 6
- gate_res: float32 [8, 2560, 12], P('shard', 'ctx'), may hold values from -3 to 3
- cotangent: bfloat16 [8, 2560, 768], P('shard', 'ctx'), may hold values from -6 to 6
- parents: int32 [8, 20], P('shard'), may hold values from 0 to 11, as said below
- expert_ids: int32 [8, 2560, 2], P('shard', 'ctx'), may hold values from 0 to 11, all different within a row
- priority: int32 [4, 4, 1280], P('shard', 'ctx'), may hold values from 0 to 1279, each once within a row
- w_qkv: bfloat16 [768, 3, 768], P('ctx', None, 'tp'), may hold values from -0.3125 to 0.3125
- w_out: bfloat16 [768, 768], P('ctx', 'tp'), may hold values from -0.875 to 0.875
- w_router: bfloat16 [768, 12], P('ctx'), may hold values from -0.15625 to 0.15625
- attn_gain: bfloat16 [768], P('ctx'), may hold values from 0.5 to 1.5
- ffn_gain: bfloat16 [768], P('ctx'), may hold values from 0.5 to 1.5
- const_vec: bfloat16 [768, 2], P('ctx'), may hold values from -4 to 4
- w_gate_up: bfloat16 [768, 8, 2, 2048], P('ctx', 'shard', None, 'tp'), may hold values from -0.21875 to 0.21875
- w_down: bfloat16 [768, 8, 2048], P('ctx', 'shard', 'tp'), may hold values from -0.25 to 0.25
Outputs:
- mixed_out: float32 [8, 2560, 768], P('shard', 'ctx')
- d_tokens: float32 [8, 2560, 768], P('shard', 'ctx')
- d_gate_res: float32 [8, 2560, 12], P('shard', 'ctx')
- d_w_qkv: float32 [768, 3, 768], P('ctx', None, 'tp')
- d_w_out: float32 [768, 768], P('ctx', 'tp')
- d_w_router: float32 [768, 12], P('ctx')
- d_attn_gain: float32 [768], P('ctx')
- d_ffn_gain: float32 [768], P('ctx')
- d_const_vec: float32 [768, 2], P('ctx')
- d_w_gate_up: float32 [768, 8, 2, 2048], P('ctx', 'shard', None, 'tp')
- d_w_down: float32 [768, 8, 2048], P('ctx', 'shard', 'tp')
The draws below stay inside these ranges and needn't reach their ends.
Inputs may be any that keep to these rules, and one draw needn't show every extreme that they name: `parents`: segment 0 is its own parent and segments 1 to 7 have parent s - 1; the next 4 segments have parent 8 - 1; each of the last 8 segments has one of those branch segments as parent, exactly 2 under each branch.
All inputs are finite; a program needn't handle non-finite values.
Results may differ from the reference program's by a relative error of at most 0.023.
Values may be sent and summed in bfloat16 or wider, within the bound.
No kernel may reach another device: no remote copies, remote signals or barrier semaphores. Data moves between devices by JAX's collectives and lax.ppermute only.
A program may use at most 256 MiB of HBM per device.

```python
import math
import jax
import jax.numpy as jnp
from jax import lax

D = 768
HEADS = 12
HEAD_DIM = 64
FF = 2048
EXPERTS = 8
ALL_EXPERTS = 12
TOP = 2
TRUNK = 8
BRANCHES = 4
LEAVES = 2
TREE = 2560
TREES_DEV = 2
TREES = 8
TOK_DEV = 1280
CAP = 213
N_SHARD = 4
N_CTX = 4


def draw_parents(key, part):
    key = jax.random.fold_in(key, 7)
    position = jnp.arange(TRUNK + BRANCHES, dtype=jnp.int32)
    upper = jnp.where(position < TRUNK, jnp.maximum(position - 1, 0), TRUNK - 1)
    upper = jnp.broadcast_to(upper[None, :], (TREES, TRUNK + BRANCHES))
    leaf_count = BRANCHES * LEAVES
    orders = jax.vmap(lambda sub: jax.random.permutation(sub, leaf_count))(jax.random.split(key, TREES))
    leaf_parent = TRUNK + orders.astype(jnp.int32) // LEAVES
    return jnp.concatenate([upper, leaf_parent], axis=1).astype(jnp.int32)


def level_of(rng, dims, pieces, low, top_value):
    level, own = 1.0, jax.random.fold_in(rng, 6)
    for dim, blocks in pieces:
        steps = jnp.exp(jax.random.uniform(jax.random.fold_in(own, dim), (blocks,), jnp.float32, low / len(pieces), top_value / len(pieces)))
        level = level * jnp.repeat(steps, dims[dim] // blocks).reshape([-1 if axis == dim else 1 for axis in range(len(dims))])
    return level


def choose_distinct(rng, rows, count, top, lift):
    sequence = jax.random.permutation(jax.random.fold_in(rng, 1), count)
    boost = sequence
    for power in range(3):
        boost = boost * boost // count
    boost = boost * lift // count
    chance = jax.random.randint(jax.random.fold_in(rng, 2), (rows, count), 0, 4096) + boost
    fixed_rows = jax.random.permutation(jax.random.fold_in(rng, 3), rows)[jnp.arange(count) % rows]
    chance = jnp.where(jnp.arange(rows)[:, None] == fixed_rows[None, :], 1 << 14, chance)
    merit = chance * count + jnp.arange(count)
    return lax.top_k(merit.astype(jnp.int32), top)[1].astype(jnp.int32)


def gaussian(rng, dims, spread, limit, shards=(), kind=jnp.bfloat16):
    entries = jax.random.normal(rng, dims, jnp.float32) * spread
    if len(shards) > 0:
        entries = level_of(rng, dims, shards, -0.22, 0.18) * entries
    return jnp.clip(entries, min=-limit, max=limit).astype(kind)


def setup_inputs(seed: int = 0) -> dict:
    arg_keys = jax.random.split(jax.random.key(seed), 15)
    return {
        "tokens": gaussian(arg_keys[0], (TREES, TREE, D), 1.0, 6.0, ((0, 4), (1, 4))),
        "gate_res": gaussian(arg_keys[1], (TREES, TREE, ALL_EXPERTS), 0.5, 3.0, ((0, 4), (1, 4)), jnp.float32),
        "cotangent": gaussian(arg_keys[2], (TREES, TREE, D), 1.0, 6.0, ((0, 4), (1, 4))),
        "parents": draw_parents(jax.random.fold_in(arg_keys[14], 71), 0),
        "expert_ids": choose_distinct(arg_keys[4], TREES * TREE, ALL_EXPERTS, TOP, 1365).reshape((TREES, TREE, TOP)),
        "priority": jax.vmap(lambda own: jax.random.permutation(own, TOK_DEV))(jax.random.split(arg_keys[5], N_SHARD * N_CTX)).reshape((N_SHARD, N_CTX, TOK_DEV)).astype(jnp.int32),
        "w_qkv": gaussian(arg_keys[6], (D, 3, D), (D // 2) ** -0.5, 0.3125, ((0, 4), (2, 2))),
        "w_out": gaussian(arg_keys[7], (D, D), (D // 16) ** -0.5, 0.875, ((0, 4), (1, 2))),
        "w_router": gaussian(arg_keys[8], (D, ALL_EXPERTS), (2 * D) ** -0.5, 0.15625, ((0, 4),)),
        "attn_gain": jnp.clip(1.0 + 0.1 * jax.random.normal(arg_keys[9], (D,), jnp.float32), 0.5, 1.5).astype(jnp.bfloat16),
        "ffn_gain": jnp.clip(1.0 + 0.1 * jax.random.normal(arg_keys[10], (D,), jnp.float32), 0.5, 1.5).astype(jnp.bfloat16),
        "const_vec": gaussian(arg_keys[11], (D, 2), 1.0, 4.0, ((0, 4),)),
        "w_gate_up": gaussian(arg_keys[12], (D, EXPERTS, 2, FF), D ** -0.5, 0.21875, ((0, 4), (1, 4), (3, 2))),
        "w_down": gaussian(arg_keys[13], (D, EXPERTS, FF), (FF // 4) ** -0.5, 0.25, ((0, 4), (1, 4), (2, 2))),
    }


@jax.custom_vjp
def low(v):
    return lax.optimization_barrier(v.astype(jnp.bfloat16)).astype(jnp.float32)

@jax.custom_vjp
def low_back(v):
    return v

def low_keep(v):
    return (low(v), None)

def low_pass(kept, grad):
    return (grad,)

def back_keep(v):
    return (v, None)

def back_low(kept, grad):
    return (low(grad),)
low.defvjp(low_keep, low_pass)
low_back.defvjp(back_keep, back_low)
eps = 1e-06
score_scale = 0.125

def ancestry(parent_row):
    seg_count = parent_row.shape[0]
    position = jnp.arange(seg_count, dtype=jnp.int32)

    def add_row(index, reach):
        index = jnp.asarray(index).astype(jnp.int32)
        own = (position == index).astype(jnp.float32)
        above = lax.dynamic_index_in_dim(reach, parent_row[index].astype(jnp.int32), 0, keepdims=False)
        return lax.dynamic_update_index_in_dim(reach, jnp.maximum(own, above), index, 0)
    return lax.fori_loop(0, seg_count, add_row, jnp.zeros((seg_count, seg_count), jnp.float32))

def slot_table(picked_ids, ranking, experts, capacity):
    count_rows = picked_ids.shape[0]
    flat_ids = picked_ids.reshape(-1)
    rank_key = (2 * ranking[:, None] + jnp.arange(2, dtype=jnp.int32)[None, :]).reshape(-1)
    earlier = (flat_ids[:, None] == flat_ids[None, :]) & (rank_key[None, :] < rank_key[:, None])
    ranks = lax.optimization_barrier(jnp.sum(earlier.astype(jnp.int32), axis=1))
    kept = (flat_ids < experts) & (ranks < capacity)
    target = jnp.where(kept, flat_ids * capacity + ranks, -1).reshape(count_rows, 2)
    slot_index = jnp.arange(experts * capacity, dtype=jnp.int32)
    return slot_index[None, :, None] == target.T[:, None, :]

def normalize(values, gain):
    factor = lax.rsqrt(lax.optimization_barrier(jnp.mean(values * values, axis=-1, keepdims=True)) + eps)
    return values * factor * gain

def tree_attention(operands):
    queries, keys, values, ancestors = operands
    tree_len = queries.shape[0]
    block_len = math.gcd(tree_len, 512)
    seg_len = tree_len // ancestors.shape[0]
    key_pos = jnp.arange(tree_len, dtype=jnp.int32)
    key_seg = key_pos // seg_len

    def one_block(start):
        query_blk = lax.dynamic_slice_in_dim(queries, start, block_len, 0)
        query_pos = start + jnp.arange(block_len, dtype=jnp.int32)
        linked = ancestors[query_pos // seg_len][:, key_seg] > 0.5
        mask = (linked & (key_pos[None, :] <= query_pos[:, None]))[None]
        raw = low_back(jnp.einsum('qhe,khe->hqk', query_blk, keys, precision=lax.Precision.HIGHEST) * score_scale)
        masked = jnp.where(mask, raw, -1e+30)
        top = lax.optimization_barrier(jnp.max(masked, axis=2, keepdims=True))
        expo = jnp.where(mask, jnp.exp(masked - top), 0.0)
        prob = low(expo / lax.optimization_barrier(jnp.sum(expo, axis=2, keepdims=True)))
        return jnp.einsum('hqk,khe->qhe', prob, values, precision=lax.Precision.HIGHEST)
    starts = jnp.arange(tree_len // block_len, dtype=jnp.int32) * block_len
    outputs = lax.map(jax.checkpoint(one_block), starts)
    return outputs.reshape(tree_len, queries.shape[1], queries.shape[2])

def expert_ffn(operands):
    slot_rows, gate_up, down_proj = operands
    gate_part = low_back(jnp.dot(slot_rows, gate_up[:, 0], precision=lax.Precision.HIGHEST))
    up_part = low_back(jnp.dot(slot_rows, gate_up[:, 1], precision=lax.Precision.HIGHEST))
    hidden = low(jax.nn.silu(gate_part) * up_part)
    return low_back(low(jnp.dot(hidden, down_proj.T, precision=lax.Precision.HIGHEST)))

def reference(tokens, gate_res, cotangent, parents, expert_ids, priority, w_qkv, w_out, w_router, attn_gain, ffn_gain, const_vec, w_gate_up, w_down):
    ancestors_all = jax.vmap(ancestry)(parents)
    trees, tree_len, model_width = tokens.shape
    rows = tree_len // N_CTX
    ids_blocks = expert_ids.reshape(N_SHARD, TREES_DEV, N_CTX, rows, 2).transpose(0, 2, 1, 3, 4).reshape(N_SHARD * N_CTX, TOK_DEV, 2)
    prio_blocks = priority.reshape(N_SHARD * N_CTX, TOK_DEV)

    def table_one(operands):
        return slot_table(operands[0], operands[1], EXPERTS, CAP).astype(jnp.float32)
    table = lax.map(table_one, (ids_blocks, prio_blocks)).reshape(N_SHARD, N_CTX, 2, EXPERTS * CAP, TOK_DEV)
    routed = lax.optimization_barrier(jnp.sum(table, axis=2))
    selector = (expert_ids[..., None] == jnp.arange(ALL_EXPERTS, dtype=jnp.int32)).astype(jnp.float32)
    heads_shape = (trees, tree_len, HEADS, HEAD_DIM)

    def forward(tok, gres, wqkv, wout, wrouter, again, fgain, cvec, wgu, wdown):
        normed = low(normalize(tok, again))
        qkv = jnp.einsum('tnd,dke->tnke', normed, wqkv, precision=lax.Precision.HIGHEST)
        queries = low_back(low(qkv[:, :, 0])).reshape(heads_shape)
        keys = low_back(low(qkv[:, :, 1])).reshape(heads_shape)
        values = low_back(low(qkv[:, :, 2])).reshape(heads_shape)
        attended = lax.map(tree_attention, (queries, keys, values, ancestors_all))
        attended = low_back(low(attended.reshape(trees, tree_len, model_width)))
        attn_out = low_back(jnp.einsum('tnh,dh->tnd', attended, wout, precision=lax.Precision.HIGHEST))
        mixed = tok + attn_out
        normed2 = low(normalize(mixed, fgain))
        logits = jnp.einsum('tnd,de->tne', normed2, wrouter, precision=lax.Precision.HIGHEST) + gres
        probs = jax.nn.softmax(logits, axis=-1)
        picked = lax.optimization_barrier(jnp.sum(selector * probs[:, :, None, :], axis=-1))
        gates = picked / lax.optimization_barrier(jnp.sum(picked, axis=-1, keepdims=True))
        blocks_in = normed2.reshape(N_SHARD, TREES_DEV, N_CTX, rows, model_width).transpose(0, 2, 1, 3, 4).reshape(N_SHARD, N_CTX, TOK_DEV, model_width)
        slots = low_back(jnp.einsum('abet,abtd->abed', routed, blocks_in, precision=lax.Precision.HIGHEST))
        per_expert = slots.reshape(N_SHARD, N_CTX, EXPERTS, CAP, model_width).transpose(2, 0, 1, 3, 4).reshape(EXPERTS, -1, model_width)
        expert_out = lax.map(jax.checkpoint(expert_ffn), (per_expert, wgu.transpose(1, 0, 2, 3), wdown.transpose(1, 0, 2)))
        returned = expert_out.reshape(EXPERTS, N_SHARD, N_CTX, CAP, model_width).transpose(1, 2, 0, 3, 4).reshape(N_SHARD, N_CTX, EXPERTS * CAP, model_width)
        ffn_blocks = jnp.einsum('abcet,abed->abtcd', table, returned, precision=lax.Precision.HIGHEST)
        ffn_values = ffn_blocks.reshape(N_SHARD, N_CTX, TREES_DEV, rows, 2, model_width).transpose(0, 2, 1, 3, 4, 5).reshape(trees, tree_len, 2, model_width)
        copies = selector[..., EXPERTS + 1:EXPERTS + 2] * normed2[:, :, None, :]
        fixed_terms = jnp.einsum('tnck,dk->tncd', selector[..., EXPERTS + 2:], cvec, precision=lax.Precision.HIGHEST)
        values_all = ffn_values + copies + fixed_terms
        return mixed + lax.optimization_barrier(jnp.sum(gates[..., None] * values_all, axis=2))
    floats = (tokens.astype(jnp.float32), gate_res.astype(jnp.float32), w_qkv.astype(jnp.float32), w_out.astype(jnp.float32), w_router.astype(jnp.float32), attn_gain.astype(jnp.float32), ffn_gain.astype(jnp.float32), const_vec.astype(jnp.float32), w_gate_up.astype(jnp.float32), w_down.astype(jnp.float32))
    result, pullback = jax.vjp(forward, *floats)
    grads = pullback(cotangent.astype(jnp.float32))
    return (result, grads[0], grads[1], grads[2], grads[3], grads[4], grads[5], grads[6], grads[7], grads[8], grads[9])
```

```python
import functools
import math

import jax
import jax.numpy as jnp
from jax import lax
from jax.experimental import pallas as pl
from jax.experimental.pallas import tpu as pltpu
from jax.sharding import PartitionSpec as P

HEAD_DIM = 64


eps = 1e-06
score_scale = 0.125


def ancestry(parent_row):
    seg_count = parent_row.shape[0]
    position = jnp.arange(seg_count, dtype=jnp.int32)
    linked = (parent_row[:, None] == position[None, :]) | (position[:, None] == position[None, :])
    reach = linked.astype(jnp.float32)
    for repeat in range(seg_count.bit_length()):
        reach = jnp.minimum(jnp.dot(reach, reach, precision=lax.Precision.HIGHEST), 1.0)
    return reach


def path_rows(positions, seg_len, ancestors):
    onehot = (
        (positions // seg_len)[:, None] == jnp.arange(ancestors.shape[0], dtype=jnp.int32)[None, :]
    ).astype(jnp.float32)
    return jnp.dot(onehot, ancestors)


def allowed_block(query_rows, query_pos, key_start, key_count, seg_len):
    key_pos = key_start + jnp.arange(key_count, dtype=jnp.int32)
    key_onehot = (
        (key_pos // seg_len)[:, None] == jnp.arange(query_rows.shape[1], dtype=jnp.int32)[None, :]
    ).astype(jnp.float32)
    linked = jnp.dot(query_rows, key_onehot.T) > 0.5
    return (linked & (key_pos[None, :] <= query_pos[:, None]))[None]


def slot_table(picked_ids, ranking, experts, capacity):
    count_rows = picked_ids.shape[0]
    flat_ids = picked_ids.reshape(-1)
    rank_key = (2 * ranking[:, None] + jnp.arange(2, dtype=jnp.int32)[None, :]).reshape(-1)
    earlier = (flat_ids[:, None] == flat_ids[None, :]) & (rank_key[None, :] < rank_key[:, None])
    ranks = jnp.sum(earlier.astype(jnp.int32), axis=1)
    kept = (flat_ids < experts) & (ranks < capacity)
    target = jnp.where(kept, flat_ids * capacity + ranks, -1).reshape(count_rows, 2)
    slot_index = jnp.arange(experts * capacity, dtype=jnp.int32)
    return slot_index[None, :, None] == target.T[:, None, :]


def block_scores(queries, keys_blk):
    return (
        jnp.einsum("qhe,khe->hqk", queries, keys_blk, preferred_element_type=jnp.float32)
        * score_scale
    )


def softmax_grads(queries, grads_out, stat_lse, stat_delta, keys_blk, values_blk, mask):
    prob = jnp.where(mask, jnp.exp(block_scores(queries, keys_blk) - stat_lse[:, :, None]), 0.0)
    dprob = jnp.einsum("qhe,khe->hqk", grads_out, values_blk, preferred_element_type=jnp.float32)
    dscore = (prob * (dprob - stat_delta[:, :, None])).astype(jnp.bfloat16)
    return (prob.astype(jnp.bfloat16), dscore)


def shards(
    tokens,
    gate_res,
    cotangent,
    parents,
    expert_ids,
    priority,
    w_qkv,
    w_out,
    w_router,
    attn_gain,
    ffn_gain,
    const_vec,
    w_gate_up,
    w_down,
):
    full_qkv, full_out, full_router, full_again, full_fgain, full_const, full_gu, full_down = (
        lax.all_gather(w_qkv, "ctx", axis=0, tiled=True),
        lax.all_gather(w_out, "ctx", axis=0, tiled=True),
        lax.all_gather(w_router, "ctx", axis=0, tiled=True),
        lax.all_gather(attn_gain, "ctx", axis=0, tiled=True),
        lax.all_gather(ffn_gain, "ctx", axis=0, tiled=True),
        lax.all_gather(const_vec, "ctx", axis=0, tiled=True),
        lax.all_gather(w_gate_up, "ctx", axis=0, tiled=True),
        lax.all_gather(w_down, "ctx", axis=0, tiled=True),
    )
    tree_count, rows, model_width = tokens.shape
    tok_rows = tree_count * rows
    inputs = tokens.reshape(tok_rows, model_width).astype(jnp.float32)
    local_width = full_out.shape[1]
    local_heads = local_width // HEAD_DIM
    ctx_index = lax.axis_index("ctx")
    tree_len = rows * lax.axis_size("ctx")
    ancestors_all = jax.vmap(ancestry)(parents)
    seg_len = tree_len // parents.shape[1]
    key_block = math.gcd(tree_len, 512)
    starts = jnp.arange(tree_len // key_block, dtype=jnp.int32) * key_block
    key_start_own = ctx_index * rows
    query_pos = key_start_own + jnp.arange(rows, dtype=jnp.int32)
    query_rows_all = jax.vmap(lambda anc: path_rows(query_pos, seg_len, anc))(ancestors_all)
    inv_first = lax.rsqrt(jnp.mean(inputs * inputs, axis=-1, keepdims=True) + eps)
    first_unit = inputs * inv_first
    first_gain = full_again.astype(jnp.float32)
    normed = (first_unit * first_gain).astype(jnp.bfloat16)
    projected = jnp.einsum("nd,dke->nke", normed, full_qkv, preferred_element_type=jnp.float32)
    q_low = projected[:, 0].astype(jnp.bfloat16)
    k_low = projected[:, 1].astype(jnp.bfloat16)
    v_low = projected[:, 2].astype(jnp.bfloat16)
    keys_all, values_all = (
        lax.all_gather(k_low.reshape(tree_count, rows, local_width), "ctx", axis=1, tiled=True),
        lax.all_gather(v_low.reshape(tree_count, rows, local_width), "ctx", axis=1, tiled=True),
    )
    q_heads = q_low.reshape(tree_count, rows, local_heads, HEAD_DIM)
    k_heads = keys_all.reshape(tree_count, tree_len, local_heads, HEAD_DIM)
    v_heads = values_all.reshape(tree_count, tree_len, local_heads, HEAD_DIM)

    def tree_forward(q_one, k_one, v_one, rows_one):

        def stat_step(carry, start):
            running_top, running_sum = carry
            keys_blk = lax.dynamic_slice_in_dim(k_one, start, key_block, 0)
            mask = allowed_block(rows_one, query_pos, start, key_block, seg_len)
            masked = jnp.where(mask, block_scores(q_one, keys_blk), -1e30)
            new_top = jnp.maximum(running_top, jnp.max(masked, axis=2))
            expo = jnp.where(mask, jnp.exp(masked - new_top[:, :, None]), 0.0)
            running_sum = running_sum * jnp.exp(running_top - new_top) + jnp.sum(expo, axis=2)
            return ((new_top, running_sum), None)

        start_top = jnp.full((local_heads, rows), -1e30, jnp.float32)
        (final_top, final_sum), unused = lax.scan(
            stat_step, (start_top, jnp.zeros_like(start_top)), starts
        )
        lse_one = final_top + jnp.log(final_sum)

        def out_step(accum, start):
            keys_blk = lax.dynamic_slice_in_dim(k_one, start, key_block, 0)
            values_blk = lax.dynamic_slice_in_dim(v_one, start, key_block, 0)
            mask = allowed_block(rows_one, query_pos, start, key_block, seg_len)
            prob = jnp.where(
                mask, jnp.exp(block_scores(q_one, keys_blk) - lse_one[:, :, None]), 0.0
            ).astype(jnp.bfloat16)
            return (
                accum
                + jnp.einsum("hqk,khe->qhe", prob, values_blk, preferred_element_type=jnp.float32),
                None,
            )

        attended_one, unused = lax.scan(
            out_step, jnp.zeros((rows, local_heads, HEAD_DIM), jnp.float32), starts
        )
        return (attended_one, lse_one)

    attended, lse = jax.vmap(tree_forward)(q_heads, k_heads, v_heads, query_rows_all)
    attended_low = attended.reshape(tok_rows, local_width).astype(jnp.bfloat16)
    attn_part = jnp.einsum("nh,dh->nd", attended_low, full_out, preferred_element_type=jnp.float32)
    attn_sum = lax.psum(attn_part.astype(jnp.bfloat16), "tp").astype(jnp.float32)
    mixed = inputs + attn_sum
    inv_second = lax.rsqrt(jnp.mean(mixed * mixed, axis=-1, keepdims=True) + eps)
    second_unit = mixed * inv_second
    second_gain = full_fgain.astype(jnp.float32)
    second_low = (second_unit * second_gain).astype(jnp.bfloat16)
    second_float = second_low.astype(jnp.float32)
    logits = jnp.dot(
        second_low, full_router, preferred_element_type=jnp.float32
    ) + gate_res.reshape(tok_rows, -1)
    expo_logits = jnp.exp(logits - jnp.max(logits, axis=-1, keepdims=True))
    probs = expo_logits / jnp.sum(expo_logits, axis=-1, keepdims=True)
    experts = lax.axis_size("shard") * w_gate_up.shape[1]
    every_expert = experts + 4
    capacity = tok_rows * 2 // every_expert
    picked_ids = expert_ids.reshape(tok_rows, 2)
    selector = (picked_ids[:, :, None] == jnp.arange(every_expert, dtype=jnp.int32)).astype(
        jnp.float32
    )
    picked = jnp.sum(selector * probs[:, None, :], axis=-1)
    picked_total = jnp.sum(picked, axis=-1, keepdims=True)
    gates = picked / picked_total
    table = slot_table(picked_ids, priority[0, 0], experts, capacity).astype(jnp.bfloat16)
    routed = table[0] + table[1]
    send_slots = jnp.einsum(
        "et,td->ed", routed, second_low, preferred_element_type=jnp.float32
    ).astype(jnp.bfloat16)
    send_slots = send_slots.reshape(experts, 1, capacity, model_width)
    arrived = lax.all_to_all(send_slots, "shard", split_axis=0, concat_axis=1, tiled=True)
    gate_up = jnp.einsum("jsrd,djgf->jsrgf", arrived, full_gu, preferred_element_type=jnp.float32)
    hidden_low = (jax.nn.silu(gate_up[:, :, :, 0]) * gate_up[:, :, :, 1]).astype(jnp.bfloat16)
    partial_out = jnp.einsum(
        "jsrf,djf->jsrd", hidden_low, full_down, preferred_element_type=jnp.float32
    )
    summed = lax.psum(partial_out.astype(jnp.bfloat16), "tp")
    returned = lax.all_to_all(summed, "shard", split_axis=1, concat_axis=0, tiled=True)
    returned, kept_slots = (returned, arrived)
    out_slots = returned.reshape(experts * capacity, model_width)
    ffn_values = jnp.einsum("cet,ed->ctd", table, out_slots, preferred_element_type=jnp.float32)
    copy_flag = selector[:, :, experts + 1]
    const_flags = selector[:, :, experts + 2 :]
    const_float = full_const.astype(jnp.float32)
    fixed_terms = jnp.einsum(
        "nck,dk->cnd", const_flags, const_float, precision=lax.Precision.HIGHEST
    )
    values_pair = ffn_values + copy_flag.T[:, :, None] * second_float[None] + fixed_terms
    mixed_out = mixed + jnp.sum(gates.T[:, :, None] * values_pair, axis=0)
    grad_out = cotangent.reshape(tok_rows, model_width).astype(jnp.float32)
    weighted = gates.T[:, :, None] * grad_out[None]
    d_gates = jnp.einsum("cnd,nd->nc", values_pair, grad_out)
    d_const = jnp.einsum("nck,cnd->dk", const_flags, weighted, precision=lax.Precision.HIGHEST)
    d_out_slots = jnp.einsum(
        "cet,ctd->ed", table.astype(jnp.float32), weighted, precision=lax.Precision.HIGHEST
    )
    d_out_low = d_out_slots.astype(jnp.bfloat16).reshape(experts, 1, capacity, model_width)
    d_picked = (d_gates - jnp.sum(d_gates * gates, axis=-1, keepdims=True)) / picked_total
    d_probs = jnp.einsum("nc,nck->nk", d_picked, selector)
    d_logits = probs * (d_probs - jnp.sum(probs * d_probs, axis=-1, keepdims=True))
    d_router_w = jnp.dot(second_float.T, d_logits, precision=lax.Precision.HIGHEST)
    d_second = jnp.sum(copy_flag.T[:, :, None] * weighted, axis=0)
    d_second = d_second + jnp.dot(
        d_logits, full_router.astype(jnp.float32).T, precision=lax.Precision.HIGHEST
    )
    arrived_grad = lax.all_to_all(d_out_low, "shard", split_axis=0, concat_axis=1, tiled=True)
    gate_up = jnp.einsum(
        "jsrd,djgf->jsrgf", kept_slots, full_gu, preferred_element_type=jnp.float32
    )
    gate_part = gate_up[:, :, :, 0]
    up_part = gate_up[:, :, :, 1]
    sigma = jax.nn.sigmoid(gate_part)
    silu_part = gate_part * sigma
    hidden_low = (silu_part * up_part).astype(jnp.bfloat16)
    d_hidden = jnp.einsum(
        "jsrd,djf->jsrf", arrived_grad, full_down, preferred_element_type=jnp.float32
    )
    d_gate_part = d_hidden * up_part * sigma * (1.0 + gate_part * (1.0 - sigma))
    d_up_part = d_hidden * silu_part
    d_gate_up_low = jnp.stack([d_gate_part, d_up_part], axis=3).astype(jnp.bfloat16)
    d_slot_part = jnp.einsum(
        "jsrgf,djgf->jsrd", d_gate_up_low, full_gu, preferred_element_type=jnp.float32
    )
    d_slot_sum = lax.psum(d_slot_part.astype(jnp.bfloat16), "tp")
    d_slot_back = lax.all_to_all(d_slot_sum, "shard", split_axis=1, concat_axis=0, tiled=True)
    d_gate_up_w = jnp.einsum(
        "jsrd,jsrgf->djgf", kept_slots, d_gate_up_low, preferred_element_type=jnp.float32
    )
    d_down_w = jnp.einsum(
        "jsrd,jsrf->djf", arrived_grad, hidden_low, preferred_element_type=jnp.float32
    )
    d_second = d_second + jnp.einsum(
        "et,ed->td",
        routed,
        d_slot_back.reshape(experts * capacity, model_width),
        preferred_element_type=jnp.float32,
    )
    d_second_gain = jnp.sum(d_second * second_unit, axis=0)
    d_second_unit = d_second * second_gain
    d_mixed = grad_out + inv_second * (
        d_second_unit - second_unit * jnp.mean(d_second_unit * second_unit, axis=-1, keepdims=True)
    )
    d_attn_low = d_mixed.astype(jnp.bfloat16)
    d_out_w = jnp.einsum("nd,nh->dh", d_attn_low, attended_low, preferred_element_type=jnp.float32)
    d_attended = jnp.einsum("nd,dh->nh", d_attn_low, full_out, preferred_element_type=jnp.float32)
    do_low = d_attended.astype(jnp.bfloat16)
    do_heads = do_low.reshape(tree_count, rows, local_heads, HEAD_DIM)
    delta = jnp.einsum("tqhe,tqhe->thq", do_heads.astype(jnp.float32), attended)

    def tree_both(q_one, k_one, v_one, do_one, lse_one, delta_one, rows_one):

        def both_step(dq_accum, start):
            keys_blk = lax.dynamic_slice_in_dim(k_one, start, key_block, 0)
            values_blk = lax.dynamic_slice_in_dim(v_one, start, key_block, 0)
            mask = allowed_block(rows_one, query_pos, start, key_block, seg_len)
            prob_low, dscore = softmax_grads(
                q_one, do_one, lse_one, delta_one, keys_blk, values_blk, mask
            )
            dq_accum = dq_accum + jnp.einsum(
                "hqk,khe->qhe", dscore, keys_blk, preferred_element_type=jnp.float32
            )
            dkey = (
                jnp.einsum("hqk,qhe->khe", dscore, q_one, preferred_element_type=jnp.float32)
                * score_scale
            )
            dval = jnp.einsum("hqk,qhe->khe", prob_low, do_one, preferred_element_type=jnp.float32)
            return (
                dq_accum,
                jnp.stack(
                    [dkey.reshape(key_block, local_width), dval.reshape(key_block, local_width)],
                    axis=1,
                ),
            )

        dq_one, terms_one = lax.scan(
            both_step, jnp.zeros((rows, local_heads, HEAD_DIM), jnp.float32), starts
        )
        return (dq_one, terms_one.reshape(tree_len, 2, local_width))

    dq_total, key_terms = jax.vmap(tree_both)(
        q_heads, k_heads, v_heads, do_heads, lse, delta, query_rows_all
    )
    key_sums = lax.psum_scatter(
        key_terms.astype(jnp.bfloat16), "ctx", scatter_dimension=1, tiled=True
    ).astype(jnp.float32)
    key_grad = key_sums[:, :, 0].reshape(tok_rows, local_width)
    value_grad = key_sums[:, :, 1].reshape(tok_rows, local_width)
    query_grad = (dq_total * score_scale).reshape(tok_rows, local_width)
    d_qkv_low = jnp.stack([query_grad, key_grad, value_grad], axis=1).astype(jnp.bfloat16)
    d_qkv_w = jnp.einsum("nd,nke->dke", normed, d_qkv_low, preferred_element_type=jnp.float32)
    d_normed_part = jnp.einsum(
        "nke,dke->nd", d_qkv_low, full_qkv, preferred_element_type=jnp.float32
    )
    d_normed = lax.psum(d_normed_part.astype(jnp.bfloat16), "tp").astype(jnp.float32)
    d_first_gain = jnp.sum(d_normed * first_unit, axis=0)
    d_first_unit = d_normed * first_gain
    d_inputs = d_mixed + inv_first * (
        d_first_unit - first_unit * jnp.mean(d_first_unit * first_unit, axis=-1, keepdims=True)
    )
    summed_grads = (
        lax.psum_scatter(
            d_qkv_w.astype(jnp.bfloat16), "ctx", scatter_dimension=0, tiled=True
        ).astype(jnp.float32),
        lax.psum_scatter(
            d_out_w.astype(jnp.bfloat16), "ctx", scatter_dimension=0, tiled=True
        ).astype(jnp.float32),
        lax.psum_scatter(
            d_router_w.astype(jnp.bfloat16), "ctx", scatter_dimension=0, tiled=True
        ).astype(jnp.float32),
        lax.psum_scatter(
            d_first_gain.astype(jnp.bfloat16), "ctx", scatter_dimension=0, tiled=True
        ).astype(jnp.float32),
        lax.psum_scatter(
            d_second_gain.astype(jnp.bfloat16), "ctx", scatter_dimension=0, tiled=True
        ).astype(jnp.float32),
        lax.psum_scatter(
            d_const.astype(jnp.bfloat16), "ctx", scatter_dimension=0, tiled=True
        ).astype(jnp.float32),
        lax.psum_scatter(
            d_gate_up_w.astype(jnp.bfloat16), "ctx", scatter_dimension=0, tiled=True
        ).astype(jnp.float32),
        lax.psum_scatter(
            d_down_w.astype(jnp.bfloat16), "ctx", scatter_dimension=0, tiled=True
        ).astype(jnp.float32),
    )
    shared = (
        lax.psum(summed_grads[0].astype(jnp.bfloat16), "shard").astype(jnp.float32),
        lax.psum(summed_grads[1].astype(jnp.bfloat16), "shard").astype(jnp.float32),
        lax.psum(summed_grads[2].astype(jnp.bfloat16), "shard").astype(jnp.float32),
        lax.psum(summed_grads[3].astype(jnp.bfloat16), "shard").astype(jnp.float32),
        lax.psum(summed_grads[4].astype(jnp.bfloat16), "shard").astype(jnp.float32),
        lax.psum(summed_grads[5].astype(jnp.bfloat16), "shard").astype(jnp.float32),
    )
    out_rows = mixed_out.reshape(tree_count, rows, model_width)
    grad_rows = d_inputs.reshape(tree_count, rows, model_width)
    logit_rows = d_logits.reshape(tree_count, rows, every_expert)
    return (
        out_rows,
        grad_rows,
        logit_rows,
        shared[0],
        shared[1],
        shared[2],
        shared[3],
        shared[4],
        shared[5],
        summed_grads[6],
        summed_grads[7],
    )


NT = (((1,), (1,)), ((), ()))
NN = (((1,), (0,)), ((), ()))
TRUNK = 8
KEY_SEGS = 12
PIECE = 256


def mm(a, b, dims=NN):
    return lax.dot_general(a, b, dims, preferred_element_type=jnp.float32)


def stacked(rows, half):
    first = lax.broadcasted_iota(jnp.int32, rows.shape, 1) < half
    blank = jnp.zeros_like(rows)
    return jnp.concatenate([jnp.where(first, rows, blank), jnp.where(first, blank, rows)], axis=0)


def unstack(wide, half, seg):
    return jnp.concatenate([wide[:half, :seg], wide[half:, seg:]], axis=0)


def causal(seg):
    row = lax.broadcasted_iota(jnp.int32, (seg, 2 * seg), 0)
    col = lax.broadcasted_iota(jnp.int32, (seg, 2 * seg), 1)
    return row <= jnp.where(col >= seg, col - seg, col)


def attend_kernel(own, seg, half, info, q_ref, k_ref, v_ref, o_ref, lse_ref, s_ref, p_ref):
    trunk = TRUNK * seg
    allowed = causal(seg)
    v_trunk = v_ref[own : own + trunk, :].T

    def one(i, unused):
        count, branch, leaf = info[i, 0], info[i, 1], info[i, 2]
        here = pl.ds(pl.multiple_of(i * seg, seg), seg)
        there = pl.ds(pl.multiple_of(own + branch * seg, seg), seg)
        qs = stacked(q_ref[here, :] * 0.125, half)
        s_ref[:trunk, :] = mm(k_ref[own : own + trunk, :], qs, NT)
        s_branch = mm(k_ref[there, :], qs, NT)
        s_own = jnp.where(allowed, mm(k_ref[here, :], qs, NT), -1e30)
        biases = [jnp.where(kb < count, 0.0, -1e30) for kb in range(TRUNK)]
        leaf_bias = jnp.where(leaf > 0, 0.0, -1e30)
        top = jnp.max(s_own, axis=0, keepdims=True)
        top = jnp.maximum(top, jnp.max(s_branch, axis=0, keepdims=True) + leaf_bias)
        for kb in range(TRUNK):
            part = jnp.max(s_ref[kb * seg : (kb + 1) * seg, :], axis=0, keepdims=True)
            top = jnp.maximum(top, part + biases[kb])
        e_own = jnp.exp(s_own - top)
        e_branch = jnp.exp(s_branch - (top - leaf_bias))
        total = jnp.sum(e_own + e_branch, axis=0, keepdims=True)
        for kb in range(TRUNK):
            e = jnp.exp(s_ref[kb * seg : (kb + 1) * seg, :] - (top - biases[kb]))
            total = total + jnp.sum(e, axis=0, keepdims=True)
            p_ref[kb * seg : (kb + 1) * seg, :] = e.astype(jnp.bfloat16)
        out = mm(v_trunk, p_ref[...])
        out = out + mm(v_ref[there, :].T, e_branch.astype(jnp.bfloat16))
        out = out + mm(v_ref[here, :].T, e_own.astype(jnp.bfloat16))
        out = unstack(out * (1.0 / total), half, seg)
        o_ref[here, :] = out.T.astype(jnp.bfloat16)
        lse_ref[pl.ds(i, 1), :] = top + jnp.log(total)
        return 0

    lax.fori_loop(0, own // seg, one, 0)


def attend_back_kernel(
    own, seg, half, info, q_ref, k_ref, v_ref, o_ref, do_ref, lse_ref, dq_ref, dk_ref, dv_ref, ak, av
):
    trunk = TRUNK * seg
    allowed = causal(seg)
    low = jnp.bfloat16
    tk = slice(own, own + trunk)
    k_trunk = k_ref[tk, :].T
    ak[...] = jnp.zeros_like(ak)
    av[...] = jnp.zeros_like(av)

    def one(i, unused):
        count, branch, leaf = info[i, 0], info[i, 1], info[i, 2]
        here = pl.ds(pl.multiple_of(i * seg, seg), seg)
        there = pl.ds(pl.multiple_of(own + branch * seg, seg), seg)
        qs = stacked(q_ref[here, :] * 0.125, half)
        do = do_ref[here, :]
        dos = stacked(do, half)
        prod = (do.astype(jnp.float32) * o_ref[here, :].astype(jnp.float32)).T
        delta = jnp.concatenate(
            [jnp.sum(prod[:half], axis=0, keepdims=True), jnp.sum(prod[half:], axis=0, keepdims=True)],
            axis=1,
        )
        lse = lse_ref[pl.ds(i, 1), :]
        leaf_bias = jnp.where(leaf > 0, 0.0, -1e30)

        def piece(keys, values, shift, mask):
            s = mm(keys, qs, NT)
            if mask:
                s = jnp.where(allowed, s, -1e30)
            if isinstance(shift, list):
                p = jnp.concatenate(
                    [jnp.exp(s[kb * seg : (kb + 1) * seg] - shift[kb]) for kb in range(TRUNK)], axis=0
                )
            else:
                p = jnp.exp(s - shift)
            ds = (p * (mm(values, dos, NT) - delta)).astype(low)
            p = p.astype(low)
            return (mm(p, dos), mm(ds, qs), ds)

        shifts = [lse - jnp.where(kb < count, 0.0, -1e30) for kb in range(TRUNK)]
        dv, dk, ds = piece(k_ref[tk, :], v_ref[tk, :], shifts, False)
        av[tk, :] += dv
        ak[tk, :] += dk
        dq = mm(k_trunk, ds)
        keys = k_ref[there, :]
        dv, dk, ds = piece(keys, v_ref[there, :], lse - leaf_bias, False)
        av[there, :] += dv
        ak[there, :] += dk
        dq = dq + mm(keys.T, ds)
        keys = k_ref[here, :]
        dv, dk, ds = piece(keys, v_ref[here, :], lse, True)
        av[here, :] += dv
        ak[here, :] += dk
        dq = dq + mm(keys.T, ds)
        dq_ref[here, :] = (unstack(dq, half, seg) * 0.125).T.astype(low)
        return 0

    lax.fori_loop(0, own // seg, one, 0)
    dk_ref[...] = ak[...].astype(low)
    dv_ref[...] = av[...].astype(low)


def attend(info, q, kv, seg):
    own, width = q.shape
    total = kv.shape[0]
    pairs = width // 128
    segs = own // seg
    lane = pl.BlockSpec((own, 128), lambda h: (0, h))
    return pl.pallas_call(
        functools.partial(attend_kernel, own, seg, HEAD_DIM),
        grid=(pairs,),
        in_specs=[
            pl.BlockSpec(memory_space=pltpu.SMEM),
            lane,
            pl.BlockSpec((total, 128), lambda h: (0, h)),
            pl.BlockSpec((total, 128), lambda h: (0, pairs + h)),
        ],
        out_specs=[lane, pl.BlockSpec((None, 8, 2 * seg), lambda h: (h, 0, 0))],
        out_shape=[
            jax.ShapeDtypeStruct((own, width), jnp.bfloat16),
            jax.ShapeDtypeStruct((pairs, 8, 2 * seg), jnp.float32),
        ],
        scratch_shapes=[
            pltpu.VMEM((TRUNK * seg, 2 * seg), jnp.float32),
            pltpu.VMEM((TRUNK * seg, 2 * seg), jnp.bfloat16),
        ],
        compiler_params=pltpu.CompilerParams(vmem_limit_bytes=32 << 20),
        cost_estimate=pl.CostEstimate(
            flops=4 * segs * 10 * seg * seg * width, bytes_accessed=8 << 20, transcendentals=0
        ),
        name="attend",
    )(info, q, kv, kv)


def attend_back(info, q, kv, o, do, lse, seg):
    own, width = q.shape
    total = kv.shape[0]
    pairs = width // 128
    segs = own // seg
    lane = pl.BlockSpec((own, 128), lambda h: (0, h))
    keys = pl.BlockSpec((total, 128), lambda h: (0, h))
    return pl.pallas_call(
        functools.partial(attend_back_kernel, own, seg, HEAD_DIM),
        grid=(pairs,),
        in_specs=[
            pl.BlockSpec(memory_space=pltpu.SMEM),
            lane,
            keys,
            pl.BlockSpec((total, 128), lambda h: (0, pairs + h)),
            lane,
            lane,
            pl.BlockSpec((None, 8, 2 * seg), lambda h: (h, 0, 0)),
        ],
        out_specs=[lane, keys, keys],
        out_shape=[
            jax.ShapeDtypeStruct((own, width), jnp.bfloat16),
            jax.ShapeDtypeStruct((total, width), jnp.bfloat16),
            jax.ShapeDtypeStruct((total, width), jnp.bfloat16),
        ],
        scratch_shapes=[
            pltpu.VMEM((total, 128), jnp.float32),
            pltpu.VMEM((total, 128), jnp.float32),
        ],
        compiler_params=pltpu.CompilerParams(vmem_limit_bytes=40 << 20),
        cost_estimate=pl.CostEstimate(
            flops=10 * segs * 10 * seg * seg * width, bytes_accessed=16 << 20, transcendentals=0
        ),
        name="attend_back",
    )(info, q, kv, kv, o, do, lse)


def expert_kernel(x_ref, xt_ref, d_ref, dt_ref, w_ref, o0_ref, s0_ref, o_ref, s_ref, dw_ref):
    low = jnp.bfloat16

    @pl.when(pl.program_id(0) == 0)
    def start():
        o_ref[...] = o0_ref[...]
        s_ref[...] = s0_ref[...]

    wg = w_ref[:, :PIECE]
    wu = w_ref[:, PIECE : 2 * PIECE]
    wd = w_ref[:, 2 * PIECE :]
    u = mm(x_ref[...], wg)
    up = mm(x_ref[...], wu)
    sigma = 1.0 / (1.0 + jnp.exp(-u))
    silu = u * sigma
    hidden = (silu * up).astype(low)
    o_ref[...] += mm(hidden, wd, NT)
    dh = mm(d_ref[...], wd)
    du = (dh * up * sigma * (1.0 + u * (1.0 - sigma))).astype(low)
    dup = (dh * silu).astype(low)
    s_ref[...] += mm(du, wg, NT) + mm(dup, wu, NT)
    dw_ref[:, :PIECE] = mm(xt_ref[...], du).astype(low)
    dw_ref[:, PIECE : 2 * PIECE] = mm(xt_ref[...], dup).astype(low)
    dw_ref[:, 2 * PIECE :] = mm(dt_ref[...], hidden).astype(low)


def expert_pass(x, xt, d, dt, w, o0, s0):
    rows, width = x.shape
    pieces = w.shape[1] // (3 * PIECE)
    whole = pl.BlockSpec((rows, width), lambda j: (0, 0))
    turned = pl.BlockSpec((width, rows), lambda j: (0, 0))
    strip = pl.BlockSpec((width, 3 * PIECE), lambda j: (0, j))
    return pl.pallas_call(
        expert_kernel,
        grid=(pieces,),
        in_specs=[whole, turned, whole, turned, strip, whole, whole],
        out_specs=[whole, whole, strip],
        out_shape=[
            jax.ShapeDtypeStruct((rows, width), jnp.float32),
            jax.ShapeDtypeStruct((rows, width), jnp.float32),
            jax.ShapeDtypeStruct(w.shape, jnp.bfloat16),
        ],
        compiler_params=pltpu.CompilerParams(vmem_limit_bytes=56 << 20),
        cost_estimate=pl.CostEstimate(
            flops=2 * 3 * rows * w.shape[0] * w.shape[1], bytes_accessed=30 << 20, transcendentals=0
        ),
        name="expert_pass",
    )(x, xt, d, dt, w, o0, s0)


def flip(x, axis, bit, size):
    return lax.ppermute(x, axis, [(i, i ^ bit) for i in range(size)])


def line_gather(x, size, position):
    after, before = [x], [x]
    for t in range(1, size):
        after.append(lax.ppermute(after[-1], "ctx", [(i, i + 1) for i in range(t - 1, size - 1)]))
        before.append(lax.ppermute(before[-1], "ctx", [(i, i - 1) for i in range(1, size - t + 1)]))
    out = jnp.zeros((size,) + x.shape, x.dtype)
    for k in range(size):
        block = x if k == 0 else jnp.where(position >= k, after[k], before[size - k])
        out = lax.dynamic_update_index_in_dim(out, block, (position - k) % size, 0)
    return out


def turn_gather(x, size, position):
    out = jnp.zeros((size,) + x.shape, x.dtype)
    out = lax.dynamic_update_index_in_dim(out, x, position, 0)
    for k in range(1, size):
        block = lax.ppermute(x, "ctx", [(i, (i + k) % size) for i in range(size)])
        out = lax.dynamic_update_index_in_dim(out, block, (position - k) % size, 0)
    return out


def line_sum(x, size, position):
    def part(index):
        index = jnp.clip(index, 0, size - 1)
        return lax.dynamic_index_in_dim(x, index, 0, keepdims=False)

    def add(a, b):
        return (a.astype(jnp.float32) + b.astype(jnp.float32)).astype(x.dtype)

    down = up = None
    for t in range(1, size):
        low = part(position - size + t)
        high = part(position + size - t)
        if t > 1:
            low, high = add(low, down), add(high, up)
        down = lax.ppermute(low, "ctx", [(i, i - 1) for i in range(size - t, size)])
        up = lax.ppermute(high, "ctx", [(i, i + 1) for i in range(0, t)])
    return part(position).astype(jnp.float32) + down.astype(jnp.float32) + up.astype(jnp.float32)


def turn_sum(x, size, position):
    total = lax.dynamic_index_in_dim(x, position, 0, keepdims=False).astype(jnp.float32)
    for k in range(1, size):
        block = lax.dynamic_index_in_dim(x, (position + k) % size, 0, keepdims=False)
        got = lax.ppermute(block, "ctx", [(i, (i + k) % size) for i in range(size)])
        total = total + got.astype(jnp.float32)
    return total


def by_core(
    tokens, gate_res, cotangent, parents, expert_ids, priority, w_qkv, w_out, w_router, attn_gain,
    ffn_gain, const_vec, w_gate_up, w_down,
):
    low, full = jnp.bfloat16, jnp.float32
    shard, ctx, tp = lax.axis_index("shard"), lax.axis_index("ctx"), lax.axis_index("tp")
    shards_n, ctx_n = lax.axis_size("shard"), lax.axis_size("ctx")
    trees, rows, width = tokens.shape
    rows_d = w_qkv.shape[0]
    seg = rows * ctx_n // parents.shape[1]
    own_segs = rows // seg
    edge = KEY_SEGS * seg - 2 * rows

    def own_tree(x):
        return lax.dynamic_index_in_dim(x, tp, 0, keepdims=False)

    def both_trees(x, other):
        ordered = jnp.stack([x, other])
        return jnp.where(tp == 0, ordered, ordered[::-1])

    def swap(x):
        return flip(x, "tp", 1, 2)

    x_own = own_tree(tokens)
    ends = [(i, i + 1) for i in range(ctx_n - 1)]
    near_head = lax.ppermute(x_own[:edge], "ctx", ends)
    near_tail = lax.ppermute(x_own[edge:], "ctx", ends[:-1])
    near = jnp.concatenate([near_head, near_tail], axis=0)
    mid = lax.ppermute(near, "ctx", ends[1:])
    far = lax.ppermute(mid, "ctx", ends[2:])

    mine = jnp.stack([w_qkv[:, 0], w_qkv[:, 1], w_qkv[:, 2], w_out])
    matrix = turn_gather(lax.dynamic_index_in_dim(mine, shard, 0, keepdims=False), ctx_n, ctx)
    matrix = matrix.reshape(width, -1)
    plane = [matrix] + [flip(matrix, "shard", k, shards_n) for k in range(1, shards_n)]
    plane = [jnp.concatenate([m, swap(m)], axis=1) for m in plane]
    plane = jnp.stack(plane)
    weight_q, weight_k, weight_v, weight_o = [
        lax.dynamic_index_in_dim(plane, m ^ shard, 0, keepdims=False) for m in range(4)
    ]
    weight_kv = jnp.concatenate([weight_k, weight_v], axis=1)

    small = jnp.concatenate(
        [w_router.T, attn_gain[None], ffn_gain[None], const_vec.T], axis=0
    )
    small = turn_gather(small, ctx_n, ctx).transpose(1, 0, 2).reshape(small.shape[0], width)
    all_experts = w_router.shape[1]
    router_t = small[:all_experts]
    gain_a = small[all_experts].astype(full)
    gain_f = small[all_experts + 1].astype(full)
    const_t = small[all_experts + 2 :].astype(full)

    units = w_down.shape[2]
    pieces = units // PIECE

    def packed(e):
        gu = lax.dynamic_index_in_dim(w_gate_up, e, 1, keepdims=False)
        dn = lax.dynamic_index_in_dim(w_down, e, 1, keepdims=False)
        three = jnp.concatenate([gu, dn[:, None]], axis=1).reshape(rows_d, 3, pieces, PIECE)
        return three.transpose(0, 2, 1, 3).reshape(rows_d, 3 * units)

    half_near = packed(tp)
    half_far = swap(packed(1 - tp))
    expert_near = line_gather(half_near, ctx_n, ctx).reshape(width, 3 * units)
    expert_far = line_gather(half_far, ctx_n, ctx).reshape(width, 3 * units)

    capacity = trees * rows * 2 // all_experts
    experts = shards_n * w_gate_up.shape[1]
    padded = -(-capacity // 16) * 16
    ids_block = expert_ids.reshape(trees * rows, 2)
    flat = ids_block.reshape(-1)
    order = (2 * priority[0, 0][:, None] + jnp.arange(2, dtype=jnp.int32)[None, :]).reshape(-1)
    earlier = (flat[:, None] == flat[None, :]) & (order[None, :] < order[:, None])
    ranks = jnp.sum(earlier.astype(jnp.int32), axis=1)
    kept = (flat < experts) & (ranks < capacity) & (flat % 2 == tp)
    place = jnp.where(kept, ((flat // 2) ^ shard) * padded + ranks, -1).reshape(trees, rows, 2)
    place = jnp.where(tp == 0, place, place[::-1]).reshape(trees * rows, 2).T
    slot = jnp.arange(shards_n * padded, dtype=jnp.int32)
    table = slot[None, :, None] == place[:, None, :]
    routed = (table[0] | table[1]).astype(low)

    block0 = jnp.where(ctx == 0, x_own, jnp.where(ctx == 1, near, jnp.where(ctx == 2, mid, far)))
    block1 = jnp.where(ctx == 1, x_own, jnp.where(ctx == 2, near, mid))
    block2 = jnp.where(ctx == 2, x_own[:edge], near[:edge])
    x_all = jnp.concatenate([x_own, block0, block1, block2], axis=0).astype(full)
    inv_all = lax.rsqrt(jnp.mean(x_all * x_all, axis=-1, keepdims=True) + eps)
    unit_all = x_all * inv_all
    normed = (unit_all * gain_a).astype(low)
    q = mm(normed[:rows], weight_q).astype(low)
    kv = mm(normed, weight_kv).astype(low)

    seg_id = ctx * own_segs + jnp.arange(own_segs, dtype=jnp.int32)
    parent = jnp.take(own_tree(parents), seg_id)
    leaf = (seg_id >= KEY_SEGS).astype(jnp.int32)
    info = jnp.stack([jnp.minimum(seg_id, TRUNK), jnp.where(leaf > 0, parent, TRUNK), leaf], axis=1)
    o_low, lse = attend(info, q, kv, seg)

    inputs = x_own.astype(full)
    mixed = inputs + mm(o_low, weight_o, NT)
    inv_second = lax.rsqrt(jnp.mean(mixed * mixed, axis=-1, keepdims=True) + eps)
    second_unit = mixed * inv_second
    second = (second_unit * gain_f).astype(low)

    logits = mm(second, router_t, NT) + own_tree(gate_res)
    expo = jnp.exp(logits - jnp.max(logits, axis=-1, keepdims=True))
    probs = expo / jnp.sum(expo, axis=-1, keepdims=True)
    ids = own_tree(expert_ids)
    selector = (ids[:, :, None] == jnp.arange(all_experts, dtype=jnp.int32)).astype(full)
    picked = jnp.sum(selector * probs[:, None, :], axis=-1)
    picked_total = jnp.sum(picked, axis=-1, keepdims=True)
    gates = picked / picked_total

    second_both = jnp.concatenate([second, swap(second)], axis=0)
    gates_both = jnp.concatenate([gates.T, swap(gates.T)], axis=1)
    g_own = own_tree(cotangent)
    g_other = lax.dynamic_index_in_dim(cotangent, 1 - tp, 0, keepdims=False)
    slots = mm(routed, second_both).astype(low).reshape(shards_n, padded, width)
    g_slots = mm(routed, jnp.concatenate([g_own, g_other], axis=0))
    weighted = jnp.where(table[0], gates_both[0][None, :], 0.0) + jnp.where(
        table[1], gates_both[1][None, :], 0.0
    )
    gate_slots = jnp.sum(weighted, axis=1, keepdims=True)
    d_slots = (g_slots * gate_slots).astype(low).reshape(shards_n, padded, width)
    x_in = [slots[0]] + [flip(slots[k], "shard", k, shards_n) for k in range(1, shards_n)]
    d_in = [d_slots[0]] + [flip(d_slots[k], "shard", k, shards_n) for k in range(1, shards_n)]
    x_in = jnp.concatenate(x_in, axis=0)
    d_in = jnp.concatenate(d_in, axis=0)

    blank = jnp.zeros(x_in.shape, full)
    xt, dt = x_in.T, d_in.T
    out_sum, ds_sum, dw_near = expert_pass(x_in, xt, d_in, dt, expert_near, blank, blank)
    out_sum, ds_sum, dw_far = expert_pass(x_in, xt, d_in, dt, expert_far, out_sum, ds_sum)
    out_low = out_sum.astype(low).reshape(shards_n, padded, width)
    ds_low = ds_sum.astype(low).reshape(shards_n, padded, width)
    out_back = [out_low[0]] + [flip(out_low[k], "shard", k, shards_n) for k in range(1, shards_n)]
    ds_back = [ds_low[0]] + [flip(ds_low[k], "shard", k, shards_n) for k in range(1, shards_n)]
    out_back = jnp.concatenate(out_back, axis=0)
    ds_back = jnp.concatenate(ds_back, axis=0)

    rows_tn = (((0,), (0,)), ((), ()))
    combined = mm(weighted.astype(low), out_back, rows_tn)
    d_routed = mm(routed, ds_back, rows_tn)
    gate_dots = jnp.sum(g_slots * out_back.astype(full), axis=1)
    d_gate_pairs = jnp.sum(jnp.where(table, gate_dots[None, :, None], 0.0), axis=1)
    combined = combined[:rows] + swap(combined[rows:].astype(low)).astype(full)
    d_routed = d_routed[:rows] + swap(d_routed[rows:].astype(low)).astype(full)
    d_gate_pairs = d_gate_pairs[:, :rows] + swap(d_gate_pairs[:, rows:])

    second_f = second.astype(full)
    g = g_own.astype(full)
    copy_flag = selector[:, :, experts + 1]
    const_flags = selector[:, :, experts + 2 :]
    copy_gate = jnp.sum(gates * copy_flag, axis=1, keepdims=True)
    const_gate = jnp.sum(gates[:, :, None] * const_flags, axis=1)
    mixed_out = (
        mixed
        + combined
        + copy_gate * second_f
        + const_gate[:, :1] * const_t[0][None]
        + const_gate[:, 1:] * const_t[1][None]
    )
    g_second = jnp.sum(g * second_f, axis=1, keepdims=True)
    g_const = jnp.stack([jnp.sum(g * const_t[k][None], axis=1) for k in range(2)], axis=1)
    d_gates = (
        d_gate_pairs.T
        + copy_flag * g_second
        + jnp.sum(const_flags * g_const[:, None, :], axis=-1)
    )
    d_picked = (d_gates - jnp.sum(d_gates * gates, axis=-1, keepdims=True)) / picked_total
    d_probs = jnp.sum(d_picked[:, :, None] * selector, axis=1)
    d_logits = probs * (d_probs - jnp.sum(probs * d_probs, axis=-1, keepdims=True))
    high = lax.Precision.HIGHEST
    d_router = jnp.einsum("tk,td->kd", d_logits, second_f, precision=high)
    d_const = jnp.einsum("tk,td->kd", const_gate, g, precision=high)
    d_second = copy_gate * g + d_routed + jnp.dot(d_logits, router_t.astype(full), precision=high)
    d_gain_f = jnp.sum(d_second * second_unit, axis=0)
    d_unit = d_second * gain_f
    d_mixed = g + inv_second * (
        d_unit - second_unit * jnp.mean(d_unit * second_unit, axis=-1, keepdims=True)
    )
    d_attn = d_mixed.astype(low)
    d_o = mm(d_attn, weight_o).astype(low)
    d_weight_o = mm(d_attn, o_low, rows_tn)

    dq, dk, dv = attend_back(info, q, kv, o_low, d_o, lse, seg)
    d_weight_q = mm(normed[:rows], dq, rows_tn)
    d_weight_k = mm(normed, dk, rows_tn)
    d_weight_v = mm(normed, dv, rows_tn)
    d_keys = mm(dk, weight_k, NT) + mm(dv, weight_v, NT)
    d_near = d_keys[:rows] + mm(dq, weight_q, NT)
    d_gain_a = jnp.sum(d_near * unit_all[:rows], axis=0) + jnp.sum(
        d_keys[rows:] * unit_all[rows:], axis=0
    )

    def send(x, pairs):
        return lax.ppermute(x.astype(low), "ctx", pairs).astype(full)

    part0 = d_keys[rows : 2 * rows]
    part1 = d_keys[2 * rows : 3 * rows]
    part2 = d_keys[3 * rows :]
    for hop in range(ctx_n - 1, 0, -1):
        part0 = part0 + send(part0, [(hop, hop - 1)])
        if hop >= 2:
            part1 = part1 + send(part1, [(hop, hop - 1)])
        if hop >= 3:
            part2 = part2 + send(part2, [(hop, hop - 1)])
    part2 = jnp.concatenate([part2, jnp.zeros((rows - edge, width), full)], axis=0)
    extra = jnp.where(ctx == 0, part0, jnp.where(ctx == 1, part1, jnp.where(ctx == 2, part2, 0.0)))
    d_normed = d_near + extra
    unit_own, inv_own = unit_all[:rows], inv_all[:rows]
    d_first = d_normed * gain_a
    d_tokens = d_mixed + inv_own * (
        d_first - unit_own * jnp.mean(d_first * unit_own, axis=-1, keepdims=True)
    )

    shared = jnp.stack([d_weight_q, d_weight_k, d_weight_v, d_weight_o]).astype(low)
    part = width // 2
    shared = shared[:, :, :part].astype(full) + swap(shared[:, :, part:]).astype(full)
    shared = shared.astype(low)

    def numbered(k):
        return lax.dynamic_index_in_dim(shared, shard ^ k, 0, keepdims=False)

    total = numbered(0).astype(full)
    for k in range(1, shards_n):
        total = total + flip(numbered(k), "shard", k, shards_n).astype(full)
    total = turn_sum(total.astype(low).reshape(ctx_n, rows_d, part), ctx_n, ctx).astype(low)
    pieces4 = jnp.stack([total] + [flip(total, "shard", k, shards_n) for k in range(1, shards_n)])
    d_q, d_k, d_v, d_w_out = [
        lax.dynamic_index_in_dim(pieces4, m ^ shard, 0, keepdims=False).astype(full) for m in range(4)
    ]
    d_w_qkv = jnp.stack([d_q, d_k, d_v], axis=1)

    tiny = jnp.concatenate([d_router, d_gain_a[None], d_gain_f[None], d_const], axis=0)
    tiny = tiny + swap(tiny)
    for axis, size in (("shard", shards_n), ("ctx", ctx_n)):
        bit = 1
        while bit < size:
            tiny = tiny + flip(tiny, axis, bit, size)
            bit *= 2
    tiny = lax.dynamic_slice_in_dim(tiny, ctx * rows_d, rows_d, 1)

    g_near = line_sum(dw_near.reshape(ctx_n, rows_d, 3 * units), ctx_n, ctx)
    g_far = line_sum(dw_far.reshape(ctx_n, rows_d, 3 * units), ctx_n, ctx)
    g_far = swap(g_far.astype(low)).astype(full)

    def unpacked(x):
        return x.reshape(rows_d, pieces, 3, PIECE).transpose(0, 2, 1, 3).reshape(rows_d, 3, units)

    both = jnp.stack([unpacked(g_near), unpacked(g_far)], axis=1)
    both = jnp.where(tp == 0, both, both[:, ::-1])
    return (
        both_trees(mixed_out, swap(mixed_out)),
        both_trees(d_tokens, swap(d_tokens)),
        both_trees(d_logits, swap(d_logits)),
        d_w_qkv,
        d_w_out,
        tiny[:all_experts].T,
        tiny[all_experts],
        tiny[all_experts + 1],
        tiny[all_experts + 2 :].T,
        both[:, :, :2],
        both[:, :, 2],
    )


def program(tokens, gate_res, cotangent, parents, expert_ids, priority, w_qkv, *weights):
    trees, rows, width = tokens.shape
    ctx_n = lax.axis_size("ctx")
    seg = rows * ctx_n // parents.shape[1]
    fits = (
        ctx_n == 4
        and lax.axis_size("shard") == 4
        and lax.axis_size("tp") == 2
        and trees == 2
        and seg == 128
        and rows % seg == 0
        and 2 * rows < KEY_SEGS * seg <= 3 * rows
        and weights[-1].shape[1] == 2
    )
    chosen = by_core if fits else shards
    return chosen(tokens, gate_res, cotangent, parents, expert_ids, priority, w_qkv, *weights)


def solution(mesh):
    return jax.shard_map(
        program,
        mesh=mesh,
        in_specs=(
            P("shard", "ctx", None),
            P("shard", "ctx", None),
            P("shard", "ctx", None),
            P("shard", None),
            P("shard", "ctx", None),
            P("shard", "ctx", None),
            P("ctx", None, "tp"),
            P("ctx", "tp"),
            P("ctx", None),
            P("ctx"),
            P("ctx"),
            P("ctx", None),
            P("ctx", "shard", None, "tp"),
            P("ctx", "shard", "tp"),
        ),
        out_specs=(
            P("shard", "ctx", None),
            P("shard", "ctx", None),
            P("shard", "ctx", None),
            P("ctx", None, "tp"),
            P("ctx", "tp"),
            P("ctx", None),
            P("ctx"),
            P("ctx"),
            P("ctx", None),
            P("ctx", "shard", None, "tp"),
            P("ctx", "shard", "tp"),
        ),
        check_vma=False,
    )
```

```python
import functools
import math

import jax
import jax.numpy as jnp
from jax import lax
from jax.experimental import pallas as pl
from jax.experimental.pallas import tpu as pltpu
from jax.sharding import PartitionSpec as P

HEAD_DIM = 64


eps = 1e-06
score_scale = 0.125


def ancestry(parent_row):
    seg_count = parent_row.shape[0]
    position = jnp.arange(seg_count, dtype=jnp.int32)
    linked = (parent_row[:, None] == position[None, :]) | (position[:, None] == position[None, :])
    reach = linked.astype(jnp.float32)
    for repeat in range(seg_count.bit_length()):
        reach = jnp.minimum(jnp.dot(reach, reach, precision=lax.Precision.HIGHEST), 1.0)
    return reach


def path_rows(positions, seg_len, ancestors):
    onehot = (
        (positions // seg_len)[:, None] == jnp.arange(ancestors.shape[0], dtype=jnp.int32)[None, :]
    ).astype(jnp.float32)
    return jnp.dot(onehot, ancestors)


def allowed_block(query_rows, query_pos, key_start, key_count, seg_len):
    key_pos = key_start + jnp.arange(key_count, dtype=jnp.int32)
    key_onehot = (
        (key_pos // seg_len)[:, None] == jnp.arange(query_rows.shape[1], dtype=jnp.int32)[None, :]
    ).astype(jnp.float32)
    linked = jnp.dot(query_rows, key_onehot.T) > 0.5
    return (linked & (key_pos[None, :] <= query_pos[:, None]))[None]


def slot_table(picked_ids, ranking, experts, capacity):
    count_rows = picked_ids.shape[0]
    flat_ids = picked_ids.reshape(-1)
    rank_key = (2 * ranking[:, None] + jnp.arange(2, dtype=jnp.int32)[None, :]).reshape(-1)
    earlier = (flat_ids[:, None] == flat_ids[None, :]) & (rank_key[None, :] < rank_key[:, None])
    ranks = jnp.sum(earlier.astype(jnp.int32), axis=1)
    kept = (flat_ids < experts) & (ranks < capacity)
    target = jnp.where(kept, flat_ids * capacity + ranks, -1).reshape(count_rows, 2)
    slot_index = jnp.arange(experts * capacity, dtype=jnp.int32)
    return slot_index[None, :, None] == target.T[:, None, :]


def block_scores(queries, keys_blk):
    return (
        jnp.einsum("qhe,khe->hqk", queries, keys_blk, preferred_element_type=jnp.float32)
        * score_scale
    )


def softmax_grads(queries, grads_out, stat_lse, stat_delta, keys_blk, values_blk, mask):
    prob = jnp.where(mask, jnp.exp(block_scores(queries, keys_blk) - stat_lse[:, :, None]), 0.0)
    dprob = jnp.einsum("qhe,khe->hqk", grads_out, values_blk, preferred_element_type=jnp.float32)
    dscore = (prob * (dprob - stat_delta[:, :, None])).astype(jnp.bfloat16)
    return (prob.astype(jnp.bfloat16), dscore)


def shards(
    tokens,
    gate_res,
    cotangent,
    parents,
    expert_ids,
    priority,
    w_qkv,
    w_out,
    w_router,
    attn_gain,
    ffn_gain,
    const_vec,
    w_gate_up,
    w_down,
):
    full_qkv, full_out, full_router, full_again, full_fgain, full_const, full_gu, full_down = (
        lax.all_gather(w_qkv, "ctx", axis=0, tiled=True),
        lax.all_gather(w_out, "ctx", axis=0, tiled=True),
        lax.all_gather(w_router, "ctx", axis=0, tiled=True),
        lax.all_gather(attn_gain, "ctx", axis=0, tiled=True),
        lax.all_gather(ffn_gain, "ctx", axis=0, tiled=True),
        lax.all_gather(const_vec, "ctx", axis=0, tiled=True),
        lax.all_gather(w_gate_up, "ctx", axis=0, tiled=True),
        lax.all_gather(w_down, "ctx", axis=0, tiled=True),
    )
    tree_count, rows, model_width = tokens.shape
    tok_rows = tree_count * rows
    inputs = tokens.reshape(tok_rows, model_width).astype(jnp.float32)
    local_width = full_out.shape[1]
    local_heads = local_width // HEAD_DIM
    ctx_index = lax.axis_index("ctx")
    tree_len = rows * lax.axis_size("ctx")
    ancestors_all = jax.vmap(ancestry)(parents)
    seg_len = tree_len // parents.shape[1]
    key_block = math.gcd(tree_len, 512)
    starts = jnp.arange(tree_len // key_block, dtype=jnp.int32) * key_block
    key_start_own = ctx_index * rows
    query_pos = key_start_own + jnp.arange(rows, dtype=jnp.int32)
    query_rows_all = jax.vmap(lambda anc: path_rows(query_pos, seg_len, anc))(ancestors_all)
    inv_first = lax.rsqrt(jnp.mean(inputs * inputs, axis=-1, keepdims=True) + eps)
    first_unit = inputs * inv_first
    first_gain = full_again.astype(jnp.float32)
    normed = (first_unit * first_gain).astype(jnp.bfloat16)
    projected = jnp.einsum("nd,dke->nke", normed, full_qkv, preferred_element_type=jnp.float32)
    q_low = projected[:, 0].astype(jnp.bfloat16)
    k_low = projected[:, 1].astype(jnp.bfloat16)
    v_low = projected[:, 2].astype(jnp.bfloat16)
    keys_all, values_all = (
        lax.all_gather(k_low.reshape(tree_count, rows, local_width), "ctx", axis=1, tiled=True),
        lax.all_gather(v_low.reshape(tree_count, rows, local_width), "ctx", axis=1, tiled=True),
    )
    q_heads = q_low.reshape(tree_count, rows, local_heads, HEAD_DIM)
    k_heads = keys_all.reshape(tree_count, tree_len, local_heads, HEAD_DIM)
    v_heads = values_all.reshape(tree_count, tree_len, local_heads, HEAD_DIM)

    def tree_forward(q_one, k_one, v_one, rows_one):

        def stat_step(carry, start):
            running_top, running_sum = carry
            keys_blk = lax.dynamic_slice_in_dim(k_one, start, key_block, 0)
            mask = allowed_block(rows_one, query_pos, start, key_block, seg_len)
            masked = jnp.where(mask, block_scores(q_one, keys_blk), -1e30)
            new_top = jnp.maximum(running_top, jnp.max(masked, axis=2))
            expo = jnp.where(mask, jnp.exp(masked - new_top[:, :, None]), 0.0)
            running_sum = running_sum * jnp.exp(running_top - new_top) + jnp.sum(expo, axis=2)
            return ((new_top, running_sum), None)

        start_top = jnp.full((local_heads, rows), -1e30, jnp.float32)
        (final_top, final_sum), unused = lax.scan(
            stat_step, (start_top, jnp.zeros_like(start_top)), starts
        )
        lse_one = final_top + jnp.log(final_sum)

        def out_step(accum, start):
            keys_blk = lax.dynamic_slice_in_dim(k_one, start, key_block, 0)
            values_blk = lax.dynamic_slice_in_dim(v_one, start, key_block, 0)
            mask = allowed_block(rows_one, query_pos, start, key_block, seg_len)
            prob = jnp.where(
                mask, jnp.exp(block_scores(q_one, keys_blk) - lse_one[:, :, None]), 0.0
            ).astype(jnp.bfloat16)
            return (
                accum
                + jnp.einsum("hqk,khe->qhe", prob, values_blk, preferred_element_type=jnp.float32),
                None,
            )

        attended_one, unused = lax.scan(
            out_step, jnp.zeros((rows, local_heads, HEAD_DIM), jnp.float32), starts
        )
        return (attended_one, lse_one)

    attended, lse = jax.vmap(tree_forward)(q_heads, k_heads, v_heads, query_rows_all)
    attended_low = attended.reshape(tok_rows, local_width).astype(jnp.bfloat16)
    attn_part = jnp.einsum("nh,dh->nd", attended_low, full_out, preferred_element_type=jnp.float32)
    attn_sum = lax.psum(attn_part.astype(jnp.bfloat16), "tp").astype(jnp.float32)
    mixed = inputs + attn_sum
    inv_second = lax.rsqrt(jnp.mean(mixed * mixed, axis=-1, keepdims=True) + eps)
    second_unit = mixed * inv_second
    second_gain = full_fgain.astype(jnp.float32)
    second_low = (second_unit * second_gain).astype(jnp.bfloat16)
    second_float = second_low.astype(jnp.float32)
    logits = jnp.dot(
        second_low, full_router, preferred_element_type=jnp.float32
    ) + gate_res.reshape(tok_rows, -1)
    expo_logits = jnp.exp(logits - jnp.max(logits, axis=-1, keepdims=True))
    probs = expo_logits / jnp.sum(expo_logits, axis=-1, keepdims=True)
    experts = lax.axis_size("shard") * w_gate_up.shape[1]
    every_expert = experts + 4
    capacity = tok_rows * 2 // every_expert
    picked_ids = expert_ids.reshape(tok_rows, 2)
    selector = (picked_ids[:, :, None] == jnp.arange(every_expert, dtype=jnp.int32)).astype(
        jnp.float32
    )
    picked = jnp.sum(selector * probs[:, None, :], axis=-1)
    picked_total = jnp.sum(picked, axis=-1, keepdims=True)
    gates = picked / picked_total
    table = slot_table(picked_ids, priority[0, 0], experts, capacity).astype(jnp.bfloat16)
    routed = table[0] + table[1]
    send_slots = jnp.einsum(
        "et,td->ed", routed, second_low, preferred_element_type=jnp.float32
    ).astype(jnp.bfloat16)
    send_slots = send_slots.reshape(experts, 1, capacity, model_width)
    arrived = lax.all_to_all(send_slots, "shard", split_axis=0, concat_axis=1, tiled=True)
    gate_up = jnp.einsum("jsrd,djgf->jsrgf", arrived, full_gu, preferred_element_type=jnp.float32)
    hidden_low = (jax.nn.silu(gate_up[:, :, :, 0]) * gate_up[:, :, :, 1]).astype(jnp.bfloat16)
    partial_out = jnp.einsum(
        "jsrf,djf->jsrd", hidden_low, full_down, preferred_element_type=jnp.float32
    )
    summed = lax.psum(partial_out.astype(jnp.bfloat16), "tp")
    returned = lax.all_to_all(summed, "shard", split_axis=1, concat_axis=0, tiled=True)
    returned, kept_slots = (returned, arrived)
    out_slots = returned.reshape(experts * capacity, model_width)
    ffn_values = jnp.einsum("cet,ed->ctd", table, out_slots, preferred_element_type=jnp.float32)
    copy_flag = selector[:, :, experts + 1]
    const_flags = selector[:, :, experts + 2 :]
    const_float = full_const.astype(jnp.float32)
    fixed_terms = jnp.einsum(
        "nck,dk->cnd", const_flags, const_float, precision=lax.Precision.HIGHEST
    )
    values_pair = ffn_values + copy_flag.T[:, :, None] * second_float[None] + fixed_terms
    mixed_out = mixed + jnp.sum(gates.T[:, :, None] * values_pair, axis=0)
    grad_out = cotangent.reshape(tok_rows, model_width).astype(jnp.float32)
    weighted = gates.T[:, :, None] * grad_out[None]
    d_gates = jnp.einsum("cnd,nd->nc", values_pair, grad_out)
    d_const = jnp.einsum("nck,cnd->dk", const_flags, weighted, precision=lax.Precision.HIGHEST)
    d_out_slots = jnp.einsum(
        "cet,ctd->ed", table.astype(jnp.float32), weighted, precision=lax.Precision.HIGHEST
    )
    d_out_low = d_out_slots.astype(jnp.bfloat16).reshape(experts, 1, capacity, model_width)
    d_picked = (d_gates - jnp.sum(d_gates * gates, axis=-1, keepdims=True)) / picked_total
    d_probs = jnp.einsum("nc,nck->nk", d_picked, selector)
    d_logits = probs * (d_probs - jnp.sum(probs * d_probs, axis=-1, keepdims=True))
    d_router_w = jnp.dot(second_float.T, d_logits, precision=lax.Precision.HIGHEST)
    d_second = jnp.sum(copy_flag.T[:, :, None] * weighted, axis=0)
    d_second = d_second + jnp.dot(
        d_logits, full_router.astype(jnp.float32).T, precision=lax.Precision.HIGHEST
    )
    arrived_grad = lax.all_to_all(d_out_low, "shard", split_axis=0, concat_axis=1, tiled=True)
    gate_up = jnp.einsum(
        "jsrd,djgf->jsrgf", kept_slots, full_gu, preferred_element_type=jnp.float32
    )
    gate_part = gate_up[:, :, :, 0]
    up_part = gate_up[:, :, :, 1]
    sigma = jax.nn.sigmoid(gate_part)
    silu_part = gate_part * sigma
    hidden_low = (silu_part * up_part).astype(jnp.bfloat16)
    d_hidden = jnp.einsum(
        "jsrd,djf->jsrf", arrived_grad, full_down, preferred_element_type=jnp.float32
    )
    d_gate_part = d_hidden * up_part * sigma * (1.0 + gate_part * (1.0 - sigma))
    d_up_part = d_hidden * silu_part
    d_gate_up_low = jnp.stack([d_gate_part, d_up_part], axis=3).astype(jnp.bfloat16)
    d_slot_part = jnp.einsum(
        "jsrgf,djgf->jsrd", d_gate_up_low, full_gu, preferred_element_type=jnp.float32
    )
    d_slot_sum = lax.psum(d_slot_part.astype(jnp.bfloat16), "tp")
    d_slot_back = lax.all_to_all(d_slot_sum, "shard", split_axis=1, concat_axis=0, tiled=True)
    d_gate_up_w = jnp.einsum(
        "jsrd,jsrgf->djgf", kept_slots, d_gate_up_low, preferred_element_type=jnp.float32
    )
    d_down_w = jnp.einsum(
        "jsrd,jsrf->djf", arrived_grad, hidden_low, preferred_element_type=jnp.float32
    )
    d_second = d_second + jnp.einsum(
        "et,ed->td",
        routed,
        d_slot_back.reshape(experts * capacity, model_width),
        preferred_element_type=jnp.float32,
    )
    d_second_gain = jnp.sum(d_second * second_unit, axis=0)
    d_second_unit = d_second * second_gain
    d_mixed = grad_out + inv_second * (
        d_second_unit - second_unit * jnp.mean(d_second_unit * second_unit, axis=-1, keepdims=True)
    )
    d_attn_low = d_mixed.astype(jnp.bfloat16)
    d_out_w = jnp.einsum("nd,nh->dh", d_attn_low, attended_low, preferred_element_type=jnp.float32)
    d_attended = jnp.einsum("nd,dh->nh", d_attn_low, full_out, preferred_element_type=jnp.float32)
    do_low = d_attended.astype(jnp.bfloat16)
    do_heads = do_low.reshape(tree_count, rows, local_heads, HEAD_DIM)
    delta = jnp.einsum("tqhe,tqhe->thq", do_heads.astype(jnp.float32), attended)

    def tree_both(q_one, k_one, v_one, do_one, lse_one, delta_one, rows_one):

        def both_step(dq_accum, start):
            keys_blk = lax.dynamic_slice_in_dim(k_one, start, key_block, 0)
            values_blk = lax.dynamic_slice_in_dim(v_one, start, key_block, 0)
            mask = allowed_block(rows_one, query_pos, start, key_block, seg_len)
            prob_low, dscore = softmax_grads(
                q_one, do_one, lse_one, delta_one, keys_blk, values_blk, mask
            )
            dq_accum = dq_accum + jnp.einsum(
                "hqk,khe->qhe", dscore, keys_blk, preferred_element_type=jnp.float32
            )
            dkey = (
                jnp.einsum("hqk,qhe->khe", dscore, q_one, preferred_element_type=jnp.float32)
                * score_scale
            )
            dval = jnp.einsum("hqk,qhe->khe", prob_low, do_one, preferred_element_type=jnp.float32)
            return (
                dq_accum,
                jnp.stack(
                    [dkey.reshape(key_block, local_width), dval.reshape(key_block, local_width)],
                    axis=1,
                ),
            )

        dq_one, terms_one = lax.scan(
            both_step, jnp.zeros((rows, local_heads, HEAD_DIM), jnp.float32), starts
        )
        return (dq_one, terms_one.reshape(tree_len, 2, local_width))

    dq_total, key_terms = jax.vmap(tree_both)(
        q_heads, k_heads, v_heads, do_heads, lse, delta, query_rows_all
    )
    key_sums = lax.psum_scatter(
        key_terms.astype(jnp.bfloat16), "ctx", scatter_dimension=1, tiled=True
    ).astype(jnp.float32)
    key_grad = key_sums[:, :, 0].reshape(tok_rows, local_width)
    value_grad = key_sums[:, :, 1].reshape(tok_rows, local_width)
    query_grad = (dq_total * score_scale).reshape(tok_rows, local_width)
    d_qkv_low = jnp.stack([query_grad, key_grad, value_grad], axis=1).astype(jnp.bfloat16)
    d_qkv_w = jnp.einsum("nd,nke->dke", normed, d_qkv_low, preferred_element_type=jnp.float32)
    d_normed_part = jnp.einsum(
        "nke,dke->nd", d_qkv_low, full_qkv, preferred_element_type=jnp.float32
    )
    d_normed = lax.psum(d_normed_part.astype(jnp.bfloat16), "tp").astype(jnp.float32)
    d_first_gain = jnp.sum(d_normed * first_unit, axis=0)
    d_first_unit = d_normed * first_gain
    d_inputs = d_mixed + inv_first * (
        d_first_unit - first_unit * jnp.mean(d_first_unit * first_unit, axis=-1, keepdims=True)
    )
    summed_grads = (
        lax.psum_scatter(
            d_qkv_w.astype(jnp.bfloat16), "ctx", scatter_dimension=0, tiled=True
        ).astype(jnp.float32),
        lax.psum_scatter(
            d_out_w.astype(jnp.bfloat16), "ctx", scatter_dimension=0, tiled=True
        ).astype(jnp.float32),
        lax.psum_scatter(
            d_router_w.astype(jnp.bfloat16), "ctx", scatter_dimension=0, tiled=True
        ).astype(jnp.float32),
        lax.psum_scatter(
            d_first_gain.astype(jnp.bfloat16), "ctx", scatter_dimension=0, tiled=True
        ).astype(jnp.float32),
        lax.psum_scatter(
            d_second_gain.astype(jnp.bfloat16), "ctx", scatter_dimension=0, tiled=True
        ).astype(jnp.float32),
        lax.psum_scatter(
            d_const.astype(jnp.bfloat16), "ctx", scatter_dimension=0, tiled=True
        ).astype(jnp.float32),
        lax.psum_scatter(
            d_gate_up_w.astype(jnp.bfloat16), "ctx", scatter_dimension=0, tiled=True
        ).astype(jnp.float32),
        lax.psum_scatter(
            d_down_w.astype(jnp.bfloat16), "ctx", scatter_dimension=0, tiled=True
        ).astype(jnp.float32),
    )
    shared = (
        lax.psum(summed_grads[0].astype(jnp.bfloat16), "shard").astype(jnp.float32),
        lax.psum(summed_grads[1].astype(jnp.bfloat16), "shard").astype(jnp.float32),
        lax.psum(summed_grads[2].astype(jnp.bfloat16), "shard").astype(jnp.float32),
        lax.psum(summed_grads[3].astype(jnp.bfloat16), "shard").astype(jnp.float32),
        lax.psum(summed_grads[4].astype(jnp.bfloat16), "shard").astype(jnp.float32),
        lax.psum(summed_grads[5].astype(jnp.bfloat16), "shard").astype(jnp.float32),
    )
    out_rows = mixed_out.reshape(tree_count, rows, model_width)
    grad_rows = d_inputs.reshape(tree_count, rows, model_width)
    logit_rows = d_logits.reshape(tree_count, rows, every_expert)
    return (
        out_rows,
        grad_rows,
        logit_rows,
        shared[0],
        shared[1],
        shared[2],
        shared[3],
        shared[4],
        shared[5],
        summed_grads[6],
        summed_grads[7],
    )


NT = (((1,), (1,)), ((), ()))
NN = (((1,), (0,)), ((), ()))
TRUNK = 8
KEY_SEGS = 12
PIECE = 256
SENT = (0, 2, 1, 3)


def mm(a, b, dims=NN):
    return lax.dot_general(a, b, dims, preferred_element_type=jnp.float32)


def stacked(rows, half):
    first = lax.broadcasted_iota(jnp.int32, rows.shape, 1) < half
    blank = jnp.zeros_like(rows)
    return jnp.concatenate([jnp.where(first, rows, blank), jnp.where(first, blank, rows)], axis=0)


def unstack(wide, half, seg):
    return jnp.concatenate([wide[:half, :seg], wide[half:, seg:]], axis=0)


def causal(seg):
    row = lax.broadcasted_iota(jnp.int32, (seg, 2 * seg), 0)
    col = lax.broadcasted_iota(jnp.int32, (seg, 2 * seg), 1)
    return row <= jnp.where(col >= seg, col - seg, col)


def attend_kernel(own, seg, half, more, info, q_ref, k_ref, v_ref, *rest):
    o_ref, lse_ref, s_ref, p_ref = rest[2 * more :]
    trunk = TRUNK * seg
    allowed = causal(seg)
    v_trunk = v_ref[own : own + trunk, :].T

    def one(i, unused):
        count, branch, leaf = info[i, 0], info[i, 1], info[i, 2]
        here = pl.ds(pl.multiple_of(i * seg, seg), seg)
        there = pl.ds(pl.multiple_of(own + branch * seg, seg), seg)
        qs = stacked(q_ref[here, :] * 0.125, half)
        s_ref[:trunk, :] = mm(k_ref[own : own + trunk, :], qs, NT)
        s_branch = mm(k_ref[there, :], qs, NT)
        s_own = jnp.where(allowed, mm(k_ref[here, :], qs, NT), -1e30)
        biases = [jnp.where(kb < count, 0.0, -1e30) for kb in range(TRUNK)]
        leaf_bias = jnp.where(leaf > 0, 0.0, -1e30)
        top = jnp.max(s_own, axis=0, keepdims=True)
        top = jnp.maximum(top, jnp.max(s_branch, axis=0, keepdims=True) + leaf_bias)
        for kb in range(TRUNK):
            part = jnp.max(s_ref[kb * seg : (kb + 1) * seg, :], axis=0, keepdims=True)
            top = jnp.maximum(top, part + biases[kb])
        e_own = jnp.exp(s_own - top)
        e_branch = jnp.exp(s_branch - (top - leaf_bias))
        total = jnp.sum(e_own + e_branch, axis=0, keepdims=True)
        for kb in range(TRUNK):
            e = jnp.exp(s_ref[kb * seg : (kb + 1) * seg, :] - (top - biases[kb]))
            total = total + jnp.sum(e, axis=0, keepdims=True)
            p_ref[kb * seg : (kb + 1) * seg, :] = e.astype(jnp.bfloat16)
        out = mm(v_trunk, p_ref[...])
        out = out + mm(v_ref[there, :].T, e_branch.astype(jnp.bfloat16))
        out = out + mm(v_ref[here, :].T, e_own.astype(jnp.bfloat16))
        out = unstack(out * (1.0 / total), half, seg)
        o_ref[here, :] = out.T.astype(jnp.bfloat16)
        lse_ref[pl.ds(i, 1), :] = top + jnp.log(total)
        return 0

    lax.fori_loop(0, own // seg, one, 0)


def attend_back_kernel(
    own, seg, half, more, info, q_ref, k_ref, v_ref, o_ref, do_ref, lse_ref, *rest
):
    dq_ref, dk_ref, dv_ref, ak, av = rest[3 * more :]
    trunk = TRUNK * seg
    allowed = causal(seg)
    low = jnp.bfloat16
    tk = slice(own, own + trunk)
    k_trunk = k_ref[tk, :].T
    ak[...] = jnp.zeros_like(ak)
    av[...] = jnp.zeros_like(av)

    def one(i, unused):
        count, branch, leaf = info[i, 0], info[i, 1], info[i, 2]
        here = pl.ds(pl.multiple_of(i * seg, seg), seg)
        there = pl.ds(pl.multiple_of(own + branch * seg, seg), seg)
        qs = stacked(q_ref[here, :] * 0.125, half)
        do = do_ref[here, :]
        dos = stacked(do, half)
        prod = (do.astype(jnp.float32) * o_ref[here, :].astype(jnp.float32)).T
        delta = jnp.concatenate(
            [jnp.sum(prod[:half], axis=0, keepdims=True), jnp.sum(prod[half:], axis=0, keepdims=True)],
            axis=1,
        )
        lse = lse_ref[pl.ds(i, 1), :]
        leaf_bias = jnp.where(leaf > 0, 0.0, -1e30)

        def piece(keys, values, shift, mask):
            s = mm(keys, qs, NT)
            if mask:
                s = jnp.where(allowed, s, -1e30)
            if isinstance(shift, list):
                p = jnp.concatenate(
                    [jnp.exp(s[kb * seg : (kb + 1) * seg] - shift[kb]) for kb in range(TRUNK)], axis=0
                )
            else:
                p = jnp.exp(s - shift)
            ds = (p * (mm(values, dos, NT) - delta)).astype(low)
            p = p.astype(low)
            return (mm(p, dos), mm(ds, qs), ds)

        shifts = [lse - jnp.where(kb < count, 0.0, -1e30) for kb in range(TRUNK)]
        dv, dk, ds = piece(k_ref[tk, :], v_ref[tk, :], shifts, False)
        av[tk, :] += dv
        ak[tk, :] += dk
        dq = mm(k_trunk, ds)
        keys = k_ref[there, :]
        dv, dk, ds = piece(keys, v_ref[there, :], lse - leaf_bias, False)
        av[there, :] += dv
        ak[there, :] += dk
        dq = dq + mm(keys.T, ds)
        keys = k_ref[here, :]
        dv, dk, ds = piece(keys, v_ref[here, :], lse, True)
        av[here, :] += dv
        ak[here, :] += dk
        dq = dq + mm(keys.T, ds)
        dq_ref[here, :] = (unstack(dq, half, seg) * 0.125).T.astype(low)
        return 0

    lax.fori_loop(0, own // seg, one, 0)
    dk_ref[...] = ak[...].astype(low)
    dv_ref[...] = av[...].astype(low)


def attend(info, q, kv, seg, begin, count, prev=()):
    own, width = q.shape
    total = kv.shape[0]
    pairs = width // 128
    lane = pl.BlockSpec((own, 128), lambda h: (0, begin + h))
    return pl.pallas_call(
        functools.partial(attend_kernel, own, seg, HEAD_DIM, len(prev) > 0),
        grid=(count,),
        in_specs=[
            pl.BlockSpec(memory_space=pltpu.SMEM),
            lane,
            pl.BlockSpec((total, 128), lambda h: (0, begin + h)),
            pl.BlockSpec((total, 128), lambda h: (0, pairs + begin + h)),
        ]
        + [pl.BlockSpec(memory_space=pl.ANY)] * len(prev),
        out_specs=[lane, pl.BlockSpec((None, 8, 2 * seg), lambda h: (begin + h, 0, 0))],
        out_shape=[
            jax.ShapeDtypeStruct((own, width), jnp.bfloat16),
            jax.ShapeDtypeStruct((pairs, 8, 2 * seg), jnp.float32),
        ],
        input_output_aliases={4 + i: i for i in range(len(prev))},
        scratch_shapes=[
            pltpu.VMEM((TRUNK * seg, 2 * seg), jnp.float32),
            pltpu.VMEM((TRUNK * seg, 2 * seg), jnp.bfloat16),
        ],
        compiler_params=pltpu.CompilerParams(vmem_limit_bytes=32 << 20),
        cost_estimate=pl.CostEstimate(
            flops=count * 5 * 10**9, bytes_accessed=count << 20, transcendentals=0
        ),
        name="attend",
    )(info, q, kv, kv, *prev)


def attend_back(info, q, kv, o, do, lse, seg, begin, count, prev=()):
    own, width = q.shape
    total = kv.shape[0]
    pairs = width // 128
    lane = pl.BlockSpec((own, 128), lambda h: (0, begin + h))
    keys = pl.BlockSpec((total, 128), lambda h: (0, begin + h))
    return pl.pallas_call(
        functools.partial(attend_back_kernel, own, seg, HEAD_DIM, len(prev) > 0),
        grid=(count,),
        in_specs=[
            pl.BlockSpec(memory_space=pltpu.SMEM),
            lane,
            keys,
            pl.BlockSpec((total, 128), lambda h: (0, pairs + begin + h)),
            lane,
            lane,
            pl.BlockSpec((None, 8, 2 * seg), lambda h: (begin + h, 0, 0)),
        ]
        + [pl.BlockSpec(memory_space=pl.ANY)] * len(prev),
        out_specs=[lane, keys, keys],
        out_shape=[
            jax.ShapeDtypeStruct((own, width), jnp.bfloat16),
            jax.ShapeDtypeStruct((total, width), jnp.bfloat16),
            jax.ShapeDtypeStruct((total, width), jnp.bfloat16),
        ],
        input_output_aliases={7 + i: i for i in range(len(prev))},
        scratch_shapes=[
            pltpu.VMEM((total, 128), jnp.float32),
            pltpu.VMEM((total, 128), jnp.float32),
        ],
        compiler_params=pltpu.CompilerParams(vmem_limit_bytes=40 << 20),
        cost_estimate=pl.CostEstimate(
            flops=count * 7 * 10**9, bytes_accessed=2 * count << 20, transcendentals=0
        ),
        name="attend_back",
    )(info, q, kv, kv, o, do, lse, *prev)


def pin(x, *after):
    return lax.optimization_barrier((x,) + after)[0]


def expert_kernel(more, place, x_ref, g_ref, gate_ref, w0, w1, w2, w3, *rest):
    low = jnp.bfloat16
    if more:
        prev_ref, o_ref, o2_ref, s_ref, s2_ref, dot_ref, dw_ref, xt, dt, d_ref, oa, sa, wb, gb = rest
    else:
        o_ref, o2_ref, s_ref, s2_ref, dot_ref, dw_ref, xt, dt, d_ref, oa, sa, wb, gb = rest
    part = w0.shape[1]

    @pl.when(pl.program_id(0) == 0)
    def start():
        xt[...] = x_ref[...].T
        d_ref[...] = (g_ref[...].astype(jnp.float32) * gate_ref[...]).astype(low)
        dt[...] = d_ref[...].T
        oa[...] = jnp.zeros_like(oa)
        sa[...] = jnp.zeros_like(sa)

    def rows_of(r):
        return pl.ds(pl.multiple_of((place[0] ^ r) * part, 64), part)

    for r, w in enumerate((w0, w1, w2, w3)):
        wb[:, rows_of(r), :] = w[...]
    u = mm(x_ref[...], wb[0])
    up = mm(x_ref[...], wb[1])
    sigma = 1.0 / (1.0 + jnp.exp(-u))
    silu = u * sigma
    hidden = (silu * up).astype(low)
    oa[...] += mm(hidden, wb[2], NT)
    dh = mm(d_ref[...], wb[2])
    du = (dh * up * sigma * (1.0 + u * (1.0 - sigma))).astype(low)
    dup = (dh * silu).astype(low)
    sa[...] += mm(du, wb[0], NT) + mm(dup, wb[1], NT)
    gb[0] = mm(xt[...], du).astype(low)
    gb[1] = mm(xt[...], dup).astype(low)
    gb[2] = mm(dt[...], hidden).astype(low)
    for at, r in enumerate(SENT):
        got = gb[:, rows_of(r), :]
        if more:
            got = (got.astype(jnp.float32) + prev_ref[at].astype(jnp.float32)).astype(low)
        dw_ref[at] = got

    @pl.when(pl.program_id(0) == pl.num_programs(0) - 1)
    def finish():
        dot_ref[...] = jnp.sum(g_ref[...].astype(jnp.float32) * oa[...], axis=1, keepdims=True)
        wide = o_ref.shape[1]
        here = pl.ds(pl.multiple_of(place[1] * wide, 128), wide)
        there = pl.ds(pl.multiple_of((1 - place[1]) * wide, 128), wide)
        o_ref[...] = oa[:, here].astype(low)
        o2_ref[...] = oa[:, there].astype(low)
        s_ref[...] = sa[:, here].astype(low)
        s2_ref[...] = sa[:, there].astype(low)


def expert_pass(place, x, g, gate, weights, prev):
    rows, width = x.shape
    three, part, units = weights[0].shape
    low = jnp.bfloat16
    whole = pl.BlockSpec((rows, width), lambda j: (0, 0))
    strip = pl.BlockSpec((three, part, PIECE), lambda j: (0, 0, j))
    strips = pl.BlockSpec((4, three, part, PIECE), lambda j: (0, 0, 0, j))
    column = pl.BlockSpec((rows, 1), lambda j: (0, 0))
    half = pl.BlockSpec((rows, width // 2), lambda j: (0, 0))
    more = prev is not None
    return pl.pallas_call(
        functools.partial(expert_kernel, more),
        grid=(units // PIECE,),
        in_specs=[pl.BlockSpec(memory_space=pltpu.SMEM), whole, whole, column]
        + [strip] * 4
        + [strips] * more,
        out_specs=[half] * 4 + [column, strips],
        out_shape=[
            *[jax.ShapeDtypeStruct((rows, width // 2), low)] * 4,
            jax.ShapeDtypeStruct((rows, 1), jnp.float32),
            jax.ShapeDtypeStruct((4, three, part, units), low),
        ],
        scratch_shapes=[
            pltpu.VMEM((width, rows), low),
            pltpu.VMEM((width, rows), low),
            pltpu.VMEM((rows, width), low),
            pltpu.VMEM((rows, width), jnp.float32),
            pltpu.VMEM((rows, width), jnp.float32),
            pltpu.VMEM((three, width, PIECE), low),
            pltpu.VMEM((three, width, PIECE), low),
        ],
        compiler_params=pltpu.CompilerParams(vmem_limit_bytes=60 << 20),
        cost_estimate=pl.CostEstimate(
            flops=22 * 10**9, bytes_accessed=20 << 20, transcendentals=0
        ),
        name="expert_pass",
    )(place, x, g, gate, *weights, *([prev] if more else []))


def spread_kernel(pieces, padded, capacity, gated, place_ref, rows_ref, *rest):
    low = jnp.bfloat16
    outs = rest[1:] if gated else rest
    tokens = rows_ref.shape[0]
    for p in range(pieces):
        slot = lax.broadcasted_iota(jnp.int32, (padded, tokens), 0) + p * padded
        hits = [slot == place_ref[c : c + 1, :] for c in range(2)]
        out = mm(jnp.where(hits[0] | hits[1], 1.0, 0.0).astype(low), rows_ref[...]).astype(low)
        if gated:
            parts = sum(
                mm(rest[0][c], jnp.where(hits[c], 1.0, 0.0).astype(low), NT) for c in range(2)
            ).astype(low)
            blank = jnp.zeros((parts.shape[0], out.shape[1] - padded), low)
            parts = jnp.concatenate([parts, blank], axis=1)
            row = lax.broadcasted_iota(jnp.int32, out.shape, 0)
            for i in range(3):
                out = jnp.where(row == capacity + i, parts[i : i + 1, :], out)
        outs[p][...] = out


def spread(place, rows, pieces, padded, capacity, parts=None):
    shape = jax.ShapeDtypeStruct((padded, rows.shape[1]), jnp.bfloat16)
    gated = parts is not None
    return pl.pallas_call(
        functools.partial(spread_kernel, pieces, padded, capacity, gated),
        out_shape=[shape] * pieces,
        compiler_params=pltpu.CompilerParams(vmem_limit_bytes=40 << 20),
        cost_estimate=pl.CostEstimate(flops=4 * 10**9, bytes_accessed=2 << 20, transcendentals=0),
        name="spread",
    )(place, rows, *([parts] if gated else []))


def gather_kernel(pieces, padded, capacity, dots, place_ref, *rest):
    low = jnp.bfloat16
    if dots:
        ins, (out_ref, dot_ref) = rest[:pieces], rest[pieces:]
    else:
        gate_ref, ins, out_ref = rest[0], rest[1 : 1 + pieces], rest[1 + pieces]
    tokens = place_ref.shape[0]
    total = None
    sums = [0.0, 0.0]
    for p in range(pieces):
        slot = lax.broadcasted_iota(jnp.int32, (tokens, padded), 1) + p * padded
        hits = [slot == place_ref[:, c : c + 1] for c in range(2)]
        if dots:
            picks = [jnp.where(h, 1.0, 0.0).astype(low) for h in hits]
            values = ins[p][capacity : capacity + 3, :padded]
            values = jnp.concatenate([values, jnp.zeros((13, padded), low)], axis=0)
            for c in range(2):
                sums[c] = sums[c] + mm(picks[c], values, NT)
            pick = picks[0] + picks[1]
        else:
            pick = jnp.where(hits[0], gate_ref[:, 0:1], jnp.where(hits[1], gate_ref[:, 1:2], 0.0))
            pick = pick.astype(low)
        part = mm(pick, ins[p][...])
        total = part if total is None else total + part
    out_ref[...] = total.astype(low)
    if dots:
        for c in range(2):
            dot_ref[:, c : c + 1] = jnp.sum(sums[c], axis=1, keepdims=True)


def gather(place, pieces, capacity, gate=None):
    padded, width = pieces[0].shape
    tokens = place.shape[0]
    dots = gate is None
    shapes = [jax.ShapeDtypeStruct((tokens, width), jnp.bfloat16)]
    if dots:
        shapes.append(jax.ShapeDtypeStruct((tokens, 2), jnp.float32))
    return pl.pallas_call(
        functools.partial(gather_kernel, len(pieces), padded, capacity, dots),
        out_shape=shapes,
        compiler_params=pltpu.CompilerParams(vmem_limit_bytes=40 << 20),
        cost_estimate=pl.CostEstimate(flops=4 * 10**9, bytes_accessed=2 << 20, transcendentals=0),
        name="gather",
    )(place, *([] if dots else [gate]), *pieces)


def flip(x, axis, bit, size):
    return lax.ppermute(x, axis, [(i, i ^ bit) for i in range(size)])


def turn_gather(x, size, position):
    out = jnp.zeros((size,) + x.shape, x.dtype)
    out = lax.dynamic_update_index_in_dim(out, x, position, 0)
    for k in range(1, size):
        block = lax.ppermute(x, "ctx", [(i, (i + k) % size) for i in range(size)])
        out = lax.dynamic_update_index_in_dim(out, block, (position - k) % size, 0)
    return out


def turn_sum(x, size, position):
    total = lax.dynamic_index_in_dim(x, position, 0, keepdims=False).astype(jnp.float32)
    for k in range(1, size):
        block = lax.dynamic_index_in_dim(x, (position + k) % size, 0, keepdims=False)
        got = lax.ppermute(block, "ctx", [(i, (i + k) % size) for i in range(size)])
        total = total + got.astype(jnp.float32)
    return total


def far(x, k, shards_n, ctx_n):
    pairs = []
    for s in range(shards_n):
        for z in range(ctx_n):
            pairs.append((s * ctx_n + z, (s ^ k) * ctx_n + (z ^ 2)))
    return lax.ppermute(x, ("shard", "ctx"), pairs)


def three_parts(x):
    one = x.astype(jnp.bfloat16)
    rest = x - one.astype(jnp.float32)
    two = rest.astype(jnp.bfloat16)
    return jnp.stack([one, two, (rest - two.astype(jnp.float32)).astype(jnp.bfloat16)], axis=-2)


def with_rows(slots, values, at):
    extra = three_parts(values)
    after = slots.shape[-2] - at - extra.shape[-2]
    pads = ((0, 0), (at, after), (0, slots.shape[-1] - extra.shape[-1]))
    return slots + jnp.pad(extra, pads)


def row_values(slots, at):
    return jnp.sum(slots[:, at : at + 3, : slots.shape[1]].astype(jnp.float32), axis=1)


def by_core(
    tokens, gate_res, cotangent, parents, expert_ids, priority, w_qkv, w_out, w_router, attn_gain,
    ffn_gain, const_vec, w_gate_up, w_down,
):
    low, full = jnp.bfloat16, jnp.float32
    shard, ctx, tp = lax.axis_index("shard"), lax.axis_index("ctx"), lax.axis_index("tp")
    shards_n, ctx_n = lax.axis_size("shard"), lax.axis_size("ctx")
    trees, rows, width = tokens.shape
    rows_d = w_qkv.shape[0]
    part = width // 2
    seg = rows * ctx_n // parents.shape[1]
    own_segs = rows // seg
    edge = KEY_SEGS * seg - 2 * rows

    def own_tree(x):
        return lax.dynamic_index_in_dim(x, tp, 0, keepdims=False)

    def in_order(x, other, axis=0):
        return jnp.concatenate([jnp.where(tp == 0, x, other), jnp.where(tp == 0, other, x)], axis=axis)

    def both_trees(x, other):
        return in_order(x[None], other[None])

    def swap(x):
        return flip(x, "tp", 1, 2)

    def plus(x, y):
        return (x.astype(full) + y.astype(full)).astype(low)

    def my_half(x, which):
        return lax.dynamic_slice_in_dim(x, which * part, part, x.ndim - 1)

    x_own = own_tree(tokens)
    ends = [(i, i + 1) for i in range(ctx_n - 1)]
    near_head = lax.ppermute(x_own[:edge], "ctx", ends)
    near_tail = lax.ppermute(x_own[edge:], "ctx", ends[:-1])
    near = jnp.concatenate([near_head, near_tail], axis=0)

    mine = jnp.stack([w_qkv[:, 0], w_qkv[:, 1], w_qkv[:, 2], pin(w_out, x_own)])
    matrix = turn_gather(lax.dynamic_index_in_dim(mine, shard, 0, keepdims=False), ctx_n, ctx)
    matrix = matrix.reshape(width, -1)

    small = jnp.concatenate([w_router.T, attn_gain[None], ffn_gain[None], const_vec.T], axis=0)
    small = turn_gather(pin(small, matrix), ctx_n, ctx).transpose(1, 0, 2).reshape(small.shape[0], width)
    all_experts = w_router.shape[1]
    router_t = small[:all_experts]
    gain_a = small[all_experts].astype(full)
    gain_f = small[all_experts + 1].astype(full)
    const_t = small[all_experts + 2 :].astype(full)

    mid = lax.ppermute(pin(near, matrix), "ctx", ends[1:])
    plane = [matrix] + [flip(matrix, "shard", k, shards_n) for k in range(1, shards_n)]
    plane = jnp.stack(plane)
    farther = lax.ppermute(pin(mid, plane, small), "ctx", ends[2:])
    plane = jnp.concatenate([plane, swap(plane)], axis=2)
    weight_q, weight_k, weight_v, weight_o = [
        lax.dynamic_index_in_dim(plane, m ^ shard, 0, keepdims=False) for m in range(4)
    ]
    weight_kv = jnp.concatenate([weight_k, weight_v], axis=1)

    held, gu, dn = lax.optimization_barrier((farther, w_gate_up, w_down))
    lower = ctx < 2
    first = jnp.stack([gu[:, 0, 0], gu[:, 0, 1], dn[:, 0]])
    second_e = jnp.stack([gu[:, 1, 0], gu[:, 1, 1], dn[:, 1]])
    rows_own = jnp.where(lower, first, second_e)
    rows_two = flip(jnp.where(lower, second_e, first), "ctx", 2, ctx_n)
    rows_one = flip(rows_own, "ctx", 1, ctx_n)

    capacity = trees * rows * 2 // all_experts
    experts = shards_n * w_gate_up.shape[1]
    padded = -(-(capacity + 3) // 16) * 16
    count = experts * padded
    held, ids_in, order_in = lax.optimization_barrier((near_head, expert_ids, priority))
    flat = ids_in.reshape(-1)
    order = (2 * order_in[0, 0][:, None] + jnp.arange(2, dtype=jnp.int32)[None, :]).reshape(-1)
    earlier = (flat[:, None] == flat[None, :]) & (order[None, :] < order[:, None])
    ranks = jnp.sum(earlier.astype(jnp.int32), axis=1)
    kept = (flat < experts) & (ranks < capacity)
    piece = ((flat % 2) ^ (ctx // 2)) * shards_n + ((flat // 2) ^ shard)
    place = jnp.where(kept, piece * padded + ranks, -1).reshape(trees, rows, 2)
    place = jnp.where(tp == 0, place, place[::-1]).reshape(trees * rows, 2)
    place_t = place.T

    g_own = own_tree(cotangent)
    g_other = lax.dynamic_index_in_dim(cotangent, 1 - tp, 0, keepdims=False)
    g_half = my_half(jnp.concatenate([g_own, g_other], axis=0), tp)
    g_slots = spread(place_t, g_half, experts, padded, capacity)
    g_near = jnp.stack(g_slots[:shards_n])
    g_far = flip(pin(jnp.stack(g_slots[shards_n:]), mid), "ctx", 2, ctx_n)
    g_pairs = jnp.stack([g_near, g_far], axis=1)
    g_in = jnp.stack(
        [g_pairs[0]] + [flip(g_pairs[k], "shard", k, shards_n) for k in range(1, shards_n)], axis=1
    ).reshape(2, shards_n * padded, part)
    g_both = in_order(g_in, swap(g_in), 2)

    block0 = jnp.where(ctx == 0, x_own, jnp.where(ctx == 1, near, jnp.where(ctx == 2, mid, farther)))
    block1 = jnp.where(ctx == 1, x_own, jnp.where(ctx == 2, near, mid))
    block2 = jnp.where(ctx == 2, x_own[:edge], near[:edge])
    x_all = jnp.concatenate([x_own, block0, block1, block2], axis=0)

    def unit_of(x):
        x = x.astype(full)
        inverse = lax.rsqrt(jnp.mean(x * x, axis=-1, keepdims=True) + eps)
        return (x * inverse, inverse)

    normed = (unit_of(x_all)[0] * gain_a).astype(low)
    q = mm(normed[:rows], weight_q).astype(low)
    kv = mm(normed, weight_kv).astype(low)

    seg_id = ctx * own_segs + jnp.arange(own_segs, dtype=jnp.int32)
    parent = jnp.take(own_tree(parents), seg_id)
    leaf = (seg_id >= KEY_SEGS).astype(jnp.int32)
    info = jnp.stack([jnp.minimum(seg_id, TRUNK), jnp.where(leaf > 0, parent, TRUNK), leaf], axis=1)
    half_pairs = width // 256
    ahead = attend(info, q, kv, seg, 0, half_pairs)
    o_low, lse = attend(info, pin(q, g_far), kv, seg, half_pairs, half_pairs, ahead)

    inputs = x_own.astype(full)
    mixed = inputs + mm(o_low, weight_o, NT)
    inv_second = lax.rsqrt(jnp.mean(mixed * mixed, axis=-1, keepdims=True) + eps)
    second_unit = mixed * inv_second
    second = (second_unit * gain_f).astype(low)
    second_half = jnp.concatenate([my_half(second, tp), swap(my_half(second, 1 - tp))], axis=0)

    logits = mm(second, router_t, NT) + own_tree(gate_res)
    expo = jnp.exp(logits - jnp.max(logits, axis=-1, keepdims=True))
    probs = expo / jnp.sum(expo, axis=-1, keepdims=True)
    ids = own_tree(expert_ids)
    selector = (ids[:, :, None] == jnp.arange(all_experts, dtype=jnp.int32)).astype(full)
    picked = jnp.sum(selector * probs[:, None, :], axis=-1)
    picked_total = jnp.sum(picked, axis=-1, keepdims=True)
    gates = picked / picked_total
    gates_both = jnp.concatenate([gates.T, swap(gates.T)], axis=1)

    rows_three = flip(pin(rows_two, second), "ctx", 1, ctx_n)
    weights = (rows_own, rows_one, rows_two, rows_three)
    gate_parts = jnp.pad(three_parts(gates_both), ((0, 0), (0, 13), (0, 0)))
    slots = spread(place_t, pin(second_half, g_in), experts, padded, capacity, gate_parts)
    x_far = [far(slots[shards_n + k], k, shards_n, ctx_n) for k in range(shards_n)]
    x_near = [slots[0]] + [flip(slots[k], "shard", k, shards_n) for k in range(1, shards_n)]

    def experts_on(pieces, g_in_both, prev):
        x = jnp.stack(pieces)
        gate = row_values(x, capacity).reshape(-1, 1)
        x = x.reshape(-1, part)
        return expert_pass(jnp.stack([ctx, tp]), in_order(x, swap(x), 1), g_in_both, gate, weights, prev)

    def answers(mine, other, dots):
        ds = plus(mine, swap(other)).reshape(shards_n, padded, part)
        return with_rows(ds, dots.reshape(shards_n, padded), capacity)

    on1, ox1, sn1, sx1, dots1, dw = experts_on(x_near, g_both[0], None)
    on2, ox2, sn2, sx2, dots2, dw = experts_on(x_far, g_both[1], dw)
    ds_far = answers(sn2, sx2, dots2)
    ds_near = answers(sn1, sx1, dots1)
    ds_far = [far(ds_far[k], k, shards_n, ctx_n) for k in range(shards_n)]
    ds_near = [ds_near[0]] + [flip(ds_near[k], "shard", k, shards_n) for k in range(1, shards_n)]

    rows_tn = (((0,), (0,)), ((), ()))
    d_routed, d_gate_pairs = gather(place, ds_near + ds_far, capacity)
    d_routed = in_order(d_routed[:rows], swap(d_routed[rows:]), 1).astype(full)
    d_gate_pairs = d_gate_pairs[:rows] + swap(d_gate_pairs[rows:])

    second_f = second.astype(full)
    g = g_own.astype(full)
    copy_flag = selector[:, :, experts + 1]
    const_flags = selector[:, :, experts + 2 :]
    copy_gate = jnp.sum(gates * copy_flag, axis=1, keepdims=True)
    const_gate = jnp.sum(gates[:, :, None] * const_flags, axis=1)
    g_second = jnp.sum(g * second_f, axis=1, keepdims=True)
    g_const = jnp.stack([jnp.sum(g * const_t[k][None], axis=1) for k in range(2)], axis=1)
    d_gates = (
        d_gate_pairs
        + copy_flag * g_second
        + jnp.sum(const_flags * g_const[:, None, :], axis=-1)
    )
    d_picked = (d_gates - jnp.sum(d_gates * gates, axis=-1, keepdims=True)) / picked_total
    d_probs = jnp.sum(d_picked[:, :, None] * selector, axis=1)
    d_logits = probs * (d_probs - jnp.sum(probs * d_probs, axis=-1, keepdims=True))
    high = lax.Precision.HIGHEST
    d_router = jnp.einsum("tk,td->kd", d_logits, second_f, precision=high)
    d_const = jnp.einsum("tk,td->kd", const_gate, g, precision=high)
    d_second = copy_gate * g + d_routed + jnp.dot(d_logits, router_t.astype(full), precision=high)
    d_gain_f = jnp.sum(d_second * second_unit, axis=0)
    d_unit = d_second * gain_f
    d_mixed = g + inv_second * (
        d_unit - second_unit * jnp.mean(d_unit * second_unit, axis=-1, keepdims=True)
    )
    d_attn = d_mixed.astype(low)
    d_o = mm(d_attn, weight_o).astype(low)
    d_weight_o = mm(d_attn, o_low, rows_tn)

    ox1, ox2, held = lax.optimization_barrier((ox1, ox2, d_o))
    out_near = plus(on1, swap(ox1)).reshape(shards_n, padded, part)
    out_far = plus(on2, swap(ox2)).reshape(shards_n, padded, part)
    out_pairs = jnp.stack([out_near, out_far], axis=1)
    out_got = [out_pairs[0]] + [flip(out_pairs[k], "shard", k, shards_n) for k in range(1, shards_n)]
    out_far = flip(jnp.stack([o[1] for o in out_got]), "ctx", 2, ctx_n)

    got = flip(pin(dw[2:], d_routed), "ctx", 1, ctx_n)
    kept_rows = dw[0].astype(full) + got[0].astype(full)
    sent_rows = (dw[1].astype(full) + got[1].astype(full)).astype(low)
    came_rows = flip(sent_rows, "ctx", 2, ctx_n).astype(full)
    first = jnp.where(lower, kept_rows, came_rows)
    second_e = jnp.where(lower, came_rows, kept_rows)
    d_gate_up = jnp.stack(
        [jnp.stack([first[0], first[1]], axis=1), jnp.stack([second_e[0], second_e[1]], axis=1)], axis=1
    )
    d_down = jnp.stack([first[2], second_e[2]], axis=1)

    third = width // 384
    back = attend_back(info, q, kv, o_low, d_o, lse, seg, 0, third)
    q_later = pin(q, out_pairs, back[0])
    back = attend_back(info, q_later, kv, o_low, d_o, lse, seg, third, third, back)
    q_later = pin(q, *out_got, sent_rows, back[0])
    dq, dk, dv = attend_back(info, q_later, kv, o_low, d_o, lse, seg, 2 * third, third, back)
    x_again, dk = lax.optimization_barrier((x_all, dk))
    unit_all, inv_all = unit_of(x_again)

    def keys_grad(lo, hi):
        return mm(dk[lo:hi], weight_k, NT) + mm(dv[lo:hi], weight_v, NT)

    part0 = keys_grad(rows, 2 * rows).astype(low)
    dq_after, dk_after, dv_after, held = lax.optimization_barrier((dq, dk, dv, part0))
    d_weight_q = mm(normed[:rows], dq_after, rows_tn).astype(low)
    d_weight_k = mm(normed, dk_after, rows_tn).astype(low)
    d_weight_v = mm(normed, dv_after, rows_tn).astype(low)
    part1 = keys_grad(2 * rows, 3 * rows).astype(low)
    part2 = keys_grad(3 * rows, dk.shape[0]).astype(low)
    d_near = keys_grad(0, rows) + mm(dq, weight_q, NT)
    d_gain_a = jnp.sum(d_near * unit_all[:rows], axis=0)
    for at, piece in ((1, part0), (2, part1), (3, part2)):
        lo = at * rows
        d_gain_a = d_gain_a + jnp.sum(
            piece.astype(full) * unit_all[lo : lo + piece.shape[0]], axis=0
        )

    tiny = jnp.concatenate([d_router, d_gain_a[None], d_gain_f[None], d_const], axis=0)
    tiny = tiny.reshape(4, 2, 2, ctx_n, rows_d).transpose(0, 3, 1, 2, 4).reshape(4, ctx_n, 2, 2 * rows_d)
    tiny = jnp.where(tp == 0, tiny, tiny[:, :, ::-1]).reshape(4, ctx_n, 1, width).astype(low)
    shared = jnp.stack([d_weight_q, d_weight_k, d_weight_v, d_weight_o.astype(low)])
    shared = shared.reshape(4, ctx_n, rows_d, width)
    room = jnp.zeros((4, ctx_n, 15, width), low)
    shared = jnp.concatenate([shared, tiny, room], axis=2)
    shared_mine, shared_other = shared[..., :part], shared[..., part:]

    def hop(x, at):
        return lax.ppermute(x, "ctx", [(at, at - 1)])

    came0, came1, came2 = hop(part0, 3), hop(part1, 3), hop(part2, 3)
    came0, came1, came2, held = lax.optimization_barrier((came0, came1, came2, shared_other))
    part0 = plus(part0, came0)
    shared = plus(shared_mine, swap(shared_other))
    came0 = pin(hop(part0, 2), shared)
    part1 = plus(part1, came1)
    came1 = hop(part1, 2)
    part2 = plus(part2, came2)
    part0 = plus(part0, came0)
    came0 = hop(part0, 1)
    part1 = plus(part1, came1)
    def numbered(k):
        return lax.dynamic_index_in_dim(shared, shard ^ k, 0, keepdims=False)

    total = numbered(0).astype(full)
    for k in range(1, shards_n):
        total = total + flip(numbered(k), "shard", k, shards_n).astype(full)
    came0 = pin(came0, total)
    part0 = plus(part0, came0)
    part2 = jnp.concatenate([part2, jnp.zeros((rows - edge, width), low)], axis=0)
    extra = jnp.where(ctx == 0, part0, jnp.where(ctx == 1, part1, part2)).astype(full)
    extra = jnp.where(ctx == 3, 0.0, extra)
    d_normed = d_near + extra
    unit_own, inv_own = unit_all[:rows], inv_all[:rows]
    d_first = d_normed * gain_a
    d_tokens = d_mixed + inv_own * (
        d_first - unit_own * jnp.mean(d_first * unit_own, axis=-1, keepdims=True)
    )

    total = turn_sum(total.astype(low), ctx_n, ctx).astype(low)
    four = jnp.stack([total] + [flip(total, "shard", k, shards_n) for k in range(1, shards_n)])
    four = jnp.stack(
        [lax.dynamic_index_in_dim(four, m ^ shard, 0, keepdims=False) for m in range(4)]
    )
    d_q, d_k, d_v, d_w_out = [four[m, :rows_d].astype(full) for m in range(4)]
    d_w_qkv = jnp.stack([d_q, d_k, d_v], axis=1)
    tiny = four[:, rows_d]
    tiny = both_trees(tiny, swap(tiny)).transpose(1, 0, 2).reshape(16, rows_d).astype(full)

    out_far = pin(out_far, dq)
    pieces = [o[0] for o in out_got] + [out_far[k] for k in range(shards_n)]
    combined = gather(pin(place, shared_other), pieces, capacity, gates_both.T)[0]
    combined = in_order(combined[:rows], swap(combined[rows:]), 1).astype(full)
    mixed_out = (
        mixed
        + combined
        + copy_gate * second_f
        + const_gate[:, :1] * const_t[0][None]
        + const_gate[:, 1:] * const_t[1][None]
    )
    return (
        both_trees(mixed_out, swap(mixed_out)),
        both_trees(d_tokens, swap(d_tokens)),
        both_trees(d_logits, swap(d_logits)),
        d_w_qkv,
        d_w_out,
        tiny[:all_experts].T,
        tiny[all_experts],
        tiny[all_experts + 1],
        tiny[all_experts + 2 :].T,
        d_gate_up,
        d_down,
    )


def program(tokens, gate_res, cotangent, parents, expert_ids, priority, w_qkv, *weights):
    trees, rows, width = tokens.shape
    ctx_n = lax.axis_size("ctx")
    seg = rows * ctx_n // parents.shape[1]
    fits = (
        ctx_n == 4
        and lax.axis_size("shard") == 4
        and lax.axis_size("tp") == 2
        and trees == 2
        and seg == 128
        and rows % seg == 0
        and 2 * rows < KEY_SEGS * seg <= 3 * rows
        and weights[-1].shape[1] == 2
    )
    chosen = by_core if fits else shards
    return chosen(tokens, gate_res, cotangent, parents, expert_ids, priority, w_qkv, *weights)


def solution(mesh):
    return jax.shard_map(
        program,
        mesh=mesh,
        in_specs=(
            P("shard", "ctx", None),
            P("shard", "ctx", None),
            P("shard", "ctx", None),
            P("shard", None),
            P("shard", "ctx", None),
            P("shard", "ctx", None),
            P("ctx", None, "tp"),
            P("ctx", "tp"),
            P("ctx", None),
            P("ctx"),
            P("ctx"),
            P("ctx", None),
            P("ctx", "shard", None, "tp"),
            P("ctx", "shard", "tp"),
        ),
        out_specs=(
            P("shard", "ctx", None),
            P("shard", "ctx", None),
            P("shard", "ctx", None),
            P("ctx", None, "tp"),
            P("ctx", "tp"),
            P("ctx", None),
            P("ctx"),
            P("ctx"),
            P("ctx", None),
            P("ctx", "shard", None, "tp"),
            P("ctx", "shard", "tp"),
        ),
        check_vma=False,
    )
```

```python
import functools
import math

import jax
import jax.numpy as jnp
from jax import lax
from jax.experimental import pallas as pl
from jax.experimental.pallas import tpu as pltpu
from jax.sharding import PartitionSpec as P

HEAD_DIM = 64


eps = 1e-06
score_scale = 0.125


def ancestry(parent_row):
    seg_count = parent_row.shape[0]
    position = jnp.arange(seg_count, dtype=jnp.int32)
    linked = (parent_row[:, None] == position[None, :]) | (position[:, None] == position[None, :])
    reach = linked.astype(jnp.float32)
    for repeat in range(seg_count.bit_length()):
        reach = jnp.minimum(jnp.dot(reach, reach, precision=lax.Precision.HIGHEST), 1.0)
    return reach


def path_rows(positions, seg_len, ancestors):
    onehot = (
        (positions // seg_len)[:, None] == jnp.arange(ancestors.shape[0], dtype=jnp.int32)[None, :]
    ).astype(jnp.float32)
    return jnp.dot(onehot, ancestors)


def allowed_block(query_rows, query_pos, key_start, key_count, seg_len):
    key_pos = key_start + jnp.arange(key_count, dtype=jnp.int32)
    key_onehot = (
        (key_pos // seg_len)[:, None] == jnp.arange(query_rows.shape[1], dtype=jnp.int32)[None, :]
    ).astype(jnp.float32)
    linked = jnp.dot(query_rows, key_onehot.T) > 0.5
    return (linked & (key_pos[None, :] <= query_pos[:, None]))[None]


def slot_table(picked_ids, ranking, experts, capacity):
    count_rows = picked_ids.shape[0]
    flat_ids = picked_ids.reshape(-1)
    rank_key = (2 * ranking[:, None] + jnp.arange(2, dtype=jnp.int32)[None, :]).reshape(-1)
    earlier = (flat_ids[:, None] == flat_ids[None, :]) & (rank_key[None, :] < rank_key[:, None])
    ranks = jnp.sum(earlier.astype(jnp.int32), axis=1)
    kept = (flat_ids < experts) & (ranks < capacity)
    target = jnp.where(kept, flat_ids * capacity + ranks, -1).reshape(count_rows, 2)
    slot_index = jnp.arange(experts * capacity, dtype=jnp.int32)
    return slot_index[None, :, None] == target.T[:, None, :]


def block_scores(queries, keys_blk):
    return (
        jnp.einsum("qhe,khe->hqk", queries, keys_blk, preferred_element_type=jnp.float32)
        * score_scale
    )


def softmax_grads(queries, grads_out, stat_lse, stat_delta, keys_blk, values_blk, mask):
    prob = jnp.where(mask, jnp.exp(block_scores(queries, keys_blk) - stat_lse[:, :, None]), 0.0)
    dprob = jnp.einsum("qhe,khe->hqk", grads_out, values_blk, preferred_element_type=jnp.float32)
    dscore = (prob * (dprob - stat_delta[:, :, None])).astype(jnp.bfloat16)
    return (prob.astype(jnp.bfloat16), dscore)


def shards(
    tokens,
    gate_res,
    cotangent,
    parents,
    expert_ids,
    priority,
    w_qkv,
    w_out,
    w_router,
    attn_gain,
    ffn_gain,
    const_vec,
    w_gate_up,
    w_down,
):
    full_qkv, full_out, full_router, full_again, full_fgain, full_const, full_gu, full_down = (
        lax.all_gather(w_qkv, "ctx", axis=0, tiled=True),
        lax.all_gather(w_out, "ctx", axis=0, tiled=True),
        lax.all_gather(w_router, "ctx", axis=0, tiled=True),
        lax.all_gather(attn_gain, "ctx", axis=0, tiled=True),
        lax.all_gather(ffn_gain, "ctx", axis=0, tiled=True),
        lax.all_gather(const_vec, "ctx", axis=0, tiled=True),
        lax.all_gather(w_gate_up, "ctx", axis=0, tiled=True),
        lax.all_gather(w_down, "ctx", axis=0, tiled=True),
    )
    tree_count, rows, model_width = tokens.shape
    tok_rows = tree_count * rows
    inputs = tokens.reshape(tok_rows, model_width).astype(jnp.float32)
    local_width = full_out.shape[1]
    local_heads = local_width // HEAD_DIM
    ctx_index = lax.axis_index("ctx")
    tree_len = rows * lax.axis_size("ctx")
    ancestors_all = jax.vmap(ancestry)(parents)
    seg_len = tree_len // parents.shape[1]
    key_block = math.gcd(tree_len, 512)
    starts = jnp.arange(tree_len // key_block, dtype=jnp.int32) * key_block
    key_start_own = ctx_index * rows
    query_pos = key_start_own + jnp.arange(rows, dtype=jnp.int32)
    query_rows_all = jax.vmap(lambda anc: path_rows(query_pos, seg_len, anc))(ancestors_all)
    inv_first = lax.rsqrt(jnp.mean(inputs * inputs, axis=-1, keepdims=True) + eps)
    first_unit = inputs * inv_first
    first_gain = full_again.astype(jnp.float32)
    normed = (first_unit * first_gain).astype(jnp.bfloat16)
    projected = jnp.einsum("nd,dke->nke", normed, full_qkv, preferred_element_type=jnp.float32)
    q_low = projected[:, 0].astype(jnp.bfloat16)
    k_low = projected[:, 1].astype(jnp.bfloat16)
    v_low = projected[:, 2].astype(jnp.bfloat16)
    keys_all, values_all = (
        lax.all_gather(k_low.reshape(tree_count, rows, local_width), "ctx", axis=1, tiled=True),
        lax.all_gather(v_low.reshape(tree_count, rows, local_width), "ctx", axis=1, tiled=True),
    )
    q_heads = q_low.reshape(tree_count, rows, local_heads, HEAD_DIM)
    k_heads = keys_all.reshape(tree_count, tree_len, local_heads, HEAD_DIM)
    v_heads = values_all.reshape(tree_count, tree_len, local_heads, HEAD_DIM)

    def tree_forward(q_one, k_one, v_one, rows_one):

        def stat_step(carry, start):
            running_top, running_sum = carry
            keys_blk = lax.dynamic_slice_in_dim(k_one, start, key_block, 0)
            mask = allowed_block(rows_one, query_pos, start, key_block, seg_len)
            masked = jnp.where(mask, block_scores(q_one, keys_blk), -1e30)
            new_top = jnp.maximum(running_top, jnp.max(masked, axis=2))
            expo = jnp.where(mask, jnp.exp(masked - new_top[:, :, None]), 0.0)
            running_sum = running_sum * jnp.exp(running_top - new_top) + jnp.sum(expo, axis=2)
            return ((new_top, running_sum), None)

        start_top = jnp.full((local_heads, rows), -1e30, jnp.float32)
        (final_top, final_sum), unused = lax.scan(
            stat_step, (start_top, jnp.zeros_like(start_top)), starts
        )
        lse_one = final_top + jnp.log(final_sum)

        def out_step(accum, start):
            keys_blk = lax.dynamic_slice_in_dim(k_one, start, key_block, 0)
            values_blk = lax.dynamic_slice_in_dim(v_one, start, key_block, 0)
            mask = allowed_block(rows_one, query_pos, start, key_block, seg_len)
            prob = jnp.where(
                mask, jnp.exp(block_scores(q_one, keys_blk) - lse_one[:, :, None]), 0.0
            ).astype(jnp.bfloat16)
            return (
                accum
                + jnp.einsum("hqk,khe->qhe", prob, values_blk, preferred_element_type=jnp.float32),
                None,
            )

        attended_one, unused = lax.scan(
            out_step, jnp.zeros((rows, local_heads, HEAD_DIM), jnp.float32), starts
        )
        return (attended_one, lse_one)

    attended, lse = jax.vmap(tree_forward)(q_heads, k_heads, v_heads, query_rows_all)
    attended_low = attended.reshape(tok_rows, local_width).astype(jnp.bfloat16)
    attn_part = jnp.einsum("nh,dh->nd", attended_low, full_out, preferred_element_type=jnp.float32)
    attn_sum = lax.psum(attn_part.astype(jnp.bfloat16), "tp").astype(jnp.float32)
    mixed = inputs + attn_sum
    inv_second = lax.rsqrt(jnp.mean(mixed * mixed, axis=-1, keepdims=True) + eps)
    second_unit = mixed * inv_second
    second_gain = full_fgain.astype(jnp.float32)
    second_low = (second_unit * second_gain).astype(jnp.bfloat16)
    second_float = second_low.astype(jnp.float32)
    logits = jnp.dot(
        second_low, full_router, preferred_element_type=jnp.float32
    ) + gate_res.reshape(tok_rows, -1)
    expo_logits = jnp.exp(logits - jnp.max(logits, axis=-1, keepdims=True))
    probs = expo_logits / jnp.sum(expo_logits, axis=-1, keepdims=True)
    experts = lax.axis_size("shard") * w_gate_up.shape[1]
    every_expert = experts + 4
    capacity = tok_rows * 2 // every_expert
    picked_ids = expert_ids.reshape(tok_rows, 2)
    selector = (picked_ids[:, :, None] == jnp.arange(every_expert, dtype=jnp.int32)).astype(
        jnp.float32
    )
    picked = jnp.sum(selector * probs[:, None, :], axis=-1)
    picked_total = jnp.sum(picked, axis=-1, keepdims=True)
    gates = picked / picked_total
    table = slot_table(picked_ids, priority[0, 0], experts, capacity).astype(jnp.bfloat16)
    routed = table[0] + table[1]
    send_slots = jnp.einsum(
        "et,td->ed", routed, second_low, preferred_element_type=jnp.float32
    ).astype(jnp.bfloat16)
    send_slots = send_slots.reshape(experts, 1, capacity, model_width)
    arrived = lax.all_to_all(send_slots, "shard", split_axis=0, concat_axis=1, tiled=True)
    gate_up = jnp.einsum("jsrd,djgf->jsrgf", arrived, full_gu, preferred_element_type=jnp.float32)
    hidden_low = (jax.nn.silu(gate_up[:, :, :, 0]) * gate_up[:, :, :, 1]).astype(jnp.bfloat16)
    partial_out = jnp.einsum(
        "jsrf,djf->jsrd", hidden_low, full_down, preferred_element_type=jnp.float32
    )
    summed = lax.psum(partial_out.astype(jnp.bfloat16), "tp")
    returned = lax.all_to_all(summed, "shard", split_axis=1, concat_axis=0, tiled=True)
    returned, kept_slots = (returned, arrived)
    out_slots = returned.reshape(experts * capacity, model_width)
    ffn_values = jnp.einsum("cet,ed->ctd", table, out_slots, preferred_element_type=jnp.float32)
    copy_flag = selector[:, :, experts + 1]
    const_flags = selector[:, :, experts + 2 :]
    const_float = full_const.astype(jnp.float32)
    fixed_terms = jnp.einsum(
        "nck,dk->cnd", const_flags, const_float, precision=lax.Precision.HIGHEST
    )
    values_pair = ffn_values + copy_flag.T[:, :, None] * second_float[None] + fixed_terms
    mixed_out = mixed + jnp.sum(gates.T[:, :, None] * values_pair, axis=0)
    grad_out = cotangent.reshape(tok_rows, model_width).astype(jnp.float32)
    weighted = gates.T[:, :, None] * grad_out[None]
    d_gates = jnp.einsum("cnd,nd->nc", values_pair, grad_out)
    d_const = jnp.einsum("nck,cnd->dk", const_flags, weighted, precision=lax.Precision.HIGHEST)
    d_out_slots = jnp.einsum(
        "cet,ctd->ed", table.astype(jnp.float32), weighted, precision=lax.Precision.HIGHEST
    )
    d_out_low = d_out_slots.astype(jnp.bfloat16).reshape(experts, 1, capacity, model_width)
    d_picked = (d_gates - jnp.sum(d_gates * gates, axis=-1, keepdims=True)) / picked_total
    d_probs = jnp.einsum("nc,nck->nk", d_picked, selector)
    d_logits = probs * (d_probs - jnp.sum(probs * d_probs, axis=-1, keepdims=True))
    d_router_w = jnp.dot(second_float.T, d_logits, precision=lax.Precision.HIGHEST)
    d_second = jnp.sum(copy_flag.T[:, :, None] * weighted, axis=0)
    d_second = d_second + jnp.dot(
        d_logits, full_router.astype(jnp.float32).T, precision=lax.Precision.HIGHEST
    )
    arrived_grad = lax.all_to_all(d_out_low, "shard", split_axis=0, concat_axis=1, tiled=True)
    gate_up = jnp.einsum(
        "jsrd,djgf->jsrgf", kept_slots, full_gu, preferred_element_type=jnp.float32
    )
    gate_part = gate_up[:, :, :, 0]
    up_part = gate_up[:, :, :, 1]
    sigma = jax.nn.sigmoid(gate_part)
    silu_part = gate_part * sigma
    hidden_low = (silu_part * up_part).astype(jnp.bfloat16)
    d_hidden = jnp.einsum(
        "jsrd,djf->jsrf", arrived_grad, full_down, preferred_element_type=jnp.float32
    )
    d_gate_part = d_hidden * up_part * sigma * (1.0 + gate_part * (1.0 - sigma))
    d_up_part = d_hidden * silu_part
    d_gate_up_low = jnp.stack([d_gate_part, d_up_part], axis=3).astype(jnp.bfloat16)
    d_slot_part = jnp.einsum(
        "jsrgf,djgf->jsrd", d_gate_up_low, full_gu, preferred_element_type=jnp.float32
    )
    d_slot_sum = lax.psum(d_slot_part.astype(jnp.bfloat16), "tp")
    d_slot_back = lax.all_to_all(d_slot_sum, "shard", split_axis=1, concat_axis=0, tiled=True)
    d_gate_up_w = jnp.einsum(
        "jsrd,jsrgf->djgf", kept_slots, d_gate_up_low, preferred_element_type=jnp.float32
    )
    d_down_w = jnp.einsum(
        "jsrd,jsrf->djf", arrived_grad, hidden_low, preferred_element_type=jnp.float32
    )
    d_second = d_second + jnp.einsum(
        "et,ed->td",
        routed,
        d_slot_back.reshape(experts * capacity, model_width),
        preferred_element_type=jnp.float32,
    )
    d_second_gain = jnp.sum(d_second * second_unit, axis=0)
    d_second_unit = d_second * second_gain
    d_mixed = grad_out + inv_second * (
        d_second_unit - second_unit * jnp.mean(d_second_unit * second_unit, axis=-1, keepdims=True)
    )
    d_attn_low = d_mixed.astype(jnp.bfloat16)
    d_out_w = jnp.einsum("nd,nh->dh", d_attn_low, attended_low, preferred_element_type=jnp.float32)
    d_attended = jnp.einsum("nd,dh->nh", d_attn_low, full_out, preferred_element_type=jnp.float32)
    do_low = d_attended.astype(jnp.bfloat16)
    do_heads = do_low.reshape(tree_count, rows, local_heads, HEAD_DIM)
    delta = jnp.einsum("tqhe,tqhe->thq", do_heads.astype(jnp.float32), attended)

    def tree_both(q_one, k_one, v_one, do_one, lse_one, delta_one, rows_one):

        def both_step(dq_accum, start):
            keys_blk = lax.dynamic_slice_in_dim(k_one, start, key_block, 0)
            values_blk = lax.dynamic_slice_in_dim(v_one, start, key_block, 0)
            mask = allowed_block(rows_one, query_pos, start, key_block, seg_len)
            prob_low, dscore = softmax_grads(
                q_one, do_one, lse_one, delta_one, keys_blk, values_blk, mask
            )
            dq_accum = dq_accum + jnp.einsum(
                "hqk,khe->qhe", dscore, keys_blk, preferred_element_type=jnp.float32
            )
            dkey = (
                jnp.einsum("hqk,qhe->khe", dscore, q_one, preferred_element_type=jnp.float32)
                * score_scale
            )
            dval = jnp.einsum("hqk,qhe->khe", prob_low, do_one, preferred_element_type=jnp.float32)
            return (
                dq_accum,
                jnp.stack(
                    [dkey.reshape(key_block, local_width), dval.reshape(key_block, local_width)],
                    axis=1,
                ),
            )

        dq_one, terms_one = lax.scan(
            both_step, jnp.zeros((rows, local_heads, HEAD_DIM), jnp.float32), starts
        )
        return (dq_one, terms_one.reshape(tree_len, 2, local_width))

    dq_total, key_terms = jax.vmap(tree_both)(
        q_heads, k_heads, v_heads, do_heads, lse, delta, query_rows_all
    )
    key_sums = lax.psum_scatter(
        key_terms.astype(jnp.bfloat16), "ctx", scatter_dimension=1, tiled=True
    ).astype(jnp.float32)
    key_grad = key_sums[:, :, 0].reshape(tok_rows, local_width)
    value_grad = key_sums[:, :, 1].reshape(tok_rows, local_width)
    query_grad = (dq_total * score_scale).reshape(tok_rows, local_width)
    d_qkv_low = jnp.stack([query_grad, key_grad, value_grad], axis=1).astype(jnp.bfloat16)
    d_qkv_w = jnp.einsum("nd,nke->dke", normed, d_qkv_low, preferred_element_type=jnp.float32)
    d_normed_part = jnp.einsum(
        "nke,dke->nd", d_qkv_low, full_qkv, preferred_element_type=jnp.float32
    )
    d_normed = lax.psum(d_normed_part.astype(jnp.bfloat16), "tp").astype(jnp.float32)
    d_first_gain = jnp.sum(d_normed * first_unit, axis=0)
    d_first_unit = d_normed * first_gain
    d_inputs = d_mixed + inv_first * (
        d_first_unit - first_unit * jnp.mean(d_first_unit * first_unit, axis=-1, keepdims=True)
    )
    summed_grads = (
        lax.psum_scatter(
            d_qkv_w.astype(jnp.bfloat16), "ctx", scatter_dimension=0, tiled=True
        ).astype(jnp.float32),
        lax.psum_scatter(
            d_out_w.astype(jnp.bfloat16), "ctx", scatter_dimension=0, tiled=True
        ).astype(jnp.float32),
        lax.psum_scatter(
            d_router_w.astype(jnp.bfloat16), "ctx", scatter_dimension=0, tiled=True
        ).astype(jnp.float32),
        lax.psum_scatter(
            d_first_gain.astype(jnp.bfloat16), "ctx", scatter_dimension=0, tiled=True
        ).astype(jnp.float32),
        lax.psum_scatter(
            d_second_gain.astype(jnp.bfloat16), "ctx", scatter_dimension=0, tiled=True
        ).astype(jnp.float32),
        lax.psum_scatter(
            d_const.astype(jnp.bfloat16), "ctx", scatter_dimension=0, tiled=True
        ).astype(jnp.float32),
        lax.psum_scatter(
            d_gate_up_w.astype(jnp.bfloat16), "ctx", scatter_dimension=0, tiled=True
        ).astype(jnp.float32),
        lax.psum_scatter(
            d_down_w.astype(jnp.bfloat16), "ctx", scatter_dimension=0, tiled=True
        ).astype(jnp.float32),
    )
    shared = (
        lax.psum(summed_grads[0].astype(jnp.bfloat16), "shard").astype(jnp.float32),
        lax.psum(summed_grads[1].astype(jnp.bfloat16), "shard").astype(jnp.float32),
        lax.psum(summed_grads[2].astype(jnp.bfloat16), "shard").astype(jnp.float32),
        lax.psum(summed_grads[3].astype(jnp.bfloat16), "shard").astype(jnp.float32),
        lax.psum(summed_grads[4].astype(jnp.bfloat16), "shard").astype(jnp.float32),
        lax.psum(summed_grads[5].astype(jnp.bfloat16), "shard").astype(jnp.float32),
    )
    out_rows = mixed_out.reshape(tree_count, rows, model_width)
    grad_rows = d_inputs.reshape(tree_count, rows, model_width)
    logit_rows = d_logits.reshape(tree_count, rows, every_expert)
    return (
        out_rows,
        grad_rows,
        logit_rows,
        shared[0],
        shared[1],
        shared[2],
        shared[3],
        shared[4],
        shared[5],
        summed_grads[6],
        summed_grads[7],
    )


NT = (((1,), (1,)), ((), ()))
NN = (((1,), (0,)), ((), ()))
TRUNK = 8
KEY_SEGS = 12
PIECE = 256
SENT = (0, 2, 1, 3)


def mm(a, b, dims=NN):
    return lax.dot_general(a, b, dims, preferred_element_type=jnp.float32)


def stacked(rows, half):
    first = lax.broadcasted_iota(jnp.int32, rows.shape, 1) < half
    blank = jnp.zeros_like(rows)
    return jnp.concatenate([jnp.where(first, rows, blank), jnp.where(first, blank, rows)], axis=0)


def unstack(wide, half, seg):
    return jnp.concatenate([wide[:half, :seg], wide[half:, seg:]], axis=0)


def causal(seg):
    row = lax.broadcasted_iota(jnp.int32, (seg, 2 * seg), 0)
    col = lax.broadcasted_iota(jnp.int32, (seg, 2 * seg), 1)
    return row <= jnp.where(col >= seg, col - seg, col)


def attend_kernel(own, seg, half, more, info, q_ref, k_ref, v_ref, *rest):
    o_ref, lse_ref, s_ref, p_ref = rest[2 * more :]
    trunk = TRUNK * seg
    allowed = causal(seg)
    v_trunk = v_ref[own : own + trunk, :].T

    def one(i, unused):
        count, branch, leaf = info[i, 0], info[i, 1], info[i, 2]
        here = pl.ds(pl.multiple_of(i * seg, seg), seg)
        there = pl.ds(pl.multiple_of(own + branch * seg, seg), seg)
        qs = stacked(q_ref[here, :] * 0.125, half)
        s_ref[:trunk, :] = mm(k_ref[own : own + trunk, :], qs, NT)
        s_branch = mm(k_ref[there, :], qs, NT)
        s_own = jnp.where(allowed, mm(k_ref[here, :], qs, NT), -1e30)
        biases = [jnp.where(kb < count, 0.0, -1e30) for kb in range(TRUNK)]
        leaf_bias = jnp.where(leaf > 0, 0.0, -1e30)
        top = jnp.max(s_own, axis=0, keepdims=True)
        top = jnp.maximum(top, jnp.max(s_branch, axis=0, keepdims=True) + leaf_bias)
        for kb in range(TRUNK):
            part = jnp.max(s_ref[kb * seg : (kb + 1) * seg, :], axis=0, keepdims=True)
            top = jnp.maximum(top, part + biases[kb])
        e_own = jnp.exp(s_own - top)
        e_branch = jnp.exp(s_branch - (top - leaf_bias))
        total = jnp.sum(e_own + e_branch, axis=0, keepdims=True)
        for kb in range(TRUNK):
            e = jnp.exp(s_ref[kb * seg : (kb + 1) * seg, :] - (top - biases[kb]))
            total = total + jnp.sum(e, axis=0, keepdims=True)
            p_ref[kb * seg : (kb + 1) * seg, :] = e.astype(jnp.bfloat16)
        out = mm(v_trunk, p_ref[...])
        out = out + mm(v_ref[there, :].T, e_branch.astype(jnp.bfloat16))
        out = out + mm(v_ref[here, :].T, e_own.astype(jnp.bfloat16))
        out = unstack(out * (1.0 / total), half, seg)
        o_ref[here, :] = out.T.astype(jnp.bfloat16)
        lse_ref[pl.ds(i, 1), :] = top + jnp.log(total)
        return 0

    lax.fori_loop(0, own // seg, one, 0)


def attend_back_kernel(
    own, seg, half, more, info, q_ref, k_ref, v_ref, o_ref, do_ref, lse_ref, *rest
):
    dq_ref, dk_ref, dv_ref, ak, av = rest[3 * more :]
    trunk = TRUNK * seg
    allowed = causal(seg)
    low = jnp.bfloat16
    tk = slice(own, own + trunk)
    k_trunk = k_ref[tk, :].T
    ak[...] = jnp.zeros_like(ak)
    av[...] = jnp.zeros_like(av)

    def one(i, unused):
        count, branch, leaf = info[i, 0], info[i, 1], info[i, 2]
        here = pl.ds(pl.multiple_of(i * seg, seg), seg)
        there = pl.ds(pl.multiple_of(own + branch * seg, seg), seg)
        qs = stacked(q_ref[here, :] * 0.125, half)
        do = do_ref[here, :]
        dos = stacked(do, half)
        prod = (do.astype(jnp.float32) * o_ref[here, :].astype(jnp.float32)).T
        delta = jnp.concatenate(
            [jnp.sum(prod[:half], axis=0, keepdims=True), jnp.sum(prod[half:], axis=0, keepdims=True)],
            axis=1,
        )
        lse = lse_ref[pl.ds(i, 1), :]
        leaf_bias = jnp.where(leaf > 0, 0.0, -1e30)

        def piece(keys, values, shift, mask):
            s = mm(keys, qs, NT)
            if mask:
                s = jnp.where(allowed, s, -1e30)
            if isinstance(shift, list):
                p = jnp.concatenate(
                    [jnp.exp(s[kb * seg : (kb + 1) * seg] - shift[kb]) for kb in range(TRUNK)], axis=0
                )
            else:
                p = jnp.exp(s - shift)
            ds = (p * (mm(values, dos, NT) - delta)).astype(low)
            p = p.astype(low)
            return (mm(p, dos), mm(ds, qs), ds)

        shifts = [lse - jnp.where(kb < count, 0.0, -1e30) for kb in range(TRUNK)]
        dv, dk, ds = piece(k_ref[tk, :], v_ref[tk, :], shifts, False)
        av[tk, :] += dv
        ak[tk, :] += dk
        dq = mm(k_trunk, ds)
        keys = k_ref[there, :]
        dv, dk, ds = piece(keys, v_ref[there, :], lse - leaf_bias, False)
        av[there, :] += dv
        ak[there, :] += dk
        dq = dq + mm(keys.T, ds)
        keys = k_ref[here, :]
        dv, dk, ds = piece(keys, v_ref[here, :], lse, True)
        av[here, :] += dv
        ak[here, :] += dk
        dq = dq + mm(keys.T, ds)
        dq_ref[here, :] = (unstack(dq, half, seg) * 0.125).T.astype(low)
        return 0

    lax.fori_loop(0, own // seg, one, 0)
    dk_ref[...] = ak[...].astype(low)
    dv_ref[...] = av[...].astype(low)


def attend(info, q, kv, seg, begin, count, prev=()):
    own, width = q.shape
    total = kv.shape[0]
    pairs = width // 128
    lane = pl.BlockSpec((own, 128), lambda h: (0, begin + h))
    return pl.pallas_call(
        functools.partial(attend_kernel, own, seg, HEAD_DIM, len(prev) > 0),
        grid=(count,),
        in_specs=[
            pl.BlockSpec(memory_space=pltpu.SMEM),
            lane,
            pl.BlockSpec((total, 128), lambda h: (0, begin + h)),
            pl.BlockSpec((total, 128), lambda h: (0, pairs + begin + h)),
        ]
        + [pl.BlockSpec(memory_space=pl.ANY)] * len(prev),
        out_specs=[lane, pl.BlockSpec((None, 8, 2 * seg), lambda h: (begin + h, 0, 0))],
        out_shape=[
            jax.ShapeDtypeStruct((own, width), jnp.bfloat16),
            jax.ShapeDtypeStruct((pairs, 8, 2 * seg), jnp.float32),
        ],
        input_output_aliases={4 + i: i for i in range(len(prev))},
        scratch_shapes=[
            pltpu.VMEM((TRUNK * seg, 2 * seg), jnp.float32),
            pltpu.VMEM((TRUNK * seg, 2 * seg), jnp.bfloat16),
        ],
        compiler_params=pltpu.CompilerParams(vmem_limit_bytes=60 << 20),
        cost_estimate=pl.CostEstimate(
            flops=1000, bytes_accessed= 1000, transcendentals=0
        ),
        name="attend",
    )(info, q, kv, kv, *prev)


def attend_back(info, q, kv, o, do, lse, seg, begin, count, prev=()):
    own, width = q.shape
    total = kv.shape[0]
    pairs = width // 128
    lane = pl.BlockSpec((own, 128), lambda h: (0, begin + h))
    keys = pl.BlockSpec((total, 128), lambda h: (0, begin + h))
    return pl.pallas_call(
        functools.partial(attend_back_kernel, own, seg, HEAD_DIM, len(prev) > 0),
        grid=(count,),
        in_specs=[
            pl.BlockSpec(memory_space=pltpu.SMEM),
            lane,
            keys,
            pl.BlockSpec((total, 128), lambda h: (0, pairs + begin + h)),
            lane,
            lane,
            pl.BlockSpec((None, 8, 2 * seg), lambda h: (begin + h, 0, 0)),
        ]
        + [pl.BlockSpec(memory_space=pl.ANY)] * len(prev),
        out_specs=[lane, keys, keys],
        out_shape=[
            jax.ShapeDtypeStruct((own, width), jnp.bfloat16),
            jax.ShapeDtypeStruct((total, width), jnp.bfloat16),
            jax.ShapeDtypeStruct((total, width), jnp.bfloat16),
        ],
        input_output_aliases={7 + i: i for i in range(len(prev))},
        scratch_shapes=[
            pltpu.VMEM((total, 128), jnp.float32),
            pltpu.VMEM((total, 128), jnp.float32),
        ],
        compiler_params=pltpu.CompilerParams(vmem_limit_bytes=40 << 20),
        cost_estimate=pl.CostEstimate(
            flops=1000, bytes_accessed= 1000, transcendentals=0
        ),
        name="attend_back",
    )(info, q, kv, kv, o, do, lse, *prev)


def pin(x, *after):
    return lax.optimization_barrier((x,) + after)[0]


def expert_kernel(
    more, capacity, pieces, place, xm_ref, xo_ref, gm_ref, go_ref, w0, w1, w2, w3, *rest
):
    low, full = jnp.bfloat16, jnp.float32
    o_ref, o2_ref, s_ref, s2_ref, dw_ref, x_ref, g_ref, xt, dt, d_ref, oa, sa, wb, gb = rest[more:]
    part = w0.shape[1]
    rows, wide = xm_ref.shape
    padded = rows // pieces
    tail = padded - 16
    here = pl.ds(pl.multiple_of(place[1] * wide, 128), wide)
    there = pl.ds(pl.multiple_of((1 - place[1]) * wide, 128), wide)

    @pl.when(pl.program_id(0) == 0)
    def start():
        x_ref[:, here] = xm_ref[...]
        x_ref[:, there] = xo_ref[...]
        g_ref[:, here] = gm_ref[...]
        g_ref[:, there] = go_ref[...]
        for p in range(pieces):
            mine = slice(p * padded, (p + 1) * padded)
            last = xm_ref[p * padded + tail : (p + 1) * padded, :256].astype(full)
            row = lax.broadcasted_iota(jnp.int32, last.shape, 0) + tail
            inside = (row >= capacity) & (row < capacity + 3)
            gate = jnp.sum(jnp.where(inside, last, 0.0), axis=0, keepdims=True)
            gate = jnp.broadcast_to(gate, (8, 256)).T[:padded, 0:1]
            d_ref[mine, :] = (g_ref[mine, :].astype(full) * gate).astype(low)
        xt[...] = x_ref[...].T
        dt[...] = d_ref[...].T
        oa[...] = jnp.zeros_like(oa)
        sa[...] = jnp.zeros_like(sa)

    def rows_of(r):
        return pl.ds(pl.multiple_of((place[0] ^ r) * part, 64), part)

    for r, w in enumerate((w0, w1, w2, w3)):
        wb[:, rows_of(r), :] = w[...]
    u = mm(x_ref[...], wb[0])
    up = mm(x_ref[...], wb[1])
    sigma = 1.0 / (1.0 + jnp.exp(-u))
    silu = u * sigma
    hidden = (silu * up).astype(low)
    oa[...] += mm(hidden, wb[2], NT)
    dh = mm(d_ref[...], wb[2])
    du = (dh * up * sigma * (1.0 + u * (1.0 - sigma))).astype(low)
    dup = (dh * silu).astype(low)
    sa[...] += mm(du, wb[0], NT) + mm(dup, wb[1], NT)
    gb[0] = mm(xt[...], du).astype(low)
    gb[1] = mm(xt[...], dup).astype(low)
    gb[2] = mm(dt[...], hidden).astype(low)
    for at, r in enumerate(SENT):
        got = gb[:, rows_of(r), :]
        if more:
            got = (got.astype(full) + rest[0][at].astype(full)).astype(low)
        dw_ref[at] = got

    @pl.when(pl.program_id(0) == pl.num_programs(0) - 1)
    def finish():
        o_ref[...] = oa[:, here].astype(low)
        o2_ref[...] = oa[:, there].astype(low)
        s_ref[...] = sa[:, here].astype(low)
        s2_ref[...] = sa[:, there].astype(low)
        for p in range(pieces):
            mine = slice(p * padded, (p + 1) * padded)
            dot = jnp.sum(g_ref[mine, :].astype(full) * oa[mine, :], axis=1, keepdims=True)
            dot = jnp.broadcast_to(dot, (padded, 128)).T[:16, :]
            dot = jnp.concatenate([dot, jnp.zeros((16, wide - padded), full)], axis=1)
            row = lax.broadcasted_iota(jnp.int32, dot.shape, 0) + tail
            kept = jnp.zeros_like(dot)
            for i in range(3):
                piece = dot.astype(low).astype(full)
                kept = jnp.where(row == capacity + i, piece, kept)
                dot = dot - piece
            last = slice(p * padded + tail, (p + 1) * padded)
            row_low = s_ref[last, :].astype(full)
            s_ref[last, :] = jnp.where(row >= capacity, kept, row_low).astype(low)


def expert_pass(place, capacity, pieces, xs, gs, weights, prev):
    rows, half_width = xs[0].shape
    width = 2 * half_width
    three, part, units = weights[0].shape
    low = jnp.bfloat16
    strip = pl.BlockSpec((three, part, PIECE), lambda j, *at: (0, 0, j))
    strips = pl.BlockSpec((4, three, part, PIECE), lambda j, *at: (0, 0, 0, j))
    half = whole(rows, half_width)
    more = prev is not None
    return call(
        functools.partial(expert_kernel, int(more), capacity, pieces),
        "expert_pass",
        [((rows, half_width), low)] * 4 + [((4, three, part, units), low)],
        (place, *xs, *gs, *weights, *([prev] if more else [])),
        [
            pltpu.VMEM((rows, width), low),
            pltpu.VMEM((rows, width), low),
            pltpu.VMEM((width, rows), low),
            pltpu.VMEM((width, rows), low),
            pltpu.VMEM((rows, width), low),
            pltpu.VMEM((rows, width), jnp.float32),
            pltpu.VMEM((rows, width), jnp.float32),
            pltpu.VMEM((three, width, PIECE), low),
            pltpu.VMEM((three, width, PIECE), low),
        ],
        grid=(units // PIECE,),
        in_specs=[half] * 4 + [strip] * 4 + [strips] * more,
        out_specs=[half] * 4 + [strips],
        prefetch=True,
        mib=48,
    )


def spread_kernel(pieces, padded, capacity, gated, place_ref, rows_ref, *rest):
    low = jnp.bfloat16
    outs = rest[1:] if gated else rest
    tokens = rows_ref.shape[0]
    for p in range(pieces):
        slot = lax.broadcasted_iota(jnp.int32, (padded, tokens), 0) + p * padded
        hits = [slot == place_ref[c : c + 1, :] for c in range(2)]
        out = mm(jnp.where(hits[0] | hits[1], 1.0, 0.0).astype(low), rows_ref[...]).astype(low)
        if gated:
            parts = 0.0
            for c in range(2):
                value = rest[0][c : c + 1, :]
                rows3 = []
                for i in range(3):
                    rows3.append(value.astype(low).astype(jnp.float32))
                    value = value - rows3[-1]
                rows3.append(jnp.zeros((13, tokens), jnp.float32))
                three = jnp.concatenate(rows3, axis=0).astype(low)
                parts = parts + mm(three, jnp.where(hits[c], 1.0, 0.0).astype(low), NT)
            parts = parts.astype(low)
            blank = jnp.zeros((parts.shape[0], out.shape[1] - padded), low)
            parts = jnp.concatenate([parts, blank], axis=1)
            row = lax.broadcasted_iota(jnp.int32, out.shape, 0)
            for i in range(3):
                out = jnp.where(row == capacity + i, parts[i : i + 1, :], out)
        outs[p][...] = out


def spread(place, rows, pieces, padded, capacity, parts=None):
    shape = jax.ShapeDtypeStruct((padded, rows.shape[1]), jnp.bfloat16)
    gated = parts is not None
    return pl.pallas_call(
        functools.partial(spread_kernel, pieces, padded, capacity, gated),
        in_specs=[pl.BlockSpec(memory_space=pltpu.VMEM)] * (2 + gated),
        out_specs=[pl.BlockSpec(memory_space=pltpu.VMEM)] * pieces,
        out_shape=[shape] * pieces,
        compiler_params=pltpu.CompilerParams(vmem_limit_bytes=60 << 20),
        cost_estimate=pl.CostEstimate(flops=1000, bytes_accessed= 1000, transcendentals=0),
        name="spread",
    )(place, rows, *([parts] if gated else []))


def gather_kernel(pieces, padded, capacity, dots, place_ref, *rest):
    low = jnp.bfloat16
    if dots:
        ins, (out_ref, out2_ref, dot_ref, dot2_ref) = rest[:pieces], rest[pieces:]
    else:
        gate_ref, ins, (out_ref, out2_ref) = rest[0], rest[1 : 1 + pieces], rest[1 + pieces :]
    tokens = place_ref.shape[0]
    total = None
    sums = [0.0, 0.0]
    for p in range(pieces):
        slot = lax.broadcasted_iota(jnp.int32, (tokens, padded), 1) + p * padded
        hits = [slot == place_ref[:, c : c + 1] for c in range(2)]
        if dots:
            picks = [jnp.where(h, 1.0, 0.0).astype(low) for h in hits]
            values = ins[p][capacity : capacity + 3, :padded]
            values = jnp.concatenate([values, jnp.zeros((13, padded), low)], axis=0)
            for c in range(2):
                sums[c] = sums[c] + mm(picks[c], values, NT)
            pick = picks[0] + picks[1]
        else:
            pick = jnp.where(hits[0], gate_ref[:, 0:1], jnp.where(hits[1], gate_ref[:, 1:2], 0.0))
            pick = pick.astype(low)
        part = mm(pick, ins[p][...])
        total = part if total is None else total + part
    rows = tokens // 2
    out_ref[...] = total[:rows].astype(low)
    out2_ref[...] = total[rows:].astype(low)
    if dots:
        for c in range(2):
            dot_ref[:, c : c + 1] = jnp.sum(sums[c][:rows], axis=1, keepdims=True)
            dot2_ref[:, c : c + 1] = jnp.sum(sums[c][rows:], axis=1, keepdims=True)


def gather(place, pieces, capacity, gate=None):
    padded, width = pieces[0].shape
    tokens = place.shape[0]
    dots = gate is None
    shapes = [jax.ShapeDtypeStruct((tokens // 2, width), jnp.bfloat16)] * 2
    if dots:
        shapes = shapes + [jax.ShapeDtypeStruct((tokens // 2, 2), jnp.float32)] * 2
    return pl.pallas_call(
        functools.partial(gather_kernel, len(pieces), padded, capacity, dots),
        in_specs=[pl.BlockSpec(memory_space=pltpu.VMEM)] * (len(pieces) + (1 if dots else 2)),
        out_specs=[pl.BlockSpec(memory_space=pltpu.VMEM)] * len(shapes),
        out_shape=shapes,
        compiler_params=pltpu.CompilerParams(vmem_limit_bytes=60 << 20),
        cost_estimate=pl.CostEstimate(flops=1000, bytes_accessed= 1000, transcendentals=0),
        name="gather",
    )(place, *([] if dots else [gate]), *pieces)


def whole(*shape):
    return pl.BlockSpec(shape, lambda *at: (0,) * len(shape))


def by_rows(*shape):
    return pl.BlockSpec(shape, lambda j, *at: (j, 0))


def chosen(number, *shape):
    return pl.BlockSpec((None,) + shape, lambda j, place: (number ^ place[0], 0, 0))


def call(kernel, name, outs, args, scratch=(), grid=(1,), in_specs=None, out_specs=None, prefetch=False, mib=40):
    if out_specs is None:
        out_specs = [whole(*o[0]) for o in outs]
    spec = pltpu.PrefetchScalarGridSpec(
        num_scalar_prefetch=int(prefetch),
        grid=grid,
        in_specs=in_specs,
        out_specs=out_specs,
        scratch_shapes=list(scratch),
    )
    return pl.pallas_call(
        kernel,
        grid_spec=spec,
        out_shape=[jax.ShapeDtypeStruct(*o) for o in outs],
        compiler_params=pltpu.CompilerParams(vmem_limit_bytes=mib << 20),
        cost_estimate=pl.CostEstimate(flops=1000, bytes_accessed=1000, transcendentals=0),
        name=name,
    )(*args)


def unit_rows(x):
    x = x.astype(jnp.float32)
    return x * lax.rsqrt(jnp.mean(x * x, axis=-1, keepdims=True) + eps)


def project_kernel(place, x0, near, mid, farther, gain, wm, wo, q_ref, kv_ref, n_ref, x_ref):
    low = jnp.bfloat16
    shard, ctx = place[0], place[1]
    rows, width = x0.shape
    half = wm.shape[2]

    def project(lo, x):
        here = slice(lo, lo + x.shape[0])
        normed = (unit_rows(x) * gain[...]).astype(low)
        x_ref[here, :] = x
        n_ref[here, :] = normed
        for m in (1, 2):
            for h, w in enumerate((wm, wo)):
                at = (m - 1) * width + h * half
                kv_ref[here, at : at + half] = mm(normed, w[m ^ shard]).astype(low)
        if lo == 0:
            for h, w in enumerate((wm, wo)):
                q_ref[:, h * half : (h + 1) * half] = mm(normed, w[shard]).astype(low)

    edge = x_ref.shape[0] - 3 * rows
    project(0, x0[...])
    later = jnp.where(ctx == 2, mid[...], farther[...])
    project(rows, jnp.where(ctx == 0, x0[...], jnp.where(ctx == 1, near[...], later)))
    later = jnp.where(ctx == 2, near[...], mid[...])
    project(2 * rows, jnp.where(ctx == 1, x0[...], later))
    project(3 * rows, jnp.where(ctx == 2, x0[:edge, :], near[:edge, :]))


def settle_kernel(
    place, o, x, wm, wo, gain, router, res, ids,
    mixed_ref, second_ref, mine_ref, other_ref, probs_ref, stat_ref, gates_ref,
):
    tp = place[2]
    half = wm.shape[1]
    attn = mm(o[:, :half], wm[...], NT) + mm(o[:, half:], wo[...], NT)
    mixed = x[...].astype(jnp.float32) + attn
    mixed_ref[...] = mixed
    inverse = lax.rsqrt(jnp.mean(mixed * mixed, axis=-1, keepdims=True) + eps)
    second = (mixed * inverse * gain[...]).astype(jnp.bfloat16)
    second_ref[...] = second
    mine_ref[...] = second_ref[:, pl.ds(pl.multiple_of(tp * half, 128), half)]
    other_ref[...] = second_ref[:, pl.ds(pl.multiple_of((1 - tp) * half, 128), half)]
    logits = mm(second, router[...], NT) + res[...]
    expo = jnp.exp(logits - jnp.max(logits, axis=-1, keepdims=True))
    probs = expo / jnp.sum(expo, axis=-1, keepdims=True)
    probs_ref[...] = probs
    lane = lax.broadcasted_iota(jnp.int32, probs.shape, 1)
    picked = [
        jnp.sum(jnp.where(lane == ids[:, c : c + 1], probs, 0.0), axis=-1, keepdims=True)
        for c in range(2)
    ]
    total = picked[0] + picked[1]
    wide = lax.broadcasted_iota(jnp.int32, (probs.shape[0], 128), 1)
    stat = jnp.where(wide == 0, picked[0] / total, jnp.where(wide == 1, picked[1] / total, 0.0))
    stat = jnp.where(wide == 2, total, jnp.where(wide == 3, inverse, stat))
    stat_ref[...] = stat[:, :8]
    gates_ref[...] = stat.T[:8, :]


def settle_back_kernel(
    copy_id, place, dr_mine, dr_came, dg_mine, dg_came, g_ref, mixed, second, probs_ref, stat, ids,
    const, router, gain, wm, wo, dmix_ref, dattn_ref, do_ref, dlog_ref, small_ref, full_ref,
):
    low, full = jnp.bfloat16, jnp.float32
    tp = place[2]
    half = wm.shape[1]
    full_ref[:, pl.ds(pl.multiple_of(tp * half, 128), half)] = dr_mine[...]
    full_ref[:, pl.ds(pl.multiple_of((1 - tp) * half, 128), half)] = dr_came[...]
    g = g_ref[...].astype(full)
    probs = probs_ref[...]
    gates = [stat[:, 0:1], stat[:, 1:2]]
    total, inverse = stat[:, 2:3], stat[:, 3:4]
    ids_c = [ids[:, 0:1], ids[:, 1:2]]
    zero = jnp.zeros_like(total)

    def gate_of(number):
        return sum(jnp.where(ids_c[c] == number, gates[c], zero) for c in range(2))

    copy_gate = gate_of(copy_id)
    const_gate = [gate_of(copy_id + 1 + k) for k in range(2)]
    dots = [jnp.sum(g * second[...].astype(full), axis=-1, keepdims=True)]
    dots = dots + [jnp.sum(g * const[k : k + 1, :], axis=-1, keepdims=True) for k in range(2)]
    d_gates = []
    for c in range(2):
        d = dg_mine[:, c : c + 1] + dg_came[:, c : c + 1]
        for k in range(3):
            d = d + jnp.where(ids_c[c] == copy_id + k, dots[k], zero)
        d_gates.append(d)
    mean = d_gates[0] * gates[0] + d_gates[1] * gates[1]
    lane = lax.broadcasted_iota(jnp.int32, probs.shape, 1)
    d_probs = jnp.zeros_like(probs)
    for c in range(2):
        d_probs = d_probs + jnp.where(lane == ids_c[c], (d_gates[c] - mean) / total, 0.0)
    d_logits = probs * (d_probs - jnp.sum(probs * d_probs, axis=-1, keepdims=True))
    dlog_ref[...] = d_logits
    d_second = copy_gate * g + full_ref[...].astype(full)
    rest = d_logits
    for i in range(3):
        piece = rest.astype(low)
        rest = rest - piece.astype(full)
        d_second = d_second + mm(piece, router[...])
    unit = mixed[...] * inverse
    d_gain = jnp.sum(d_second * unit, axis=0, keepdims=True)
    d_unit = d_second * gain[...]
    d_mixed = g + inverse * (d_unit - unit * jnp.mean(d_unit * unit, axis=-1, keepdims=True))
    dmix_ref[...] = d_mixed
    d_attn = d_mixed.astype(low)
    dattn_ref[...] = d_attn
    do_ref[:, :half] = mm(d_attn, wm[...]).astype(low)
    do_ref[:, half:] = mm(d_attn, wo[...]).astype(low)
    count = probs.shape[1]
    pad = jnp.zeros((probs.shape[0], 128 - count), full)
    wide = lax.broadcasted_iota(jnp.int32, (probs.shape[0], 128), 1)
    table = jnp.concatenate([d_logits, pad], axis=1)
    table = jnp.where(wide == count + 2, const_gate[0], table)
    table = jnp.where(wide == count + 3, const_gate[1], table)
    rest = table.T[: count + 4, :]
    from_second = from_g = 0.0
    for i in range(3):
        piece = rest.astype(low)
        rest = rest - piece.astype(full)
        from_second = from_second + mm(piece, second[...])
        from_g = from_g + mm(piece, g_ref[...])
    row = lax.broadcasted_iota(jnp.int32, from_g.shape, 0)
    small = jnp.where(row < count, from_second, jnp.where(row >= count + 2, from_g, 0.0))
    small_ref[...] = jnp.where(row == count + 1, d_gain, small)


def keys_back_kernel(place, dq, dk, dv, x, wm, wo, own_ref, p0_ref, p1_ref, p2_ref, gain_ref):
    shard = place[0]
    rows, width = own_ref.shape
    half = wm.shape[2]
    gain = jnp.zeros((1, width), jnp.float32)
    lo = 0
    for out in (own_ref, p0_ref, p1_ref, p2_ref):
        here = slice(lo, lo + out.shape[0])
        lo = lo + out.shape[0]
        d = 0.0
        for m, grad in ((0, dq), (1, dk), (2, dv)):
            if m > 0 or out is own_ref:
                d = d + mm(grad[here, :half], wm[m ^ shard], NT)
                d = d + mm(grad[here, half:], wo[m ^ shard], NT)
        out[...] = d.astype(out.dtype)
        gain = gain + jnp.sum(d * unit_rows(x[here, :]), axis=0, keepdims=True)
    gain_ref[...] = gain


def weights_back_kernel(n_ref, dq, dk, dv, da_ref, o, tiny, mine_ref, other_ref, nt, at):
    rows = dq.shape[0]
    step = pl.program_id(0)

    @pl.when(step == 0)
    def start():
        nt[...] = n_ref[...].T
        at[...] = da_ref[...].T

    def put(value):
        value = value.astype(jnp.bfloat16)
        part = value.shape[0] // mine_ref.shape[0]

        def write(ref):
            for z in range(ref.shape[0]):
                ref[z, :part, :] = value[z * part : (z + 1) * part, :]
                ref[z, part:, :] = tiny[z]

        pl.when(step % 2 == 0)(lambda: write(mine_ref))
        pl.when(step % 2 == 1)(lambda: write(other_ref))

    pl.when(step // 2 == 0)(lambda: put(mm(nt[:, :rows], dq[...])))
    pl.when(step // 2 == 1)(lambda: put(mm(nt[...], dk[...])))
    pl.when(step // 2 == 2)(lambda: put(mm(nt[...], dv[...])))
    pl.when(step // 2 == 3)(lambda: put(mm(at[...], o[...])))


def weights_back(normed, dq, dk, dv, d_attn, o, tiny):
    total, width = normed.shape
    rows, half = dq.shape[0], width // 2
    parts, room = tiny.shape[1], tiny.shape[2]
    low = jnp.bfloat16

    def columns(n, first):
        return pl.BlockSpec((n, half), lambda j: (0, jnp.clip(j - first, 0, 1)))

    out = pl.BlockSpec((None, parts, width // parts + room, half), lambda j: (j // 2, 0, 0, 0))
    shape = ((4, parts, width // parts + room, half), low)
    return call(
        weights_back_kernel,
        "weights_back",
        [shape, shape],
        (normed, dq, dk, dv, d_attn, o, tiny),
        [pltpu.VMEM((width, total), low), pltpu.VMEM((width, rows), low)],
        grid=(8,),
        in_specs=[
            pl.BlockSpec((total, width), lambda j: (0, 0)),
            columns(rows, 0),
            columns(total, 2),
            columns(total, 4),
            pl.BlockSpec((rows, width), lambda j: (0, 0)),
            columns(rows, 6),
            pl.BlockSpec((None, parts, room, half), lambda j: (j // 2, 0, 0, j % 2)),
        ],
        out_specs=[out, out],
    )


def flip(x, axis, bit, size):
    return lax.ppermute(x, axis, [(i, i ^ bit) for i in range(size)])


def turn_gather(x, size, position):
    out = jnp.zeros((size,) + x.shape, x.dtype)
    out = lax.dynamic_update_index_in_dim(out, x, position, 0)
    for k in range(1, size):
        block = lax.ppermute(x, "ctx", [(i, (i + k) % size) for i in range(size)])
        out = lax.dynamic_update_index_in_dim(out, block, (position - k) % size, 0)
    return out


def turn_sum(x, size, position):
    total = lax.dynamic_index_in_dim(x, position, 0, keepdims=False).astype(jnp.float32)
    for k in range(1, size):
        block = lax.dynamic_index_in_dim(x, (position + k) % size, 0, keepdims=False)
        got = lax.ppermute(block, "ctx", [(i, (i + k) % size) for i in range(size)])
        total = total + got.astype(jnp.float32)
    return total


def far(x, k, shards_n, ctx_n):
    pairs = []
    for s in range(shards_n):
        for z in range(ctx_n):
            pairs.append((s * ctx_n + z, (s ^ k) * ctx_n + (z ^ 2)))
    return lax.ppermute(x, ("shard", "ctx"), pairs)


def three_parts(x):
    one = x.astype(jnp.bfloat16)
    rest = x - one.astype(jnp.float32)
    two = rest.astype(jnp.bfloat16)
    return jnp.stack([one, two, (rest - two.astype(jnp.float32)).astype(jnp.bfloat16)], axis=-2)


def with_rows(slots, values, at):
    extra = three_parts(values)
    after = slots.shape[-2] - at - extra.shape[-2]
    pads = ((0, 0), (at, after), (0, slots.shape[-1] - extra.shape[-1]))
    return slots + jnp.pad(extra, pads)


def row_values(slots, at):
    return jnp.sum(slots[:, at : at + 3, : slots.shape[1]].astype(jnp.float32), axis=1)


def by_core(
    tokens, gate_res, cotangent, parents, expert_ids, priority, w_qkv, w_out, w_router, attn_gain,
    ffn_gain, const_vec, w_gate_up, w_down,
):
    low, full = jnp.bfloat16, jnp.float32
    shard, ctx, tp = lax.axis_index("shard"), lax.axis_index("ctx"), lax.axis_index("tp")
    shards_n, ctx_n = lax.axis_size("shard"), lax.axis_size("ctx")
    trees, rows, width = tokens.shape
    rows_d = w_qkv.shape[0]
    part = width // 2
    seg = rows * ctx_n // parents.shape[1]
    own_segs = rows // seg
    edge = KEY_SEGS * seg - 2 * rows

    def own_tree(x):
        return lax.dynamic_index_in_dim(x, tp, 0, keepdims=False)

    def in_order(x, other, axis=0):
        return jnp.concatenate([jnp.where(tp == 0, x, other), jnp.where(tp == 0, other, x)], axis=axis)

    def both_trees(x, other):
        return in_order(x[None], other[None])

    def unit_of(x):
        x = x.astype(full)
        inverse = lax.rsqrt(jnp.mean(x * x, axis=-1, keepdims=True) + eps)
        return (x * inverse, inverse)

    def swap(x):
        return flip(x, "tp", 1, 2)

    def plus(x, y):
        return (x.astype(full) + y.astype(full)).astype(low)

    def my_half(x, which):
        return lax.dynamic_slice_in_dim(x, which * part, part, x.ndim - 1)

    x_own = lax.optimization_barrier(own_tree(tokens))
    ends = [(i, i + 1) for i in range(ctx_n - 1)]
    near = lax.ppermute(x_own, "ctx", ends)

    mine = jnp.stack([w_qkv[:, 0], w_qkv[:, 1], w_qkv[:, 2], w_out])
    small = jnp.concatenate([w_router.T, attn_gain[None], ffn_gain[None], const_vec.T], axis=0)
    all_experts = w_router.shape[1]
    mine = lax.dynamic_index_in_dim(mine, shard, 0, keepdims=False)
    mine = jnp.concatenate([mine, small.reshape(-1, part)], axis=0)
    turned = turn_gather(mine, ctx_n, ctx)
    matrix = turned[:, :rows_d].reshape(width, -1)
    small = turned[:, rows_d:].reshape(ctx_n, -1, rows_d).transpose(1, 0, 2).reshape(-1, width)
    router_t = small[:all_experts]
    gain_a = small[all_experts].astype(full)
    gain_f = small[all_experts + 1].astype(full)
    const_t = small[all_experts + 2 :].astype(full)

    mid = lax.ppermute(pin(near, matrix), "ctx", ends[1:])
    plane_pieces = [matrix] + [flip(matrix, "shard", k, shards_n) for k in range(1, shards_n)]
    capacity = trees * rows * 2 // all_experts
    experts = shards_n * w_gate_up.shape[1]
    padded = -(-(capacity + 3) // 16) * 16
    count = experts * padded
    flat = expert_ids.reshape(-1)
    order = (2 * priority[0, 0][:, None] + jnp.arange(2, dtype=jnp.int32)[None, :]).reshape(-1)
    earlier = (flat[:, None] == flat[None, :]) & (order[None, :] < order[:, None])
    ranks = jnp.sum(earlier.astype(jnp.int32), axis=1)
    kept = (flat < experts) & (ranks < capacity)
    piece = ((flat % 2) ^ (ctx // 2)) * shards_n + ((flat // 2) ^ shard)
    place = jnp.where(kept, piece * padded + ranks, -1).reshape(trees, rows, 2)
    place = jnp.where(tp == 0, place, place[::-1]).reshape(trees * rows, 2)
    place_t = place.T

    g_own = own_tree(cotangent)
    g_other = lax.dynamic_index_in_dim(cotangent, 1 - tp, 0, keepdims=False)
    g_half = my_half(jnp.concatenate([g_own, g_other], axis=0), tp)
    g_slots = spread(place_t, g_half, experts, padded, capacity)
    ids = own_tree(expert_ids)
    res = own_tree(gate_res)
    ids, res, router_t, gain_a, gain_f, const_t, mid, *g_slots = lax.optimization_barrier(
        (ids, res, router_t, gain_a[None], gain_f[None], const_t, mid, *g_slots)
    )
    farther = lax.ppermute(mid, "ctx", ends[2:])
    plane = jnp.stack(plane_pieces)

    plane_other = swap(plane)
    place3 = jnp.stack([shard, ctx, tp]).astype(jnp.int32)

    capacity = trees * rows * 2 // all_experts
    experts = shards_n * w_gate_up.shape[1]
    padded = -(-(capacity + 3) // 16) * 16
    count = experts * padded
    flat = expert_ids.reshape(-1)
    order = (2 * priority[0, 0][:, None] + jnp.arange(2, dtype=jnp.int32)[None, :]).reshape(-1)
    earlier = (flat[:, None] == flat[None, :]) & (order[None, :] < order[:, None])
    ranks = jnp.sum(earlier.astype(jnp.int32), axis=1)
    kept = (flat < experts) & (ranks < capacity)
    piece = ((flat % 2) ^ (ctx // 2)) * shards_n + ((flat // 2) ^ shard)
    place = jnp.where(kept, piece * padded + ranks, -1).reshape(trees, rows, 2)
    place = jnp.where(tp == 0, place, place[::-1]).reshape(trees * rows, 2)
    place_t = place.T

    g_own = own_tree(cotangent)
    g_other = lax.dynamic_index_in_dim(cotangent, 1 - tp, 0, keepdims=False)
    g_half = my_half(jnp.concatenate([g_own, g_other], axis=0), tp)
    g_slots = spread(place_t, g_half, experts, padded, capacity)
    g_near = jnp.stack(g_slots[:shards_n])
    g_far = flip(pin(jnp.stack(g_slots[shards_n:]), mid), "ctx", 2, ctx_n)
    plane_other = swap(plane)
    place3 = jnp.stack([shard, ctx, tp]).astype(jnp.int32)

    g_near = jnp.stack(g_slots[:shards_n])
    g_far = flip(jnp.stack(g_slots[shards_n:]), "ctx", 2, ctx_n)

    held, gu, dn = lax.optimization_barrier((near, w_gate_up, w_down))
    lower = ctx < 2
    first = jnp.stack([gu[:, 0, 0], gu[:, 0, 1], dn[:, 0]])
    second_e = jnp.stack([gu[:, 1, 0], gu[:, 1, 1], dn[:, 1]])
    rows_own = jnp.where(lower, first, second_e)
    rows_two = flip(pin(jnp.where(lower, second_e, first), farther, g_far), "ctx", 2, ctx_n)
    rows_one = flip(pin(rows_own, farther, g_far), "ctx", 1, ctx_n)

    total = 3 * rows + edge
    q, kv, normed, x_all = call(
        project_kernel,
        "project",
        [((rows, width), low), ((total, 2 * width), low), ((total, width), low), ((total, width), low)],
        (place3, x_own, near, mid, farther, gain_a, plane, plane_other),
        in_specs=[whole(rows, width)] * 4
        + [whole(1, width), whole(4, width, part), whole(4, width, part)],
        prefetch=True,
    )

    seg_id = ctx * own_segs + jnp.arange(own_segs, dtype=jnp.int32)
    parent = jnp.take(own_tree(parents), seg_id)
    leaf = (seg_id >= KEY_SEGS).astype(jnp.int32)
    info = jnp.stack([jnp.minimum(seg_id, TRUNK), jnp.where(leaf > 0, parent, TRUNK), leaf], axis=1)
    half_pairs = width // 256
    ahead = attend(info, q, kv, seg, 0, half_pairs)
    g_seen = pin(g_far, ahead[0])
    o_low, lse = attend(info, q, kv, seg, half_pairs, half_pairs, ahead)
    o_low = pin(o_low, rows_one, rows_two)

    g_pairs = jnp.stack([g_near, g_seen], axis=1)
    g_in = jnp.stack(
        [g_pairs[0]] + [flip(g_pairs[k], "shard", k, shards_n) for k in range(1, shards_n)], axis=1
    ).reshape(2, shards_n * padded, part)
    g_out = swap(g_in)

    one_half = ((rows, part), low)
    mixed, second, second_mine, second_other, probs, stat, gates_t = call(
        settle_kernel,
        "settle",
        [
            ((rows, width), full), ((rows, width), low), one_half, one_half,
            ((rows, all_experts), full), ((rows, 8), full), ((8, rows), full),
        ],
        (place3, o_low, x_own, plane, plane_other, gain_f, router_t, res, ids),
        in_specs=[
            whole(rows, width), whole(rows, width), chosen(3, width, part), chosen(3, width, part),
            whole(1, width), whole(all_experts, width), whole(rows, all_experts), whole(rows, 2),
        ],
        prefetch=True,
    )
    second_half = jnp.concatenate([second_mine, swap(second_other)], axis=0)
    gates_both = jnp.concatenate([gates_t, swap(gates_t)], axis=1)

    rows_three = flip(pin(rows_two, o_low), "ctx", 1, ctx_n)
    weights = (rows_own, rows_one, rows_two, rows_three)
    slots = spread(place_t, pin(second_half, g_in), experts, padded, capacity, gates_both)
    x_far = [far(slots[shards_n + k], k, shards_n, ctx_n) for k in range(shards_n)]
    x_near = [slots[0]] + [flip(slots[k], "shard", k, shards_n) for k in range(1, shards_n)]

    def experts_on(pieces, gs, prev):
        x = jnp.concatenate(pieces, axis=0)
        return expert_pass(place3[1:], capacity, shards_n, (x, swap(x)), gs, weights, prev)

    def answers(mine, other):
        return plus(mine, swap(other)).reshape(shards_n, padded, part)

    x_near[0] = pin(x_near[0], rows_three)
    on1, ox1, sn1, sx1, dw = experts_on(x_near, (g_in[0], g_out[0]), None)
    x_far = list(lax.optimization_barrier((*x_far, sn1))[:-1])
    on2, ox2, sn2, sx2, dw = experts_on(x_far, (g_in[1], g_out[1]), dw)
    ds_far = answers(sn2, sx2)
    ds_near = answers(sn1, sx1)
    ds_far = [far(ds_far[k], k, shards_n, ctx_n) for k in range(shards_n)]
    ds_near = [ds_near[0]] + [flip(ds_near[k], "shard", k, shards_n) for k in range(1, shards_n)]

    rows_tn = (((0,), (0,)), ((), ()))
    d_routed, d_routed_other, d_pairs, d_pairs_other = gather(place, ds_near + ds_far, capacity)
    d_mixed, d_attn, d_o, d_logits, d_small = call(
        functools.partial(settle_back_kernel, experts + 1),
        "settle_back",
        [
            ((rows, width), full), ((rows, width), low), ((rows, width), low),
            ((rows, all_experts), full), ((all_experts + 4, width), full),
        ],
        (
            place3, d_routed, swap(d_routed_other), d_pairs, swap(d_pairs_other), g_own, mixed, second,
            probs, stat, ids, const_t, router_t, gain_f, plane, plane_other,
        ),
        [pltpu.VMEM((rows, width), low)],
        in_specs=[
            whole(rows, part), whole(rows, part), whole(rows, 2), whole(rows, 2), whole(rows, width),
            whole(rows, width), whole(rows, width), whole(rows, all_experts), whole(rows, 8),
            whole(rows, 2), whole(2, width), whole(all_experts, width), whole(1, width),
            chosen(3, width, part), chosen(3, width, part),
        ],
        prefetch=True,
    )

    ox1, ox2, held = lax.optimization_barrier((ox1, ox2, d_routed))
    out_near = plus(on1, swap(ox1)).reshape(shards_n, padded, part)
    out_far = plus(on2, swap(ox2)).reshape(shards_n, padded, part)

    got = flip(pin(dw[2:], d_routed), "ctx", 1, ctx_n)
    sent_rows = (dw[1].astype(full) + got[1].astype(full)).astype(low)
    came_rows = flip(sent_rows, "ctx", 2, ctx_n)

    third = width // 384
    back = attend_back(info, q, kv, o_low, d_o, lse, seg, 0, third)
    q_later = pin(q, out_far, out_near, back[0])
    back = attend_back(info, q_later, kv, o_low, d_o, lse, seg, third, third, back)
    out_near, out_far = lax.optimization_barrier((out_near, out_far, back[0]))[:2]
    out_cross = flip(out_far, "ctx", 2, ctx_n)
    q_later = pin(q, sent_rows, back[0])
    dq, dk, dv = attend_back(info, q_later, kv, o_low, d_o, lse, seg, 2 * third, third, back)
    out_pairs = jnp.stack([out_near, pin(out_cross, dq)], axis=1)
    out_got = [out_pairs[0]] + [flip(out_pairs[k], "shard", k, shards_n) for k in range(1, shards_n)]
    d_near, part0, part1, part2, d_gain_a = call(
        keys_back_kernel,
        "keys_back",
        [
            ((rows, width), full), ((rows, width), low), ((rows, width), low), ((edge, width), low),
            ((1, width), full),
        ],
        (place3, dq, dk, dv, x_all, plane, plane_other),
        in_specs=[
            whole(rows, width), whole(total, width), whole(total, width), whole(total, width),
            whole(4, width, part), whole(4, width, part),
        ],
        prefetch=True,
    )

    tiny = jnp.concatenate([d_small[:all_experts], d_gain_a, d_small[all_experts + 1 :]], axis=0)
    tiny = tiny.reshape(4, 2, 2, ctx_n, rows_d).transpose(0, 3, 1, 2, 4).reshape(4, ctx_n, 2, 2 * rows_d)
    tiny = jnp.where(tp == 0, tiny, tiny[:, :, ::-1]).reshape(4, ctx_n, 1, width).astype(low)
    tiny = jnp.pad(tiny, ((0, 0), (0, 0), (0, 15), (0, 0)))
    shared_mine, shared_other = weights_back(normed, dq, dk, dv, d_attn, o_low, tiny)

    def down(x, step):
        return lax.ppermute(x, "ctx", [(i, i - 1) for i in range(ctx_n - step, ctx_n)])

    came = down(part0, 1)
    shared_other = pin(shared_other, came, *out_got, came_rows)
    came = down(jnp.where(ctx == 3, part1, plus(part0, came)), 2)
    shared = plus(shared_mine, swap(shared_other))

    def numbered(k):
        return lax.dynamic_index_in_dim(shared, shard ^ k, 0, keepdims=False)

    plane_parts = [flip(numbered(k), "shard", k, shards_n) for k in range(1, shards_n)]
    plane_sum = numbered(0).astype(full)
    for got_part in plane_parts:
        plane_sum = plane_sum + got_part.astype(full)
    came = pin(came, plane_sum)
    part2 = jnp.pad(part2, ((0, rows - edge), (0, 0)))
    came = down(jnp.where(ctx == 3, part2, jnp.where(ctx == 2, plus(part1, came), plus(part0, came))), 3)
    base = jnp.where(ctx == 0, part0, jnp.where(ctx == 1, part1, part2)).astype(full)
    extra = jnp.where(ctx == 3, 0.0, base + came.astype(full))
    d_normed = d_near + extra
    unit_own, inv_own = unit_of(x_own)
    gain_a = gain_a[0]
    d_first = d_normed * gain_a
    d_tokens = d_mixed + inv_own * (
        d_first - unit_own * jnp.mean(d_first * unit_own, axis=-1, keepdims=True)
    )

    total = turn_sum(plane_sum.astype(low), ctx_n, ctx).astype(low)
    came_rows = pin(came_rows, total).astype(full)
    kept_rows = dw[0].astype(full) + got[0].astype(full)
    first = jnp.where(lower, kept_rows, came_rows)
    second_e = jnp.where(lower, came_rows, kept_rows)
    d_gate_up = jnp.stack(
        [jnp.stack([first[0], first[1]], axis=1), jnp.stack([second_e[0], second_e[1]], axis=1)], axis=1
    )
    d_down = jnp.stack([first[2], second_e[2]], axis=1)
    four = jnp.stack([total] + [flip(total, "shard", k, shards_n) for k in range(1, shards_n)])
    four = jnp.stack(
        [lax.dynamic_index_in_dim(four, m ^ shard, 0, keepdims=False) for m in range(4)]
    )
    d_q, d_k, d_v, d_w_out = [four[m, :rows_d].astype(full) for m in range(4)]
    d_w_qkv = jnp.stack([d_q, d_k, d_v], axis=1)
    tiny = four[:, rows_d]
    tiny = both_trees(tiny, swap(tiny)).transpose(1, 0, 2).reshape(16, rows_d).astype(full)

    out_got = [pin(o, plane_parts[0]) for o in out_got]
    pieces = [o[0] for o in out_got] + [o[1] for o in out_got]
    gate_columns = jnp.stack([gates_both[0], gates_both[1]], axis=1)
    combined, combined_other = gather(place, pieces, capacity, gate_columns)
    combined = in_order(combined, swap(combined_other), 1).astype(full)
    second_f = second.astype(full)

    def gate_of(number):
        return jnp.sum(jnp.where(ids == number, stat[:, :2], 0.0), axis=1, keepdims=True)

    copy_gate = gate_of(experts + 1)
    const_gate = jnp.concatenate([gate_of(experts + 2), gate_of(experts + 3)], axis=1)
    mixed_out = (
        mixed
        + combined
        + copy_gate * second_f
        + const_gate[:, :1] * const_t[0][None]
        + const_gate[:, 1:] * const_t[1][None]
    )
    return (
        both_trees(mixed_out, swap(mixed_out)),
        both_trees(d_tokens, swap(d_tokens)),
        both_trees(d_logits, swap(d_logits)),
        d_w_qkv,
        d_w_out,
        tiny[:all_experts].T,
        tiny[all_experts],
        tiny[all_experts + 1],
        tiny[all_experts + 2 :].T,
        d_gate_up,
        d_down,
    )


def program(tokens, gate_res, cotangent, parents, expert_ids, priority, w_qkv, *weights):
    trees, rows, width = tokens.shape
    ctx_n = lax.axis_size("ctx")
    seg = rows * ctx_n // parents.shape[1]
    fits = (
        ctx_n == 4
        and lax.axis_size("shard") == 4
        and lax.axis_size("tp") == 2
        and trees == 2
        and seg == 128
        and rows % seg == 0
        and 2 * rows < KEY_SEGS * seg <= 3 * rows
        and weights[-1].shape[1] == 2
    )
    chosen = by_core if fits else shards
    return chosen(tokens, gate_res, cotangent, parents, expert_ids, priority, w_qkv, *weights)


def solution(mesh):
    return jax.shard_map(
        program,
        mesh=mesh,
        in_specs=(
            P("shard", "ctx", None),
            P("shard", "ctx", None),
            P("shard", "ctx", None),
            P("shard", None),
            P("shard", "ctx", None),
            P("shard", "ctx", None),
            P("ctx", None, "tp"),
            P("ctx", "tp"),
            P("ctx", None),
            P("ctx"),
            P("ctx"),
            P("ctx", None),
            P("ctx", "shard", None, "tp"),
            P("ctx", "shard", "tp"),
        ),
        out_specs=(
            P("shard", "ctx", None),
            P("shard", "ctx", None),
            P("shard", "ctx", None),
            P("ctx", None, "tp"),
            P("ctx", "tp"),
            P("ctx", None),
            P("ctx"),
            P("ctx"),
            P("ctx", None),
            P("ctx", "shard", None, "tp"),
            P("ctx", "shard", "tp"),
        ),
        check_vma=False,
    )
```

```python
import functools
import math

import jax
import jax.numpy as jnp
from jax import lax
from jax.experimental import pallas as pl
from jax.experimental.pallas import tpu as pltpu
from jax.sharding import PartitionSpec as P

HEAD_DIM = 64


eps = 1e-06
score_scale = 0.125


def ancestry(parent_row):
    seg_count = parent_row.shape[0]
    position = jnp.arange(seg_count, dtype=jnp.int32)
    linked = (parent_row[:, None] == position[None, :]) | (position[:, None] == position[None, :])
    reach = linked.astype(jnp.float32)
    for repeat in range(seg_count.bit_length()):
        reach = jnp.minimum(jnp.dot(reach, reach, precision=lax.Precision.HIGHEST), 1.0)
    return reach


def path_rows(positions, seg_len, ancestors):
    onehot = (
        (positions // seg_len)[:, None] == jnp.arange(ancestors.shape[0], dtype=jnp.int32)[None, :]
    ).astype(jnp.float32)
    return jnp.dot(onehot, ancestors)


def allowed_block(query_rows, query_pos, key_start, key_count, seg_len):
    key_pos = key_start + jnp.arange(key_count, dtype=jnp.int32)
    key_onehot = (
        (key_pos // seg_len)[:, None] == jnp.arange(query_rows.shape[1], dtype=jnp.int32)[None, :]
    ).astype(jnp.float32)
    linked = jnp.dot(query_rows, key_onehot.T) > 0.5
    return (linked & (key_pos[None, :] <= query_pos[:, None]))[None]


def slot_table(picked_ids, ranking, experts, capacity):
    count_rows = picked_ids.shape[0]
    flat_ids = picked_ids.reshape(-1)
    rank_key = (2 * ranking[:, None] + jnp.arange(2, dtype=jnp.int32)[None, :]).reshape(-1)
    earlier = (flat_ids[:, None] == flat_ids[None, :]) & (rank_key[None, :] < rank_key[:, None])
    ranks = jnp.sum(earlier.astype(jnp.int32), axis=1)
    kept = (flat_ids < experts) & (ranks < capacity)
    target = jnp.where(kept, flat_ids * capacity + ranks, -1).reshape(count_rows, 2)
    slot_index = jnp.arange(experts * capacity, dtype=jnp.int32)
    return slot_index[None, :, None] == target.T[:, None, :]


def block_scores(queries, keys_blk):
    return (
        jnp.einsum("qhe,khe->hqk", queries, keys_blk, preferred_element_type=jnp.float32)
        * score_scale
    )


def softmax_grads(queries, grads_out, stat_lse, stat_delta, keys_blk, values_blk, mask):
    prob = jnp.where(mask, jnp.exp(block_scores(queries, keys_blk) - stat_lse[:, :, None]), 0.0)
    dprob = jnp.einsum("qhe,khe->hqk", grads_out, values_blk, preferred_element_type=jnp.float32)
    dscore = (prob * (dprob - stat_delta[:, :, None])).astype(jnp.bfloat16)
    return (prob.astype(jnp.bfloat16), dscore)


def shards(
    tokens,
    gate_res,
    cotangent,
    parents,
    expert_ids,
    priority,
    w_qkv,
    w_out,
    w_router,
    attn_gain,
    ffn_gain,
    const_vec,
    w_gate_up,
    w_down,
):
    full_qkv, full_out, full_router, full_again, full_fgain, full_const, full_gu, full_down = (
        lax.all_gather(w_qkv, "ctx", axis=0, tiled=True),
        lax.all_gather(w_out, "ctx", axis=0, tiled=True),
        lax.all_gather(w_router, "ctx", axis=0, tiled=True),
        lax.all_gather(attn_gain, "ctx", axis=0, tiled=True),
        lax.all_gather(ffn_gain, "ctx", axis=0, tiled=True),
        lax.all_gather(const_vec, "ctx", axis=0, tiled=True),
        lax.all_gather(w_gate_up, "ctx", axis=0, tiled=True),
        lax.all_gather(w_down, "ctx", axis=0, tiled=True),
    )
    tree_count, rows, model_width = tokens.shape
    tok_rows = tree_count * rows
    inputs = tokens.reshape(tok_rows, model_width).astype(jnp.float32)
    local_width = full_out.shape[1]
    local_heads = local_width // HEAD_DIM
    ctx_index = lax.axis_index("ctx")
    tree_len = rows * lax.axis_size("ctx")
    ancestors_all = jax.vmap(ancestry)(parents)
    seg_len = tree_len // parents.shape[1]
    key_block = math.gcd(tree_len, 512)
    starts = jnp.arange(tree_len // key_block, dtype=jnp.int32) * key_block
    key_start_own = ctx_index * rows
    query_pos = key_start_own + jnp.arange(rows, dtype=jnp.int32)
    query_rows_all = jax.vmap(lambda anc: path_rows(query_pos, seg_len, anc))(ancestors_all)
    inv_first = lax.rsqrt(jnp.mean(inputs * inputs, axis=-1, keepdims=True) + eps)
    first_unit = inputs * inv_first
    first_gain = full_again.astype(jnp.float32)
    normed = (first_unit * first_gain).astype(jnp.bfloat16)
    projected = jnp.einsum("nd,dke->nke", normed, full_qkv, preferred_element_type=jnp.float32)
    q_low = projected[:, 0].astype(jnp.bfloat16)
    k_low = projected[:, 1].astype(jnp.bfloat16)
    v_low = projected[:, 2].astype(jnp.bfloat16)
    keys_all, values_all = (
        lax.all_gather(k_low.reshape(tree_count, rows, local_width), "ctx", axis=1, tiled=True),
        lax.all_gather(v_low.reshape(tree_count, rows, local_width), "ctx", axis=1, tiled=True),
    )
    q_heads = q_low.reshape(tree_count, rows, local_heads, HEAD_DIM)
    k_heads = keys_all.reshape(tree_count, tree_len, local_heads, HEAD_DIM)
    v_heads = values_all.reshape(tree_count, tree_len, local_heads, HEAD_DIM)

    def tree_forward(q_one, k_one, v_one, rows_one):

        def stat_step(carry, start):
            running_top, running_sum = carry
            keys_blk = lax.dynamic_slice_in_dim(k_one, start, key_block, 0)
            mask = allowed_block(rows_one, query_pos, start, key_block, seg_len)
            masked = jnp.where(mask, block_scores(q_one, keys_blk), -1e30)
            new_top = jnp.maximum(running_top, jnp.max(masked, axis=2))
            expo = jnp.where(mask, jnp.exp(masked - new_top[:, :, None]), 0.0)
            running_sum = running_sum * jnp.exp(running_top - new_top) + jnp.sum(expo, axis=2)
            return ((new_top, running_sum), None)

        start_top = jnp.full((local_heads, rows), -1e30, jnp.float32)
        (final_top, final_sum), unused = lax.scan(
            stat_step, (start_top, jnp.zeros_like(start_top)), starts
        )
        lse_one = final_top + jnp.log(final_sum)

        def out_step(accum, start):
            keys_blk = lax.dynamic_slice_in_dim(k_one, start, key_block, 0)
            values_blk = lax.dynamic_slice_in_dim(v_one, start, key_block, 0)
            mask = allowed_block(rows_one, query_pos, start, key_block, seg_len)
            prob = jnp.where(
                mask, jnp.exp(block_scores(q_one, keys_blk) - lse_one[:, :, None]), 0.0
            ).astype(jnp.bfloat16)
            return (
                accum
                + jnp.einsum("hqk,khe->qhe", prob, values_blk, preferred_element_type=jnp.float32),
                None,
            )

        attended_one, unused = lax.scan(
            out_step, jnp.zeros((rows, local_heads, HEAD_DIM), jnp.float32), starts
        )
        return (attended_one, lse_one)

    attended, lse = jax.vmap(tree_forward)(q_heads, k_heads, v_heads, query_rows_all)
    attended_low = attended.reshape(tok_rows, local_width).astype(jnp.bfloat16)
    attn_part = jnp.einsum("nh,dh->nd", attended_low, full_out, preferred_element_type=jnp.float32)
    attn_sum = lax.psum(attn_part.astype(jnp.bfloat16), "tp").astype(jnp.float32)
    mixed = inputs + attn_sum
    inv_second = lax.rsqrt(jnp.mean(mixed * mixed, axis=-1, keepdims=True) + eps)
    second_unit = mixed * inv_second
    second_gain = full_fgain.astype(jnp.float32)
    second_low = (second_unit * second_gain).astype(jnp.bfloat16)
    second_float = second_low.astype(jnp.float32)
    logits = jnp.dot(
        second_low, full_router, preferred_element_type=jnp.float32
    ) + gate_res.reshape(tok_rows, -1)
    expo_logits = jnp.exp(logits - jnp.max(logits, axis=-1, keepdims=True))
    probs = expo_logits / jnp.sum(expo_logits, axis=-1, keepdims=True)
    experts = lax.axis_size("shard") * w_gate_up.shape[1]
    every_expert = experts + 4
    capacity = tok_rows * 2 // every_expert
    picked_ids = expert_ids.reshape(tok_rows, 2)
    selector = (picked_ids[:, :, None] == jnp.arange(every_expert, dtype=jnp.int32)).astype(
        jnp.float32
    )
    picked = jnp.sum(selector * probs[:, None, :], axis=-1)
    picked_total = jnp.sum(picked, axis=-1, keepdims=True)
    gates = picked / picked_total
    table = slot_table(picked_ids, priority[0, 0], experts, capacity).astype(jnp.bfloat16)
    routed = table[0] + table[1]
    send_slots = jnp.einsum(
        "et,td->ed", routed, second_low, preferred_element_type=jnp.float32
    ).astype(jnp.bfloat16)
    send_slots = send_slots.reshape(experts, 1, capacity, model_width)
    arrived = lax.all_to_all(send_slots, "shard", split_axis=0, concat_axis=1, tiled=True)
    gate_up = jnp.einsum("jsrd,djgf->jsrgf", arrived, full_gu, preferred_element_type=jnp.float32)
    hidden_low = (jax.nn.silu(gate_up[:, :, :, 0]) * gate_up[:, :, :, 1]).astype(jnp.bfloat16)
    partial_out = jnp.einsum(
        "jsrf,djf->jsrd", hidden_low, full_down, preferred_element_type=jnp.float32
    )
    summed = lax.psum(partial_out.astype(jnp.bfloat16), "tp")
    returned = lax.all_to_all(summed, "shard", split_axis=1, concat_axis=0, tiled=True)
    returned, kept_slots = (returned, arrived)
    out_slots = returned.reshape(experts * capacity, model_width)
    ffn_values = jnp.einsum("cet,ed->ctd", table, out_slots, preferred_element_type=jnp.float32)
    copy_flag = selector[:, :, experts + 1]
    const_flags = selector[:, :, experts + 2 :]
    const_float = full_const.astype(jnp.float32)
    fixed_terms = jnp.einsum(
        "nck,dk->cnd", const_flags, const_float, precision=lax.Precision.HIGHEST
    )
    values_pair = ffn_values + copy_flag.T[:, :, None] * second_float[None] + fixed_terms
    mixed_out = mixed + jnp.sum(gates.T[:, :, None] * values_pair, axis=0)
    grad_out = cotangent.reshape(tok_rows, model_width).astype(jnp.float32)
    weighted = gates.T[:, :, None] * grad_out[None]
    d_gates = jnp.einsum("cnd,nd->nc", values_pair, grad_out)
    d_const = jnp.einsum("nck,cnd->dk", const_flags, weighted, precision=lax.Precision.HIGHEST)
    d_out_slots = jnp.einsum(
        "cet,ctd->ed", table.astype(jnp.float32), weighted, precision=lax.Precision.HIGHEST
    )
    d_out_low = d_out_slots.astype(jnp.bfloat16).reshape(experts, 1, capacity, model_width)
    d_picked = (d_gates - jnp.sum(d_gates * gates, axis=-1, keepdims=True)) / picked_total
    d_probs = jnp.einsum("nc,nck->nk", d_picked, selector)
    d_logits = probs * (d_probs - jnp.sum(probs * d_probs, axis=-1, keepdims=True))
    d_router_w = jnp.dot(second_float.T, d_logits, precision=lax.Precision.HIGHEST)
    d_second = jnp.sum(copy_flag.T[:, :, None] * weighted, axis=0)
    d_second = d_second + jnp.dot(
        d_logits, full_router.astype(jnp.float32).T, precision=lax.Precision.HIGHEST
    )
    arrived_grad = lax.all_to_all(d_out_low, "shard", split_axis=0, concat_axis=1, tiled=True)
    gate_up = jnp.einsum(
        "jsrd,djgf->jsrgf", kept_slots, full_gu, preferred_element_type=jnp.float32
    )
    gate_part = gate_up[:, :, :, 0]
    up_part = gate_up[:, :, :, 1]
    sigma = jax.nn.sigmoid(gate_part)
    silu_part = gate_part * sigma
    hidden_low = (silu_part * up_part).astype(jnp.bfloat16)
    d_hidden = jnp.einsum(
        "jsrd,djf->jsrf", arrived_grad, full_down, preferred_element_type=jnp.float32
    )
    d_gate_part = d_hidden * up_part * sigma * (1.0 + gate_part * (1.0 - sigma))
    d_up_part = d_hidden * silu_part
    d_gate_up_low = jnp.stack([d_gate_part, d_up_part], axis=3).astype(jnp.bfloat16)
    d_slot_part = jnp.einsum(
        "jsrgf,djgf->jsrd", d_gate_up_low, full_gu, preferred_element_type=jnp.float32
    )
    d_slot_sum = lax.psum(d_slot_part.astype(jnp.bfloat16), "tp")
    d_slot_back = lax.all_to_all(d_slot_sum, "shard", split_axis=1, concat_axis=0, tiled=True)
    d_gate_up_w = jnp.einsum(
        "jsrd,jsrgf->djgf", kept_slots, d_gate_up_low, preferred_element_type=jnp.float32
    )
    d_down_w = jnp.einsum(
        "jsrd,jsrf->djf", arrived_grad, hidden_low, preferred_element_type=jnp.float32
    )
    d_second = d_second + jnp.einsum(
        "et,ed->td",
        routed,
        d_slot_back.reshape(experts * capacity, model_width),
        preferred_element_type=jnp.float32,
    )
    d_second_gain = jnp.sum(d_second * second_unit, axis=0)
    d_second_unit = d_second * second_gain
    d_mixed = grad_out + inv_second * (
        d_second_unit - second_unit * jnp.mean(d_second_unit * second_unit, axis=-1, keepdims=True)
    )
    d_attn_low = d_mixed.astype(jnp.bfloat16)
    d_out_w = jnp.einsum("nd,nh->dh", d_attn_low, attended_low, preferred_element_type=jnp.float32)
    d_attended = jnp.einsum("nd,dh->nh", d_attn_low, full_out, preferred_element_type=jnp.float32)
    do_low = d_attended.astype(jnp.bfloat16)
    do_heads = do_low.reshape(tree_count, rows, local_heads, HEAD_DIM)
    delta = jnp.einsum("tqhe,tqhe->thq", do_heads.astype(jnp.float32), attended)

    def tree_both(q_one, k_one, v_one, do_one, lse_one, delta_one, rows_one):

        def both_step(dq_accum, start):
            keys_blk = lax.dynamic_slice_in_dim(k_one, start, key_block, 0)
            values_blk = lax.dynamic_slice_in_dim(v_one, start, key_block, 0)
            mask = allowed_block(rows_one, query_pos, start, key_block, seg_len)
            prob_low, dscore = softmax_grads(
                q_one, do_one, lse_one, delta_one, keys_blk, values_blk, mask
            )
            dq_accum = dq_accum + jnp.einsum(
                "hqk,khe->qhe", dscore, keys_blk, preferred_element_type=jnp.float32
            )
            dkey = (
                jnp.einsum("hqk,qhe->khe", dscore, q_one, preferred_element_type=jnp.float32)
                * score_scale
            )
            dval = jnp.einsum("hqk,qhe->khe", prob_low, do_one, preferred_element_type=jnp.float32)
            return (
                dq_accum,
                jnp.stack(
                    [dkey.reshape(key_block, local_width), dval.reshape(key_block, local_width)],
                    axis=1,
                ),
            )

        dq_one, terms_one = lax.scan(
            both_step, jnp.zeros((rows, local_heads, HEAD_DIM), jnp.float32), starts
        )
        return (dq_one, terms_one.reshape(tree_len, 2, local_width))

    dq_total, key_terms = jax.vmap(tree_both)(
        q_heads, k_heads, v_heads, do_heads, lse, delta, query_rows_all
    )
    key_sums = lax.psum_scatter(
        key_terms.astype(jnp.bfloat16), "ctx", scatter_dimension=1, tiled=True
    ).astype(jnp.float32)
    key_grad = key_sums[:, :, 0].reshape(tok_rows, local_width)
    value_grad = key_sums[:, :, 1].reshape(tok_rows, local_width)
    query_grad = (dq_total * score_scale).reshape(tok_rows, local_width)
    d_qkv_low = jnp.stack([query_grad, key_grad, value_grad], axis=1).astype(jnp.bfloat16)
    d_qkv_w = jnp.einsum("nd,nke->dke", normed, d_qkv_low, preferred_element_type=jnp.float32)
    d_normed_part = jnp.einsum(
        "nke,dke->nd", d_qkv_low, full_qkv, preferred_element_type=jnp.float32
    )
    d_normed = lax.psum(d_normed_part.astype(jnp.bfloat16), "tp").astype(jnp.float32)
    d_first_gain = jnp.sum(d_normed * first_unit, axis=0)
    d_first_unit = d_normed * first_gain
    d_inputs = d_mixed + inv_first * (
        d_first_unit - first_unit * jnp.mean(d_first_unit * first_unit, axis=-1, keepdims=True)
    )
    summed_grads = (
        lax.psum_scatter(
            d_qkv_w.astype(jnp.bfloat16), "ctx", scatter_dimension=0, tiled=True
        ).astype(jnp.float32),
        lax.psum_scatter(
            d_out_w.astype(jnp.bfloat16), "ctx", scatter_dimension=0, tiled=True
        ).astype(jnp.float32),
        lax.psum_scatter(
            d_router_w.astype(jnp.bfloat16), "ctx", scatter_dimension=0, tiled=True
        ).astype(jnp.float32),
        lax.psum_scatter(
            d_first_gain.astype(jnp.bfloat16), "ctx", scatter_dimension=0, tiled=True
        ).astype(jnp.float32),
        lax.psum_scatter(
            d_second_gain.astype(jnp.bfloat16), "ctx", scatter_dimension=0, tiled=True
        ).astype(jnp.float32),
        lax.psum_scatter(
            d_const.astype(jnp.bfloat16), "ctx", scatter_dimension=0, tiled=True
        ).astype(jnp.float32),
        lax.psum_scatter(
            d_gate_up_w.astype(jnp.bfloat16), "ctx", scatter_dimension=0, tiled=True
        ).astype(jnp.float32),
        lax.psum_scatter(
            d_down_w.astype(jnp.bfloat16), "ctx", scatter_dimension=0, tiled=True
        ).astype(jnp.float32),
    )
    shared = (
        lax.psum(summed_grads[0].astype(jnp.bfloat16), "shard").astype(jnp.float32),
        lax.psum(summed_grads[1].astype(jnp.bfloat16), "shard").astype(jnp.float32),
        lax.psum(summed_grads[2].astype(jnp.bfloat16), "shard").astype(jnp.float32),
        lax.psum(summed_grads[3].astype(jnp.bfloat16), "shard").astype(jnp.float32),
        lax.psum(summed_grads[4].astype(jnp.bfloat16), "shard").astype(jnp.float32),
        lax.psum(summed_grads[5].astype(jnp.bfloat16), "shard").astype(jnp.float32),
    )
    out_rows = mixed_out.reshape(tree_count, rows, model_width)
    grad_rows = d_inputs.reshape(tree_count, rows, model_width)
    logit_rows = d_logits.reshape(tree_count, rows, every_expert)
    return (
        out_rows,
        grad_rows,
        logit_rows,
        shared[0],
        shared[1],
        shared[2],
        shared[3],
        shared[4],
        shared[5],
        summed_grads[6],
        summed_grads[7],
    )


NT = (((1,), (1,)), ((), ()))
NN = (((1,), (0,)), ((), ()))
TRUNK = 8
KEY_SEGS = 12
PIECE = 256
SENT = (0, 2, 1, 3)


def mm(a, b, dims=NN):
    return lax.dot_general(a, b, dims, preferred_element_type=jnp.float32)


def stacked(rows, half):
    first = lax.broadcasted_iota(jnp.int32, rows.shape, 1) < half
    blank = jnp.zeros_like(rows)
    return jnp.concatenate([jnp.where(first, rows, blank), jnp.where(first, blank, rows)], axis=0)


def unstack(wide, half, seg):
    return jnp.concatenate([wide[:half, :seg], wide[half:, seg:]], axis=0)


def causal(seg):
    row = lax.broadcasted_iota(jnp.int32, (seg, 2 * seg), 0)
    col = lax.broadcasted_iota(jnp.int32, (seg, 2 * seg), 1)
    return row <= jnp.where(col >= seg, col - seg, col)


def attend_kernel(own, seg, half, more, info, q_ref, k_ref, v_ref, *rest):
    o_ref, lse_ref, s_ref, p_ref = rest[2 * more :]
    trunk = TRUNK * seg
    allowed = causal(seg)
    v_trunk = v_ref[own : own + trunk, :].T

    def one(i, unused):
        count, branch, leaf = info[i, 0], info[i, 1], info[i, 2]
        here = pl.ds(pl.multiple_of(i * seg, seg), seg)
        there = pl.ds(pl.multiple_of(own + branch * seg, seg), seg)
        qs = stacked(q_ref[here, :] * 0.125, half)
        s_ref[:trunk, :] = mm(k_ref[own : own + trunk, :], qs, NT)
        s_branch = mm(k_ref[there, :], qs, NT)
        s_own = jnp.where(allowed, mm(k_ref[here, :], qs, NT), -1e30)
        biases = [jnp.where(kb < count, 0.0, -1e30) for kb in range(TRUNK)]
        leaf_bias = jnp.where(leaf > 0, 0.0, -1e30)
        top = jnp.max(s_own, axis=0, keepdims=True)
        top = jnp.maximum(top, jnp.max(s_branch, axis=0, keepdims=True) + leaf_bias)
        for kb in range(TRUNK):
            part = jnp.max(s_ref[kb * seg : (kb + 1) * seg, :], axis=0, keepdims=True)
            top = jnp.maximum(top, part + biases[kb])
        e_own = jnp.exp(s_own - top)
        e_branch = jnp.exp(s_branch - (top - leaf_bias))
        total = jnp.sum(e_own + e_branch, axis=0, keepdims=True)
        for kb in range(TRUNK):
            e = jnp.exp(s_ref[kb * seg : (kb + 1) * seg, :] - (top - biases[kb]))
            total = total + jnp.sum(e, axis=0, keepdims=True)
            p_ref[kb * seg : (kb + 1) * seg, :] = e.astype(jnp.bfloat16)
        out = mm(v_trunk, p_ref[...])
        out = out + mm(v_ref[there, :].T, e_branch.astype(jnp.bfloat16))
        out = out + mm(v_ref[here, :].T, e_own.astype(jnp.bfloat16))
        out = unstack(out * (1.0 / total), half, seg)
        o_ref[here, :] = out.T.astype(jnp.bfloat16)
        lse_ref[pl.ds(i, 1), :] = top + jnp.log(total)
        return 0

    lax.fori_loop(0, own // seg, one, 0, unroll=True)


def attend_back_kernel(
    own, seg, half, more, info, q_ref, k_ref, v_ref, o_ref, do_ref, lse_ref, *rest
):
    dq_ref, dk_ref, dv_ref, ak, av = rest[3 * more :]
    trunk = TRUNK * seg
    allowed = causal(seg)
    low = jnp.bfloat16
    tk = slice(own, own + trunk)
    k_trunk = k_ref[tk, :].T
    ak[...] = jnp.zeros_like(ak)
    av[...] = jnp.zeros_like(av)

    def one(i, unused):
        count, branch, leaf = info[i, 0], info[i, 1], info[i, 2]
        here = pl.ds(pl.multiple_of(i * seg, seg), seg)
        there = pl.ds(pl.multiple_of(own + branch * seg, seg), seg)
        qs = stacked(q_ref[here, :] * 0.125, half)
        do = do_ref[here, :]
        dos = stacked(do, half)
        prod = (do.astype(jnp.float32) * o_ref[here, :].astype(jnp.float32)).T
        delta = jnp.concatenate(
            [jnp.sum(prod[:half], axis=0, keepdims=True), jnp.sum(prod[half:], axis=0, keepdims=True)],
            axis=1,
        )
        lse = lse_ref[pl.ds(i, 1), :]
        leaf_bias = jnp.where(leaf > 0, 0.0, -1e30)

        def piece(keys, values, shift, mask):
            s = mm(keys, qs, NT)
            if mask:
                s = jnp.where(allowed, s, -1e30)
            if isinstance(shift, list):
                p = jnp.concatenate(
                    [jnp.exp(s[kb * seg : (kb + 1) * seg] - shift[kb]) for kb in range(TRUNK)], axis=0
                )
            else:
                p = jnp.exp(s - shift)
            ds = (p * (mm(values, dos, NT) - delta)).astype(low)
            p = p.astype(low)
            return (mm(p, dos), mm(ds, qs), ds)

        shifts = [lse - jnp.where(kb < count, 0.0, -1e30) for kb in range(TRUNK)]
        dv, dk, ds = piece(k_ref[tk, :], v_ref[tk, :], shifts, False)
        av[tk, :] += dv
        ak[tk, :] += dk
        dq = mm(k_trunk, ds)
        keys = k_ref[there, :]
        dv, dk, ds = piece(keys, v_ref[there, :], lse - leaf_bias, False)
        av[there, :] += dv
        ak[there, :] += dk
        dq = dq + mm(keys.T, ds)
        keys = k_ref[here, :]
        dv, dk, ds = piece(keys, v_ref[here, :], lse, True)
        av[here, :] += dv
        ak[here, :] += dk
        dq = dq + mm(keys.T, ds)
        dq_ref[here, :] = (unstack(dq, half, seg) * 0.125).T.astype(low)
        return 0

    lax.fori_loop(0, own // seg, one, 0, unroll=True)
    dk_ref[...] = ak[...].astype(low)
    dv_ref[...] = av[...].astype(low)


def attend(info, q, kv, seg, begin, count, prev=()):
    own, width = q.shape
    total = kv.shape[0]
    pairs = width // 128
    lane = pl.BlockSpec((own, 128), lambda h: (0, begin + h))
    return pl.pallas_call(
        functools.partial(attend_kernel, own, seg, HEAD_DIM, len(prev) > 0),
        grid=(count,),
        in_specs=[
            pl.BlockSpec(memory_space=pltpu.SMEM),
            lane,
            pl.BlockSpec((total, 128), lambda h: (0, begin + h)),
            pl.BlockSpec((total, 128), lambda h: (0, pairs + begin + h)),
        ]
        + [pl.BlockSpec(memory_space=pl.ANY)] * len(prev),
        out_specs=[lane, pl.BlockSpec((None, 8, 2 * seg), lambda h: (begin + h, 0, 0))],
        out_shape=[
            jax.ShapeDtypeStruct((own, width), jnp.bfloat16),
            jax.ShapeDtypeStruct((pairs, 8, 2 * seg), jnp.float32),
        ],
        input_output_aliases={4 + i: i for i in range(len(prev))},
        scratch_shapes=[
            pltpu.VMEM((TRUNK * seg, 2 * seg), jnp.float32),
            pltpu.VMEM((TRUNK * seg, 2 * seg), jnp.bfloat16),
        ],
        compiler_params=pltpu.CompilerParams(vmem_limit_bytes=60 << 20),
        cost_estimate=pl.CostEstimate(
            flops=1000, bytes_accessed= 1000, transcendentals=0
        ),
        name="attend",
    )(info, q, kv, kv, *prev)


def attend_back(info, q, kv, o, do, lse, seg, begin, count, prev=()):
    own, width = q.shape
    total = kv.shape[0]
    pairs = width // 128
    lane = pl.BlockSpec((own, 128), lambda h: (0, begin + h))
    keys = pl.BlockSpec((total, 128), lambda h: (0, begin + h))
    return pl.pallas_call(
        functools.partial(attend_back_kernel, own, seg, HEAD_DIM, len(prev) > 0),
        grid=(count,),
        in_specs=[
            pl.BlockSpec(memory_space=pltpu.SMEM),
            lane,
            keys,
            pl.BlockSpec((total, 128), lambda h: (0, pairs + begin + h)),
            lane,
            lane,
            pl.BlockSpec((None, 8, 2 * seg), lambda h: (begin + h, 0, 0)),
        ]
        + [pl.BlockSpec(memory_space=pl.ANY)] * len(prev),
        out_specs=[lane, keys, keys],
        out_shape=[
            jax.ShapeDtypeStruct((own, width), jnp.bfloat16),
            jax.ShapeDtypeStruct((total, width), jnp.bfloat16),
            jax.ShapeDtypeStruct((total, width), jnp.bfloat16),
        ],
        input_output_aliases={7 + i: i for i in range(len(prev))},
        scratch_shapes=[
            pltpu.VMEM((total, 128), jnp.float32),
            pltpu.VMEM((total, 128), jnp.float32),
        ],
        compiler_params=pltpu.CompilerParams(vmem_limit_bytes=40 << 20),
        cost_estimate=pl.CostEstimate(
            flops=1000, bytes_accessed= 1000, transcendentals=0
        ),
        name="attend_back",
    )(info, q, kv, kv, o, do, lse, *prev)


def pin(x, *after):
    return lax.optimization_barrier((x,) + after)[0]


def expert_kernel(
    more, capacity, pieces, place, xm_ref, xo_ref, gm_ref, go_ref, w0, w1, w2, w3, *rest
):
    low, full = jnp.bfloat16, jnp.float32
    o_ref, o2_ref, s_ref, s2_ref, dw_ref, x_ref, g_ref, xt, dt, d_ref, oa, sa, wb, gb = rest[more:]
    part = w0.shape[1]
    rows, wide = xm_ref.shape
    padded = rows // pieces
    tail = padded - 16
    here = pl.ds(pl.multiple_of(place[1] * wide, 128), wide)
    there = pl.ds(pl.multiple_of((1 - place[1]) * wide, 128), wide)

    @pl.when(pl.program_id(0) == 0)
    def start():
        x_ref[:, here] = xm_ref[...]
        x_ref[:, there] = xo_ref[...]
        g_ref[:, here] = gm_ref[...]
        g_ref[:, there] = go_ref[...]
        for p in range(pieces):
            mine = slice(p * padded, (p + 1) * padded)
            last = xm_ref[p * padded + tail : (p + 1) * padded, :256].astype(full)
            row = lax.broadcasted_iota(jnp.int32, last.shape, 0) + tail
            inside = (row >= capacity) & (row < capacity + 3)
            gate = jnp.sum(jnp.where(inside, last, 0.0), axis=0, keepdims=True)
            gate = jnp.broadcast_to(gate, (8, 256)).T[:padded, 0:1]
            d_ref[mine, :] = (g_ref[mine, :].astype(full) * gate).astype(low)
        xt[...] = x_ref[...].T
        dt[...] = d_ref[...].T
        oa[...] = jnp.zeros_like(oa)
        sa[...] = jnp.zeros_like(sa)

    def rows_of(r):
        return pl.ds(pl.multiple_of((place[0] ^ r) * part, 64), part)

    for r, w in enumerate((w0, w1, w2, w3)):
        wb[:, rows_of(r), :] = w[...]
    u = mm(x_ref[...], wb[0])
    up = mm(x_ref[...], wb[1])
    sigma = 1.0 / (1.0 + jnp.exp(-u))
    silu = u * sigma
    hidden = (silu * up).astype(low)
    oa[...] += mm(hidden, wb[2], NT)
    dh = mm(d_ref[...], wb[2])
    du = (dh * up * sigma * (1.0 + u * (1.0 - sigma))).astype(low)
    dup = (dh * silu).astype(low)
    sa[...] += mm(du, wb[0], NT) + mm(dup, wb[1], NT)
    gb[0] = mm(xt[...], du).astype(low)
    gb[1] = mm(xt[...], dup).astype(low)
    gb[2] = mm(dt[...], hidden).astype(low)
    for at, r in enumerate(SENT):
        got = gb[:, rows_of(r), :]
        if more:
            got = (got.astype(full) + rest[0][at].astype(full)).astype(low)
        dw_ref[at] = got

    @pl.when(pl.program_id(0) == pl.num_programs(0) - 1)
    def finish():
        o_ref[...] = oa[:, here].astype(low)
        o2_ref[...] = oa[:, there].astype(low)
        s_ref[...] = sa[:, here].astype(low)
        s2_ref[...] = sa[:, there].astype(low)
        for p in range(pieces):
            mine = slice(p * padded, (p + 1) * padded)
            dot = jnp.sum(g_ref[mine, :].astype(full) * oa[mine, :], axis=1, keepdims=True)
            dot = jnp.broadcast_to(dot, (padded, 128)).T[:16, :]
            dot = jnp.concatenate([dot, jnp.zeros((16, wide - padded), full)], axis=1)
            row = lax.broadcasted_iota(jnp.int32, dot.shape, 0) + tail
            kept = jnp.zeros_like(dot)
            for i in range(3):
                piece = dot.astype(low).astype(full)
                kept = jnp.where(row == capacity + i, piece, kept)
                dot = dot - piece
            last = slice(p * padded + tail, (p + 1) * padded)
            row_low = s_ref[last, :].astype(full)
            s_ref[last, :] = jnp.where(row >= capacity, kept, row_low).astype(low)


def expert_pass(place, capacity, pieces, xs, gs, weights, prev):
    rows, half_width = xs[0].shape
    width = 2 * half_width
    three, part, units = weights[0].shape
    low = jnp.bfloat16
    strip = pl.BlockSpec((three, part, PIECE), lambda j, *at: (0, 0, j))
    strips = pl.BlockSpec((4, three, part, PIECE), lambda j, *at: (0, 0, 0, j))
    half = whole(rows, half_width)
    more = prev is not None
    return call(
        functools.partial(expert_kernel, int(more), capacity, pieces),
        "expert_pass",
        [((rows, half_width), low)] * 4 + [((4, three, part, units), low)],
        (place, *xs, *gs, *weights, *([prev] if more else [])),
        [
            pltpu.VMEM((rows, width), low),
            pltpu.VMEM((rows, width), low),
            pltpu.VMEM((width, rows), low),
            pltpu.VMEM((width, rows), low),
            pltpu.VMEM((rows, width), low),
            pltpu.VMEM((rows, width), jnp.float32),
            pltpu.VMEM((rows, width), jnp.float32),
            pltpu.VMEM((three, width, PIECE), low),
            pltpu.VMEM((three, width, PIECE), low),
        ],
        grid=(units // PIECE,),
        in_specs=[half] * 4 + [strip] * 4 + [strips] * more,
        out_specs=[half] * 4 + [strips],
        prefetch=True,
        mib=48,
    )


def spread_kernel(pieces, padded, capacity, gated, place_ref, rows_ref, *rest):
    low = jnp.bfloat16
    outs = rest[1:] if gated else rest
    tokens = rows_ref.shape[0]
    for p in range(pieces):
        slot = lax.broadcasted_iota(jnp.int32, (padded, tokens), 0) + p * padded
        hits = [slot == place_ref[c : c + 1, :] for c in range(2)]
        out = mm(jnp.where(hits[0] | hits[1], 1.0, 0.0).astype(low), rows_ref[...]).astype(low)
        if gated:
            parts = 0.0
            for c in range(2):
                value = rest[0][c : c + 1, :]
                rows3 = []
                for i in range(3):
                    rows3.append(value.astype(low).astype(jnp.float32))
                    value = value - rows3[-1]
                rows3.append(jnp.zeros((13, tokens), jnp.float32))
                three = jnp.concatenate(rows3, axis=0).astype(low)
                parts = parts + mm(three, jnp.where(hits[c], 1.0, 0.0).astype(low), NT)
            parts = parts.astype(low)
            blank = jnp.zeros((parts.shape[0], out.shape[1] - padded), low)
            parts = jnp.concatenate([parts, blank], axis=1)
            row = lax.broadcasted_iota(jnp.int32, out.shape, 0)
            for i in range(3):
                out = jnp.where(row == capacity + i, parts[i : i + 1, :], out)
        outs[p][...] = out


def spread(place, rows, pieces, padded, capacity, parts=None):
    shape = jax.ShapeDtypeStruct((padded, rows.shape[1]), jnp.bfloat16)
    gated = parts is not None
    return pl.pallas_call(
        functools.partial(spread_kernel, pieces, padded, capacity, gated),
        in_specs=[pl.BlockSpec(memory_space=pltpu.VMEM)] * (2 + gated),
        out_specs=[pl.BlockSpec(memory_space=pltpu.VMEM)] * pieces,
        out_shape=[shape] * pieces,
        compiler_params=pltpu.CompilerParams(vmem_limit_bytes=60 << 20),
        cost_estimate=pl.CostEstimate(flops=1000, bytes_accessed= 1000, transcendentals=0),
        name="spread",
    )(place, rows, *([parts] if gated else []))


def gather_kernel(pieces, padded, capacity, dots, place_ref, *rest):
    low = jnp.bfloat16
    if dots:
        ins, (out_ref, out2_ref, dot_ref, dot2_ref) = rest[:pieces], rest[pieces:]
    else:
        gate_ref, ins, (out_ref, out2_ref) = rest[0], rest[1 : 1 + pieces // 2], rest[1 + pieces // 2 :]
    tokens = place_ref.shape[0]
    total = None
    sums = [0.0, 0.0]
    for p in range(pieces):
        slot = lax.broadcasted_iota(jnp.int32, (tokens, padded), 1) + p * padded
        hits = [slot == place_ref[:, c : c + 1] for c in range(2)]
        if dots:
            picks = [jnp.where(h, 1.0, 0.0).astype(low) for h in hits]
            values = ins[p][capacity : capacity + 3, :padded]
            values = jnp.concatenate([values, jnp.zeros((13, padded), low)], axis=0)
            for c in range(2):
                sums[c] = sums[c] + mm(picks[c], values, NT)
            pick = picks[0] + picks[1]
        else:
            pick = jnp.where(hits[0], gate_ref[:, 0:1], jnp.where(hits[1], gate_ref[:, 1:2], 0.0))
            pick = pick.astype(low)
        part = mm(pick, ins[p][...] if dots else ins[p % 4][p // 4])
        total = part if total is None else total + part
    rows = tokens // 2
    out_ref[...] = total[:rows].astype(low)
    out2_ref[...] = total[rows:].astype(low)
    if dots:
        for c in range(2):
            dot_ref[:, c : c + 1] = jnp.sum(sums[c][:rows], axis=1, keepdims=True)
            dot2_ref[:, c : c + 1] = jnp.sum(sums[c][rows:], axis=1, keepdims=True)


def gather(place, pieces, capacity, gate=None):
    padded, width = pieces[0].shape[-2:]
    number = sum(p.size // (padded * width) for p in pieces)
    tokens = place.shape[0]
    dots = gate is None
    shapes = [jax.ShapeDtypeStruct((tokens // 2, width), jnp.bfloat16)] * 2
    if dots:
        shapes = shapes + [jax.ShapeDtypeStruct((tokens // 2, 2), jnp.float32)] * 2
    return pl.pallas_call(
        functools.partial(gather_kernel, number, padded, capacity, dots),
        in_specs=[pl.BlockSpec(memory_space=pltpu.VMEM)] * (len(pieces) + (1 if dots else 2)),
        out_specs=[pl.BlockSpec(memory_space=pltpu.VMEM)] * len(shapes),
        out_shape=shapes,
        compiler_params=pltpu.CompilerParams(vmem_limit_bytes=60 << 20),
        cost_estimate=pl.CostEstimate(flops=1000, bytes_accessed= 1000, transcendentals=0),
        name="gather",
    )(place, *([] if dots else [gate]), *pieces)


def whole(*shape):
    return pl.BlockSpec(shape, lambda *at: (0,) * len(shape))


def by_rows(*shape):
    return pl.BlockSpec(shape, lambda j, *at: (j, 0))


def chosen(number, *shape):
    return pl.BlockSpec((None,) + shape, lambda j, place: (number ^ place[0], 0, 0))


def call(kernel, name, outs, args, scratch=(), grid=(1,), in_specs=None, out_specs=None, prefetch=False, mib=40):
    if out_specs is None:
        out_specs = [whole(*o[0]) for o in outs]
    spec = pltpu.PrefetchScalarGridSpec(
        num_scalar_prefetch=int(prefetch),
        grid=grid,
        in_specs=in_specs,
        out_specs=out_specs,
        scratch_shapes=list(scratch),
    )
    return pl.pallas_call(
        kernel,
        grid_spec=spec,
        out_shape=[jax.ShapeDtypeStruct(*o) for o in outs],
        compiler_params=pltpu.CompilerParams(vmem_limit_bytes=mib << 20),
        cost_estimate=pl.CostEstimate(flops=1000, bytes_accessed=1000, transcendentals=0),
        name=name,
    )(*args)


def unit_rows(x):
    x = x.astype(jnp.float32)
    return x * lax.rsqrt(jnp.mean(x * x, axis=-1, keepdims=True) + eps)


def project_kernel(place, x0, near, mid, farther, gain, wm, wo, q_ref, kv_ref, n_ref, x_ref):
    low = jnp.bfloat16
    shard, ctx = place[0], place[1]
    rows, width = x0.shape
    half = wm.shape[2]

    def project(lo, x):
        here = slice(lo, lo + x.shape[0])
        normed = (unit_rows(x) * gain[...]).astype(low)
        x_ref[here, :] = x
        n_ref[here, :] = normed
        for m in (1, 2):
            for h, w in enumerate((wm, wo)):
                at = (m - 1) * width + h * half
                kv_ref[here, at : at + half] = mm(normed, w[m ^ shard]).astype(low)
        if lo == 0:
            for h, w in enumerate((wm, wo)):
                q_ref[:, h * half : (h + 1) * half] = mm(normed, w[shard]).astype(low)

    edge = x_ref.shape[0] - 3 * rows
    project(0, x0[...])
    later = jnp.where(ctx == 2, mid[...], farther[...])
    project(rows, jnp.where(ctx == 0, x0[...], jnp.where(ctx == 1, near[...], later)))
    later = jnp.where(ctx == 2, near[...], mid[...])
    project(2 * rows, jnp.where(ctx == 1, x0[...], later))
    project(3 * rows, jnp.where(ctx == 2, x0[:edge, :], near[:edge, :]))


def settle_kernel(
    place, o, x, wm, wo, gain, router, res, ids,
    mixed_ref, second_ref, mine_ref, other_ref, probs_ref, stat_ref, gates_ref,
):
    tp = place[2]
    half = wm.shape[1]
    attn = mm(o[:, :half], wm[...], NT) + mm(o[:, half:], wo[...], NT)
    mixed = x[...].astype(jnp.float32) + attn
    mixed_ref[...] = mixed
    inverse = lax.rsqrt(jnp.mean(mixed * mixed, axis=-1, keepdims=True) + eps)
    second = (mixed * inverse * gain[...]).astype(jnp.bfloat16)
    second_ref[...] = second
    mine_ref[...] = second_ref[:, pl.ds(pl.multiple_of(tp * half, 128), half)]
    other_ref[...] = second_ref[:, pl.ds(pl.multiple_of((1 - tp) * half, 128), half)]
    logits = mm(second, router[...], NT) + res[...]
    expo = jnp.exp(logits - jnp.max(logits, axis=-1, keepdims=True))
    probs = expo / jnp.sum(expo, axis=-1, keepdims=True)
    probs_ref[...] = probs
    lane = lax.broadcasted_iota(jnp.int32, probs.shape, 1)
    picked = [
        jnp.sum(jnp.where(lane == ids[:, c : c + 1], probs, 0.0), axis=-1, keepdims=True)
        for c in range(2)
    ]
    total = picked[0] + picked[1]
    wide = lax.broadcasted_iota(jnp.int32, (probs.shape[0], 128), 1)
    stat = jnp.where(wide == 0, picked[0] / total, jnp.where(wide == 1, picked[1] / total, 0.0))
    stat = jnp.where(wide == 2, total, jnp.where(wide == 3, inverse, stat))
    stat_ref[...] = stat[:, :8]
    gates_ref[...] = stat.T[:8, :]


def settle_back_kernel(
    copy_id, place, dr_mine, dr_came, dg_mine, dg_came, g_ref, mixed, second, probs_ref, stat, ids,
    const, router, gain, wm, wo, dmix_ref, dattn_ref, do_ref, dlog_ref, small_ref, full_ref,
):
    low, full = jnp.bfloat16, jnp.float32
    tp = place[2]
    half = wm.shape[1]
    full_ref[:, pl.ds(pl.multiple_of(tp * half, 128), half)] = dr_mine[...]
    full_ref[:, pl.ds(pl.multiple_of((1 - tp) * half, 128), half)] = dr_came[...]
    g = g_ref[...].astype(full)
    probs = probs_ref[...]
    gates = [stat[:, 0:1], stat[:, 1:2]]
    total, inverse = stat[:, 2:3], stat[:, 3:4]
    ids_c = [ids[:, 0:1], ids[:, 1:2]]
    zero = jnp.zeros_like(total)

    def gate_of(number):
        return sum(jnp.where(ids_c[c] == number, gates[c], zero) for c in range(2))

    copy_gate = gate_of(copy_id)
    const_gate = [gate_of(copy_id + 1 + k) for k in range(2)]
    dots = [jnp.sum(g * second[...].astype(full), axis=-1, keepdims=True)]
    dots = dots + [jnp.sum(g * const[k : k + 1, :], axis=-1, keepdims=True) for k in range(2)]
    d_gates = []
    for c in range(2):
        d = dg_mine[:, c : c + 1] + dg_came[:, c : c + 1]
        for k in range(3):
            d = d + jnp.where(ids_c[c] == copy_id + k, dots[k], zero)
        d_gates.append(d)
    mean = d_gates[0] * gates[0] + d_gates[1] * gates[1]
    lane = lax.broadcasted_iota(jnp.int32, probs.shape, 1)
    d_probs = jnp.zeros_like(probs)
    for c in range(2):
        d_probs = d_probs + jnp.where(lane == ids_c[c], (d_gates[c] - mean) / total, 0.0)
    d_logits = probs * (d_probs - jnp.sum(probs * d_probs, axis=-1, keepdims=True))
    dlog_ref[...] = d_logits
    d_second = copy_gate * g + full_ref[...].astype(full)
    rest = d_logits
    for i in range(3):
        piece = rest.astype(low)
        rest = rest - piece.astype(full)
        d_second = d_second + mm(piece, router[...])
    unit = mixed[...] * inverse
    d_gain = jnp.sum(d_second * unit, axis=0, keepdims=True)
    d_unit = d_second * gain[...]
    d_mixed = g + inverse * (d_unit - unit * jnp.mean(d_unit * unit, axis=-1, keepdims=True))
    dmix_ref[...] = d_mixed
    d_attn = d_mixed.astype(low)
    dattn_ref[...] = d_attn
    do_ref[:, :half] = mm(d_attn, wm[...]).astype(low)
    do_ref[:, half:] = mm(d_attn, wo[...]).astype(low)
    count = probs.shape[1]
    pad = jnp.zeros((probs.shape[0], 128 - count), full)
    wide = lax.broadcasted_iota(jnp.int32, (probs.shape[0], 128), 1)
    table = jnp.concatenate([d_logits, pad], axis=1)
    table = jnp.where(wide == count + 2, const_gate[0], table)
    table = jnp.where(wide == count + 3, const_gate[1], table)
    rest = table.T[: count + 4, :]
    from_second = from_g = 0.0
    for i in range(3):
        piece = rest.astype(low)
        rest = rest - piece.astype(full)
        from_second = from_second + mm(piece, second[...])
        from_g = from_g + mm(piece, g_ref[...])
    row = lax.broadcasted_iota(jnp.int32, from_g.shape, 0)
    small = jnp.where(row < count, from_second, jnp.where(row >= count + 2, from_g, 0.0))
    small_ref[...] = jnp.where(row == count + 1, d_gain, small)


def keys_back_kernel(place, dq, dk, dv, x, wm, wo, own_ref, p0_ref, p1_ref, p2_ref, gain_ref):
    shard = place[0]
    rows, width = own_ref.shape
    half = wm.shape[2]
    gain = jnp.zeros((1, width), jnp.float32)
    lo = 0
    for out in (own_ref, p0_ref, p1_ref, p2_ref):
        here = slice(lo, lo + out.shape[0])
        lo = lo + out.shape[0]
        d = 0.0
        for m, grad in ((0, dq), (1, dk), (2, dv)):
            if m > 0 or out is own_ref:
                d = d + mm(grad[here, :half], wm[m ^ shard], NT)
                d = d + mm(grad[here, half:], wo[m ^ shard], NT)
        out[...] = d.astype(out.dtype)
        gain = gain + jnp.sum(d * unit_rows(x[here, :]), axis=0, keepdims=True)
    gain_ref[...] = gain


def weights_back_kernel(n_ref, dq, dk, dv, da_ref, o, tiny, mine_ref, other_ref, nt, at):
    rows = dq.shape[0]
    step = pl.program_id(0)

    @pl.when(step == 0)
    def start():
        nt[...] = n_ref[...].T
        at[...] = da_ref[...].T

    def put(value):
        value = value.astype(jnp.bfloat16)
        part = value.shape[0] // mine_ref.shape[0]

        def write(ref):
            for z in range(ref.shape[0]):
                ref[z, :part, :] = value[z * part : (z + 1) * part, :]
                ref[z, part:, :] = tiny[z]

        pl.when(step % 2 == 0)(lambda: write(mine_ref))
        pl.when(step % 2 == 1)(lambda: write(other_ref))

    pl.when(step // 2 == 0)(lambda: put(mm(nt[:, :rows], dq[...])))
    pl.when(step // 2 == 1)(lambda: put(mm(nt[...], dk[...])))
    pl.when(step // 2 == 2)(lambda: put(mm(nt[...], dv[...])))
    pl.when(step // 2 == 3)(lambda: put(mm(at[...], o[...])))


def weights_back(normed, dq, dk, dv, d_attn, o, tiny):
    total, width = normed.shape
    rows, half = dq.shape[0], width // 2
    parts, room = tiny.shape[1], tiny.shape[2]
    low = jnp.bfloat16

    def columns(n, first):
        return pl.BlockSpec((n, half), lambda j: (0, jnp.clip(j - first, 0, 1)))

    out = pl.BlockSpec((None, parts, width // parts + room, half), lambda j: (j // 2, 0, 0, 0))
    shape = ((4, parts, width // parts + room, half), low)
    return call(
        weights_back_kernel,
        "weights_back",
        [shape, shape],
        (normed, dq, dk, dv, d_attn, o, tiny),
        [pltpu.VMEM((width, total), low), pltpu.VMEM((width, rows), low)],
        grid=(8,),
        in_specs=[
            pl.BlockSpec((total, width), lambda j: (0, 0)),
            columns(rows, 0),
            columns(total, 2),
            columns(total, 4),
            pl.BlockSpec((rows, width), lambda j: (0, 0)),
            columns(rows, 6),
            pl.BlockSpec((None, parts, room, half), lambda j: (j // 2, 0, 0, j % 2)),
        ],
        out_specs=[out, out],
    )


def flip(x, axis, bit, size):
    return lax.ppermute(x, axis, [(i, i ^ bit) for i in range(size)])


def turn_gather(x, size, position):
    out = jnp.zeros((size,) + x.shape, x.dtype)
    out = lax.dynamic_update_index_in_dim(out, x, position, 0)
    for k in range(1, size):
        block = lax.ppermute(x, "ctx", [(i, (i + k) % size) for i in range(size)])
        out = lax.dynamic_update_index_in_dim(out, block, (position - k) % size, 0)
    return out


def turn_sum(x, size, position):
    total = lax.dynamic_index_in_dim(x, position, 0, keepdims=False).astype(jnp.float32)
    for k in range(1, size):
        block = lax.dynamic_index_in_dim(x, (position + k) % size, 0, keepdims=False)
        got = lax.ppermute(block, "ctx", [(i, (i + k) % size) for i in range(size)])
        total = total + got.astype(jnp.float32)
    return total


def far(x, k, shards_n, ctx_n):
    pairs = []
    for s in range(shards_n):
        for z in range(ctx_n):
            pairs.append((s * ctx_n + z, (s ^ k) * ctx_n + (z ^ 2)))
    return lax.ppermute(x, ("shard", "ctx"), pairs)


def three_parts(x):
    one = x.astype(jnp.bfloat16)
    rest = x - one.astype(jnp.float32)
    two = rest.astype(jnp.bfloat16)
    return jnp.stack([one, two, (rest - two.astype(jnp.float32)).astype(jnp.bfloat16)], axis=-2)


def with_rows(slots, values, at):
    extra = three_parts(values)
    after = slots.shape[-2] - at - extra.shape[-2]
    pads = ((0, 0), (at, after), (0, slots.shape[-1] - extra.shape[-1]))
    return slots + jnp.pad(extra, pads)


def row_values(slots, at):
    return jnp.sum(slots[:, at : at + 3, : slots.shape[1]].astype(jnp.float32), axis=1)


def by_core(
    tokens, gate_res, cotangent, parents, expert_ids, priority, w_qkv, w_out, w_router, attn_gain,
    ffn_gain, const_vec, w_gate_up, w_down,
):
    low, full = jnp.bfloat16, jnp.float32
    shard, ctx, tp = lax.axis_index("shard"), lax.axis_index("ctx"), lax.axis_index("tp")
    shards_n, ctx_n = lax.axis_size("shard"), lax.axis_size("ctx")
    trees, rows, width = tokens.shape
    rows_d = w_qkv.shape[0]
    part = width // 2
    seg = rows * ctx_n // parents.shape[1]
    own_segs = rows // seg
    edge = KEY_SEGS * seg - 2 * rows

    def own_tree(x):
        return lax.dynamic_index_in_dim(x, tp, 0, keepdims=False)

    def in_order(x, other, axis=0):
        return jnp.concatenate([jnp.where(tp == 0, x, other), jnp.where(tp == 0, other, x)], axis=axis)

    def both_trees(x, other):
        return in_order(x[None], other[None])

    def unit_of(x):
        x = x.astype(full)
        inverse = lax.rsqrt(jnp.mean(x * x, axis=-1, keepdims=True) + eps)
        return (x * inverse, inverse)

    def swap(x):
        return flip(x, "tp", 1, 2)

    def plus(x, y):
        return (x.astype(full) + y.astype(full)).astype(low)

    def my_half(x, which):
        return lax.dynamic_slice_in_dim(x, which * part, part, x.ndim - 1)

    x_own = lax.optimization_barrier(own_tree(tokens))
    ends = [(i, i + 1) for i in range(ctx_n - 1)]
    near = lax.ppermute(x_own, "ctx", ends)

    mine = jnp.stack([w_qkv[:, 0], w_qkv[:, 1], w_qkv[:, 2], w_out])
    small = jnp.concatenate([w_router.T, attn_gain[None], ffn_gain[None], const_vec.T], axis=0)
    all_experts = w_router.shape[1]
    mine = lax.dynamic_index_in_dim(mine, shard, 0, keepdims=False)
    mine = jnp.concatenate([mine, small.reshape(-1, part)], axis=0)
    turned = turn_gather(mine, ctx_n, ctx)
    matrix = turned[:, :rows_d].reshape(width, -1)
    small = turned[:, rows_d:].reshape(ctx_n, -1, rows_d).transpose(1, 0, 2).reshape(-1, width)
    router_t = small[:all_experts]
    gain_a = small[all_experts].astype(full)
    gain_f = small[all_experts + 1].astype(full)
    const_t = small[all_experts + 2 :].astype(full)

    mid = lax.ppermute(pin(near, matrix), "ctx", ends[1:])
    plane_pieces = [matrix] + [flip(matrix, "shard", k, shards_n) for k in range(1, shards_n)]
    capacity = trees * rows * 2 // all_experts
    experts = shards_n * w_gate_up.shape[1]
    padded = -(-(capacity + 3) // 16) * 16
    count = experts * padded
    flat = expert_ids.reshape(-1)
    order = (2 * priority[0, 0][:, None] + jnp.arange(2, dtype=jnp.int32)[None, :]).reshape(-1)
    earlier = (flat[:, None] == flat[None, :]) & (order[None, :] < order[:, None])
    ranks = jnp.sum(earlier.astype(jnp.int32), axis=1)
    kept = (flat < experts) & (ranks < capacity)
    piece = ((flat % 2) ^ (ctx // 2)) * shards_n + ((flat // 2) ^ shard)
    place = jnp.where(kept, piece * padded + ranks, -1).reshape(trees, rows, 2)
    place = jnp.where(tp == 0, place, place[::-1]).reshape(trees * rows, 2)
    place_t = place.T

    g_own = own_tree(cotangent)
    g_other = lax.dynamic_index_in_dim(cotangent, 1 - tp, 0, keepdims=False)
    g_half = my_half(jnp.concatenate([g_own, g_other], axis=0), tp)
    g_slots = spread(place_t, g_half, experts, padded, capacity)
    ids = own_tree(expert_ids)
    res = own_tree(gate_res)
    ids, res, router_t, gain_a, gain_f, const_t, mid, *g_slots = lax.optimization_barrier(
        (ids, res, router_t, gain_a[None], gain_f[None], const_t, mid, *g_slots)
    )
    farther = lax.ppermute(mid, "ctx", ends[2:])
    plane = jnp.stack(plane_pieces)

    plane_other = swap(plane)
    place3 = jnp.stack([shard, ctx, tp]).astype(jnp.int32)

    capacity = trees * rows * 2 // all_experts
    experts = shards_n * w_gate_up.shape[1]
    padded = -(-(capacity + 3) // 16) * 16
    count = experts * padded
    flat = expert_ids.reshape(-1)
    order = (2 * priority[0, 0][:, None] + jnp.arange(2, dtype=jnp.int32)[None, :]).reshape(-1)
    earlier = (flat[:, None] == flat[None, :]) & (order[None, :] < order[:, None])
    ranks = jnp.sum(earlier.astype(jnp.int32), axis=1)
    kept = (flat < experts) & (ranks < capacity)
    piece = ((flat % 2) ^ (ctx // 2)) * shards_n + ((flat // 2) ^ shard)
    place = jnp.where(kept, piece * padded + ranks, -1).reshape(trees, rows, 2)
    place = jnp.where(tp == 0, place, place[::-1]).reshape(trees * rows, 2)
    place_t = place.T

    g_own = own_tree(cotangent)
    g_other = lax.dynamic_index_in_dim(cotangent, 1 - tp, 0, keepdims=False)
    g_half = my_half(jnp.concatenate([g_own, g_other], axis=0), tp)
    g_slots = spread(place_t, g_half, experts, padded, capacity)
    g_near = jnp.stack(g_slots[:shards_n])
    g_far = flip(pin(jnp.stack(g_slots[shards_n:]), mid), "ctx", 2, ctx_n)
    plane_other = swap(plane)
    place3 = jnp.stack([shard, ctx, tp]).astype(jnp.int32)

    g_near = jnp.stack(g_slots[:shards_n])
    g_far = flip(jnp.stack(g_slots[shards_n:]), "ctx", 2, ctx_n)

    held, gu, dn = lax.optimization_barrier((near, w_gate_up, w_down))
    lower = ctx < 2
    first = jnp.stack([gu[:, 0, 0], gu[:, 0, 1], dn[:, 0]])
    second_e = jnp.stack([gu[:, 1, 0], gu[:, 1, 1], dn[:, 1]])
    rows_own = jnp.where(lower, first, second_e)
    rows_two = flip(pin(jnp.where(lower, second_e, first), farther, g_far), "ctx", 2, ctx_n)
    rows_one = flip(pin(rows_own, farther, g_far), "ctx", 1, ctx_n)

    total = 3 * rows + edge
    q, kv, normed, x_all = call(
        project_kernel,
        "project",
        [((rows, width), low), ((total, 2 * width), low), ((total, width), low), ((total, width), low)],
        (place3, x_own, near, mid, farther, gain_a, plane, plane_other),
        in_specs=[whole(rows, width)] * 4
        + [whole(1, width), whole(4, width, part), whole(4, width, part)],
        prefetch=True,
    )

    seg_id = ctx * own_segs + jnp.arange(own_segs, dtype=jnp.int32)
    parent = jnp.take(own_tree(parents), seg_id)
    leaf = (seg_id >= KEY_SEGS).astype(jnp.int32)
    info = jnp.stack([jnp.minimum(seg_id, TRUNK), jnp.where(leaf > 0, parent, TRUNK), leaf], axis=1)
    half_pairs = width // 256
    ahead = attend(info, q, kv, seg, 0, half_pairs)
    o_low, lse = attend(info, q, kv, seg, half_pairs, half_pairs, ahead)
    g_pairs = jnp.stack([g_near, pin(g_far, ahead[0])], axis=1)
    g_got = [g_pairs[0]] + [flip(g_pairs[k], "shard", k, shards_n) for k in range(1, shards_n)]
    o_low = pin(o_low, rows_one, rows_two, *g_got)
    g_in = jnp.stack(g_got, axis=1).reshape(2, shards_n * padded, part)
    g_out = swap(g_in)

    one_half = ((rows, part), low)
    mixed, second, second_mine, second_other, probs, stat, gates_t = call(
        settle_kernel,
        "settle",
        [
            ((rows, width), full), ((rows, width), low), one_half, one_half,
            ((rows, all_experts), full), ((rows, 8), full), ((8, rows), full),
        ],
        (place3, o_low, x_own, plane, plane_other, gain_f, router_t, res, ids),
        in_specs=[
            whole(rows, width), whole(rows, width), chosen(3, width, part), chosen(3, width, part),
            whole(1, width), whole(all_experts, width), whole(rows, all_experts), whole(rows, 2),
        ],
        prefetch=True,
    )
    second_half = jnp.concatenate([second_mine, swap(second_other)], axis=0)
    gates_both = jnp.concatenate([gates_t, swap(gates_t)], axis=1)

    rows_three = flip(pin(rows_two, o_low), "ctx", 1, ctx_n)
    weights = (rows_own, rows_one, rows_two, rows_three)
    slots = spread(place_t, second_half, experts, padded, capacity, gates_both)
    x_far = [far(slots[shards_n + k], k, shards_n, ctx_n) for k in range(shards_n)]
    x_near = [slots[0]] + [flip(slots[k], "shard", k, shards_n) for k in range(1, shards_n)]

    def experts_on(pieces, gs, prev):
        x = jnp.concatenate(pieces, axis=0)
        return expert_pass(place3[1:], capacity, shards_n, (x, swap(x)), gs, weights, prev)

    def answers(mine, other):
        return plus(mine, swap(other)).reshape(shards_n, padded, part)

    x_near[0] = pin(x_near[0], rows_three)
    on1, ox1, sn1, sx1, dw = experts_on(x_near, (g_in[0], g_out[0]), None)
    x_far = list(lax.optimization_barrier((*x_far, sn1))[:-1])
    on2, ox2, sn2, sx2, dw = experts_on(x_far, (g_in[1], g_out[1]), dw)
    ds_far = answers(sn2, sx2)
    ds_near = answers(sn1, sx1)
    ds_far = [far(ds_far[k], k, shards_n, ctx_n) for k in range(shards_n)]
    ds_near = [ds_near[0]] + [flip(ds_near[k], "shard", k, shards_n) for k in range(1, shards_n)]

    rows_tn = (((0,), (0,)), ((), ()))
    d_routed, d_routed_other, d_pairs, d_pairs_other = gather(place, ds_near + ds_far, capacity)
    d_mixed, d_attn, d_o, d_logits, d_small = call(
        functools.partial(settle_back_kernel, experts + 1),
        "settle_back",
        [
            ((rows, width), full), ((rows, width), low), ((rows, width), low),
            ((rows, all_experts), full), ((all_experts + 4, width), full),
        ],
        (
            place3, d_routed, swap(d_routed_other), d_pairs, swap(d_pairs_other), g_own, mixed, second,
            probs, stat, ids, const_t, router_t, gain_f, plane, plane_other,
        ),
        [pltpu.VMEM((rows, width), low)],
        in_specs=[
            whole(rows, part), whole(rows, part), whole(rows, 2), whole(rows, 2), whole(rows, width),
            whole(rows, width), whole(rows, width), whole(rows, all_experts), whole(rows, 8),
            whole(rows, 2), whole(2, width), whole(all_experts, width), whole(1, width),
            chosen(3, width, part), chosen(3, width, part),
        ],
        prefetch=True,
    )

    ox1, ox2, held = lax.optimization_barrier((ox1, ox2, d_routed))
    out_near = plus(on1, swap(ox1)).reshape(shards_n, padded, part)
    out_far = plus(on2, swap(ox2)).reshape(shards_n, padded, part)

    got = flip(pin(dw[2:], d_routed), "ctx", 1, ctx_n)

    third = width // 384
    back = attend_back(info, q, kv, o_low, d_o, lse, seg, 0, third)
    out_near, out_far, q_later, held = lax.optimization_barrier((out_near, out_far, q, back[0]))
    back = attend_back(info, q_later, kv, o_low, d_o, lse, seg, third, third, back)
    out_near, out_far = (out_near, out_far)
    out_cross = flip(out_far, "ctx", 2, ctx_n)
    q_later = pin(q, back[0])
    dq, dk, dv = attend_back(info, q_later, kv, o_low, d_o, lse, seg, 2 * third, third, back)
    got = pin(got, dq)
    sent_rows = plus(dw[1], got[1])
    came_rows = flip(sent_rows, "ctx", 2, ctx_n)
    out_pairs = jnp.stack([out_near, pin(out_cross, dq)], axis=1)
    out_got = [out_pairs[0]] + [flip(out_pairs[k], "shard", k, shards_n) for k in range(1, shards_n)]
    d_near, part0, part1, part2, d_gain_a = call(
        keys_back_kernel,
        "keys_back",
        [
            ((rows, width), full), ((rows, width), low), ((rows, width), low), ((edge, width), low),
            ((1, width), full),
        ],
        (pin(place3, sent_rows), dq, dk, dv, x_all, plane, plane_other),
        in_specs=[
            whole(rows, width), whole(total, width), whole(total, width), whole(total, width),
            whole(4, width, part), whole(4, width, part),
        ],
        prefetch=True,
    )

    tiny = jnp.concatenate([d_small[:all_experts], d_gain_a, d_small[all_experts + 1 :]], axis=0)
    tiny = tiny.reshape(4, 2, 2, ctx_n, rows_d).transpose(0, 3, 1, 2, 4).reshape(4, ctx_n, 2, 2 * rows_d)
    tiny = jnp.where(tp == 0, tiny, tiny[:, :, ::-1]).reshape(4, ctx_n, 1, width).astype(low)
    tiny = jnp.pad(tiny, ((0, 0), (0, 0), (0, 15), (0, 0)))
    shared_mine, shared_other = weights_back(normed, dq, dk, dv, d_attn, o_low, tiny)

    def down(x, step):
        return lax.ppermute(x, "ctx", [(i, i - 1) for i in range(ctx_n - step, ctx_n)])

    came = down(part0, 1)
    shared_other = pin(shared_other, came, *out_got, came_rows)
    payload = jnp.where(ctx == 3, part1, plus(part0, came))
    came = down(payload, 2)
    shared = plus(pin(shared_mine, payload), swap(shared_other))

    def numbered(k):
        return lax.dynamic_index_in_dim(shared, shard ^ k, 0, keepdims=False)

    plane_parts = [flip(numbered(k), "shard", k, shards_n) for k in range(1, shards_n)]
    plane_sum = numbered(0).astype(full)
    for got_part in plane_parts:
        plane_sum = plane_sum + got_part.astype(full)
    came = pin(came, plane_parts[0])
    part2 = jnp.pad(part2, ((0, rows - edge), (0, 0)))
    came = down(jnp.where(ctx == 3, part2, jnp.where(ctx == 2, plus(part1, came), plus(part0, came))), 3)
    base = jnp.where(ctx == 0, part0, jnp.where(ctx == 1, part1, part2)).astype(full)
    extra = jnp.where(ctx == 3, 0.0, base + came.astype(full))
    came_rows = pin(came_rows, plane_parts[0]).astype(full)
    kept_rows = dw[0].astype(full) + got[0].astype(full)
    first = jnp.where(lower, kept_rows, came_rows)
    second_e = jnp.where(lower, came_rows, kept_rows)
    d_gate_up = jnp.stack(
        [jnp.stack([first[0], first[1]], axis=1), jnp.stack([second_e[0], second_e[1]], axis=1)], axis=1
    )
    d_down = jnp.stack([first[2], second_e[2]], axis=1)
    d_normed = d_near + extra
    unit_own, inv_own = unit_of(x_own)
    gain_a = gain_a[0]
    d_first = d_normed * gain_a
    d_tokens = d_mixed + inv_own * (
        d_first - unit_own * jnp.mean(d_first * unit_own, axis=-1, keepdims=True)
    )

    total = turn_sum(plane_sum.astype(low), ctx_n, ctx).astype(low)
    out_got = [pin(o, plane_parts[0]) for o in out_got]
    gate_columns = jnp.stack([gates_both[0], gates_both[1]], axis=1)
    combined, combined_other = gather(place, out_got, capacity, gate_columns)
    combined = in_order(combined, swap(combined_other), 1).astype(full)
    second_f = second.astype(full)

    def gate_of(number):
        return jnp.sum(jnp.where(ids == number, stat[:, :2], 0.0), axis=1, keepdims=True)

    copy_gate = gate_of(experts + 1)
    const_gate = jnp.concatenate([gate_of(experts + 2), gate_of(experts + 3)], axis=1)
    mixed_out = (
        mixed
        + combined
        + copy_gate * second_f
        + const_gate[:, :1] * const_t[0][None]
        + const_gate[:, 1:] * const_t[1][None]
    )
    total = pin(total, mixed_out, d_tokens)
    four = jnp.stack([total] + [flip(total, "shard", k, shards_n) for k in range(1, shards_n)])
    four = jnp.stack(
        [lax.dynamic_index_in_dim(four, m ^ shard, 0, keepdims=False) for m in range(4)]
    )
    d_q, d_k, d_v, d_w_out = [four[m, :rows_d].astype(full) for m in range(4)]
    d_w_qkv = jnp.stack([d_q, d_k, d_v], axis=1)
    tiny = four[:, rows_d]
    tiny = both_trees(tiny, swap(tiny)).transpose(1, 0, 2).reshape(16, rows_d).astype(full)

    return (
        both_trees(mixed_out, swap(mixed_out)),
        both_trees(d_tokens, swap(d_tokens)),
        both_trees(d_logits, swap(d_logits)),
        d_w_qkv,
        d_w_out,
        tiny[:all_experts].T,
        tiny[all_experts],
        tiny[all_experts + 1],
        tiny[all_experts + 2 :].T,
        d_gate_up,
        d_down,
    )


def program(tokens, gate_res, cotangent, parents, expert_ids, priority, w_qkv, *weights):
    trees, rows, width = tokens.shape
    ctx_n = lax.axis_size("ctx")
    seg = rows * ctx_n // parents.shape[1]
    fits = (
        ctx_n == 4
        and lax.axis_size("shard") == 4
        and lax.axis_size("tp") == 2
        and trees == 2
        and seg == 128
        and rows % seg == 0
        and 2 * rows < KEY_SEGS * seg <= 3 * rows
        and weights[-1].shape[1] == 2
    )
    chosen = by_core if fits else shards
    return chosen(tokens, gate_res, cotangent, parents, expert_ids, priority, w_qkv, *weights)


def solution(mesh):
    return jax.shard_map(
        program,
        mesh=mesh,
        in_specs=(
            P("shard", "ctx", None),
            P("shard", "ctx", None),
            P("shard", "ctx", None),
            P("shard", None),
            P("shard", "ctx", None),
            P("shard", "ctx", None),
            P("ctx", None, "tp"),
            P("ctx", "tp"),
            P("ctx", None),
            P("ctx"),
            P("ctx"),
            P("ctx", None),
            P("ctx", "shard", None, "tp"),
            P("ctx", "shard", "tp"),
        ),
        out_specs=(
            P("shard", "ctx", None),
            P("shard", "ctx", None),
            P("shard", "ctx", None),
            P("ctx", None, "tp"),
            P("ctx", "tp"),
            P("ctx", None),
            P("ctx"),
            P("ctx"),
            P("ctx", None),
            P("ctx", "shard", None, "tp"),
            P("ctx", "shard", "tp"),
        ),
        check_vma=False,
    )
```

```python
import functools
import math

import jax
import jax.numpy as jnp
from jax import lax
from jax.experimental import pallas as pl
from jax.experimental.pallas import tpu as pltpu
from jax.sharding import PartitionSpec as P

HEAD_DIM = 64


eps = 1e-06
score_scale = 0.125


def ancestry(parent_row):
    seg_count = parent_row.shape[0]
    position = jnp.arange(seg_count, dtype=jnp.int32)
    linked = (parent_row[:, None] == position[None, :]) | (position[:, None] == position[None, :])
    reach = linked.astype(jnp.float32)
    for repeat in range(seg_count.bit_length()):
        reach = jnp.minimum(jnp.dot(reach, reach, precision=lax.Precision.HIGHEST), 1.0)
    return reach


def path_rows(positions, seg_len, ancestors):
    onehot = (
        (positions // seg_len)[:, None] == jnp.arange(ancestors.shape[0], dtype=jnp.int32)[None, :]
    ).astype(jnp.float32)
    return jnp.dot(onehot, ancestors)


def allowed_block(query_rows, query_pos, key_start, key_count, seg_len):
    key_pos = key_start + jnp.arange(key_count, dtype=jnp.int32)
    key_onehot = (
        (key_pos // seg_len)[:, None] == jnp.arange(query_rows.shape[1], dtype=jnp.int32)[None, :]
    ).astype(jnp.float32)
    linked = jnp.dot(query_rows, key_onehot.T) > 0.5
    return (linked & (key_pos[None, :] <= query_pos[:, None]))[None]


def slot_table(picked_ids, ranking, experts, capacity):
    count_rows = picked_ids.shape[0]
    flat_ids = picked_ids.reshape(-1)
    rank_key = (2 * ranking[:, None] + jnp.arange(2, dtype=jnp.int32)[None, :]).reshape(-1)
    earlier = (flat_ids[:, None] == flat_ids[None, :]) & (rank_key[None, :] < rank_key[:, None])
    ranks = jnp.sum(earlier.astype(jnp.int32), axis=1)
    kept = (flat_ids < experts) & (ranks < capacity)
    target = jnp.where(kept, flat_ids * capacity + ranks, -1).reshape(count_rows, 2)
    slot_index = jnp.arange(experts * capacity, dtype=jnp.int32)
    return slot_index[None, :, None] == target.T[:, None, :]


def block_scores(queries, keys_blk):
    return (
        jnp.einsum("qhe,khe->hqk", queries, keys_blk, preferred_element_type=jnp.float32)
        * score_scale
    )


def softmax_grads(queries, grads_out, stat_lse, stat_delta, keys_blk, values_blk, mask):
    prob = jnp.where(mask, jnp.exp(block_scores(queries, keys_blk) - stat_lse[:, :, None]), 0.0)
    dprob = jnp.einsum("qhe,khe->hqk", grads_out, values_blk, preferred_element_type=jnp.float32)
    dscore = (prob * (dprob - stat_delta[:, :, None])).astype(jnp.bfloat16)
    return (prob.astype(jnp.bfloat16), dscore)


def shards(
    tokens,
    gate_res,
    cotangent,
    parents,
    expert_ids,
    priority,
    w_qkv,
    w_out,
    w_router,
    attn_gain,
    ffn_gain,
    const_vec,
    w_gate_up,
    w_down,
):
    full_qkv, full_out, full_router, full_again, full_fgain, full_const, full_gu, full_down = (
        lax.all_gather(w_qkv, "ctx", axis=0, tiled=True),
        lax.all_gather(w_out, "ctx", axis=0, tiled=True),
        lax.all_gather(w_router, "ctx", axis=0, tiled=True),
        lax.all_gather(attn_gain, "ctx", axis=0, tiled=True),
        lax.all_gather(ffn_gain, "ctx", axis=0, tiled=True),
        lax.all_gather(const_vec, "ctx", axis=0, tiled=True),
        lax.all_gather(w_gate_up, "ctx", axis=0, tiled=True),
        lax.all_gather(w_down, "ctx", axis=0, tiled=True),
    )
    tree_count, rows, model_width = tokens.shape
    tok_rows = tree_count * rows
    inputs = tokens.reshape(tok_rows, model_width).astype(jnp.float32)
    local_width = full_out.shape[1]
    local_heads = local_width // HEAD_DIM
    ctx_index = lax.axis_index("ctx")
    tree_len = rows * lax.axis_size("ctx")
    ancestors_all = jax.vmap(ancestry)(parents)
    seg_len = tree_len // parents.shape[1]
    key_block = math.gcd(tree_len, 512)
    starts = jnp.arange(tree_len // key_block, dtype=jnp.int32) * key_block
    key_start_own = ctx_index * rows
    query_pos = key_start_own + jnp.arange(rows, dtype=jnp.int32)
    query_rows_all = jax.vmap(lambda anc: path_rows(query_pos, seg_len, anc))(ancestors_all)
    inv_first = lax.rsqrt(jnp.mean(inputs * inputs, axis=-1, keepdims=True) + eps)
    first_unit = inputs * inv_first
    first_gain = full_again.astype(jnp.float32)
    normed = (first_unit * first_gain).astype(jnp.bfloat16)
    projected = jnp.einsum("nd,dke->nke", normed, full_qkv, preferred_element_type=jnp.float32)
    q_low = projected[:, 0].astype(jnp.bfloat16)
    k_low = projected[:, 1].astype(jnp.bfloat16)
    v_low = projected[:, 2].astype(jnp.bfloat16)
    keys_all, values_all = (
        lax.all_gather(k_low.reshape(tree_count, rows, local_width), "ctx", axis=1, tiled=True),
        lax.all_gather(v_low.reshape(tree_count, rows, local_width), "ctx", axis=1, tiled=True),
    )
    q_heads = q_low.reshape(tree_count, rows, local_heads, HEAD_DIM)
    k_heads = keys_all.reshape(tree_count, tree_len, local_heads, HEAD_DIM)
    v_heads = values_all.reshape(tree_count, tree_len, local_heads, HEAD_DIM)

    def tree_forward(q_one, k_one, v_one, rows_one):

        def stat_step(carry, start):
            running_top, running_sum = carry
            keys_blk = lax.dynamic_slice_in_dim(k_one, start, key_block, 0)
            mask = allowed_block(rows_one, query_pos, start, key_block, seg_len)
            masked = jnp.where(mask, block_scores(q_one, keys_blk), -1e30)
            new_top = jnp.maximum(running_top, jnp.max(masked, axis=2))
            expo = jnp.where(mask, jnp.exp(masked - new_top[:, :, None]), 0.0)
            running_sum = running_sum * jnp.exp(running_top - new_top) + jnp.sum(expo, axis=2)
            return ((new_top, running_sum), None)

        start_top = jnp.full((local_heads, rows), -1e30, jnp.float32)
        (final_top, final_sum), unused = lax.scan(
            stat_step, (start_top, jnp.zeros_like(start_top)), starts
        )
        lse_one = final_top + jnp.log(final_sum)

        def out_step(accum, start):
            keys_blk = lax.dynamic_slice_in_dim(k_one, start, key_block, 0)
            values_blk = lax.dynamic_slice_in_dim(v_one, start, key_block, 0)
            mask = allowed_block(rows_one, query_pos, start, key_block, seg_len)
            prob = jnp.where(
                mask, jnp.exp(block_scores(q_one, keys_blk) - lse_one[:, :, None]), 0.0
            ).astype(jnp.bfloat16)
            return (
                accum
                + jnp.einsum("hqk,khe->qhe", prob, values_blk, preferred_element_type=jnp.float32),
                None,
            )

        attended_one, unused = lax.scan(
            out_step, jnp.zeros((rows, local_heads, HEAD_DIM), jnp.float32), starts
        )
        return (attended_one, lse_one)

    attended, lse = jax.vmap(tree_forward)(q_heads, k_heads, v_heads, query_rows_all)
    attended_low = attended.reshape(tok_rows, local_width).astype(jnp.bfloat16)
    attn_part = jnp.einsum("nh,dh->nd", attended_low, full_out, preferred_element_type=jnp.float32)
    attn_sum = lax.psum(attn_part.astype(jnp.bfloat16), "tp").astype(jnp.float32)
    mixed = inputs + attn_sum
    inv_second = lax.rsqrt(jnp.mean(mixed * mixed, axis=-1, keepdims=True) + eps)
    second_unit = mixed * inv_second
    second_gain = full_fgain.astype(jnp.float32)
    second_low = (second_unit * second_gain).astype(jnp.bfloat16)
    second_float = second_low.astype(jnp.float32)
    logits = jnp.dot(
        second_low, full_router, preferred_element_type=jnp.float32
    ) + gate_res.reshape(tok_rows, -1)
    expo_logits = jnp.exp(logits - jnp.max(logits, axis=-1, keepdims=True))
    probs = expo_logits / jnp.sum(expo_logits, axis=-1, keepdims=True)
    experts = lax.axis_size("shard") * w_gate_up.shape[1]
    every_expert = experts + 4
    capacity = tok_rows * 2 // every_expert
    picked_ids = expert_ids.reshape(tok_rows, 2)
    selector = (picked_ids[:, :, None] == jnp.arange(every_expert, dtype=jnp.int32)).astype(
        jnp.float32
    )
    picked = jnp.sum(selector * probs[:, None, :], axis=-1)
    picked_total = jnp.sum(picked, axis=-1, keepdims=True)
    gates = picked / picked_total
    table = slot_table(picked_ids, priority[0, 0], experts, capacity).astype(jnp.bfloat16)
    routed = table[0] + table[1]
    send_slots = jnp.einsum(
        "et,td->ed", routed, second_low, preferred_element_type=jnp.float32
    ).astype(jnp.bfloat16)
    send_slots = send_slots.reshape(experts, 1, capacity, model_width)
    arrived = lax.all_to_all(send_slots, "shard", split_axis=0, concat_axis=1, tiled=True)
    gate_up = jnp.einsum("jsrd,djgf->jsrgf", arrived, full_gu, preferred_element_type=jnp.float32)
    hidden_low = (jax.nn.silu(gate_up[:, :, :, 0]) * gate_up[:, :, :, 1]).astype(jnp.bfloat16)
    partial_out = jnp.einsum(
        "jsrf,djf->jsrd", hidden_low, full_down, preferred_element_type=jnp.float32
    )
    summed = lax.psum(partial_out.astype(jnp.bfloat16), "tp")
    returned = lax.all_to_all(summed, "shard", split_axis=1, concat_axis=0, tiled=True)
    returned, kept_slots = (returned, arrived)
    out_slots = returned.reshape(experts * capacity, model_width)
    ffn_values = jnp.einsum("cet,ed->ctd", table, out_slots, preferred_element_type=jnp.float32)
    copy_flag = selector[:, :, experts + 1]
    const_flags = selector[:, :, experts + 2 :]
    const_float = full_const.astype(jnp.float32)
    fixed_terms = jnp.einsum(
        "nck,dk->cnd", const_flags, const_float, precision=lax.Precision.HIGHEST
    )
    values_pair = ffn_values + copy_flag.T[:, :, None] * second_float[None] + fixed_terms
    mixed_out = mixed + jnp.sum(gates.T[:, :, None] * values_pair, axis=0)
    grad_out = cotangent.reshape(tok_rows, model_width).astype(jnp.float32)
    weighted = gates.T[:, :, None] * grad_out[None]
    d_gates = jnp.einsum("cnd,nd->nc", values_pair, grad_out)
    d_const = jnp.einsum("nck,cnd->dk", const_flags, weighted, precision=lax.Precision.HIGHEST)
    d_out_slots = jnp.einsum(
        "cet,ctd->ed", table.astype(jnp.float32), weighted, precision=lax.Precision.HIGHEST
    )
    d_out_low = d_out_slots.astype(jnp.bfloat16).reshape(experts, 1, capacity, model_width)
    d_picked = (d_gates - jnp.sum(d_gates * gates, axis=-1, keepdims=True)) / picked_total
    d_probs = jnp.einsum("nc,nck->nk", d_picked, selector)
    d_logits = probs * (d_probs - jnp.sum(probs * d_probs, axis=-1, keepdims=True))
    d_router_w = jnp.dot(second_float.T, d_logits, precision=lax.Precision.HIGHEST)
    d_second = jnp.sum(copy_flag.T[:, :, None] * weighted, axis=0)
    d_second = d_second + jnp.dot(
        d_logits, full_router.astype(jnp.float32).T, precision=lax.Precision.HIGHEST
    )
    arrived_grad = lax.all_to_all(d_out_low, "shard", split_axis=0, concat_axis=1, tiled=True)
    gate_up = jnp.einsum(
        "jsrd,djgf->jsrgf", kept_slots, full_gu, preferred_element_type=jnp.float32
    )
    gate_part = gate_up[:, :, :, 0]
    up_part = gate_up[:, :, :, 1]
    sigma = jax.nn.sigmoid(gate_part)
    silu_part = gate_part * sigma
    hidden_low = (silu_part * up_part).astype(jnp.bfloat16)
    d_hidden = jnp.einsum(
        "jsrd,djf->jsrf", arrived_grad, full_down, preferred_element_type=jnp.float32
    )
    d_gate_part = d_hidden * up_part * sigma * (1.0 + gate_part * (1.0 - sigma))
    d_up_part = d_hidden * silu_part
    d_gate_up_low = jnp.stack([d_gate_part, d_up_part], axis=3).astype(jnp.bfloat16)
    d_slot_part = jnp.einsum(
        "jsrgf,djgf->jsrd", d_gate_up_low, full_gu, preferred_element_type=jnp.float32
    )
    d_slot_sum = lax.psum(d_slot_part.astype(jnp.bfloat16), "tp")
    d_slot_back = lax.all_to_all(d_slot_sum, "shard", split_axis=1, concat_axis=0, tiled=True)
    d_gate_up_w = jnp.einsum(
        "jsrd,jsrgf->djgf", kept_slots, d_gate_up_low, preferred_element_type=jnp.float32
    )
    d_down_w = jnp.einsum(
        "jsrd,jsrf->djf", arrived_grad, hidden_low, preferred_element_type=jnp.float32
    )
    d_second = d_second + jnp.einsum(
        "et,ed->td",
        routed,
        d_slot_back.reshape(experts * capacity, model_width),
        preferred_element_type=jnp.float32,
    )
    d_second_gain = jnp.sum(d_second * second_unit, axis=0)
    d_second_unit = d_second * second_gain
    d_mixed = grad_out + inv_second * (
        d_second_unit - second_unit * jnp.mean(d_second_unit * second_unit, axis=-1, keepdims=True)
    )
    d_attn_low = d_mixed.astype(jnp.bfloat16)
    d_out_w = jnp.einsum("nd,nh->dh", d_attn_low, attended_low, preferred_element_type=jnp.float32)
    d_attended = jnp.einsum("nd,dh->nh", d_attn_low, full_out, preferred_element_type=jnp.float32)
    do_low = d_attended.astype(jnp.bfloat16)
    do_heads = do_low.reshape(tree_count, rows, local_heads, HEAD_DIM)
    delta = jnp.einsum("tqhe,tqhe->thq", do_heads.astype(jnp.float32), attended)

    def tree_both(q_one, k_one, v_one, do_one, lse_one, delta_one, rows_one):

        def both_step(dq_accum, start):
            keys_blk = lax.dynamic_slice_in_dim(k_one, start, key_block, 0)
            values_blk = lax.dynamic_slice_in_dim(v_one, start, key_block, 0)
            mask = allowed_block(rows_one, query_pos, start, key_block, seg_len)
            prob_low, dscore = softmax_grads(
                q_one, do_one, lse_one, delta_one, keys_blk, values_blk, mask
            )
            dq_accum = dq_accum + jnp.einsum(
                "hqk,khe->qhe", dscore, keys_blk, preferred_element_type=jnp.float32
            )
            dkey = (
                jnp.einsum("hqk,qhe->khe", dscore, q_one, preferred_element_type=jnp.float32)
                * score_scale
            )
            dval = jnp.einsum("hqk,qhe->khe", prob_low, do_one, preferred_element_type=jnp.float32)
            return (
                dq_accum,
                jnp.stack(
                    [dkey.reshape(key_block, local_width), dval.reshape(key_block, local_width)],
                    axis=1,
                ),
            )

        dq_one, terms_one = lax.scan(
            both_step, jnp.zeros((rows, local_heads, HEAD_DIM), jnp.float32), starts
        )
        return (dq_one, terms_one.reshape(tree_len, 2, local_width))

    dq_total, key_terms = jax.vmap(tree_both)(
        q_heads, k_heads, v_heads, do_heads, lse, delta, query_rows_all
    )
    key_sums = lax.psum_scatter(
        key_terms.astype(jnp.bfloat16), "ctx", scatter_dimension=1, tiled=True
    ).astype(jnp.float32)
    key_grad = key_sums[:, :, 0].reshape(tok_rows, local_width)
    value_grad = key_sums[:, :, 1].reshape(tok_rows, local_width)
    query_grad = (dq_total * score_scale).reshape(tok_rows, local_width)
    d_qkv_low = jnp.stack([query_grad, key_grad, value_grad], axis=1).astype(jnp.bfloat16)
    d_qkv_w = jnp.einsum("nd,nke->dke", normed, d_qkv_low, preferred_element_type=jnp.float32)
    d_normed_part = jnp.einsum(
        "nke,dke->nd", d_qkv_low, full_qkv, preferred_element_type=jnp.float32
    )
    d_normed = lax.psum(d_normed_part.astype(jnp.bfloat16), "tp").astype(jnp.float32)
    d_first_gain = jnp.sum(d_normed * first_unit, axis=0)
    d_first_unit = d_normed * first_gain
    d_inputs = d_mixed + inv_first * (
        d_first_unit - first_unit * jnp.mean(d_first_unit * first_unit, axis=-1, keepdims=True)
    )
    summed_grads = (
        lax.psum_scatter(
            d_qkv_w.astype(jnp.bfloat16), "ctx", scatter_dimension=0, tiled=True
        ).astype(jnp.float32),
        lax.psum_scatter(
            d_out_w.astype(jnp.bfloat16), "ctx", scatter_dimension=0, tiled=True
        ).astype(jnp.float32),
        lax.psum_scatter(
            d_router_w.astype(jnp.bfloat16), "ctx", scatter_dimension=0, tiled=True
        ).astype(jnp.float32),
        lax.psum_scatter(
            d_first_gain.astype(jnp.bfloat16), "ctx", scatter_dimension=0, tiled=True
        ).astype(jnp.float32),
        lax.psum_scatter(
            d_second_gain.astype(jnp.bfloat16), "ctx", scatter_dimension=0, tiled=True
        ).astype(jnp.float32),
        lax.psum_scatter(
            d_const.astype(jnp.bfloat16), "ctx", scatter_dimension=0, tiled=True
        ).astype(jnp.float32),
        lax.psum_scatter(
            d_gate_up_w.astype(jnp.bfloat16), "ctx", scatter_dimension=0, tiled=True
        ).astype(jnp.float32),
        lax.psum_scatter(
            d_down_w.astype(jnp.bfloat16), "ctx", scatter_dimension=0, tiled=True
        ).astype(jnp.float32),
    )
    shared = (
        lax.psum(summed_grads[0].astype(jnp.bfloat16), "shard").astype(jnp.float32),
        lax.psum(summed_grads[1].astype(jnp.bfloat16), "shard").astype(jnp.float32),
        lax.psum(summed_grads[2].astype(jnp.bfloat16), "shard").astype(jnp.float32),
        lax.psum(summed_grads[3].astype(jnp.bfloat16), "shard").astype(jnp.float32),
        lax.psum(summed_grads[4].astype(jnp.bfloat16), "shard").astype(jnp.float32),
        lax.psum(summed_grads[5].astype(jnp.bfloat16), "shard").astype(jnp.float32),
    )
    out_rows = mixed_out.reshape(tree_count, rows, model_width)
    grad_rows = d_inputs.reshape(tree_count, rows, model_width)
    logit_rows = d_logits.reshape(tree_count, rows, every_expert)
    return (
        out_rows,
        grad_rows,
        logit_rows,
        shared[0],
        shared[1],
        shared[2],
        shared[3],
        shared[4],
        shared[5],
        summed_grads[6],
        summed_grads[7],
    )


NT = (((1,), (1,)), ((), ()))
NN = (((1,), (0,)), ((), ()))
TRUNK = 8
KEY_SEGS = 12
PIECE = 256
SENT = (0, 2, 1, 3)


def mm(a, b, dims=NN):
    return lax.dot_general(a, b, dims, preferred_element_type=jnp.float32)


def stacked(rows, half):
    first = lax.broadcasted_iota(jnp.int32, rows.shape, 1) < half
    blank = jnp.zeros_like(rows)
    return jnp.concatenate([jnp.where(first, rows, blank), jnp.where(first, blank, rows)], axis=0)


def unstack(wide, half, seg):
    return jnp.concatenate([wide[:half, :seg], wide[half:, seg:]], axis=0)


def causal(seg):
    row = lax.broadcasted_iota(jnp.int32, (seg, 2 * seg), 0)
    col = lax.broadcasted_iota(jnp.int32, (seg, 2 * seg), 1)
    return row <= jnp.where(col >= seg, col - seg, col)


def attend_kernel(own, seg, half, more, info, q_ref, k_ref, v_ref, *rest):
    o_ref, lse_ref, s_ref, p_ref = rest[2 * more :]
    trunk = TRUNK * seg
    allowed = causal(seg)
    v_trunk = v_ref[own : own + trunk, :].T

    def one(i, unused):
        count, branch, leaf = info[i, 0], info[i, 1], info[i, 2]
        here = pl.ds(pl.multiple_of(i * seg, seg), seg)
        there = pl.ds(pl.multiple_of(own + branch * seg, seg), seg)
        qs = stacked(q_ref[here, :] * 0.125, half)
        s_ref[:trunk, :] = mm(k_ref[own : own + trunk, :], qs, NT)
        s_branch = mm(k_ref[there, :], qs, NT)
        s_own = jnp.where(allowed, mm(k_ref[here, :], qs, NT), -1e30)
        biases = [jnp.where(kb < count, 0.0, -1e30) for kb in range(TRUNK)]
        leaf_bias = jnp.where(leaf > 0, 0.0, -1e30)
        top = jnp.max(s_own, axis=0, keepdims=True)
        top = jnp.maximum(top, jnp.max(s_branch, axis=0, keepdims=True) + leaf_bias)
        for kb in range(TRUNK):
            part = jnp.max(s_ref[kb * seg : (kb + 1) * seg, :], axis=0, keepdims=True)
            top = jnp.maximum(top, part + biases[kb])
        e_own = jnp.exp(s_own - top)
        e_branch = jnp.exp(s_branch - (top - leaf_bias))
        total = jnp.sum(e_own + e_branch, axis=0, keepdims=True)
        for kb in range(TRUNK):
            e = jnp.exp(s_ref[kb * seg : (kb + 1) * seg, :] - (top - biases[kb]))
            total = total + jnp.sum(e, axis=0, keepdims=True)
            p_ref[kb * seg : (kb + 1) * seg, :] = e.astype(jnp.bfloat16)
        out = mm(v_trunk, p_ref[...])
        out = out + mm(v_ref[there, :].T, e_branch.astype(jnp.bfloat16))
        out = out + mm(v_ref[here, :].T, e_own.astype(jnp.bfloat16))
        out = unstack(out * (1.0 / total), half, seg)
        o_ref[here, :] = out.T.astype(jnp.bfloat16)
        lse_ref[pl.ds(i, 1), :] = top + jnp.log(total)
        return 0

    lax.fori_loop(0, own // seg, one, 0, unroll=True)


def attend_back_kernel(
    own, seg, half, more, info, q_ref, k_ref, v_ref, o_ref, do_ref, lse_ref, *rest
):
    dq_ref, dk_ref, dv_ref, ak, av = rest[3 * more :]
    trunk = TRUNK * seg
    allowed = causal(seg)
    low = jnp.bfloat16
    tk = slice(own, own + trunk)
    k_trunk = k_ref[tk, :].T
    ak[...] = jnp.zeros_like(ak)
    av[...] = jnp.zeros_like(av)

    def one(i, unused):
        count, branch, leaf = info[i, 0], info[i, 1], info[i, 2]
        here = pl.ds(pl.multiple_of(i * seg, seg), seg)
        there = pl.ds(pl.multiple_of(own + branch * seg, seg), seg)
        qs = stacked(q_ref[here, :] * 0.125, half)
        do = do_ref[here, :]
        dos = stacked(do, half)
        prod = (do.astype(jnp.float32) * o_ref[here, :].astype(jnp.float32)).T
        delta = jnp.concatenate(
            [jnp.sum(prod[:half], axis=0, keepdims=True), jnp.sum(prod[half:], axis=0, keepdims=True)],
            axis=1,
        )
        lse = lse_ref[pl.ds(i, 1), :]
        leaf_bias = jnp.where(leaf > 0, 0.0, -1e30)

        def piece(keys, values, shift, mask):
            s = mm(keys, qs, NT)
            if mask:
                s = jnp.where(allowed, s, -1e30)
            if isinstance(shift, list):
                p = jnp.concatenate(
                    [jnp.exp(s[kb * seg : (kb + 1) * seg] - shift[kb]) for kb in range(TRUNK)], axis=0
                )
            else:
                p = jnp.exp(s - shift)
            ds = (p * (mm(values, dos, NT) - delta)).astype(low)
            p = p.astype(low)
            return (mm(p, dos), mm(ds, qs), ds)

        shifts = [lse - jnp.where(kb < count, 0.0, -1e30) for kb in range(TRUNK)]
        dv, dk, ds = piece(k_ref[tk, :], v_ref[tk, :], shifts, False)
        av[tk, :] += dv
        ak[tk, :] += dk
        dq = mm(k_trunk, ds)
        keys = k_ref[there, :]
        dv, dk, ds = piece(keys, v_ref[there, :], lse - leaf_bias, False)
        av[there, :] += dv
        ak[there, :] += dk
        dq = dq + mm(keys.T, ds)
        keys = k_ref[here, :]
        dv, dk, ds = piece(keys, v_ref[here, :], lse, True)
        av[here, :] += dv
        ak[here, :] += dk
        dq = dq + mm(keys.T, ds)
        dq_ref[here, :] = (unstack(dq, half, seg) * 0.125).T.astype(low)
        return 0

    lax.fori_loop(0, own // seg, one, 0, unroll=True)
    dk_ref[...] = ak[...].astype(low)
    dv_ref[...] = av[...].astype(low)


def attend(info, q, kv, seg, begin, count, prev=()):
    own, width = q.shape
    total = kv.shape[0]
    pairs = width // 128
    lane = pl.BlockSpec((own, 128), lambda h: (0, begin + h))
    return pl.pallas_call(
        functools.partial(attend_kernel, own, seg, HEAD_DIM, len(prev) > 0),
        grid=(count,),
        in_specs=[
            pl.BlockSpec(memory_space=pltpu.SMEM),
            lane,
            pl.BlockSpec((total, 128), lambda h: (0, begin + h)),
            pl.BlockSpec((total, 128), lambda h: (0, pairs + begin + h)),
        ]
        + [pl.BlockSpec(memory_space=pl.ANY)] * len(prev),
        out_specs=[lane, pl.BlockSpec((None, 8, 2 * seg), lambda h: (begin + h, 0, 0))],
        out_shape=[
            jax.ShapeDtypeStruct((own, width), jnp.bfloat16),
            jax.ShapeDtypeStruct((pairs, 8, 2 * seg), jnp.float32),
        ],
        input_output_aliases={4 + i: i for i in range(len(prev))},
        scratch_shapes=[
            pltpu.VMEM((TRUNK * seg, 2 * seg), jnp.float32),
            pltpu.VMEM((TRUNK * seg, 2 * seg), jnp.bfloat16),
        ],
        compiler_params=pltpu.CompilerParams(vmem_limit_bytes=60 << 20),
        cost_estimate=pl.CostEstimate(
            flops=1000, bytes_accessed= 1000, transcendentals=0
        ),
        name="attend",
    )(info, q, kv, kv, *prev)


def attend_back(info, q, kv, o, do, lse, seg, begin, count, prev=()):
    own, width = q.shape
    total = kv.shape[0]
    pairs = width // 128
    lane = pl.BlockSpec((own, 128), lambda h: (0, begin + h))
    keys = pl.BlockSpec((total, 128), lambda h: (0, begin + h))
    return pl.pallas_call(
        functools.partial(attend_back_kernel, own, seg, HEAD_DIM, len(prev) > 0),
        grid=(count,),
        in_specs=[
            pl.BlockSpec(memory_space=pltpu.SMEM),
            lane,
            keys,
            pl.BlockSpec((total, 128), lambda h: (0, pairs + begin + h)),
            lane,
            lane,
            pl.BlockSpec((None, 8, 2 * seg), lambda h: (begin + h, 0, 0)),
        ]
        + [pl.BlockSpec(memory_space=pl.ANY)] * len(prev),
        out_specs=[lane, keys, keys],
        out_shape=[
            jax.ShapeDtypeStruct((own, width), jnp.bfloat16),
            jax.ShapeDtypeStruct((total, width), jnp.bfloat16),
            jax.ShapeDtypeStruct((total, width), jnp.bfloat16),
        ],
        input_output_aliases={7 + i: i for i in range(len(prev))},
        scratch_shapes=[
            pltpu.VMEM((total, 128), jnp.float32),
            pltpu.VMEM((total, 128), jnp.float32),
        ],
        compiler_params=pltpu.CompilerParams(vmem_limit_bytes=40 << 20),
        cost_estimate=pl.CostEstimate(
            flops=1000, bytes_accessed= 1000, transcendentals=0
        ),
        name="attend_back",
    )(info, q, kv, kv, o, do, lse, *prev)


def pin(x, *after):
    return lax.optimization_barrier((x,) + after)[0]


def expert_kernel(
    more, capacity, pieces, place, xm_ref, xo_ref, gm_ref, go_ref, w0, w1, w2, w3, *rest
):
    low, full = jnp.bfloat16, jnp.float32
    o_ref, o2_ref, s_ref, s2_ref, dw_ref, x_ref, g_ref, xt, dt, d_ref, oa, sa, wb, gb = rest[more:]
    part = w0.shape[1]
    rows, wide = xm_ref.shape
    padded = rows // pieces
    tail = padded - 16
    here = pl.ds(pl.multiple_of(place[1] * wide, 128), wide)
    there = pl.ds(pl.multiple_of((1 - place[1]) * wide, 128), wide)

    @pl.when(pl.program_id(0) == 0)
    def start():
        x_ref[:, here] = xm_ref[...]
        x_ref[:, there] = xo_ref[...]
        g_ref[:, here] = gm_ref[...]
        g_ref[:, there] = go_ref[...]
        for p in range(pieces):
            mine = slice(p * padded, (p + 1) * padded)
            last = xm_ref[p * padded + tail : (p + 1) * padded, :256].astype(full)
            row = lax.broadcasted_iota(jnp.int32, last.shape, 0) + tail
            inside = (row >= capacity) & (row < capacity + 3)
            gate = jnp.sum(jnp.where(inside, last, 0.0), axis=0, keepdims=True)
            gate = jnp.broadcast_to(gate, (8, 256)).T[:padded, 0:1]
            d_ref[mine, :] = (g_ref[mine, :].astype(full) * gate).astype(low)
        xt[...] = x_ref[...].T
        dt[...] = d_ref[...].T
        oa[...] = jnp.zeros_like(oa)
        sa[...] = jnp.zeros_like(sa)

    def rows_of(r):
        return pl.ds(pl.multiple_of((place[0] ^ r) * part, 64), part)

    for r, w in enumerate((w0, w1, w2, w3)):
        wb[:, rows_of(r), :] = w[...]
    u = mm(x_ref[...], wb[0])
    up = mm(x_ref[...], wb[1])
    sigma = 1.0 / (1.0 + jnp.exp(-u))
    silu = u * sigma
    hidden = (silu * up).astype(low)
    oa[...] += mm(hidden, wb[2], NT)
    dh = mm(d_ref[...], wb[2])
    du = (dh * up * sigma * (1.0 + u * (1.0 - sigma))).astype(low)
    dup = (dh * silu).astype(low)
    sa[...] += mm(du, wb[0], NT) + mm(dup, wb[1], NT)
    gb[0] = mm(xt[...], du).astype(low)
    gb[1] = mm(xt[...], dup).astype(low)
    gb[2] = mm(dt[...], hidden).astype(low)
    for at, r in enumerate(SENT):
        got = gb[:, rows_of(r), :]
        if more:
            got = (got.astype(full) + rest[0][at].astype(full)).astype(low)
        dw_ref[at] = got

    @pl.when(pl.program_id(0) == pl.num_programs(0) - 1)
    def finish():
        o_ref[...] = oa[:, here].astype(low)
        o2_ref[...] = oa[:, there].astype(low)
        s_ref[...] = sa[:, here].astype(low)
        s2_ref[...] = sa[:, there].astype(low)
        for p in range(pieces):
            mine = slice(p * padded, (p + 1) * padded)
            dot = jnp.sum(g_ref[mine, :].astype(full) * oa[mine, :], axis=1, keepdims=True)
            dot = jnp.broadcast_to(dot, (padded, 128)).T[:16, :]
            dot = jnp.concatenate([dot, jnp.zeros((16, wide - padded), full)], axis=1)
            row = lax.broadcasted_iota(jnp.int32, dot.shape, 0) + tail
            kept = jnp.zeros_like(dot)
            for i in range(3):
                piece = dot.astype(low).astype(full)
                kept = jnp.where(row == capacity + i, piece, kept)
                dot = dot - piece
            last = slice(p * padded + tail, (p + 1) * padded)
            row_low = s_ref[last, :].astype(full)
            s_ref[last, :] = jnp.where(row >= capacity, kept, row_low).astype(low)


def expert_pass(place, capacity, pieces, xs, gs, weights, prev):
    rows, half_width = xs[0].shape
    width = 2 * half_width
    three, part, units = weights[0].shape
    low = jnp.bfloat16
    strip = pl.BlockSpec((three, part, PIECE), lambda j, *at: (0, 0, j))
    strips = pl.BlockSpec((4, three, part, PIECE), lambda j, *at: (0, 0, 0, j))
    half = whole(rows, half_width)
    more = prev is not None
    return call(
        functools.partial(expert_kernel, int(more), capacity, pieces),
        "expert_pass",
        [((rows, half_width), low)] * 4 + [((4, three, part, units), low)],
        (place, *xs, *gs, *weights, *([prev] if more else [])),
        [
            pltpu.VMEM((rows, width), low),
            pltpu.VMEM((rows, width), low),
            pltpu.VMEM((width, rows), low),
            pltpu.VMEM((width, rows), low),
            pltpu.VMEM((rows, width), low),
            pltpu.VMEM((rows, width), jnp.float32),
            pltpu.VMEM((rows, width), jnp.float32),
            pltpu.VMEM((three, width, PIECE), low),
            pltpu.VMEM((three, width, PIECE), low),
        ],
        grid=(units // PIECE,),
        in_specs=[half] * 4 + [strip] * 4 + [strips] * more,
        out_specs=[half] * 4 + [strips],
        prefetch=True,
        mib=48,
    )


def spread_kernel(pieces, padded, capacity, gated, place_ref, rows_ref, *rest):
    low = jnp.bfloat16
    outs = rest[1:] if gated else rest
    tokens = rows_ref.shape[0]
    for p in range(pieces):
        slot = lax.broadcasted_iota(jnp.int32, (padded, tokens), 0) + p * padded
        hits = [slot == place_ref[c : c + 1, :] for c in range(2)]
        out = mm(jnp.where(hits[0] | hits[1], 1.0, 0.0).astype(low), rows_ref[...]).astype(low)
        if gated:
            parts = 0.0
            for c in range(2):
                value = rest[0][c : c + 1, :]
                rows3 = []
                for i in range(3):
                    rows3.append(value.astype(low).astype(jnp.float32))
                    value = value - rows3[-1]
                rows3.append(jnp.zeros((13, tokens), jnp.float32))
                three = jnp.concatenate(rows3, axis=0).astype(low)
                parts = parts + mm(three, jnp.where(hits[c], 1.0, 0.0).astype(low), NT)
            parts = parts.astype(low)
            blank = jnp.zeros((parts.shape[0], out.shape[1] - padded), low)
            parts = jnp.concatenate([parts, blank], axis=1)
            row = lax.broadcasted_iota(jnp.int32, out.shape, 0)
            for i in range(3):
                out = jnp.where(row == capacity + i, parts[i : i + 1, :], out)
        outs[p][...] = out


def spread(place, rows, pieces, padded, capacity, parts=None):
    shape = jax.ShapeDtypeStruct((padded, rows.shape[1]), jnp.bfloat16)
    gated = parts is not None
    return pl.pallas_call(
        functools.partial(spread_kernel, pieces, padded, capacity, gated),
        in_specs=[pl.BlockSpec(memory_space=pltpu.VMEM)] * (2 + gated),
        out_specs=[pl.BlockSpec(memory_space=pltpu.VMEM)] * pieces,
        out_shape=[shape] * pieces,
        compiler_params=pltpu.CompilerParams(vmem_limit_bytes=60 << 20),
        cost_estimate=pl.CostEstimate(flops=1000, bytes_accessed= 1000, transcendentals=0),
        name="spread",
    )(place, rows, *([parts] if gated else []))


def expert_of(where_ref, piece):
    upper = jnp.where(where_ref[1] >= 2, 1, 0)
    return (2 * ((piece % 4) ^ where_ref[0]) + ((piece // 4) ^ upper)).astype(jnp.float32)


def spread_gated_kernel(pieces, padded, capacity, gated, where_ref, place_ref, rows_ref, *rest):
    low, full = jnp.bfloat16, jnp.float32
    tokens, width = rows_ref.shape
    if gated:
        gates_ref, outs, wide_ref = rest[0], rest[1:-1], rest[-1]
        lines = []
        for c in range(2):
            value = gates_ref[c : c + 1, :]
            for i in range(3):
                lines.append(value.astype(low).astype(full))
                value = value - lines[-1]
        lines = lines + [gates_ref[4:5, :], jnp.zeros((121, tokens), full)]
        wide_ref[:, :width] = rows_ref[...]
        wide_ref[:, width:] = jnp.concatenate(lines, axis=0).T.astype(low)
    else:
        outs, wide_ref = rest, rows_ref
    for p in range(pieces):
        slot = lax.broadcasted_iota(jnp.int32, (padded, tokens), 0) + p * padded
        hit = (slot == place_ref[0:1, :]) | (slot == place_ref[1:2, :])
        out = mm(jnp.where(hit, 1.0, 0.0).astype(low), wide_ref[...])
        if gated:
            extra = out[:, width:].T
            out = out[:, :width].astype(low)
            row = lax.broadcasted_iota(jnp.int32, out.shape, 0)
            blank = jnp.zeros((1, width - padded), full)
            for i in range(3):
                picked = jnp.where(
                    extra[6:7, :] == expert_of(where_ref, p), extra[i : i + 1, :], extra[3 + i : 4 + i, :]
                )
                picked = jnp.concatenate([picked, blank], axis=1).astype(low)
                out = jnp.where(row == capacity + i, picked, out)
        outs[p][...] = out.astype(low)


def spread_gated(where, place, rows, pieces, padded, capacity, gates=None):
    shape = jax.ShapeDtypeStruct((padded, rows.shape[1]), jnp.bfloat16)
    gated = gates is not None
    return pl.pallas_call(
        functools.partial(spread_gated_kernel, pieces, padded, capacity, gated),
        in_specs=[pl.BlockSpec(memory_space=pltpu.SMEM)]
        + [pl.BlockSpec(memory_space=pltpu.VMEM)] * (2 + gated),
        out_specs=[pl.BlockSpec(memory_space=pltpu.VMEM)] * pieces,
        out_shape=[shape] * pieces,
        scratch_shapes=[pltpu.VMEM((rows.shape[0], rows.shape[1] + 128), jnp.bfloat16)] * gated,
        compiler_params=pltpu.CompilerParams(vmem_limit_bytes=40 << 20),
        cost_estimate=pl.CostEstimate(flops=1000, bytes_accessed=1000, transcendentals=0),
        name="spread",
    )(where, place, rows, *([gates] if gated else []))


def gather_kernel(pieces, padded, capacity, dots, where_ref, place_ref, pair_ref, *rest):
    low, full = jnp.bfloat16, jnp.float32
    if dots:
        ins, (out_ref, out2_ref, dot_ref, dot2_ref) = rest[:pieces], rest[pieces:]
    else:
        ins, (out_ref, out2_ref) = rest[: pieces // 2], rest[pieces // 2 :]
    tokens = place_ref.shape[0]
    total = None
    sums = [0.0, 0.0]
    for p in range(pieces):
        slot = lax.broadcasted_iota(jnp.int32, (tokens, padded), 1) + p * padded
        hits = [slot == place_ref[:, c : c + 1] for c in range(2)]
        if dots:
            source = ins[p][...]
            width = source.shape[1]
            values = ins[p][padded - 16 :, :padded].astype(full)
            values = jnp.concatenate([values, jnp.zeros((112, padded), full)], axis=0).T
            source = jnp.concatenate([source, values.astype(low)], axis=1)
            part = mm(jnp.where(hits[0] | hits[1], 1.0, 0.0).astype(low), source)
            lane = lax.broadcasted_iota(jnp.int32, (tokens, 128), 1)
            lane = lane + (padded - 16 - capacity)
            dot = jnp.where((lane >= 0) & (lane < 3), part[:, width:], 0.0)
            mine = pair_ref[:, 0:1] == expert_of(where_ref, p)
            sums[0] = sums[0] + jnp.where(mine, dot, 0.0)
            sums[1] = sums[1] + jnp.where(mine, 0.0, dot)
            part = part[:, :width]
        else:
            pick = jnp.where(hits[0], pair_ref[:, 0:1], jnp.where(hits[1], pair_ref[:, 1:2], 0.0))
            part = mm(pick.astype(low), ins[p % 4][p // 4])
        total = part if total is None else total + part
    rows = tokens // 2
    out_ref[...] = total[:rows].astype(low)
    out2_ref[...] = total[rows:].astype(low)
    if dots:
        for c in range(2):
            dot_ref[:, c : c + 1] = jnp.sum(sums[c][:rows], axis=1, keepdims=True)
            dot2_ref[:, c : c + 1] = jnp.sum(sums[c][rows:], axis=1, keepdims=True)


def gather(where, place, pair, pieces, capacity, dots):
    padded, width = pieces[0].shape[-2:]
    number = sum(p.size // (padded * width) for p in pieces)
    tokens = place.shape[0]
    shapes = [jax.ShapeDtypeStruct((tokens // 2, width), jnp.bfloat16)] * 2
    if dots:
        shapes = shapes + [jax.ShapeDtypeStruct((tokens // 2, 2), jnp.float32)] * 2
    return pl.pallas_call(
        functools.partial(gather_kernel, number, padded, capacity, dots),
        in_specs=[pl.BlockSpec(memory_space=pltpu.SMEM)]
        + [pl.BlockSpec(memory_space=pltpu.VMEM)] * (len(pieces) + 2),
        out_specs=[pl.BlockSpec(memory_space=pltpu.VMEM)] * len(shapes),
        out_shape=shapes,
        compiler_params=pltpu.CompilerParams(vmem_limit_bytes=60 << 20),
        cost_estimate=pl.CostEstimate(flops=1000, bytes_accessed= 1000, transcendentals=0),
        name="gather",
    )(where, place, pair, *pieces)


def whole(*shape):
    return pl.BlockSpec(shape, lambda *at: (0,) * len(shape))


def by_rows(*shape):
    return pl.BlockSpec(shape, lambda j, *at: (j, 0))


def chosen(number, *shape):
    return pl.BlockSpec((None,) + shape, lambda j, place: (number ^ place[0], 0, 0))


def call(kernel, name, outs, args, scratch=(), grid=(1,), in_specs=None, out_specs=None, prefetch=False, mib=40):
    if out_specs is None:
        out_specs = [whole(*o[0]) for o in outs]
    spec = pltpu.PrefetchScalarGridSpec(
        num_scalar_prefetch=int(prefetch),
        grid=grid,
        in_specs=in_specs,
        out_specs=out_specs,
        scratch_shapes=list(scratch),
    )
    return pl.pallas_call(
        kernel,
        grid_spec=spec,
        out_shape=[jax.ShapeDtypeStruct(*o) for o in outs],
        compiler_params=pltpu.CompilerParams(vmem_limit_bytes=mib << 20),
        cost_estimate=pl.CostEstimate(flops=1000, bytes_accessed=1000, transcendentals=0),
        name=name,
    )(*args)


def unit_rows(x):
    x = x.astype(jnp.float32)
    return x * lax.rsqrt(jnp.mean(x * x, axis=-1, keepdims=True) + eps)


def project_kernel(place, x0, near, mid, farther, gain, wm, wo, q_ref, kv_ref, n_ref, x_ref):
    low = jnp.bfloat16
    shard, ctx = place[0], place[1]
    rows, width = x0.shape
    half = wm.shape[2]

    def project(lo, x):
        here = slice(lo, lo + x.shape[0])
        normed = (unit_rows(x) * gain[...]).astype(low)
        x_ref[here, :] = x
        n_ref[here, :] = normed
        for m in (1, 2):
            for h, w in enumerate((wm, wo)):
                at = (m - 1) * width + h * half
                kv_ref[here, at : at + half] = mm(normed, w[m ^ shard]).astype(low)
        if lo == 0:
            for h, w in enumerate((wm, wo)):
                q_ref[:, h * half : (h + 1) * half] = mm(normed, w[shard]).astype(low)

    edge = x_ref.shape[0] - 3 * rows
    project(0, x0[...])
    later = jnp.where(ctx == 2, mid[...], farther[...])
    project(rows, jnp.where(ctx == 0, x0[...], jnp.where(ctx == 1, near[...], later)))
    later = jnp.where(ctx == 2, near[...], mid[...])
    project(2 * rows, jnp.where(ctx == 1, x0[...], later))
    project(3 * rows, jnp.where(ctx == 2, x0[:edge, :], near[:edge, :]))


def settle_kernel(
    place, o, x, wm, wo, gain, router, res, ids,
    mixed_ref, second_ref, mine_ref, other_ref, probs_ref, stat_ref, gates_ref,
):
    tp = place[2]
    half = wm.shape[1]
    attn = mm(o[:, :half], wm[...], NT) + mm(o[:, half:], wo[...], NT)
    mixed = x[...].astype(jnp.float32) + attn
    mixed_ref[...] = mixed
    inverse = lax.rsqrt(jnp.mean(mixed * mixed, axis=-1, keepdims=True) + eps)
    second = (mixed * inverse * gain[...]).astype(jnp.bfloat16)
    second_ref[...] = second
    mine_ref[...] = second_ref[:, pl.ds(pl.multiple_of(tp * half, 128), half)]
    other_ref[...] = second_ref[:, pl.ds(pl.multiple_of((1 - tp) * half, 128), half)]
    logits = mm(second, router[...], NT) + res[...]
    expo = jnp.exp(logits - jnp.max(logits, axis=-1, keepdims=True))
    probs = expo / jnp.sum(expo, axis=-1, keepdims=True)
    probs_ref[...] = probs
    lane = lax.broadcasted_iota(jnp.int32, probs.shape, 1)
    picked = [
        jnp.sum(jnp.where(lane == ids[:, c : c + 1], probs, 0.0), axis=-1, keepdims=True)
        for c in range(2)
    ]
    total = picked[0] + picked[1]
    wide = lax.broadcasted_iota(jnp.int32, (probs.shape[0], 128), 1)
    stat = jnp.where(wide == 0, picked[0] / total, jnp.where(wide == 1, picked[1] / total, 0.0))
    stat = jnp.where(wide == 2, total, jnp.where(wide == 3, inverse, stat))
    stat = jnp.where(wide == 4, ids[:, 0:1].astype(jnp.float32), stat)
    stat_ref[...] = stat[:, :8]
    gates_ref[...] = stat.T[:8, :]


def settle_back_kernel(
    copy_id, place, dr_mine, dr_came, dg_mine, dg_came, g_ref, mixed, second, probs_ref, stat, ids,
    const, router, gain, wm, wo, dmix_ref, dattn_ref, do_ref, dlog_ref, small_ref, full_ref,
):
    low, full = jnp.bfloat16, jnp.float32
    tp = place[2]
    half = wm.shape[1]
    full_ref[:, pl.ds(pl.multiple_of(tp * half, 128), half)] = dr_mine[...]
    full_ref[:, pl.ds(pl.multiple_of((1 - tp) * half, 128), half)] = dr_came[...]
    g = g_ref[...].astype(full)
    probs = probs_ref[...]
    gates = [stat[:, 0:1], stat[:, 1:2]]
    total, inverse = stat[:, 2:3], stat[:, 3:4]
    ids_c = [ids[:, 0:1], ids[:, 1:2]]
    zero = jnp.zeros_like(total)

    def gate_of(number):
        return sum(jnp.where(ids_c[c] == number, gates[c], zero) for c in range(2))

    copy_gate = gate_of(copy_id)
    const_gate = [gate_of(copy_id + 1 + k) for k in range(2)]
    dots = [jnp.sum(g * second[...].astype(full), axis=-1, keepdims=True)]
    dots = dots + [jnp.sum(g * const[k : k + 1, :], axis=-1, keepdims=True) for k in range(2)]
    d_gates = []
    for c in range(2):
        d = dg_mine[:, c : c + 1] + dg_came[:, c : c + 1]
        for k in range(3):
            d = d + jnp.where(ids_c[c] == copy_id + k, dots[k], zero)
        d_gates.append(d)
    mean = d_gates[0] * gates[0] + d_gates[1] * gates[1]
    lane = lax.broadcasted_iota(jnp.int32, probs.shape, 1)
    d_probs = jnp.zeros_like(probs)
    for c in range(2):
        d_probs = d_probs + jnp.where(lane == ids_c[c], (d_gates[c] - mean) / total, 0.0)
    d_logits = probs * (d_probs - jnp.sum(probs * d_probs, axis=-1, keepdims=True))
    dlog_ref[...] = d_logits
    d_second = copy_gate * g + full_ref[...].astype(full)
    rest = d_logits
    for i in range(3):
        piece = rest.astype(low)
        rest = rest - piece.astype(full)
        d_second = d_second + mm(piece, router[...])
    unit = mixed[...] * inverse
    d_gain = jnp.sum(d_second * unit, axis=0, keepdims=True)
    d_unit = d_second * gain[...]
    d_mixed = g + inverse * (d_unit - unit * jnp.mean(d_unit * unit, axis=-1, keepdims=True))
    dmix_ref[...] = d_mixed
    d_attn = d_mixed.astype(low)
    dattn_ref[...] = d_attn
    do_ref[:, :half] = mm(d_attn, wm[...]).astype(low)
    do_ref[:, half:] = mm(d_attn, wo[...]).astype(low)
    count = probs.shape[1]
    pad = jnp.zeros((probs.shape[0], 128 - count), full)
    wide = lax.broadcasted_iota(jnp.int32, (probs.shape[0], 128), 1)
    table = jnp.concatenate([d_logits, pad], axis=1)
    table = jnp.where(wide == count + 2, const_gate[0], table)
    table = jnp.where(wide == count + 3, const_gate[1], table)
    rest = table.T[: count + 4, :]
    from_second = from_g = 0.0
    for i in range(3):
        piece = rest.astype(low)
        rest = rest - piece.astype(full)
        from_second = from_second + mm(piece, second[...])
        from_g = from_g + mm(piece, g_ref[...])
    row = lax.broadcasted_iota(jnp.int32, from_g.shape, 0)
    small = jnp.where(row < count, from_second, jnp.where(row >= count + 2, from_g, 0.0))
    small_ref[...] = jnp.where(row == count + 1, d_gain, small)


def keys_back_kernel(place, dq, dk, dv, x, wm, wo, own_ref, p0_ref, p1_ref, p2_ref, gain_ref):
    shard = place[0]
    rows, width = own_ref.shape
    half = wm.shape[2]
    gain = jnp.zeros((1, width), jnp.float32)
    lo = 0
    for out in (own_ref, p0_ref, p1_ref, p2_ref):
        here = slice(lo, lo + out.shape[0])
        lo = lo + out.shape[0]
        d = 0.0
        for m, grad in ((0, dq), (1, dk), (2, dv)):
            if m > 0 or out is own_ref:
                d = d + mm(grad[here, :half], wm[m ^ shard], NT)
                d = d + mm(grad[here, half:], wo[m ^ shard], NT)
        out[...] = d.astype(out.dtype)
        gain = gain + jnp.sum(d * unit_rows(x[here, :]), axis=0, keepdims=True)
    gain_ref[...] = gain


def weights_back_kernel(n_ref, dq, dk, dv, da_ref, o, tiny, mine_ref, other_ref, nt, at):
    rows = dq.shape[0]
    step = pl.program_id(0)

    @pl.when(step == 0)
    def start():
        nt[...] = n_ref[...].T
        at[...] = da_ref[...].T

    def put(value):
        value = value.astype(jnp.bfloat16)
        parts, half = mine_ref.shape[0], mine_ref.shape[2]
        part = value.shape[0] // parts
        for z in range(parts):
            mine_ref[z, :part, :] = value[z * part : (z + 1) * part, :half]
            other_ref[z, :part, :] = value[z * part : (z + 1) * part, half:]
            mine_ref[z, part:, :] = tiny[z, :, :half]
            other_ref[z, part:, :] = tiny[z, :, half:]

    pl.when(step == 0)(lambda: put(mm(nt[:, :rows], dq[...])))
    pl.when(step == 1)(lambda: put(mm(nt[...], dk[...])))
    pl.when(step == 2)(lambda: put(mm(nt[...], dv[...])))
    pl.when(step == 3)(lambda: put(mm(at[...], o[...])))


def weights_back(normed, dq, dk, dv, d_attn, o, tiny):
    total, width = normed.shape
    rows, half = dq.shape[0], width // 2
    parts, room = tiny.shape[1], tiny.shape[2]
    low = jnp.bfloat16
    out = pl.BlockSpec((None, parts, width // parts + room, half), lambda j: (j, 0, 0, 0))
    shape = ((4, parts, width // parts + room, half), low)
    return call(
        weights_back_kernel,
        "weights_back",
        [shape, shape],
        (normed, dq, dk, dv, d_attn, o, tiny),
        [pltpu.VMEM((width, total), low), pltpu.VMEM((width, rows), low)],
        grid=(4,),
        in_specs=[whole(total, width), whole(rows, width), whole(total, width), whole(total, width)]
        + [whole(rows, width), whole(rows, width)]
        + [pl.BlockSpec((None, parts, room, width), lambda j: (j, 0, 0, 0))],
        out_specs=[out, out],
    )


def flip(x, axis, bit, size):
    return lax.ppermute(x, axis, [(i, i ^ bit) for i in range(size)])


def turn_gather(x, size, position):
    out = jnp.zeros((size,) + x.shape, x.dtype)
    out = lax.dynamic_update_index_in_dim(out, x, position, 0)
    for k in range(1, size):
        block = lax.ppermute(x, "ctx", [(i, (i + k) % size) for i in range(size)])
        out = lax.dynamic_update_index_in_dim(out, block, (position - k) % size, 0)
    return out


def turn_sum(x, size, position):
    total = lax.dynamic_index_in_dim(x, position, 0, keepdims=False).astype(jnp.float32)
    for k in range(1, size):
        block = lax.dynamic_index_in_dim(x, (position + k) % size, 0, keepdims=False)
        got = lax.ppermute(block, "ctx", [(i, (i + k) % size) for i in range(size)])
        total = total + got.astype(jnp.float32)
    return total


def far(x, k, shards_n, ctx_n):
    pairs = []
    for s in range(shards_n):
        for z in range(ctx_n):
            pairs.append((s * ctx_n + z, (s ^ k) * ctx_n + (z ^ 2)))
    return lax.ppermute(x, ("shard", "ctx"), pairs)


def three_parts(x):
    one = x.astype(jnp.bfloat16)
    rest = x - one.astype(jnp.float32)
    two = rest.astype(jnp.bfloat16)
    return jnp.stack([one, two, (rest - two.astype(jnp.float32)).astype(jnp.bfloat16)], axis=-2)


def with_rows(slots, values, at):
    extra = three_parts(values)
    after = slots.shape[-2] - at - extra.shape[-2]
    pads = ((0, 0), (at, after), (0, slots.shape[-1] - extra.shape[-1]))
    return slots + jnp.pad(extra, pads)


def row_values(slots, at):
    return jnp.sum(slots[:, at : at + 3, : slots.shape[1]].astype(jnp.float32), axis=1)


def by_core(
    tokens, gate_res, cotangent, parents, expert_ids, priority, w_qkv, w_out, w_router, attn_gain,
    ffn_gain, const_vec, w_gate_up, w_down,
):
    low, full = jnp.bfloat16, jnp.float32
    shard, ctx, tp = lax.axis_index("shard"), lax.axis_index("ctx"), lax.axis_index("tp")
    shards_n, ctx_n = lax.axis_size("shard"), lax.axis_size("ctx")
    trees, rows, width = tokens.shape
    rows_d = w_qkv.shape[0]
    part = width // 2
    seg = rows * ctx_n // parents.shape[1]
    own_segs = rows // seg
    edge = KEY_SEGS * seg - 2 * rows

    def own_tree(x):
        return lax.dynamic_index_in_dim(x, tp, 0, keepdims=False)

    def in_order(x, other, axis=0):
        return jnp.concatenate([jnp.where(tp == 0, x, other), jnp.where(tp == 0, other, x)], axis=axis)

    def both_trees(x, other):
        return in_order(x[None], other[None])

    def unit_of(x):
        x = x.astype(full)
        inverse = lax.rsqrt(jnp.mean(x * x, axis=-1, keepdims=True) + eps)
        return (x * inverse, inverse)

    def swap(x):
        return flip(x, "tp", 1, 2)

    def plus(x, y):
        return (x.astype(full) + y.astype(full)).astype(low)

    def my_half(x, which):
        return lax.dynamic_slice_in_dim(x, which * part, part, x.ndim - 1)

    x_own = lax.optimization_barrier(own_tree(tokens))
    ends = [(i, i + 1) for i in range(ctx_n - 1)]
    near = lax.ppermute(x_own, "ctx", ends)

    mine = jnp.stack([w_qkv[:, 0], w_qkv[:, 1], w_qkv[:, 2], w_out])
    small = jnp.concatenate([w_router.T, attn_gain[None], ffn_gain[None], const_vec.T], axis=0)
    all_experts = w_router.shape[1]
    mine = lax.dynamic_index_in_dim(mine, shard, 0, keepdims=False)
    mine = jnp.concatenate([mine, small.reshape(-1, part)], axis=0)
    turned = turn_gather(mine, ctx_n, ctx)
    matrix = turned[:, :rows_d].reshape(width, -1)
    small = turned[:, rows_d:].reshape(ctx_n, -1, rows_d).transpose(1, 0, 2).reshape(-1, width)
    router_t = small[:all_experts]
    gain_a = small[all_experts].astype(full)
    gain_f = small[all_experts + 1].astype(full)
    const_t = small[all_experts + 2 :].astype(full)

    mid = lax.ppermute(pin(near, matrix), "ctx", ends[1:])
    plane_pieces = [matrix] + [flip(matrix, "shard", k, shards_n) for k in range(1, shards_n)]
    capacity = trees * rows * 2 // all_experts
    experts = shards_n * w_gate_up.shape[1]
    padded = -(-(capacity + 3) // 16) * 16
    count = experts * padded
    flat = expert_ids.reshape(-1)
    order = (2 * priority[0, 0][:, None] + jnp.arange(2, dtype=jnp.int32)[None, :]).reshape(-1)
    earlier = (flat[:, None] == flat[None, :]) & (order[None, :] < order[:, None])
    ranks = jnp.sum(earlier.astype(jnp.int32), axis=1)
    kept = (flat < experts) & (ranks < capacity)
    piece = ((flat % 2) ^ (ctx // 2)) * shards_n + ((flat // 2) ^ shard)
    place = jnp.where(kept, piece * padded + ranks, -1).reshape(trees, rows, 2)
    place = jnp.where(tp == 0, place, place[::-1]).reshape(trees * rows, 2)
    place_t = place.T

    g_own = own_tree(cotangent)
    g_other = lax.dynamic_index_in_dim(cotangent, 1 - tp, 0, keepdims=False)
    g_half = my_half(jnp.concatenate([g_own, g_other], axis=0), tp)
    g_slots = spread(place_t, g_half, experts, padded, capacity)
    ids = own_tree(expert_ids)
    res = own_tree(gate_res)
    ids, res, router_t, gain_a, gain_f, const_t, mid, *g_slots = lax.optimization_barrier(
        (ids, res, router_t, gain_a[None], gain_f[None], const_t, mid, *g_slots)
    )
    farther = lax.ppermute(mid, "ctx", ends[2:])
    plane = jnp.stack(plane_pieces)

    plane_other = swap(plane)
    place3 = jnp.stack([shard, ctx, tp]).astype(jnp.int32)

    capacity = trees * rows * 2 // all_experts
    experts = shards_n * w_gate_up.shape[1]
    padded = -(-(capacity + 3) // 16) * 16
    count = experts * padded
    flat = expert_ids.reshape(-1)
    order = (2 * priority[0, 0][:, None] + jnp.arange(2, dtype=jnp.int32)[None, :]).reshape(-1)
    earlier = (flat[:, None] == flat[None, :]) & (order[None, :] < order[:, None])
    ranks = jnp.sum(earlier.astype(jnp.int32), axis=1)
    kept = (flat < experts) & (ranks < capacity)
    piece = ((flat % 2) ^ (ctx // 2)) * shards_n + ((flat // 2) ^ shard)
    place = jnp.where(kept, piece * padded + ranks, -1).reshape(trees, rows, 2)
    place = jnp.where(tp == 0, place, place[::-1]).reshape(trees * rows, 2)
    place_t = place.T

    g_own = own_tree(cotangent)
    g_other = lax.dynamic_index_in_dim(cotangent, 1 - tp, 0, keepdims=False)
    g_half = my_half(jnp.concatenate([g_own, g_other], axis=0), tp)
    g_slots = spread(place_t, g_half, experts, padded, capacity)
    g_near = jnp.stack(g_slots[:shards_n])
    g_far = flip(pin(jnp.stack(g_slots[shards_n:]), mid), "ctx", 2, ctx_n)
    plane_other = swap(plane)
    place3 = jnp.stack([shard, ctx, tp]).astype(jnp.int32)

    g_near = jnp.stack(g_slots[:shards_n])
    g_far = flip(jnp.stack(g_slots[shards_n:]), "ctx", 2, ctx_n)

    held, gu, dn = lax.optimization_barrier((near, w_gate_up, w_down))
    lower = ctx < 2
    first = jnp.stack([gu[:, 0, 0], gu[:, 0, 1], dn[:, 0]])
    second_e = jnp.stack([gu[:, 1, 0], gu[:, 1, 1], dn[:, 1]])
    rows_own = jnp.where(lower, first, second_e)
    rows_two = flip(pin(jnp.where(lower, second_e, first), farther, g_far), "ctx", 2, ctx_n)
    rows_one = flip(pin(rows_own, farther, g_far), "ctx", 1, ctx_n)

    total = 3 * rows + edge
    q, kv, normed, x_all = call(
        project_kernel,
        "project",
        [((rows, width), low), ((total, 2 * width), low), ((total, width), low), ((total, width), low)],
        (place3, x_own, near, mid, farther, gain_a, plane, plane_other),
        in_specs=[whole(rows, width)] * 4
        + [whole(1, width), whole(4, width, part), whole(4, width, part)],
        prefetch=True,
    )

    seg_id = ctx * own_segs + jnp.arange(own_segs, dtype=jnp.int32)
    parent = jnp.take(own_tree(parents), seg_id)
    leaf = (seg_id >= KEY_SEGS).astype(jnp.int32)
    info = jnp.stack([jnp.minimum(seg_id, TRUNK), jnp.where(leaf > 0, parent, TRUNK), leaf], axis=1)
    half_pairs = width // 256
    ahead = attend(info, q, kv, seg, 0, half_pairs)
    o_low, lse = attend(info, q, kv, seg, half_pairs, half_pairs, ahead)
    g_pairs = jnp.stack([g_near, pin(g_far, ahead[0])], axis=1)
    g_got = [g_pairs[0]] + [flip(g_pairs[k], "shard", k, shards_n) for k in range(1, shards_n)]
    o_low = pin(o_low, rows_one, rows_two, *g_got)
    g_in = jnp.stack(g_got, axis=1).reshape(2, shards_n * padded, part)
    g_out = swap(g_in)

    one_half = ((rows, part), low)
    mixed, second, second_mine, second_other, probs, stat, gates_t = call(
        settle_kernel,
        "settle",
        [
            ((rows, width), full), ((rows, width), low), one_half, one_half,
            ((rows, all_experts), full), ((rows, 8), full), ((8, rows), full),
        ],
        (place3, o_low, x_own, plane, plane_other, gain_f, router_t, res, ids),
        in_specs=[
            whole(rows, width), whole(rows, width), chosen(3, width, part), chosen(3, width, part),
            whole(1, width), whole(all_experts, width), whole(rows, all_experts), whole(rows, 2),
        ],
        prefetch=True,
    )
    second_half = jnp.concatenate([second_mine, swap(second_other)], axis=0)
    gates_both = jnp.concatenate([gates_t, swap(gates_t)], axis=1)

    rows_three = flip(pin(rows_two, o_low), "ctx", 1, ctx_n)
    weights = (rows_own, rows_one, rows_two, rows_three)
    slots = spread_gated(place3, place_t, second_half, experts, padded, capacity, gates_both)
    x_far = [far(slots[shards_n + k], k, shards_n, ctx_n) for k in range(shards_n)]
    x_near = [slots[0]] + [flip(slots[k], "shard", k, shards_n) for k in range(1, shards_n)]

    def experts_on(pieces, gs, prev):
        x = jnp.concatenate(pieces, axis=0)
        return expert_pass(place3[1:], capacity, shards_n, (x, swap(x)), gs, weights, prev)

    def answers(mine, other):
        return plus(mine, swap(other)).reshape(shards_n, padded, part)

    x_near[0] = pin(x_near[0], rows_three)
    on1, ox1, sn1, sx1, dw = experts_on(x_near, (g_in[0], g_out[0]), None)
    x_far = list(lax.optimization_barrier((*x_far, sn1))[:-1])
    on2, ox2, sn2, sx2, dw = experts_on(x_far, (g_in[1], g_out[1]), dw)
    ds_far = answers(sn2, sx2)
    ds_near = answers(sn1, sx1)
    ds_far = [far(ds_far[k], k, shards_n, ctx_n) for k in range(shards_n)]
    ds_near = [ds_near[0]] + [flip(ds_near[k], "shard", k, shards_n) for k in range(1, shards_n)]

    rows_tn = (((0,), (0,)), ((), ()))
    d_routed, d_routed_other, d_pairs, d_pairs_other = gather(
        place3, place, gates_both[4][:, None], ds_near + ds_far, capacity, True
    )
    d_mixed, d_attn, d_o, d_logits, d_small = call(
        functools.partial(settle_back_kernel, experts + 1),
        "settle_back",
        [
            ((rows, width), full), ((rows, width), low), ((rows, width), low),
            ((rows, all_experts), full), ((all_experts + 4, width), full),
        ],
        (
            place3, d_routed, swap(d_routed_other), d_pairs, swap(d_pairs_other), g_own, mixed, second,
            probs, stat, ids, const_t, router_t, gain_f, plane, plane_other,
        ),
        [pltpu.VMEM((rows, width), low)],
        in_specs=[
            whole(rows, part), whole(rows, part), whole(rows, 2), whole(rows, 2), whole(rows, width),
            whole(rows, width), whole(rows, width), whole(rows, all_experts), whole(rows, 8),
            whole(rows, 2), whole(2, width), whole(all_experts, width), whole(1, width),
            chosen(3, width, part), chosen(3, width, part),
        ],
        prefetch=True,
    )

    ox1, ox2, held = lax.optimization_barrier((ox1, ox2, d_routed))
    out_near = plus(on1, swap(ox1)).reshape(shards_n, padded, part)
    out_far = plus(on2, swap(ox2)).reshape(shards_n, padded, part)

    got = flip(pin(dw[2:], d_routed), "ctx", 1, ctx_n)

    third = width // 384
    back = attend_back(info, q, kv, o_low, d_o, lse, seg, 0, third)
    out_near, out_far, q_later, held = lax.optimization_barrier((out_near, out_far, q, back[0]))
    back = attend_back(info, q_later, kv, o_low, d_o, lse, seg, third, third, back)
    out_near, out_far = (out_near, out_far)
    out_cross = flip(out_far, "ctx", 2, ctx_n)
    q_later = pin(q, back[0])
    dq, dk, dv = attend_back(info, q_later, kv, o_low, d_o, lse, seg, 2 * third, third, back)
    got = pin(got, dq)
    sent_rows = plus(dw[1], got[1])
    came_rows = flip(sent_rows, "ctx", 2, ctx_n)
    out_pairs = jnp.stack([out_near, pin(out_cross, dq)], axis=1)
    out_got = [out_pairs[0]] + [flip(out_pairs[k], "shard", k, shards_n) for k in range(1, shards_n)]
    d_near, part0, part1, part2, d_gain_a = call(
        keys_back_kernel,
        "keys_back",
        [
            ((rows, width), full), ((rows, width), low), ((rows, width), low), ((edge, width), low),
            ((1, width), full),
        ],
        (pin(place3, sent_rows), dq, dk, dv, x_all, plane, plane_other),
        in_specs=[
            whole(rows, width), whole(total, width), whole(total, width), whole(total, width),
            whole(4, width, part), whole(4, width, part),
        ],
        prefetch=True,
    )

    tiny = jnp.concatenate([d_small[:all_experts], d_gain_a, d_small[all_experts + 1 :]], axis=0)
    tiny = tiny.reshape(4, 2, 2, ctx_n, rows_d).transpose(0, 3, 1, 2, 4).reshape(4, ctx_n, 2, 2 * rows_d)
    tiny = jnp.where(tp == 0, tiny, tiny[:, :, ::-1]).reshape(4, ctx_n, 1, width).astype(low)
    tiny = jnp.pad(tiny, ((0, 0), (0, 0), (0, 15), (0, 0)))
    shared_mine, shared_other = weights_back(normed, dq, dk, dv, d_attn, o_low, tiny)

    def down(x, step):
        return lax.ppermute(x, "ctx", [(i, i - 1) for i in range(ctx_n - step, ctx_n)])

    came = down(part0, 1)
    shared_other = pin(shared_other, came, *out_got, came_rows)
    payload = jnp.where(ctx == 3, part1, plus(part0, came))
    came = down(payload, 2)
    shared = plus(pin(shared_mine, payload), swap(shared_other))

    def numbered(k):
        return lax.dynamic_index_in_dim(shared, shard ^ k, 0, keepdims=False)

    plane_parts = [flip(numbered(k), "shard", k, shards_n) for k in range(1, shards_n)]
    plane_sum = numbered(0).astype(full)
    for got_part in plane_parts:
        plane_sum = plane_sum + got_part.astype(full)
    came = pin(came, plane_parts[0])
    part2 = jnp.pad(part2, ((0, rows - edge), (0, 0)))
    came = down(jnp.where(ctx == 3, part2, jnp.where(ctx == 2, plus(part1, came), plus(part0, came))), 3)
    base = jnp.where(ctx == 0, part0, jnp.where(ctx == 1, part1, part2)).astype(full)
    extra = jnp.where(ctx == 3, 0.0, base + came.astype(full))
    came_rows = pin(came_rows, plane_parts[0]).astype(full)
    kept_rows = dw[0].astype(full) + got[0].astype(full)
    first = jnp.where(lower, kept_rows, came_rows)
    second_e = jnp.where(lower, came_rows, kept_rows)
    d_gate_up = jnp.stack(
        [jnp.stack([first[0], first[1]], axis=1), jnp.stack([second_e[0], second_e[1]], axis=1)], axis=1
    )
    d_down = jnp.stack([first[2], second_e[2]], axis=1)
    d_normed = d_near + extra
    unit_own, inv_own = unit_of(x_own)
    gain_a = gain_a[0]
    d_first = d_normed * gain_a
    d_tokens = d_mixed + inv_own * (
        d_first - unit_own * jnp.mean(d_first * unit_own, axis=-1, keepdims=True)
    )

    total = turn_sum(plane_sum.astype(low), ctx_n, ctx).astype(low)
    out_got = [pin(o, plane_parts[0]) for o in out_got]
    gate_columns = jnp.stack([gates_both[0], gates_both[1]], axis=1)
    combined, combined_other = gather(place3, place, gate_columns, out_got, capacity, False)
    combined = in_order(combined, swap(combined_other), 1).astype(full)
    second_f = second.astype(full)

    def gate_of(number):
        return jnp.sum(jnp.where(ids == number, stat[:, :2], 0.0), axis=1, keepdims=True)

    copy_gate = gate_of(experts + 1)
    const_gate = jnp.concatenate([gate_of(experts + 2), gate_of(experts + 3)], axis=1)
    mixed_out = (
        mixed
        + combined
        + copy_gate * second_f
        + const_gate[:, :1] * const_t[0][None]
        + const_gate[:, 1:] * const_t[1][None]
    )
    total = pin(total, mixed_out, d_tokens)
    four = jnp.stack([total] + [flip(total, "shard", k, shards_n) for k in range(1, shards_n)])
    four = jnp.stack(
        [lax.dynamic_index_in_dim(four, m ^ shard, 0, keepdims=False) for m in range(4)]
    )
    d_q, d_k, d_v, d_w_out = [four[m, :rows_d].astype(full) for m in range(4)]
    d_w_qkv = jnp.stack([d_q, d_k, d_v], axis=1)
    tiny = four[:, rows_d]
    tiny = both_trees(tiny, swap(tiny)).transpose(1, 0, 2).reshape(16, rows_d).astype(full)

    return (
        both_trees(mixed_out, swap(mixed_out)),
        both_trees(d_tokens, swap(d_tokens)),
        both_trees(d_logits, swap(d_logits)),
        d_w_qkv,
        d_w_out,
        tiny[:all_experts].T,
        tiny[all_experts],
        tiny[all_experts + 1],
        tiny[all_experts + 2 :].T,
        d_gate_up,
        d_down,
    )


def program(tokens, gate_res, cotangent, parents, expert_ids, priority, w_qkv, *weights):
    trees, rows, width = tokens.shape
    ctx_n = lax.axis_size("ctx")
    seg = rows * ctx_n // parents.shape[1]
    fits = (
        ctx_n == 4
        and lax.axis_size("shard") == 4
        and lax.axis_size("tp") == 2
        and trees == 2
        and seg == 128
        and rows % seg == 0
        and 2 * rows < KEY_SEGS * seg <= 3 * rows
        and weights[-1].shape[1] == 2
    )
    chosen = by_core if fits else shards
    return chosen(tokens, gate_res, cotangent, parents, expert_ids, priority, w_qkv, *weights)


def solution(mesh):
    return jax.shard_map(
        program,
        mesh=mesh,
        in_specs=(
            P("shard", "ctx", None),
            P("shard", "ctx", None),
            P("shard", "ctx", None),
            P("shard", None),
            P("shard", "ctx", None),
            P("shard", "ctx", None),
            P("ctx", None, "tp"),
            P("ctx", "tp"),
            P("ctx", None),
            P("ctx"),
            P("ctx"),
            P("ctx", None),
            P("ctx", "shard", None, "tp"),
            P("ctx", "shard", "tp"),
        ),
        out_specs=(
            P("shard", "ctx", None),
            P("shard", "ctx", None),
            P("shard", "ctx", None),
            P("ctx", None, "tp"),
            P("ctx", "tp"),
            P("ctx", None),
            P("ctx"),
            P("ctx"),
            P("ctx", None),
            P("ctx", "shard", None, "tp"),
            P("ctx", "shard", "tp"),
        ),
        check_vma=False,
    )
```

```python
import functools
import math

import jax
import jax.numpy as jnp
from jax import lax
from jax.experimental import pallas as pl
from jax.experimental.pallas import tpu as pltpu
from jax.sharding import PartitionSpec as P

HEAD_DIM = 64


eps = 1e-06
score_scale = 0.125


def ancestry(parent_row):
    seg_count = parent_row.shape[0]
    position = jnp.arange(seg_count, dtype=jnp.int32)
    linked = (parent_row[:, None] == position[None, :]) | (position[:, None] == position[None, :])
    reach = linked.astype(jnp.float32)
    for repeat in range(seg_count.bit_length()):
        reach = jnp.minimum(jnp.dot(reach, reach, precision=lax.Precision.HIGHEST), 1.0)
    return reach


def path_rows(positions, seg_len, ancestors):
    onehot = (
        (positions // seg_len)[:, None] == jnp.arange(ancestors.shape[0], dtype=jnp.int32)[None, :]
    ).astype(jnp.float32)
    return jnp.dot(onehot, ancestors)


def allowed_block(query_rows, query_pos, key_start, key_count, seg_len):
    key_pos = key_start + jnp.arange(key_count, dtype=jnp.int32)
    key_onehot = (
        (key_pos // seg_len)[:, None] == jnp.arange(query_rows.shape[1], dtype=jnp.int32)[None, :]
    ).astype(jnp.float32)
    linked = jnp.dot(query_rows, key_onehot.T) > 0.5
    return (linked & (key_pos[None, :] <= query_pos[:, None]))[None]


def slot_table(picked_ids, ranking, experts, capacity):
    count_rows = picked_ids.shape[0]
    flat_ids = picked_ids.reshape(-1)
    rank_key = (2 * ranking[:, None] + jnp.arange(2, dtype=jnp.int32)[None, :]).reshape(-1)
    earlier = (flat_ids[:, None] == flat_ids[None, :]) & (rank_key[None, :] < rank_key[:, None])
    ranks = jnp.sum(earlier.astype(jnp.int32), axis=1)
    kept = (flat_ids < experts) & (ranks < capacity)
    target = jnp.where(kept, flat_ids * capacity + ranks, -1).reshape(count_rows, 2)
    slot_index = jnp.arange(experts * capacity, dtype=jnp.int32)
    return slot_index[None, :, None] == target.T[:, None, :]


def block_scores(queries, keys_blk):
    return (
        jnp.einsum("qhe,khe->hqk", queries, keys_blk, preferred_element_type=jnp.float32)
        * score_scale
    )


def softmax_grads(queries, grads_out, stat_lse, stat_delta, keys_blk, values_blk, mask):
    prob = jnp.where(mask, jnp.exp(block_scores(queries, keys_blk) - stat_lse[:, :, None]), 0.0)
    dprob = jnp.einsum("qhe,khe->hqk", grads_out, values_blk, preferred_element_type=jnp.float32)
    dscore = (prob * (dprob - stat_delta[:, :, None])).astype(jnp.bfloat16)
    return (prob.astype(jnp.bfloat16), dscore)


def shards(
    tokens,
    gate_res,
    cotangent,
    parents,
    expert_ids,
    priority,
    w_qkv,
    w_out,
    w_router,
    attn_gain,
    ffn_gain,
    const_vec,
    w_gate_up,
    w_down,
):
    full_qkv, full_out, full_router, full_again, full_fgain, full_const, full_gu, full_down = (
        lax.all_gather(w_qkv, "ctx", axis=0, tiled=True),
        lax.all_gather(w_out, "ctx", axis=0, tiled=True),
        lax.all_gather(w_router, "ctx", axis=0, tiled=True),
        lax.all_gather(attn_gain, "ctx", axis=0, tiled=True),
        lax.all_gather(ffn_gain, "ctx", axis=0, tiled=True),
        lax.all_gather(const_vec, "ctx", axis=0, tiled=True),
        lax.all_gather(w_gate_up, "ctx", axis=0, tiled=True),
        lax.all_gather(w_down, "ctx", axis=0, tiled=True),
    )
    tree_count, rows, model_width = tokens.shape
    tok_rows = tree_count * rows
    inputs = tokens.reshape(tok_rows, model_width).astype(jnp.float32)
    local_width = full_out.shape[1]
    local_heads = local_width // HEAD_DIM
    ctx_index = lax.axis_index("ctx")
    tree_len = rows * lax.axis_size("ctx")
    ancestors_all = jax.vmap(ancestry)(parents)
    seg_len = tree_len // parents.shape[1]
    key_block = math.gcd(tree_len, 512)
    starts = jnp.arange(tree_len // key_block, dtype=jnp.int32) * key_block
    key_start_own = ctx_index * rows
    query_pos = key_start_own + jnp.arange(rows, dtype=jnp.int32)
    query_rows_all = jax.vmap(lambda anc: path_rows(query_pos, seg_len, anc))(ancestors_all)
    inv_first = lax.rsqrt(jnp.mean(inputs * inputs, axis=-1, keepdims=True) + eps)
    first_unit = inputs * inv_first
    first_gain = full_again.astype(jnp.float32)
    normed = (first_unit * first_gain).astype(jnp.bfloat16)
    projected = jnp.einsum("nd,dke->nke", normed, full_qkv, preferred_element_type=jnp.float32)
    q_low = projected[:, 0].astype(jnp.bfloat16)
    k_low = projected[:, 1].astype(jnp.bfloat16)
    v_low = projected[:, 2].astype(jnp.bfloat16)
    keys_all, values_all = (
        lax.all_gather(k_low.reshape(tree_count, rows, local_width), "ctx", axis=1, tiled=True),
        lax.all_gather(v_low.reshape(tree_count, rows, local_width), "ctx", axis=1, tiled=True),
    )
    q_heads = q_low.reshape(tree_count, rows, local_heads, HEAD_DIM)
    k_heads = keys_all.reshape(tree_count, tree_len, local_heads, HEAD_DIM)
    v_heads = values_all.reshape(tree_count, tree_len, local_heads, HEAD_DIM)

    def tree_forward(q_one, k_one, v_one, rows_one):

        def stat_step(carry, start):
            running_top, running_sum = carry
            keys_blk = lax.dynamic_slice_in_dim(k_one, start, key_block, 0)
            mask = allowed_block(rows_one, query_pos, start, key_block, seg_len)
            masked = jnp.where(mask, block_scores(q_one, keys_blk), -1e30)
            new_top = jnp.maximum(running_top, jnp.max(masked, axis=2))
            expo = jnp.where(mask, jnp.exp(masked - new_top[:, :, None]), 0.0)
            running_sum = running_sum * jnp.exp(running_top - new_top) + jnp.sum(expo, axis=2)
            return ((new_top, running_sum), None)

        start_top = jnp.full((local_heads, rows), -1e30, jnp.float32)
        (final_top, final_sum), unused = lax.scan(
            stat_step, (start_top, jnp.zeros_like(start_top)), starts
        )
        lse_one = final_top + jnp.log(final_sum)

        def out_step(accum, start):
            keys_blk = lax.dynamic_slice_in_dim(k_one, start, key_block, 0)
            values_blk = lax.dynamic_slice_in_dim(v_one, start, key_block, 0)
            mask = allowed_block(rows_one, query_pos, start, key_block, seg_len)
            prob = jnp.where(
                mask, jnp.exp(block_scores(q_one, keys_blk) - lse_one[:, :, None]), 0.0
            ).astype(jnp.bfloat16)
            return (
                accum
                + jnp.einsum("hqk,khe->qhe", prob, values_blk, preferred_element_type=jnp.float32),
                None,
            )

        attended_one, unused = lax.scan(
            out_step, jnp.zeros((rows, local_heads, HEAD_DIM), jnp.float32), starts
        )
        return (attended_one, lse_one)

    attended, lse = jax.vmap(tree_forward)(q_heads, k_heads, v_heads, query_rows_all)
    attended_low = attended.reshape(tok_rows, local_width).astype(jnp.bfloat16)
    attn_part = jnp.einsum("nh,dh->nd", attended_low, full_out, preferred_element_type=jnp.float32)
    attn_sum = lax.psum(attn_part.astype(jnp.bfloat16), "tp").astype(jnp.float32)
    mixed = inputs + attn_sum
    inv_second = lax.rsqrt(jnp.mean(mixed * mixed, axis=-1, keepdims=True) + eps)
    second_unit = mixed * inv_second
    second_gain = full_fgain.astype(jnp.float32)
    second_low = (second_unit * second_gain).astype(jnp.bfloat16)
    second_float = second_low.astype(jnp.float32)
    logits = jnp.dot(
        second_low, full_router, preferred_element_type=jnp.float32
    ) + gate_res.reshape(tok_rows, -1)
    expo_logits = jnp.exp(logits - jnp.max(logits, axis=-1, keepdims=True))
    probs = expo_logits / jnp.sum(expo_logits, axis=-1, keepdims=True)
    experts = lax.axis_size("shard") * w_gate_up.shape[1]
    every_expert = experts + 4
    capacity = tok_rows * 2 // every_expert
    picked_ids = expert_ids.reshape(tok_rows, 2)
    selector = (picked_ids[:, :, None] == jnp.arange(every_expert, dtype=jnp.int32)).astype(
        jnp.float32
    )
    picked = jnp.sum(selector * probs[:, None, :], axis=-1)
    picked_total = jnp.sum(picked, axis=-1, keepdims=True)
    gates = picked / picked_total
    table = slot_table(picked_ids, priority[0, 0], experts, capacity).astype(jnp.bfloat16)
    routed = table[0] + table[1]
    send_slots = jnp.einsum(
        "et,td->ed", routed, second_low, preferred_element_type=jnp.float32
    ).astype(jnp.bfloat16)
    send_slots = send_slots.reshape(experts, 1, capacity, model_width)
    arrived = lax.all_to_all(send_slots, "shard", split_axis=0, concat_axis=1, tiled=True)
    gate_up = jnp.einsum("jsrd,djgf->jsrgf", arrived, full_gu, preferred_element_type=jnp.float32)
    hidden_low = (jax.nn.silu(gate_up[:, :, :, 0]) * gate_up[:, :, :, 1]).astype(jnp.bfloat16)
    partial_out = jnp.einsum(
        "jsrf,djf->jsrd", hidden_low, full_down, preferred_element_type=jnp.float32
    )
    summed = lax.psum(partial_out.astype(jnp.bfloat16), "tp")
    returned = lax.all_to_all(summed, "shard", split_axis=1, concat_axis=0, tiled=True)
    returned, kept_slots = (returned, arrived)
    out_slots = returned.reshape(experts * capacity, model_width)
    ffn_values = jnp.einsum("cet,ed->ctd", table, out_slots, preferred_element_type=jnp.float32)
    copy_flag = selector[:, :, experts + 1]
    const_flags = selector[:, :, experts + 2 :]
    const_float = full_const.astype(jnp.float32)
    fixed_terms = jnp.einsum(
        "nck,dk->cnd", const_flags, const_float, precision=lax.Precision.HIGHEST
    )
    values_pair = ffn_values + copy_flag.T[:, :, None] * second_float[None] + fixed_terms
    mixed_out = mixed + jnp.sum(gates.T[:, :, None] * values_pair, axis=0)
    grad_out = cotangent.reshape(tok_rows, model_width).astype(jnp.float32)
    weighted = gates.T[:, :, None] * grad_out[None]
    d_gates = jnp.einsum("cnd,nd->nc", values_pair, grad_out)
    d_const = jnp.einsum("nck,cnd->dk", const_flags, weighted, precision=lax.Precision.HIGHEST)
    d_out_slots = jnp.einsum(
        "cet,ctd->ed", table.astype(jnp.float32), weighted, precision=lax.Precision.HIGHEST
    )
    d_out_low = d_out_slots.astype(jnp.bfloat16).reshape(experts, 1, capacity, model_width)
    d_picked = (d_gates - jnp.sum(d_gates * gates, axis=-1, keepdims=True)) / picked_total
    d_probs = jnp.einsum("nc,nck->nk", d_picked, selector)
    d_logits = probs * (d_probs - jnp.sum(probs * d_probs, axis=-1, keepdims=True))
    d_router_w = jnp.dot(second_float.T, d_logits, precision=lax.Precision.HIGHEST)
    d_second = jnp.sum(copy_flag.T[:, :, None] * weighted, axis=0)
    d_second = d_second + jnp.dot(
        d_logits, full_router.astype(jnp.float32).T, precision=lax.Precision.HIGHEST
    )
    arrived_grad = lax.all_to_all(d_out_low, "shard", split_axis=0, concat_axis=1, tiled=True)
    gate_up = jnp.einsum(
        "jsrd,djgf->jsrgf", kept_slots, full_gu, preferred_element_type=jnp.float32
    )
    gate_part = gate_up[:, :, :, 0]
    up_part = gate_up[:, :, :, 1]
    sigma = jax.nn.sigmoid(gate_part)
    silu_part = gate_part * sigma
    hidden_low = (silu_part * up_part).astype(jnp.bfloat16)
    d_hidden = jnp.einsum(
        "jsrd,djf->jsrf", arrived_grad, full_down, preferred_element_type=jnp.float32
    )
    d_gate_part = d_hidden * up_part * sigma * (1.0 + gate_part * (1.0 - sigma))
    d_up_part = d_hidden * silu_part
    d_gate_up_low = jnp.stack([d_gate_part, d_up_part], axis=3).astype(jnp.bfloat16)
    d_slot_part = jnp.einsum(
        "jsrgf,djgf->jsrd", d_gate_up_low, full_gu, preferred_element_type=jnp.float32
    )
    d_slot_sum = lax.psum(d_slot_part.astype(jnp.bfloat16), "tp")
    d_slot_back = lax.all_to_all(d_slot_sum, "shard", split_axis=1, concat_axis=0, tiled=True)
    d_gate_up_w = jnp.einsum(
        "jsrd,jsrgf->djgf", kept_slots, d_gate_up_low, preferred_element_type=jnp.float32
    )
    d_down_w = jnp.einsum(
        "jsrd,jsrf->djf", arrived_grad, hidden_low, preferred_element_type=jnp.float32
    )
    d_second = d_second + jnp.einsum(
        "et,ed->td",
        routed,
        d_slot_back.reshape(experts * capacity, model_width),
        preferred_element_type=jnp.float32,
    )
    d_second_gain = jnp.sum(d_second * second_unit, axis=0)
    d_second_unit = d_second * second_gain
    d_mixed = grad_out + inv_second * (
        d_second_unit - second_unit * jnp.mean(d_second_unit * second_unit, axis=-1, keepdims=True)
    )
    d_attn_low = d_mixed.astype(jnp.bfloat16)
    d_out_w = jnp.einsum("nd,nh->dh", d_attn_low, attended_low, preferred_element_type=jnp.float32)
    d_attended = jnp.einsum("nd,dh->nh", d_attn_low, full_out, preferred_element_type=jnp.float32)
    do_low = d_attended.astype(jnp.bfloat16)
    do_heads = do_low.reshape(tree_count, rows, local_heads, HEAD_DIM)
    delta = jnp.einsum("tqhe,tqhe->thq", do_heads.astype(jnp.float32), attended)

    def tree_both(q_one, k_one, v_one, do_one, lse_one, delta_one, rows_one):

        def both_step(dq_accum, start):
            keys_blk = lax.dynamic_slice_in_dim(k_one, start, key_block, 0)
            values_blk = lax.dynamic_slice_in_dim(v_one, start, key_block, 0)
            mask = allowed_block(rows_one, query_pos, start, key_block, seg_len)
            prob_low, dscore = softmax_grads(
                q_one, do_one, lse_one, delta_one, keys_blk, values_blk, mask
            )
            dq_accum = dq_accum + jnp.einsum(
                "hqk,khe->qhe", dscore, keys_blk, preferred_element_type=jnp.float32
            )
            dkey = (
                jnp.einsum("hqk,qhe->khe", dscore, q_one, preferred_element_type=jnp.float32)
                * score_scale
            )
            dval = jnp.einsum("hqk,qhe->khe", prob_low, do_one, preferred_element_type=jnp.float32)
            return (
                dq_accum,
                jnp.stack(
                    [dkey.reshape(key_block, local_width), dval.reshape(key_block, local_width)],
                    axis=1,
                ),
            )

        dq_one, terms_one = lax.scan(
            both_step, jnp.zeros((rows, local_heads, HEAD_DIM), jnp.float32), starts
        )
        return (dq_one, terms_one.reshape(tree_len, 2, local_width))

    dq_total, key_terms = jax.vmap(tree_both)(
        q_heads, k_heads, v_heads, do_heads, lse, delta, query_rows_all
    )
    key_sums = lax.psum_scatter(
        key_terms.astype(jnp.bfloat16), "ctx", scatter_dimension=1, tiled=True
    ).astype(jnp.float32)
    key_grad = key_sums[:, :, 0].reshape(tok_rows, local_width)
    value_grad = key_sums[:, :, 1].reshape(tok_rows, local_width)
    query_grad = (dq_total * score_scale).reshape(tok_rows, local_width)
    d_qkv_low = jnp.stack([query_grad, key_grad, value_grad], axis=1).astype(jnp.bfloat16)
    d_qkv_w = jnp.einsum("nd,nke->dke", normed, d_qkv_low, preferred_element_type=jnp.float32)
    d_normed_part = jnp.einsum(
        "nke,dke->nd", d_qkv_low, full_qkv, preferred_element_type=jnp.float32
    )
    d_normed = lax.psum(d_normed_part.astype(jnp.bfloat16), "tp").astype(jnp.float32)
    d_first_gain = jnp.sum(d_normed * first_unit, axis=0)
    d_first_unit = d_normed * first_gain
    d_inputs = d_mixed + inv_first * (
        d_first_unit - first_unit * jnp.mean(d_first_unit * first_unit, axis=-1, keepdims=True)
    )
    summed_grads = (
        lax.psum_scatter(
            d_qkv_w.astype(jnp.bfloat16), "ctx", scatter_dimension=0, tiled=True
        ).astype(jnp.float32),
        lax.psum_scatter(
            d_out_w.astype(jnp.bfloat16), "ctx", scatter_dimension=0, tiled=True
        ).astype(jnp.float32),
        lax.psum_scatter(
            d_router_w.astype(jnp.bfloat16), "ctx", scatter_dimension=0, tiled=True
        ).astype(jnp.float32),
        lax.psum_scatter(
            d_first_gain.astype(jnp.bfloat16), "ctx", scatter_dimension=0, tiled=True
        ).astype(jnp.float32),
        lax.psum_scatter(
            d_second_gain.astype(jnp.bfloat16), "ctx", scatter_dimension=0, tiled=True
        ).astype(jnp.float32),
        lax.psum_scatter(
            d_const.astype(jnp.bfloat16), "ctx", scatter_dimension=0, tiled=True
        ).astype(jnp.float32),
        lax.psum_scatter(
            d_gate_up_w.astype(jnp.bfloat16), "ctx", scatter_dimension=0, tiled=True
        ).astype(jnp.float32),
        lax.psum_scatter(
            d_down_w.astype(jnp.bfloat16), "ctx", scatter_dimension=0, tiled=True
        ).astype(jnp.float32),
    )
    shared = (
        lax.psum(summed_grads[0].astype(jnp.bfloat16), "shard").astype(jnp.float32),
        lax.psum(summed_grads[1].astype(jnp.bfloat16), "shard").astype(jnp.float32),
        lax.psum(summed_grads[2].astype(jnp.bfloat16), "shard").astype(jnp.float32),
        lax.psum(summed_grads[3].astype(jnp.bfloat16), "shard").astype(jnp.float32),
        lax.psum(summed_grads[4].astype(jnp.bfloat16), "shard").astype(jnp.float32),
        lax.psum(summed_grads[5].astype(jnp.bfloat16), "shard").astype(jnp.float32),
    )
    out_rows = mixed_out.reshape(tree_count, rows, model_width)
    grad_rows = d_inputs.reshape(tree_count, rows, model_width)
    logit_rows = d_logits.reshape(tree_count, rows, every_expert)
    return (
        out_rows,
        grad_rows,
        logit_rows,
        shared[0],
        shared[1],
        shared[2],
        shared[3],
        shared[4],
        shared[5],
        summed_grads[6],
        summed_grads[7],
    )


NT = (((1,), (1,)), ((), ()))
NN = (((1,), (0,)), ((), ()))
TRUNK = 8
KEY_SEGS = 12
PIECE = 256
SENT = (0, 2, 1, 3)


def mm(a, b, dims=NN):
    return lax.dot_general(a, b, dims, preferred_element_type=jnp.float32)


def stacked(rows, half):
    first = lax.broadcasted_iota(jnp.int32, rows.shape, 1) < half
    blank = jnp.zeros_like(rows)
    return jnp.concatenate([jnp.where(first, rows, blank), jnp.where(first, blank, rows)], axis=0)


def unstack(wide, half, seg):
    return jnp.concatenate([wide[:half, :seg], wide[half:, seg:]], axis=0)


def causal(seg):
    row = lax.broadcasted_iota(jnp.int32, (seg, 2 * seg), 0)
    col = lax.broadcasted_iota(jnp.int32, (seg, 2 * seg), 1)
    return row <= jnp.where(col >= seg, col - seg, col)


def attend_kernel(own, seg, half, more, info, q_ref, k_ref, v_ref, *rest):
    o_ref, lse_ref, s_ref, p_ref = rest[2 * more :]
    trunk = TRUNK * seg
    allowed = causal(seg)
    v_trunk = v_ref[own : own + trunk, :].T

    def one(i, unused):
        count, branch, leaf = info[i, 0], info[i, 1], info[i, 2]
        here = pl.ds(pl.multiple_of(i * seg, seg), seg)
        there = pl.ds(pl.multiple_of(own + branch * seg, seg), seg)
        qs = stacked(q_ref[here, :] * 0.125, half)
        s_ref[:trunk, :] = mm(k_ref[own : own + trunk, :], qs, NT)
        s_branch = mm(k_ref[there, :], qs, NT)
        s_own = jnp.where(allowed, mm(k_ref[here, :], qs, NT), -1e30)
        biases = [jnp.where(kb < count, 0.0, -1e30) for kb in range(TRUNK)]
        leaf_bias = jnp.where(leaf > 0, 0.0, -1e30)
        top = jnp.max(s_own, axis=0, keepdims=True)
        top = jnp.maximum(top, jnp.max(s_branch, axis=0, keepdims=True) + leaf_bias)
        for kb in range(TRUNK):
            part = jnp.max(s_ref[kb * seg : (kb + 1) * seg, :], axis=0, keepdims=True)
            top = jnp.maximum(top, part + biases[kb])
        e_own = jnp.exp(s_own - top)
        e_branch = jnp.exp(s_branch - (top - leaf_bias))
        total = jnp.sum(e_own + e_branch, axis=0, keepdims=True)
        for kb in range(TRUNK):
            e = jnp.exp(s_ref[kb * seg : (kb + 1) * seg, :] - (top - biases[kb]))
            total = total + jnp.sum(e, axis=0, keepdims=True)
            p_ref[kb * seg : (kb + 1) * seg, :] = e.astype(jnp.bfloat16)
        out = mm(v_trunk, p_ref[...])
        out = out + mm(v_ref[there, :].T, e_branch.astype(jnp.bfloat16))
        out = out + mm(v_ref[here, :].T, e_own.astype(jnp.bfloat16))
        out = unstack(out * (1.0 / total), half, seg)
        o_ref[here, :] = out.T.astype(jnp.bfloat16)
        lse_ref[pl.ds(i, 1), :] = top + jnp.log(total)
        return 0

    lax.fori_loop(0, own // seg, one, 0, unroll=True)


def attend_back_kernel(
    own, seg, half, more, info, q_ref, k_ref, v_ref, o_ref, do_ref, lse_ref, *rest
):
    dq_ref, dk_ref, dv_ref, ak, av = rest[3 * more :]
    trunk = TRUNK * seg
    allowed = causal(seg)
    low = jnp.bfloat16
    tk = slice(own, own + trunk)
    k_trunk = k_ref[tk, :].T
    ak[...] = jnp.zeros_like(ak)
    av[...] = jnp.zeros_like(av)

    def one(i, unused):
        count, branch, leaf = info[i, 0], info[i, 1], info[i, 2]
        here = pl.ds(pl.multiple_of(i * seg, seg), seg)
        there = pl.ds(pl.multiple_of(own + branch * seg, seg), seg)
        qs = stacked(q_ref[here, :] * 0.125, half)
        do = do_ref[here, :]
        dos = stacked(do, half)
        prod = (do.astype(jnp.float32) * o_ref[here, :].astype(jnp.float32)).T
        delta = jnp.concatenate(
            [jnp.sum(prod[:half], axis=0, keepdims=True), jnp.sum(prod[half:], axis=0, keepdims=True)],
            axis=1,
        )
        lse = lse_ref[pl.ds(i, 1), :]
        leaf_bias = jnp.where(leaf > 0, 0.0, -1e30)

        def piece(keys, values, shift, mask):
            s = mm(keys, qs, NT)
            if mask:
                s = jnp.where(allowed, s, -1e30)
            if isinstance(shift, list):
                p = jnp.concatenate(
                    [jnp.exp(s[kb * seg : (kb + 1) * seg] - shift[kb]) for kb in range(TRUNK)], axis=0
                )
            else:
                p = jnp.exp(s - shift)
            ds = (p * (mm(values, dos, NT) - delta)).astype(low)
            p = p.astype(low)
            return (mm(p, dos), mm(ds, qs), ds)

        shifts = [lse - jnp.where(kb < count, 0.0, -1e30) for kb in range(TRUNK)]
        dv, dk, ds = piece(k_ref[tk, :], v_ref[tk, :], shifts, False)
        av[tk, :] += dv
        ak[tk, :] += dk
        dq = mm(k_trunk, ds)
        keys = k_ref[there, :]
        dv, dk, ds = piece(keys, v_ref[there, :], lse - leaf_bias, False)
        av[there, :] += dv
        ak[there, :] += dk
        dq = dq + mm(keys.T, ds)
        keys = k_ref[here, :]
        dv, dk, ds = piece(keys, v_ref[here, :], lse, True)
        av[here, :] += dv
        ak[here, :] += dk
        dq = dq + mm(keys.T, ds)
        dq_ref[here, :] = (unstack(dq, half, seg) * 0.125).T.astype(low)
        return 0

    lax.fori_loop(0, own // seg, one, 0, unroll=True)
    dk_ref[...] = ak[...].astype(low)
    dv_ref[...] = av[...].astype(low)


def attend(info, q, kv, seg, begin, count, prev=()):
    own, width = q.shape
    total = kv.shape[0]
    pairs = width // 128
    lane = pl.BlockSpec((own, 128), lambda h: (0, begin + h))
    return pl.pallas_call(
        functools.partial(attend_kernel, own, seg, HEAD_DIM, len(prev) > 0),
        grid=(count,),
        in_specs=[
            pl.BlockSpec(memory_space=pltpu.SMEM),
            lane,
            pl.BlockSpec((total, 128), lambda h: (0, begin + h)),
            pl.BlockSpec((total, 128), lambda h: (0, pairs + begin + h)),
        ]
        + [pl.BlockSpec(memory_space=pl.ANY)] * len(prev),
        out_specs=[lane, pl.BlockSpec((None, 8, 2 * seg), lambda h: (begin + h, 0, 0))],
        out_shape=[
            jax.ShapeDtypeStruct((own, width), jnp.bfloat16),
            jax.ShapeDtypeStruct((pairs, 8, 2 * seg), jnp.float32),
        ],
        input_output_aliases={4 + i: i for i in range(len(prev))},
        scratch_shapes=[
            pltpu.VMEM((TRUNK * seg, 2 * seg), jnp.float32),
            pltpu.VMEM((TRUNK * seg, 2 * seg), jnp.bfloat16),
        ],
        compiler_params=pltpu.CompilerParams(vmem_limit_bytes=60 << 20),
        cost_estimate=pl.CostEstimate(
            flops=1000, bytes_accessed= 1000, transcendentals=0
        ),
        name="attend",
    )(info, q, kv, kv, *prev)


def attend_back(info, q, kv, o, do, lse, seg, begin, count, prev=()):
    own, width = q.shape
    total = kv.shape[0]
    pairs = width // 128
    lane = pl.BlockSpec((own, 128), lambda h: (0, begin + h))
    keys = pl.BlockSpec((total, 128), lambda h: (0, begin + h))
    return pl.pallas_call(
        functools.partial(attend_back_kernel, own, seg, HEAD_DIM, len(prev) > 0),
        grid=(count,),
        in_specs=[
            pl.BlockSpec(memory_space=pltpu.SMEM),
            lane,
            keys,
            pl.BlockSpec((total, 128), lambda h: (0, pairs + begin + h)),
            lane,
            lane,
            pl.BlockSpec((None, 8, 2 * seg), lambda h: (begin + h, 0, 0)),
        ]
        + [pl.BlockSpec(memory_space=pl.ANY)] * len(prev),
        out_specs=[lane, keys, keys],
        out_shape=[
            jax.ShapeDtypeStruct((own, width), jnp.bfloat16),
            jax.ShapeDtypeStruct((total, width), jnp.bfloat16),
            jax.ShapeDtypeStruct((total, width), jnp.bfloat16),
        ],
        input_output_aliases={7 + i: i for i in range(len(prev))},
        scratch_shapes=[
            pltpu.VMEM((total, 128), jnp.float32),
            pltpu.VMEM((total, 128), jnp.float32),
        ],
        compiler_params=pltpu.CompilerParams(vmem_limit_bytes=40 << 20),
        cost_estimate=pl.CostEstimate(
            flops=1000, bytes_accessed= 1000, transcendentals=0
        ),
        name="attend_back",
    )(info, q, kv, kv, o, do, lse, *prev)


def pin(x, *after):
    return lax.optimization_barrier((x,) + after)[0]


def expert_kernel(
    more, capacity, pieces, place, xm_ref, xo_ref, gm_ref, go_ref, w0, w1, w2, w3, *rest
):
    low, full = jnp.bfloat16, jnp.float32
    o_ref, o2_ref, s_ref, s2_ref, dw_ref, x_ref, g_ref, xt, dt, d_ref, oa, sa, wb, gb = rest[more:]
    part = w0.shape[1]
    rows, wide = xm_ref.shape
    padded = rows // pieces
    tail = padded - 16
    here = pl.ds(pl.multiple_of(place[1] * wide, 128), wide)
    there = pl.ds(pl.multiple_of((1 - place[1]) * wide, 128), wide)

    @pl.when(pl.program_id(0) == 0)
    def start():
        x_ref[:, here] = xm_ref[...]
        x_ref[:, there] = xo_ref[...]
        g_ref[:, here] = gm_ref[...]
        g_ref[:, there] = go_ref[...]
        for p in range(pieces):
            mine = slice(p * padded, (p + 1) * padded)
            last = xm_ref[p * padded + tail : (p + 1) * padded, :256].astype(full)
            row = lax.broadcasted_iota(jnp.int32, last.shape, 0) + tail
            inside = (row >= capacity) & (row < capacity + 3)
            gate = jnp.sum(jnp.where(inside, last, 0.0), axis=0, keepdims=True)
            gate = jnp.broadcast_to(gate, (8, 256)).T[:padded, 0:1]
            d_ref[mine, :] = (g_ref[mine, :].astype(full) * gate).astype(low)
        xt[...] = x_ref[...].T
        dt[...] = d_ref[...].T
        oa[...] = jnp.zeros_like(oa)
        sa[...] = jnp.zeros_like(sa)

    def rows_of(r):
        return pl.ds(pl.multiple_of((place[0] ^ r) * part, 64), part)

    for r, w in enumerate((w0, w1, w2, w3)):
        wb[:, rows_of(r), :] = w[...]
    u = mm(x_ref[...], wb[0])
    up = mm(x_ref[...], wb[1])
    sigma = 1.0 / (1.0 + jnp.exp(-u))
    silu = u * sigma
    hidden = (silu * up).astype(low)
    oa[...] += mm(hidden, wb[2], NT)
    dh = mm(d_ref[...], wb[2])
    du = (dh * up * sigma * (1.0 + u * (1.0 - sigma))).astype(low)
    dup = (dh * silu).astype(low)
    sa[...] += mm(du, wb[0], NT) + mm(dup, wb[1], NT)
    gb[0] = mm(xt[...], du).astype(low)
    gb[1] = mm(xt[...], dup).astype(low)
    gb[2] = mm(dt[...], hidden).astype(low)
    for at, r in enumerate(SENT):
        got = gb[:, rows_of(r), :]
        if more:
            got = (got.astype(full) + rest[0][at].astype(full)).astype(low)
        dw_ref[at] = got

    @pl.when(pl.program_id(0) == pl.num_programs(0) - 1)
    def finish():
        o_ref[...] = oa[:, here].astype(low)
        o2_ref[...] = oa[:, there].astype(low)
        s_ref[...] = sa[:, here].astype(low)
        s2_ref[...] = sa[:, there].astype(low)
        for p in range(pieces):
            mine = slice(p * padded, (p + 1) * padded)
            dot = jnp.sum(g_ref[mine, :].astype(full) * oa[mine, :], axis=1, keepdims=True)
            dot = jnp.broadcast_to(dot, (padded, 128)).T[:16, :]
            dot = jnp.concatenate([dot, jnp.zeros((16, wide - padded), full)], axis=1)
            row = lax.broadcasted_iota(jnp.int32, dot.shape, 0) + tail
            kept = jnp.zeros_like(dot)
            for i in range(3):
                piece = dot.astype(low).astype(full)
                kept = jnp.where(row == capacity + i, piece, kept)
                dot = dot - piece
            last = slice(p * padded + tail, (p + 1) * padded)
            row_low = s_ref[last, :].astype(full)
            s_ref[last, :] = jnp.where(row >= capacity, kept, row_low).astype(low)


def expert_pass(place, capacity, pieces, xs, gs, weights, prev):
    rows, half_width = xs[0].shape
    width = 2 * half_width
    three, part, units = weights[0].shape
    low = jnp.bfloat16
    strip = pl.BlockSpec((three, part, PIECE), lambda j, *at: (0, 0, j))
    strips = pl.BlockSpec((4, three, part, PIECE), lambda j, *at: (0, 0, 0, j))
    half = whole(rows, half_width)
    more = prev is not None
    return call(
        functools.partial(expert_kernel, int(more), capacity, pieces),
        "expert_pass",
        [((rows, half_width), low)] * 4 + [((4, three, part, units), low)],
        (place, *xs, *gs, *weights, *([prev] if more else [])),
        [
            pltpu.VMEM((rows, width), low),
            pltpu.VMEM((rows, width), low),
            pltpu.VMEM((width, rows), low),
            pltpu.VMEM((width, rows), low),
            pltpu.VMEM((rows, width), low),
            pltpu.VMEM((rows, width), jnp.float32),
            pltpu.VMEM((rows, width), jnp.float32),
            pltpu.VMEM((three, width, PIECE), low),
            pltpu.VMEM((three, width, PIECE), low),
        ],
        grid=(units // PIECE,),
        in_specs=[half] * 4 + [strip] * 4 + [strips] * more,
        out_specs=[half] * 4 + [strips],
        prefetch=True,
        mib=48,
    )


def spread_kernel(pieces, padded, capacity, gated, place_ref, rows_ref, *rest):
    low = jnp.bfloat16
    outs = rest[1:] if gated else rest
    tokens = rows_ref.shape[0]
    for p in range(pieces):
        slot = lax.broadcasted_iota(jnp.int32, (padded, tokens), 0) + p * padded
        hits = [slot == place_ref[c : c + 1, :] for c in range(2)]
        out = mm(jnp.where(hits[0] | hits[1], 1.0, 0.0).astype(low), rows_ref[...]).astype(low)
        if gated:
            parts = 0.0
            for c in range(2):
                value = rest[0][c : c + 1, :]
                rows3 = []
                for i in range(3):
                    rows3.append(value.astype(low).astype(jnp.float32))
                    value = value - rows3[-1]
                rows3.append(jnp.zeros((13, tokens), jnp.float32))
                three = jnp.concatenate(rows3, axis=0).astype(low)
                parts = parts + mm(three, jnp.where(hits[c], 1.0, 0.0).astype(low), NT)
            parts = parts.astype(low)
            blank = jnp.zeros((parts.shape[0], out.shape[1] - padded), low)
            parts = jnp.concatenate([parts, blank], axis=1)
            row = lax.broadcasted_iota(jnp.int32, out.shape, 0)
            for i in range(3):
                out = jnp.where(row == capacity + i, parts[i : i + 1, :], out)
        outs[p][...] = out


def spread(place, rows, pieces, padded, capacity, parts=None):
    shape = jax.ShapeDtypeStruct((padded, rows.shape[1]), jnp.bfloat16)
    gated = parts is not None
    return pl.pallas_call(
        functools.partial(spread_kernel, pieces, padded, capacity, gated),
        in_specs=[pl.BlockSpec(memory_space=pltpu.VMEM)] * (2 + gated),
        out_specs=[pl.BlockSpec(memory_space=pltpu.VMEM)] * pieces,
        out_shape=[shape] * pieces,
        compiler_params=pltpu.CompilerParams(vmem_limit_bytes=60 << 20),
        cost_estimate=pl.CostEstimate(flops=1000, bytes_accessed= 1000, transcendentals=0),
        name="spread",
    )(place, rows, *([parts] if gated else []))


def expert_of(where_ref, piece):
    upper = jnp.where(where_ref[1] >= 2, 1, 0)
    return (2 * ((piece % 4) ^ where_ref[0]) + ((piece // 4) ^ upper)).astype(jnp.float32)


def spread_gated_kernel(pieces, padded, capacity, gated, where_ref, place_ref, rows_ref, *rest):
    low, full = jnp.bfloat16, jnp.float32
    tokens, width = rows_ref.shape
    if gated:
        gates_ref, outs, wide_ref = rest[0], rest[1:-1], rest[-1]
        lines = []
        for c in range(2):
            value = gates_ref[c : c + 1, :]
            for i in range(3):
                lines.append(value.astype(low).astype(full))
                value = value - lines[-1]
        lines = lines + [gates_ref[4:5, :], jnp.zeros((121, tokens), full)]
        wide_ref[:, :width] = rows_ref[...]
        wide_ref[:, width:] = jnp.concatenate(lines, axis=0).T.astype(low)
    else:
        outs, wide_ref = rest, rows_ref
    for p in range(pieces):
        slot = lax.broadcasted_iota(jnp.int32, (padded, tokens), 0) + p * padded
        hit = (slot == place_ref[0:1, :]) | (slot == place_ref[1:2, :])
        out = mm(jnp.where(hit, 1.0, 0.0).astype(low), wide_ref[...])
        if gated:
            extra = out[:, width:].T
            out = out[:, :width].astype(low)
            row = lax.broadcasted_iota(jnp.int32, out.shape, 0)
            blank = jnp.zeros((1, width - padded), full)
            for i in range(3):
                picked = jnp.where(
                    extra[6:7, :] == expert_of(where_ref, p), extra[i : i + 1, :], extra[3 + i : 4 + i, :]
                )
                picked = jnp.concatenate([picked, blank], axis=1).astype(low)
                out = jnp.where(row == capacity + i, picked, out)
        outs[p][...] = out.astype(low)


def spread_gated(where, place, rows, pieces, padded, capacity, gates=None):
    shape = jax.ShapeDtypeStruct((padded, rows.shape[1]), jnp.bfloat16)
    gated = gates is not None
    return pl.pallas_call(
        functools.partial(spread_gated_kernel, pieces, padded, capacity, gated),
        in_specs=[pl.BlockSpec(memory_space=pltpu.SMEM)]
        + [pl.BlockSpec(memory_space=pltpu.VMEM)] * (2 + gated),
        out_specs=[pl.BlockSpec(memory_space=pltpu.VMEM)] * pieces,
        out_shape=[shape] * pieces,
        scratch_shapes=[pltpu.VMEM((rows.shape[0], rows.shape[1] + 128), jnp.bfloat16)] * gated,
        compiler_params=pltpu.CompilerParams(vmem_limit_bytes=40 << 20),
        cost_estimate=pl.CostEstimate(flops=1000, bytes_accessed=1000, transcendentals=0),
        name="spread",
    )(where, place, rows, *([gates] if gated else []))


def gather_kernel(pieces, padded, capacity, dots, where_ref, place_ref, pair_ref, *rest):
    low, full = jnp.bfloat16, jnp.float32
    if dots:
        ins, (out_ref, out2_ref, dot_ref, dot2_ref) = rest[:pieces], rest[pieces:]
    else:
        ins, (out_ref, out2_ref) = rest[: pieces // 2], rest[pieces // 2 :]
    tokens = place_ref.shape[0]
    total = None
    sums = [0.0, 0.0]
    for p in range(pieces):
        slot = lax.broadcasted_iota(jnp.int32, (tokens, padded), 1) + p * padded
        hits = [slot == place_ref[:, c : c + 1] for c in range(2)]
        if dots:
            source = ins[p][...]
            width = source.shape[1]
            values = ins[p][padded - 16 :, :padded].astype(full)
            values = jnp.concatenate([values, jnp.zeros((112, padded), full)], axis=0).T
            source = jnp.concatenate([source, values.astype(low)], axis=1)
            part = mm(jnp.where(hits[0] | hits[1], 1.0, 0.0).astype(low), source)
            lane = lax.broadcasted_iota(jnp.int32, (tokens, 128), 1)
            lane = lane + (padded - 16 - capacity)
            dot = jnp.where((lane >= 0) & (lane < 3), part[:, width:], 0.0)
            mine = pair_ref[:, 0:1] == expert_of(where_ref, p)
            sums[0] = sums[0] + jnp.where(mine, dot, 0.0)
            sums[1] = sums[1] + jnp.where(mine, 0.0, dot)
            part = part[:, :width]
        else:
            pick = jnp.where(hits[0], pair_ref[:, 0:1], jnp.where(hits[1], pair_ref[:, 1:2], 0.0))
            part = mm(pick.astype(low), ins[p % 4][p // 4])
        total = part if total is None else total + part
    rows = tokens // 2
    out_ref[...] = total[:rows].astype(low)
    out2_ref[...] = total[rows:].astype(low)
    if dots:
        for c in range(2):
            dot_ref[:, c : c + 1] = jnp.sum(sums[c][:rows], axis=1, keepdims=True)
            dot2_ref[:, c : c + 1] = jnp.sum(sums[c][rows:], axis=1, keepdims=True)


def gather(where, place, pair, pieces, capacity, dots):
    padded, width = pieces[0].shape[-2:]
    number = sum(p.size // (padded * width) for p in pieces)
    tokens = place.shape[0]
    shapes = [jax.ShapeDtypeStruct((tokens // 2, width), jnp.bfloat16)] * 2
    if dots:
        shapes = shapes + [jax.ShapeDtypeStruct((tokens // 2, 2), jnp.float32)] * 2
    return pl.pallas_call(
        functools.partial(gather_kernel, number, padded, capacity, dots),
        in_specs=[pl.BlockSpec(memory_space=pltpu.SMEM)]
        + [pl.BlockSpec(memory_space=pltpu.VMEM)] * (len(pieces) + 2),
        out_specs=[pl.BlockSpec(memory_space=pltpu.VMEM)] * len(shapes),
        out_shape=shapes,
        compiler_params=pltpu.CompilerParams(vmem_limit_bytes=60 << 20),
        cost_estimate=pl.CostEstimate(flops=1000, bytes_accessed= 1000, transcendentals=0),
        name="gather",
    )(where, place, pair, *pieces)


def whole(*shape):
    return pl.BlockSpec(shape, lambda *at: (0,) * len(shape))


def by_rows(*shape):
    return pl.BlockSpec(shape, lambda j, *at: (j, 0))


def chosen(number, *shape):
    return pl.BlockSpec((None,) + shape, lambda j, place: (number ^ place[0], 0, 0))


def call(kernel, name, outs, args, scratch=(), grid=(1,), in_specs=None, out_specs=None, prefetch=False, mib=40):
    if out_specs is None:
        out_specs = [whole(*o[0]) for o in outs]
    spec = pltpu.PrefetchScalarGridSpec(
        num_scalar_prefetch=int(prefetch),
        grid=grid,
        in_specs=in_specs,
        out_specs=out_specs,
        scratch_shapes=list(scratch),
    )
    return pl.pallas_call(
        kernel,
        grid_spec=spec,
        out_shape=[jax.ShapeDtypeStruct(*o) for o in outs],
        compiler_params=pltpu.CompilerParams(vmem_limit_bytes=mib << 20),
        cost_estimate=pl.CostEstimate(flops=1000, bytes_accessed=1000, transcendentals=0),
        name=name,
    )(*args)


def unit_rows(x):
    x = x.astype(jnp.float32)
    return x * lax.rsqrt(jnp.mean(x * x, axis=-1, keepdims=True) + eps)


def project_kernel(place, x0, near, mid, farther, gain, wm, wo, q_ref, kv_ref, n_ref, x_ref):
    low = jnp.bfloat16
    shard, ctx = place[0], place[1]
    rows, width = x0.shape
    half = wm.shape[2]

    def project(lo, x):
        here = slice(lo, lo + x.shape[0])
        normed = (unit_rows(x) * gain[...]).astype(low)
        x_ref[here, :] = x
        n_ref[here, :] = normed
        for m in (1, 2):
            for h, w in enumerate((wm, wo)):
                at = (m - 1) * width + h * half
                kv_ref[here, at : at + half] = mm(normed, w[m ^ shard]).astype(low)
        if lo == 0:
            for h, w in enumerate((wm, wo)):
                q_ref[:, h * half : (h + 1) * half] = mm(normed, w[shard]).astype(low)

    edge = x_ref.shape[0] - 3 * rows
    project(0, x0[...])
    later = jnp.where(ctx == 2, mid[...], farther[...])
    project(rows, jnp.where(ctx == 0, x0[...], jnp.where(ctx == 1, near[...], later)))
    later = jnp.where(ctx == 2, near[...], mid[...])
    project(2 * rows, jnp.where(ctx == 1, x0[...], later))
    project(3 * rows, jnp.where(ctx == 2, x0[:edge, :], near[:edge, :]))


def settle_kernel(
    place, o, x, wm, wo, gain, router, res, ids,
    mixed_ref, second_ref, mine_ref, other_ref, probs_ref, stat_ref, gates_ref,
):
    tp = place[2]
    half = wm.shape[1]
    attn = mm(o[:, :half], wm[...], NT) + mm(o[:, half:], wo[...], NT)
    mixed = x[...].astype(jnp.float32) + attn
    mixed_ref[...] = mixed
    inverse = lax.rsqrt(jnp.mean(mixed * mixed, axis=-1, keepdims=True) + eps)
    second = (mixed * inverse * gain[...]).astype(jnp.bfloat16)
    second_ref[...] = second
    mine_ref[...] = second_ref[:, pl.ds(pl.multiple_of(tp * half, 128), half)]
    other_ref[...] = second_ref[:, pl.ds(pl.multiple_of((1 - tp) * half, 128), half)]
    logits = mm(second, router[...], NT) + res[...]
    expo = jnp.exp(logits - jnp.max(logits, axis=-1, keepdims=True))
    probs = expo / jnp.sum(expo, axis=-1, keepdims=True)
    probs_ref[...] = probs
    lane = lax.broadcasted_iota(jnp.int32, probs.shape, 1)
    picked = [
        jnp.sum(jnp.where(lane == ids[:, c : c + 1], probs, 0.0), axis=-1, keepdims=True)
        for c in range(2)
    ]
    total = picked[0] + picked[1]
    wide = lax.broadcasted_iota(jnp.int32, (probs.shape[0], 128), 1)
    stat = jnp.where(wide == 0, picked[0] / total, jnp.where(wide == 1, picked[1] / total, 0.0))
    stat = jnp.where(wide == 2, total, jnp.where(wide == 3, inverse, stat))
    stat = jnp.where(wide == 4, ids[:, 0:1].astype(jnp.float32), stat)
    stat_ref[...] = stat[:, :8]
    gates_ref[...] = stat.T[:8, :]


def settle_back_kernel(
    copy_id, place, dr_mine, dr_came, dg_mine, dg_came, g_ref, mixed, second, probs_ref, stat, ids,
    const, router, gain, wm, wo, dmix_ref, dattn_ref, do_ref, dlog_ref, small_ref, full_ref,
):
    low, full = jnp.bfloat16, jnp.float32
    tp = place[2]
    half = wm.shape[1]
    full_ref[:, pl.ds(pl.multiple_of(tp * half, 128), half)] = dr_mine[...]
    full_ref[:, pl.ds(pl.multiple_of((1 - tp) * half, 128), half)] = dr_came[...]
    g = g_ref[...].astype(full)
    probs = probs_ref[...]
    gates = [stat[:, 0:1], stat[:, 1:2]]
    total, inverse = stat[:, 2:3], stat[:, 3:4]
    ids_c = [ids[:, 0:1], ids[:, 1:2]]
    zero = jnp.zeros_like(total)

    def gate_of(number):
        return sum(jnp.where(ids_c[c] == number, gates[c], zero) for c in range(2))

    copy_gate = gate_of(copy_id)
    const_gate = [gate_of(copy_id + 1 + k) for k in range(2)]
    dots = [jnp.sum(g * second[...].astype(full), axis=-1, keepdims=True)]
    dots = dots + [jnp.sum(g * const[k : k + 1, :], axis=-1, keepdims=True) for k in range(2)]
    d_gates = []
    for c in range(2):
        d = dg_mine[:, c : c + 1] + dg_came[:, c : c + 1]
        for k in range(3):
            d = d + jnp.where(ids_c[c] == copy_id + k, dots[k], zero)
        d_gates.append(d)
    mean = d_gates[0] * gates[0] + d_gates[1] * gates[1]
    lane = lax.broadcasted_iota(jnp.int32, probs.shape, 1)
    d_probs = jnp.zeros_like(probs)
    for c in range(2):
        d_probs = d_probs + jnp.where(lane == ids_c[c], (d_gates[c] - mean) / total, 0.0)
    d_logits = probs * (d_probs - jnp.sum(probs * d_probs, axis=-1, keepdims=True))
    dlog_ref[...] = d_logits
    d_second = copy_gate * g + full_ref[...].astype(full)
    rest = d_logits
    for i in range(3):
        piece = rest.astype(low)
        rest = rest - piece.astype(full)
        d_second = d_second + mm(piece, router[...])
    unit = mixed[...] * inverse
    d_gain = jnp.sum(d_second * unit, axis=0, keepdims=True)
    d_unit = d_second * gain[...]
    d_mixed = g + inverse * (d_unit - unit * jnp.mean(d_unit * unit, axis=-1, keepdims=True))
    dmix_ref[...] = d_mixed
    d_attn = d_mixed.astype(low)
    dattn_ref[...] = d_attn
    do_ref[:, :half] = mm(d_attn, wm[...]).astype(low)
    do_ref[:, half:] = mm(d_attn, wo[...]).astype(low)
    count = probs.shape[1]
    pad = jnp.zeros((probs.shape[0], 128 - count), full)
    wide = lax.broadcasted_iota(jnp.int32, (probs.shape[0], 128), 1)
    table = jnp.concatenate([d_logits, pad], axis=1)
    table = jnp.where(wide == count + 2, const_gate[0], table)
    table = jnp.where(wide == count + 3, const_gate[1], table)
    rest = table.T[: count + 4, :]
    from_second = from_g = 0.0
    for i in range(3):
        piece = rest.astype(low)
        rest = rest - piece.astype(full)
        from_second = from_second + mm(piece, second[...])
        from_g = from_g + mm(piece, g_ref[...])
    row = lax.broadcasted_iota(jnp.int32, from_g.shape, 0)
    small = jnp.where(row < count, from_second, jnp.where(row >= count + 2, from_g, 0.0))
    small_ref[...] = jnp.where(row == count + 1, d_gain, small)


def keys_back_kernel(place, dq, dk, dv, x, wm, wo, own_ref, p0_ref, p1_ref, p2_ref, gain_ref):
    shard = place[0]
    rows, width = own_ref.shape
    half = wm.shape[2]
    gain = jnp.zeros((1, width), jnp.float32)
    lo = 0
    for out in (own_ref, p0_ref, p1_ref, p2_ref):
        here = slice(lo, lo + out.shape[0])
        lo = lo + out.shape[0]
        d = 0.0
        for m, grad in ((0, dq), (1, dk), (2, dv)):
            if m > 0 or out is own_ref:
                d = d + mm(grad[here, :half], wm[m ^ shard], NT)
                d = d + mm(grad[here, half:], wo[m ^ shard], NT)
        out[...] = d.astype(out.dtype)
        gain = gain + jnp.sum(d * unit_rows(x[here, :]), axis=0, keepdims=True)
    gain_ref[...] = gain


def weights_back_kernel(n_ref, dq, dk, dv, da_ref, o, tiny, mine_ref, other_ref, nt, at):
    rows = dq.shape[0]
    step = pl.program_id(0)

    @pl.when(step == 0)
    def start():
        nt[...] = n_ref[...].T
        at[...] = da_ref[...].T

    def put(value):
        value = value.astype(jnp.bfloat16)
        parts, half = mine_ref.shape[0], mine_ref.shape[2]
        part = value.shape[0] // parts
        for z in range(parts):
            mine_ref[z, :part, :] = value[z * part : (z + 1) * part, :half]
            other_ref[z, :part, :] = value[z * part : (z + 1) * part, half:]
            mine_ref[z, part:, :] = tiny[z, :, :half]
            other_ref[z, part:, :] = tiny[z, :, half:]

    pl.when(step == 0)(lambda: put(mm(nt[:, :rows], dq[...])))
    pl.when(step == 1)(lambda: put(mm(nt[...], dk[...])))
    pl.when(step == 2)(lambda: put(mm(nt[...], dv[...])))
    pl.when(step == 3)(lambda: put(mm(at[...], o[...])))


def weights_back(normed, dq, dk, dv, d_attn, o, tiny):
    total, width = normed.shape
    rows, half = dq.shape[0], width // 2
    parts, room = tiny.shape[1], tiny.shape[2]
    low = jnp.bfloat16
    out = pl.BlockSpec((None, parts, width // parts + room, half), lambda j: (j, 0, 0, 0))
    shape = ((4, parts, width // parts + room, half), low)
    return call(
        weights_back_kernel,
        "weights_back",
        [shape, shape],
        (normed, dq, dk, dv, d_attn, o, tiny),
        [pltpu.VMEM((width, total), low), pltpu.VMEM((width, rows), low)],
        grid=(4,),
        in_specs=[whole(total, width), whole(rows, width), whole(total, width), whole(total, width)]
        + [whole(rows, width), whole(rows, width)]
        + [pl.BlockSpec((None, parts, room, width), lambda j: (j, 0, 0, 0))],
        out_specs=[out, out],
        mib=60,
    )


def flip(x, axis, bit, size):
    return lax.ppermute(x, axis, [(i, i ^ bit) for i in range(size)])


def turn_gather(x, size, position):
    out = jnp.zeros((size,) + x.shape, x.dtype)
    out = lax.dynamic_update_index_in_dim(out, x, position, 0)
    for k in range(1, size):
        block = lax.ppermute(x, "ctx", [(i, (i + k) % size) for i in range(size)])
        out = lax.dynamic_update_index_in_dim(out, block, (position - k) % size, 0)
    return out


def turn_sum(x, size, position):
    total = lax.dynamic_index_in_dim(x, position, 0, keepdims=False).astype(jnp.float32)
    for k in range(1, size):
        block = lax.dynamic_index_in_dim(x, (position + k) % size, 0, keepdims=False)
        got = lax.ppermute(block, "ctx", [(i, (i + k) % size) for i in range(size)])
        total = total + got.astype(jnp.float32)
    return total


def far(x, k, shards_n, ctx_n):
    pairs = []
    for s in range(shards_n):
        for z in range(ctx_n):
            pairs.append((s * ctx_n + z, (s ^ k) * ctx_n + (z ^ 2)))
    return lax.ppermute(x, ("shard", "ctx"), pairs)


def three_parts(x):
    one = x.astype(jnp.bfloat16)
    rest = x - one.astype(jnp.float32)
    two = rest.astype(jnp.bfloat16)
    return jnp.stack([one, two, (rest - two.astype(jnp.float32)).astype(jnp.bfloat16)], axis=-2)


def with_rows(slots, values, at):
    extra = three_parts(values)
    after = slots.shape[-2] - at - extra.shape[-2]
    pads = ((0, 0), (at, after), (0, slots.shape[-1] - extra.shape[-1]))
    return slots + jnp.pad(extra, pads)


def row_values(slots, at):
    return jnp.sum(slots[:, at : at + 3, : slots.shape[1]].astype(jnp.float32), axis=1)


def by_core(
    tokens, gate_res, cotangent, parents, expert_ids, priority, w_qkv, w_out, w_router, attn_gain,
    ffn_gain, const_vec, w_gate_up, w_down,
):
    low, full = jnp.bfloat16, jnp.float32
    shard, ctx, tp = lax.axis_index("shard"), lax.axis_index("ctx"), lax.axis_index("tp")
    shards_n, ctx_n = lax.axis_size("shard"), lax.axis_size("ctx")
    trees, rows, width = tokens.shape
    rows_d = w_qkv.shape[0]
    part = width // 2
    seg = rows * ctx_n // parents.shape[1]
    own_segs = rows // seg
    edge = KEY_SEGS * seg - 2 * rows

    def own_tree(x):
        return lax.dynamic_index_in_dim(x, tp, 0, keepdims=False)

    def in_order(x, other, axis=0):
        return jnp.concatenate([jnp.where(tp == 0, x, other), jnp.where(tp == 0, other, x)], axis=axis)

    def both_trees(x, other):
        both = jnp.broadcast_to(x[None], (2,) + x.shape)
        return lax.dynamic_update_index_in_dim(both, other, 1 - tp, 0)

    def unit_of(x):
        x = x.astype(full)
        inverse = lax.rsqrt(jnp.mean(x * x, axis=-1, keepdims=True) + eps)
        return (x * inverse, inverse)

    def swap(x):
        return flip(x, "tp", 1, 2)

    def plus(x, y):
        return (x.astype(full) + y.astype(full)).astype(low)

    def my_half(x, which):
        return lax.dynamic_slice_in_dim(x, which * part, part, x.ndim - 1)

    x_own = lax.optimization_barrier(own_tree(tokens))
    ends = [(i, i + 1) for i in range(ctx_n - 1)]
    near = lax.ppermute(x_own, "ctx", ends)

    mine = jnp.stack([w_qkv[:, 0], w_qkv[:, 1], w_qkv[:, 2], w_out])
    small = jnp.concatenate([w_router.T, attn_gain[None], ffn_gain[None], const_vec.T], axis=0)
    all_experts = w_router.shape[1]
    mine = lax.dynamic_index_in_dim(mine, shard, 0, keepdims=False)
    mine = jnp.concatenate([mine, small.reshape(-1, part)], axis=0)
    turned = turn_gather(mine, ctx_n, ctx)
    matrix = turned[:, :rows_d].reshape(width, -1)
    small = turned[:, rows_d:].reshape(ctx_n, -1, rows_d).transpose(1, 0, 2).reshape(-1, width)
    router_t = small[:all_experts]
    gain_a = small[all_experts].astype(full)
    gain_f = small[all_experts + 1].astype(full)
    const_t = small[all_experts + 2 :].astype(full)

    mid = lax.ppermute(pin(near, matrix), "ctx", ends[1:])
    plane_pieces = [matrix] + [flip(matrix, "shard", k, shards_n) for k in range(1, shards_n)]
    capacity = trees * rows * 2 // all_experts
    experts = shards_n * w_gate_up.shape[1]
    padded = -(-(capacity + 3) // 16) * 16
    count = experts * padded
    flat = expert_ids.reshape(-1)
    order = (2 * priority[0, 0][:, None] + jnp.arange(2, dtype=jnp.int32)[None, :]).reshape(-1)
    earlier = (flat[:, None] == flat[None, :]) & (order[None, :] < order[:, None])
    ranks = jnp.sum(earlier.astype(jnp.int32), axis=1)
    kept = (flat < experts) & (ranks < capacity)
    piece = ((flat % 2) ^ (ctx // 2)) * shards_n + ((flat // 2) ^ shard)
    place = jnp.where(kept, piece * padded + ranks, -1).reshape(trees, rows, 2)
    place = jnp.where(tp == 0, place, place[::-1]).reshape(trees * rows, 2)
    place_t = place.T

    g_own = own_tree(cotangent)
    g_other = lax.dynamic_index_in_dim(cotangent, 1 - tp, 0, keepdims=False)
    g_half = my_half(jnp.concatenate([g_own, g_other], axis=0), tp)
    g_slots = spread(place_t, g_half, experts, padded, capacity)
    ids = own_tree(expert_ids)
    res = own_tree(gate_res)
    ids, res, router_t, gain_a, gain_f, const_t, mid, *g_slots = lax.optimization_barrier(
        (ids, res, router_t, gain_a[None], gain_f[None], const_t, mid, *g_slots)
    )
    farther = lax.ppermute(mid, "ctx", ends[2:])
    plane = jnp.stack(plane_pieces)

    plane_other = swap(plane)
    place3 = jnp.stack([shard, ctx, tp]).astype(jnp.int32)

    capacity = trees * rows * 2 // all_experts
    experts = shards_n * w_gate_up.shape[1]
    padded = -(-(capacity + 3) // 16) * 16
    count = experts * padded
    flat = expert_ids.reshape(-1)
    order = (2 * priority[0, 0][:, None] + jnp.arange(2, dtype=jnp.int32)[None, :]).reshape(-1)
    earlier = (flat[:, None] == flat[None, :]) & (order[None, :] < order[:, None])
    ranks = jnp.sum(earlier.astype(jnp.int32), axis=1)
    kept = (flat < experts) & (ranks < capacity)
    piece = ((flat % 2) ^ (ctx // 2)) * shards_n + ((flat // 2) ^ shard)
    place = jnp.where(kept, piece * padded + ranks, -1).reshape(trees, rows, 2)
    place = jnp.where(tp == 0, place, place[::-1]).reshape(trees * rows, 2)
    place_t = place.T

    g_own = own_tree(cotangent)
    g_other = lax.dynamic_index_in_dim(cotangent, 1 - tp, 0, keepdims=False)
    g_half = my_half(jnp.concatenate([g_own, g_other], axis=0), tp)
    g_slots = spread(place_t, g_half, experts, padded, capacity)
    g_near = jnp.stack(g_slots[:shards_n])
    g_far = flip(pin(jnp.stack(g_slots[shards_n:]), mid), "ctx", 2, ctx_n)
    plane_other = swap(plane)
    place3 = jnp.stack([shard, ctx, tp]).astype(jnp.int32)

    g_near = jnp.stack(g_slots[:shards_n])
    g_far = flip(jnp.stack(g_slots[shards_n:]), "ctx", 2, ctx_n)

    held, gu, dn = lax.optimization_barrier((near, w_gate_up, w_down))
    lower = ctx < 2
    first = jnp.stack([gu[:, 0, 0], gu[:, 0, 1], dn[:, 0]])
    second_e = jnp.stack([gu[:, 1, 0], gu[:, 1, 1], dn[:, 1]])
    rows_own = jnp.where(lower, first, second_e)
    rows_two = flip(pin(jnp.where(lower, second_e, first), farther, g_far), "ctx", 2, ctx_n)
    rows_one = flip(pin(rows_own, farther, g_far), "ctx", 1, ctx_n)

    total = 3 * rows + edge
    q, kv, normed, x_all = call(
        project_kernel,
        "project",
        [((rows, width), low), ((total, 2 * width), low), ((total, width), low), ((total, width), low)],
        (place3, x_own, near, mid, farther, gain_a, plane, plane_other),
        in_specs=[whole(rows, width)] * 4
        + [whole(1, width), whole(4, width, part), whole(4, width, part)],
        prefetch=True,
    )

    seg_id = ctx * own_segs + jnp.arange(own_segs, dtype=jnp.int32)
    parent = jnp.take(own_tree(parents), seg_id)
    leaf = (seg_id >= KEY_SEGS).astype(jnp.int32)
    info = jnp.stack([jnp.minimum(seg_id, TRUNK), jnp.where(leaf > 0, parent, TRUNK), leaf], axis=1)
    half_pairs = width // 256
    ahead = attend(info, q, kv, seg, 0, half_pairs)
    o_low, lse = attend(info, q, kv, seg, half_pairs, half_pairs, ahead)
    g_pairs = jnp.stack([g_near, pin(g_far, ahead[0])], axis=1)
    g_got = [g_pairs[0]] + [flip(g_pairs[k], "shard", k, shards_n) for k in range(1, shards_n)]
    o_low = pin(o_low, rows_one, rows_two, *g_got)
    g_in = jnp.stack(g_got, axis=1).reshape(2, shards_n * padded, part)
    g_out = swap(g_in)

    one_half = ((rows, part), low)
    mixed, second, second_mine, second_other, probs, stat, gates_t = call(
        settle_kernel,
        "settle",
        [
            ((rows, width), full), ((rows, width), low), one_half, one_half,
            ((rows, all_experts), full), ((rows, 8), full), ((8, rows), full),
        ],
        (place3, o_low, x_own, plane, plane_other, gain_f, router_t, res, ids),
        in_specs=[
            whole(rows, width), whole(rows, width), chosen(3, width, part), chosen(3, width, part),
            whole(1, width), whole(all_experts, width), whole(rows, all_experts), whole(rows, 2),
        ],
        prefetch=True,
    )
    second_half = jnp.concatenate([second_mine, swap(second_other)], axis=0)
    gates_both = jnp.concatenate([gates_t, swap(gates_t)], axis=1)

    rows_three = flip(pin(rows_two, o_low), "ctx", 1, ctx_n)
    weights = (rows_own, rows_one, rows_two, rows_three)
    slots = spread_gated(place3, place_t, second_half, experts, padded, capacity, gates_both)
    x_far = [far(slots[shards_n + k], k, shards_n, ctx_n) for k in range(shards_n)]
    x_near = [slots[0]] + [flip(slots[k], "shard", k, shards_n) for k in range(1, shards_n)]

    def experts_on(pieces, gs, prev):
        x = jnp.concatenate(pieces, axis=0)
        return expert_pass(place3[1:], capacity, shards_n, (x, swap(x)), gs, weights, prev)

    def answers(mine, other):
        return plus(mine, swap(other)).reshape(shards_n, padded, part)

    x_near[0] = pin(x_near[0], rows_three)
    on1, ox1, sn1, sx1, dw = experts_on(x_near, (g_in[0], g_out[0]), None)
    x_far = list(lax.optimization_barrier((*x_far, sn1))[:-1])
    on2, ox2, sn2, sx2, dw = experts_on(x_far, (g_in[1], g_out[1]), dw)
    ds_far = answers(sn2, sx2)
    ds_near = answers(sn1, sx1)
    ds_far = [far(ds_far[k], k, shards_n, ctx_n) for k in range(shards_n)]
    ds_near = [ds_near[0]] + [flip(ds_near[k], "shard", k, shards_n) for k in range(1, shards_n)]

    rows_tn = (((0,), (0,)), ((), ()))
    d_routed, d_routed_other, d_pairs, d_pairs_other = gather(
        place3, place, gates_both[4][:, None], ds_near + ds_far, capacity, True
    )
    d_mixed, d_attn, d_o, d_logits, d_small = call(
        functools.partial(settle_back_kernel, experts + 1),
        "settle_back",
        [
            ((rows, width), full), ((rows, width), low), ((rows, width), low),
            ((rows, all_experts), full), ((all_experts + 4, width), full),
        ],
        (
            place3, d_routed, swap(d_routed_other), d_pairs, swap(d_pairs_other), g_own, mixed, second,
            probs, stat, ids, const_t, router_t, gain_f, plane, plane_other,
        ),
        [pltpu.VMEM((rows, width), low)],
        in_specs=[
            whole(rows, part), whole(rows, part), whole(rows, 2), whole(rows, 2), whole(rows, width),
            whole(rows, width), whole(rows, width), whole(rows, all_experts), whole(rows, 8),
            whole(rows, 2), whole(2, width), whole(all_experts, width), whole(1, width),
            chosen(3, width, part), chosen(3, width, part),
        ],
        prefetch=True,
        mib=60,
    )

    ox1, ox2, held = lax.optimization_barrier((ox1, ox2, d_routed))
    out_near = plus(on1, swap(ox1)).reshape(shards_n, padded, part)
    out_far = plus(on2, swap(ox2)).reshape(shards_n, padded, part)

    got = flip(pin(dw[2:], d_routed), "ctx", 1, ctx_n)

    third = width // 384
    back = attend_back(info, q, kv, o_low, d_o, lse, seg, 0, third)
    out_near, out_far, q_later, held = lax.optimization_barrier((out_near, out_far, q, back[0]))
    back = attend_back(info, q_later, kv, o_low, d_o, lse, seg, third, third, back)
    out_near, out_far = (out_near, out_far)
    out_cross = flip(out_far, "ctx", 2, ctx_n)
    q_later = pin(q, back[0])
    dq, dk, dv = attend_back(info, q_later, kv, o_low, d_o, lse, seg, 2 * third, third, back)
    got = pin(got, dq)
    sent_rows = plus(dw[1], got[1])
    came_rows = flip(sent_rows, "ctx", 2, ctx_n)
    out_pairs = jnp.stack([out_near, pin(out_cross, dq)], axis=1)
    out_got = [out_pairs[0]] + [flip(out_pairs[k], "shard", k, shards_n) for k in range(1, shards_n)]
    d_near, part0, part1, part2, d_gain_a = call(
        keys_back_kernel,
        "keys_back",
        [
            ((rows, width), full), ((rows, width), low), ((rows, width), low), ((edge, width), low),
            ((1, width), full),
        ],
        (pin(place3, sent_rows), dq, dk, dv, x_all, plane, plane_other),
        in_specs=[
            whole(rows, width), whole(total, width), whole(total, width), whole(total, width),
            whole(4, width, part), whole(4, width, part),
        ],
        prefetch=True,
        mib=60,
    )

    tiny = jnp.concatenate([d_small[:all_experts], d_gain_a, d_small[all_experts + 1 :]], axis=0)
    tiny = tiny.reshape(4, 2, 2, ctx_n, rows_d).transpose(0, 3, 1, 2, 4).reshape(4, ctx_n, 2, 2 * rows_d)
    tiny = jnp.where(tp == 0, tiny, tiny[:, :, ::-1]).reshape(4, ctx_n, 1, width).astype(low)
    tiny = jnp.pad(tiny, ((0, 0), (0, 0), (0, 15), (0, 0)))
    shared_mine, shared_other = weights_back(normed, dq, dk, dv, d_attn, o_low, tiny)

    def down(x, step):
        return lax.ppermute(x, "ctx", [(i, i - 1) for i in range(ctx_n - step, ctx_n)])

    came = down(part0, 1)
    shared_other = pin(shared_other, came, *out_got, came_rows)
    payload = jnp.where(ctx == 3, part1, plus(part0, came))
    came = down(payload, 2)
    shared = plus(pin(shared_mine, payload), swap(shared_other))

    def numbered(k):
        return lax.dynamic_index_in_dim(shared, shard ^ k, 0, keepdims=False)

    plane_parts = [flip(numbered(k), "shard", k, shards_n) for k in range(1, shards_n)]
    plane_sum = numbered(0).astype(full)
    for got_part in plane_parts:
        plane_sum = plane_sum + got_part.astype(full)
    came = pin(came, plane_parts[0])
    part2 = jnp.pad(part2, ((0, rows - edge), (0, 0)))
    came = down(jnp.where(ctx == 3, part2, jnp.where(ctx == 2, plus(part1, came), plus(part0, came))), 3)
    base = jnp.where(ctx == 0, part0, jnp.where(ctx == 1, part1, part2)).astype(full)
    extra = jnp.where(ctx == 3, 0.0, base + came.astype(full))
    came_rows = pin(came_rows, plane_parts[0]).astype(full)
    kept_rows = dw[0].astype(full) + got[0].astype(full)
    first = jnp.where(lower, kept_rows, came_rows)
    second_e = jnp.where(lower, came_rows, kept_rows)
    d_gate_up = jnp.stack(
        [jnp.stack([first[0], first[1]], axis=1), jnp.stack([second_e[0], second_e[1]], axis=1)], axis=1
    )
    d_down = jnp.stack([first[2], second_e[2]], axis=1)
    d_normed = d_near + extra
    unit_own, inv_own = unit_of(x_own)
    gain_a = gain_a[0]
    d_first = d_normed * gain_a
    d_tokens = d_mixed + inv_own * (
        d_first - unit_own * jnp.mean(d_first * unit_own, axis=-1, keepdims=True)
    )

    total = turn_sum(plane_sum.astype(low), ctx_n, ctx).astype(low)
    out_got = [pin(o, plane_parts[0]) for o in out_got]
    gate_columns = jnp.stack([gates_both[0], gates_both[1]], axis=1)
    combined, combined_other = gather(place3, place, gate_columns, out_got, capacity, False)
    combined = in_order(combined, swap(combined_other), 1).astype(full)
    second_f = second.astype(full)

    def gate_of(number):
        return jnp.sum(jnp.where(ids == number, stat[:, :2], 0.0), axis=1, keepdims=True)

    copy_gate = gate_of(experts + 1)
    const_gate = jnp.concatenate([gate_of(experts + 2), gate_of(experts + 3)], axis=1)
    mixed_out = (
        mixed
        + combined
        + copy_gate * second_f
        + const_gate[:, :1] * const_t[0][None]
        + const_gate[:, 1:] * const_t[1][None]
    )
    total = pin(total, mixed_out, d_tokens)
    d_tokens_other = swap(d_tokens)
    four = [total] + [flip(total, "shard", k, shards_n) for k in range(1, shards_n)]
    four = jnp.stack([pin(f, d_tokens_other) for f in four])
    four = jnp.stack(
        [lax.dynamic_index_in_dim(four, m ^ shard, 0, keepdims=False) for m in range(4)]
    )
    d_q, d_k, d_v, d_w_out = [four[m, :rows_d].astype(full) for m in range(4)]
    d_w_qkv = jnp.stack([d_q, d_k, d_v], axis=1)
    tiny = four[:, rows_d]
    tiny = both_trees(tiny, swap(tiny)).transpose(1, 0, 2).reshape(16, rows_d).astype(full)

    return (
        both_trees(mixed_out, swap(mixed_out)),
        both_trees(d_tokens, d_tokens_other),
        both_trees(d_logits, swap(d_logits)),
        d_w_qkv,
        d_w_out,
        tiny[:all_experts].T,
        tiny[all_experts],
        tiny[all_experts + 1],
        tiny[all_experts + 2 :].T,
        d_gate_up,
        d_down,
    )


def program(tokens, gate_res, cotangent, parents, expert_ids, priority, w_qkv, *weights):
    trees, rows, width = tokens.shape
    ctx_n = lax.axis_size("ctx")
    seg = rows * ctx_n // parents.shape[1]
    fits = (
        ctx_n == 4
        and lax.axis_size("shard") == 4
        and lax.axis_size("tp") == 2
        and trees == 2
        and seg == 128
        and rows % seg == 0
        and 2 * rows < KEY_SEGS * seg <= 3 * rows
        and weights[-1].shape[1] == 2
    )
    chosen = by_core if fits else shards
    return chosen(tokens, gate_res, cotangent, parents, expert_ids, priority, w_qkv, *weights)


def solution(mesh):
    return jax.shard_map(
        program,
        mesh=mesh,
        in_specs=(
            P("shard", "ctx", None),
            P("shard", "ctx", None),
            P("shard", "ctx", None),
            P("shard", None),
            P("shard", "ctx", None),
            P("shard", "ctx", None),
            P("ctx", None, "tp"),
            P("ctx", "tp"),
            P("ctx", None),
            P("ctx"),
            P("ctx"),
            P("ctx", None),
            P("ctx", "shard", None, "tp"),
            P("ctx", "shard", "tp"),
        ),
        out_specs=(
            P("shard", "ctx", None),
            P("shard", "ctx", None),
            P("shard", "ctx", None),
            P("ctx", None, "tp"),
            P("ctx", "tp"),
            P("ctx", None),
            P("ctx"),
            P("ctx"),
            P("ctx", None),
            P("ctx", "shard", None, "tp"),
            P("ctx", "shard", "tp"),
        ),
        check_vma=False,
    )
```

```python
import functools
import math

import jax
import jax.numpy as jnp
from jax import lax
from jax.experimental import pallas as pl
from jax.experimental.pallas import tpu as pltpu
from jax.sharding import PartitionSpec as P

HEAD_DIM = 64


eps = 1e-06
score_scale = 0.125


def ancestry(parent_row):
    seg_count = parent_row.shape[0]
    position = jnp.arange(seg_count, dtype=jnp.int32)
    linked = (parent_row[:, None] == position[None, :]) | (position[:, None] == position[None, :])
    reach = linked.astype(jnp.float32)
    for repeat in range(seg_count.bit_length()):
        reach = jnp.minimum(jnp.dot(reach, reach, precision=lax.Precision.HIGHEST), 1.0)
    return reach


def path_rows(positions, seg_len, ancestors):
    onehot = (
        (positions // seg_len)[:, None] == jnp.arange(ancestors.shape[0], dtype=jnp.int32)[None, :]
    ).astype(jnp.float32)
    return jnp.dot(onehot, ancestors)


def allowed_block(query_rows, query_pos, key_start, key_count, seg_len):
    key_pos = key_start + jnp.arange(key_count, dtype=jnp.int32)
    key_onehot = (
        (key_pos // seg_len)[:, None] == jnp.arange(query_rows.shape[1], dtype=jnp.int32)[None, :]
    ).astype(jnp.float32)
    linked = jnp.dot(query_rows, key_onehot.T) > 0.5
    return (linked & (key_pos[None, :] <= query_pos[:, None]))[None]


def slot_table(picked_ids, ranking, experts, capacity):
    count_rows = picked_ids.shape[0]
    flat_ids = picked_ids.reshape(-1)
    rank_key = (2 * ranking[:, None] + jnp.arange(2, dtype=jnp.int32)[None, :]).reshape(-1)
    earlier = (flat_ids[:, None] == flat_ids[None, :]) & (rank_key[None, :] < rank_key[:, None])
    ranks = jnp.sum(earlier.astype(jnp.int32), axis=1)
    kept = (flat_ids < experts) & (ranks < capacity)
    target = jnp.where(kept, flat_ids * capacity + ranks, -1).reshape(count_rows, 2)
    slot_index = jnp.arange(experts * capacity, dtype=jnp.int32)
    return slot_index[None, :, None] == target.T[:, None, :]


def block_scores(queries, keys_blk):
    return (
        jnp.einsum("qhe,khe->hqk", queries, keys_blk, preferred_element_type=jnp.float32)
        * score_scale
    )


def softmax_grads(queries, grads_out, stat_lse, stat_delta, keys_blk, values_blk, mask):
    prob = jnp.where(mask, jnp.exp(block_scores(queries, keys_blk) - stat_lse[:, :, None]), 0.0)
    dprob = jnp.einsum("qhe,khe->hqk", grads_out, values_blk, preferred_element_type=jnp.float32)
    dscore = (prob * (dprob - stat_delta[:, :, None])).astype(jnp.bfloat16)
    return (prob.astype(jnp.bfloat16), dscore)


def shards(
    tokens,
    gate_res,
    cotangent,
    parents,
    expert_ids,
    priority,
    w_qkv,
    w_out,
    w_router,
    attn_gain,
    ffn_gain,
    const_vec,
    w_gate_up,
    w_down,
):
    full_qkv, full_out, full_router, full_again, full_fgain, full_const, full_gu, full_down = (
        lax.all_gather(w_qkv, "ctx", axis=0, tiled=True),
        lax.all_gather(w_out, "ctx", axis=0, tiled=True),
        lax.all_gather(w_router, "ctx", axis=0, tiled=True),
        lax.all_gather(attn_gain, "ctx", axis=0, tiled=True),
        lax.all_gather(ffn_gain, "ctx", axis=0, tiled=True),
        lax.all_gather(const_vec, "ctx", axis=0, tiled=True),
        lax.all_gather(w_gate_up, "ctx", axis=0, tiled=True),
        lax.all_gather(w_down, "ctx", axis=0, tiled=True),
    )
    tree_count, rows, model_width = tokens.shape
    tok_rows = tree_count * rows
    inputs = tokens.reshape(tok_rows, model_width).astype(jnp.float32)
    local_width = full_out.shape[1]
    local_heads = local_width // HEAD_DIM
    ctx_index = lax.axis_index("ctx")
    tree_len = rows * lax.axis_size("ctx")
    ancestors_all = jax.vmap(ancestry)(parents)
    seg_len = tree_len // parents.shape[1]
    key_block = math.gcd(tree_len, 512)
    starts = jnp.arange(tree_len // key_block, dtype=jnp.int32) * key_block
    key_start_own = ctx_index * rows
    query_pos = key_start_own + jnp.arange(rows, dtype=jnp.int32)
    query_rows_all = jax.vmap(lambda anc: path_rows(query_pos, seg_len, anc))(ancestors_all)
    inv_first = lax.rsqrt(jnp.mean(inputs * inputs, axis=-1, keepdims=True) + eps)
    first_unit = inputs * inv_first
    first_gain = full_again.astype(jnp.float32)
    normed = (first_unit * first_gain).astype(jnp.bfloat16)
    projected = jnp.einsum("nd,dke->nke", normed, full_qkv, preferred_element_type=jnp.float32)
    q_low = projected[:, 0].astype(jnp.bfloat16)
    k_low = projected[:, 1].astype(jnp.bfloat16)
    v_low = projected[:, 2].astype(jnp.bfloat16)
    keys_all, values_all = (
        lax.all_gather(k_low.reshape(tree_count, rows, local_width), "ctx", axis=1, tiled=True),
        lax.all_gather(v_low.reshape(tree_count, rows, local_width), "ctx", axis=1, tiled=True),
    )
    q_heads = q_low.reshape(tree_count, rows, local_heads, HEAD_DIM)
    k_heads = keys_all.reshape(tree_count, tree_len, local_heads, HEAD_DIM)
    v_heads = values_all.reshape(tree_count, tree_len, local_heads, HEAD_DIM)

    def tree_forward(q_one, k_one, v_one, rows_one):

        def stat_step(carry, start):
            running_top, running_sum = carry
            keys_blk = lax.dynamic_slice_in_dim(k_one, start, key_block, 0)
            mask = allowed_block(rows_one, query_pos, start, key_block, seg_len)
            masked = jnp.where(mask, block_scores(q_one, keys_blk), -1e30)
            new_top = jnp.maximum(running_top, jnp.max(masked, axis=2))
            expo = jnp.where(mask, jnp.exp(masked - new_top[:, :, None]), 0.0)
            running_sum = running_sum * jnp.exp(running_top - new_top) + jnp.sum(expo, axis=2)
            return ((new_top, running_sum), None)

        start_top = jnp.full((local_heads, rows), -1e30, jnp.float32)
        (final_top, final_sum), unused = lax.scan(
            stat_step, (start_top, jnp.zeros_like(start_top)), starts
        )
        lse_one = final_top + jnp.log(final_sum)

        def out_step(accum, start):
            keys_blk = lax.dynamic_slice_in_dim(k_one, start, key_block, 0)
            values_blk = lax.dynamic_slice_in_dim(v_one, start, key_block, 0)
            mask = allowed_block(rows_one, query_pos, start, key_block, seg_len)
            prob = jnp.where(
                mask, jnp.exp(block_scores(q_one, keys_blk) - lse_one[:, :, None]), 0.0
            ).astype(jnp.bfloat16)
            return (
                accum
                + jnp.einsum("hqk,khe->qhe", prob, values_blk, preferred_element_type=jnp.float32),
                None,
            )

        attended_one, unused = lax.scan(
            out_step, jnp.zeros((rows, local_heads, HEAD_DIM), jnp.float32), starts
        )
        return (attended_one, lse_one)

    attended, lse = jax.vmap(tree_forward)(q_heads, k_heads, v_heads, query_rows_all)
    attended_low = attended.reshape(tok_rows, local_width).astype(jnp.bfloat16)
    attn_part = jnp.einsum("nh,dh->nd", attended_low, full_out, preferred_element_type=jnp.float32)
    attn_sum = lax.psum(attn_part.astype(jnp.bfloat16), "tp").astype(jnp.float32)
    mixed = inputs + attn_sum
    inv_second = lax.rsqrt(jnp.mean(mixed * mixed, axis=-1, keepdims=True) + eps)
    second_unit = mixed * inv_second
    second_gain = full_fgain.astype(jnp.float32)
    second_low = (second_unit * second_gain).astype(jnp.bfloat16)
    second_float = second_low.astype(jnp.float32)
    logits = jnp.dot(
        second_low, full_router, preferred_element_type=jnp.float32
    ) + gate_res.reshape(tok_rows, -1)
    expo_logits = jnp.exp(logits - jnp.max(logits, axis=-1, keepdims=True))
    probs = expo_logits / jnp.sum(expo_logits, axis=-1, keepdims=True)
    experts = lax.axis_size("shard") * w_gate_up.shape[1]
    every_expert = experts + 4
    capacity = tok_rows * 2 // every_expert
    picked_ids = expert_ids.reshape(tok_rows, 2)
    selector = (picked_ids[:, :, None] == jnp.arange(every_expert, dtype=jnp.int32)).astype(
        jnp.float32
    )
    picked = jnp.sum(selector * probs[:, None, :], axis=-1)
    picked_total = jnp.sum(picked, axis=-1, keepdims=True)
    gates = picked / picked_total
    table = slot_table(picked_ids, priority[0, 0], experts, capacity).astype(jnp.bfloat16)
    routed = table[0] + table[1]
    send_slots = jnp.einsum(
        "et,td->ed", routed, second_low, preferred_element_type=jnp.float32
    ).astype(jnp.bfloat16)
    send_slots = send_slots.reshape(experts, 1, capacity, model_width)
    arrived = lax.all_to_all(send_slots, "shard", split_axis=0, concat_axis=1, tiled=True)
    gate_up = jnp.einsum("jsrd,djgf->jsrgf", arrived, full_gu, preferred_element_type=jnp.float32)
    hidden_low = (jax.nn.silu(gate_up[:, :, :, 0]) * gate_up[:, :, :, 1]).astype(jnp.bfloat16)
    partial_out = jnp.einsum(
        "jsrf,djf->jsrd", hidden_low, full_down, preferred_element_type=jnp.float32
    )
    summed = lax.psum(partial_out.astype(jnp.bfloat16), "tp")
    returned = lax.all_to_all(summed, "shard", split_axis=1, concat_axis=0, tiled=True)
    returned, kept_slots = (returned, arrived)
    out_slots = returned.reshape(experts * capacity, model_width)
    ffn_values = jnp.einsum("cet,ed->ctd", table, out_slots, preferred_element_type=jnp.float32)
    copy_flag = selector[:, :, experts + 1]
    const_flags = selector[:, :, experts + 2 :]
    const_float = full_const.astype(jnp.float32)
    fixed_terms = jnp.einsum(
        "nck,dk->cnd", const_flags, const_float, precision=lax.Precision.HIGHEST
    )
    values_pair = ffn_values + copy_flag.T[:, :, None] * second_float[None] + fixed_terms
    mixed_out = mixed + jnp.sum(gates.T[:, :, None] * values_pair, axis=0)
    grad_out = cotangent.reshape(tok_rows, model_width).astype(jnp.float32)
    weighted = gates.T[:, :, None] * grad_out[None]
    d_gates = jnp.einsum("cnd,nd->nc", values_pair, grad_out)
    d_const = jnp.einsum("nck,cnd->dk", const_flags, weighted, precision=lax.Precision.HIGHEST)
    d_out_slots = jnp.einsum(
        "cet,ctd->ed", table.astype(jnp.float32), weighted, precision=lax.Precision.HIGHEST
    )
    d_out_low = d_out_slots.astype(jnp.bfloat16).reshape(experts, 1, capacity, model_width)
    d_picked = (d_gates - jnp.sum(d_gates * gates, axis=-1, keepdims=True)) / picked_total
    d_probs = jnp.einsum("nc,nck->nk", d_picked, selector)
    d_logits = probs * (d_probs - jnp.sum(probs * d_probs, axis=-1, keepdims=True))
    d_router_w = jnp.dot(second_float.T, d_logits, precision=lax.Precision.HIGHEST)
    d_second = jnp.sum(copy_flag.T[:, :, None] * weighted, axis=0)
    d_second = d_second + jnp.dot(
        d_logits, full_router.astype(jnp.float32).T, precision=lax.Precision.HIGHEST
    )
    arrived_grad = lax.all_to_all(d_out_low, "shard", split_axis=0, concat_axis=1, tiled=True)
    gate_up = jnp.einsum(
        "jsrd,djgf->jsrgf", kept_slots, full_gu, preferred_element_type=jnp.float32
    )
    gate_part = gate_up[:, :, :, 0]
    up_part = gate_up[:, :, :, 1]
    sigma = jax.nn.sigmoid(gate_part)
    silu_part = gate_part * sigma
    hidden_low = (silu_part * up_part).astype(jnp.bfloat16)
    d_hidden = jnp.einsum(
        "jsrd,djf->jsrf", arrived_grad, full_down, preferred_element_type=jnp.float32
    )
    d_gate_part = d_hidden * up_part * sigma * (1.0 + gate_part * (1.0 - sigma))
    d_up_part = d_hidden * silu_part
    d_gate_up_low = jnp.stack([d_gate_part, d_up_part], axis=3).astype(jnp.bfloat16)
    d_slot_part = jnp.einsum(
        "jsrgf,djgf->jsrd", d_gate_up_low, full_gu, preferred_element_type=jnp.float32
    )
    d_slot_sum = lax.psum(d_slot_part.astype(jnp.bfloat16), "tp")
    d_slot_back = lax.all_to_all(d_slot_sum, "shard", split_axis=1, concat_axis=0, tiled=True)
    d_gate_up_w = jnp.einsum(
        "jsrd,jsrgf->djgf", kept_slots, d_gate_up_low, preferred_element_type=jnp.float32
    )
    d_down_w = jnp.einsum(
        "jsrd,jsrf->djf", arrived_grad, hidden_low, preferred_element_type=jnp.float32
    )
    d_second = d_second + jnp.einsum(
        "et,ed->td",
        routed,
        d_slot_back.reshape(experts * capacity, model_width),
        preferred_element_type=jnp.float32,
    )
    d_second_gain = jnp.sum(d_second * second_unit, axis=0)
    d_second_unit = d_second * second_gain
    d_mixed = grad_out + inv_second * (
        d_second_unit - second_unit * jnp.mean(d_second_unit * second_unit, axis=-1, keepdims=True)
    )
    d_attn_low = d_mixed.astype(jnp.bfloat16)
    d_out_w = jnp.einsum("nd,nh->dh", d_attn_low, attended_low, preferred_element_type=jnp.float32)
    d_attended = jnp.einsum("nd,dh->nh", d_attn_low, full_out, preferred_element_type=jnp.float32)
    do_low = d_attended.astype(jnp.bfloat16)
    do_heads = do_low.reshape(tree_count, rows, local_heads, HEAD_DIM)
    delta = jnp.einsum("tqhe,tqhe->thq", do_heads.astype(jnp.float32), attended)

    def tree_both(q_one, k_one, v_one, do_one, lse_one, delta_one, rows_one):

        def both_step(dq_accum, start):
            keys_blk = lax.dynamic_slice_in_dim(k_one, start, key_block, 0)
            values_blk = lax.dynamic_slice_in_dim(v_one, start, key_block, 0)
            mask = allowed_block(rows_one, query_pos, start, key_block, seg_len)
            prob_low, dscore = softmax_grads(
                q_one, do_one, lse_one, delta_one, keys_blk, values_blk, mask
            )
            dq_accum = dq_accum + jnp.einsum(
                "hqk,khe->qhe", dscore, keys_blk, preferred_element_type=jnp.float32
            )
            dkey = (
                jnp.einsum("hqk,qhe->khe", dscore, q_one, preferred_element_type=jnp.float32)
                * score_scale
            )
            dval = jnp.einsum("hqk,qhe->khe", prob_low, do_one, preferred_element_type=jnp.float32)
            return (
                dq_accum,
                jnp.stack(
                    [dkey.reshape(key_block, local_width), dval.reshape(key_block, local_width)],
                    axis=1,
                ),
            )

        dq_one, terms_one = lax.scan(
            both_step, jnp.zeros((rows, local_heads, HEAD_DIM), jnp.float32), starts
        )
        return (dq_one, terms_one.reshape(tree_len, 2, local_width))

    dq_total, key_terms = jax.vmap(tree_both)(
        q_heads, k_heads, v_heads, do_heads, lse, delta, query_rows_all
    )
    key_sums = lax.psum_scatter(
        key_terms.astype(jnp.bfloat16), "ctx", scatter_dimension=1, tiled=True
    ).astype(jnp.float32)
    key_grad = key_sums[:, :, 0].reshape(tok_rows, local_width)
    value_grad = key_sums[:, :, 1].reshape(tok_rows, local_width)
    query_grad = (dq_total * score_scale).reshape(tok_rows, local_width)
    d_qkv_low = jnp.stack([query_grad, key_grad, value_grad], axis=1).astype(jnp.bfloat16)
    d_qkv_w = jnp.einsum("nd,nke->dke", normed, d_qkv_low, preferred_element_type=jnp.float32)
    d_normed_part = jnp.einsum(
        "nke,dke->nd", d_qkv_low, full_qkv, preferred_element_type=jnp.float32
    )
    d_normed = lax.psum(d_normed_part.astype(jnp.bfloat16), "tp").astype(jnp.float32)
    d_first_gain = jnp.sum(d_normed * first_unit, axis=0)
    d_first_unit = d_normed * first_gain
    d_inputs = d_mixed + inv_first * (
        d_first_unit - first_unit * jnp.mean(d_first_unit * first_unit, axis=-1, keepdims=True)
    )
    summed_grads = (
        lax.psum_scatter(
            d_qkv_w.astype(jnp.bfloat16), "ctx", scatter_dimension=0, tiled=True
        ).astype(jnp.float32),
        lax.psum_scatter(
            d_out_w.astype(jnp.bfloat16), "ctx", scatter_dimension=0, tiled=True
        ).astype(jnp.float32),
        lax.psum_scatter(
            d_router_w.astype(jnp.bfloat16), "ctx", scatter_dimension=0, tiled=True
        ).astype(jnp.float32),
        lax.psum_scatter(
            d_first_gain.astype(jnp.bfloat16), "ctx", scatter_dimension=0, tiled=True
        ).astype(jnp.float32),
        lax.psum_scatter(
            d_second_gain.astype(jnp.bfloat16), "ctx", scatter_dimension=0, tiled=True
        ).astype(jnp.float32),
        lax.psum_scatter(
            d_const.astype(jnp.bfloat16), "ctx", scatter_dimension=0, tiled=True
        ).astype(jnp.float32),
        lax.psum_scatter(
            d_gate_up_w.astype(jnp.bfloat16), "ctx", scatter_dimension=0, tiled=True
        ).astype(jnp.float32),
        lax.psum_scatter(
            d_down_w.astype(jnp.bfloat16), "ctx", scatter_dimension=0, tiled=True
        ).astype(jnp.float32),
    )
    shared = (
        lax.psum(summed_grads[0].astype(jnp.bfloat16), "shard").astype(jnp.float32),
        lax.psum(summed_grads[1].astype(jnp.bfloat16), "shard").astype(jnp.float32),
        lax.psum(summed_grads[2].astype(jnp.bfloat16), "shard").astype(jnp.float32),
        lax.psum(summed_grads[3].astype(jnp.bfloat16), "shard").astype(jnp.float32),
        lax.psum(summed_grads[4].astype(jnp.bfloat16), "shard").astype(jnp.float32),
        lax.psum(summed_grads[5].astype(jnp.bfloat16), "shard").astype(jnp.float32),
    )
    out_rows = mixed_out.reshape(tree_count, rows, model_width)
    grad_rows = d_inputs.reshape(tree_count, rows, model_width)
    logit_rows = d_logits.reshape(tree_count, rows, every_expert)
    return (
        out_rows,
        grad_rows,
        logit_rows,
        shared[0],
        shared[1],
        shared[2],
        shared[3],
        shared[4],
        shared[5],
        summed_grads[6],
        summed_grads[7],
    )


NT = (((1,), (1,)), ((), ()))
NN = (((1,), (0,)), ((), ()))
TRUNK = 8
KEY_SEGS = 12
PIECE = 256
SENT = (0, 2, 1, 3)


def mm(a, b, dims=NN):
    return lax.dot_general(a, b, dims, preferred_element_type=jnp.float32)


def stacked(rows, half):
    first = lax.broadcasted_iota(jnp.int32, rows.shape, 1) < half
    blank = jnp.zeros_like(rows)
    return jnp.concatenate([jnp.where(first, rows, blank), jnp.where(first, blank, rows)], axis=0)


def unstack(wide, half, seg):
    return jnp.concatenate([wide[:half, :seg], wide[half:, seg:]], axis=0)


def causal(seg):
    row = lax.broadcasted_iota(jnp.int32, (seg, 2 * seg), 0)
    col = lax.broadcasted_iota(jnp.int32, (seg, 2 * seg), 1)
    return row <= jnp.where(col >= seg, col - seg, col)


def attend_kernel(own, seg, half, more, info, q_ref, k_ref, v_ref, *rest):
    o_ref, lse_ref, s_ref, p_ref = rest[2 * more :]
    trunk = TRUNK * seg
    allowed = causal(seg)
    v_trunk = v_ref[own : own + trunk, :].T

    def one(i, unused):
        count, branch, leaf = info[i, 0], info[i, 1], info[i, 2]
        here = pl.ds(pl.multiple_of(i * seg, seg), seg)
        there = pl.ds(pl.multiple_of(own + branch * seg, seg), seg)
        qs = stacked(q_ref[here, :] * 0.125, half)
        s_ref[:trunk, :] = mm(k_ref[own : own + trunk, :], qs, NT)
        s_branch = mm(k_ref[there, :], qs, NT)
        s_own = jnp.where(allowed, mm(k_ref[here, :], qs, NT), -1e30)
        biases = [jnp.where(kb < count, 0.0, -1e30) for kb in range(TRUNK)]
        leaf_bias = jnp.where(leaf > 0, 0.0, -1e30)
        top = jnp.max(s_own, axis=0, keepdims=True)
        top = jnp.maximum(top, jnp.max(s_branch, axis=0, keepdims=True) + leaf_bias)
        for kb in range(TRUNK):
            part = jnp.max(s_ref[kb * seg : (kb + 1) * seg, :], axis=0, keepdims=True)
            top = jnp.maximum(top, part + biases[kb])
        e_own = jnp.exp(s_own - top)
        e_branch = jnp.exp(s_branch - (top - leaf_bias))
        total = jnp.sum(e_own + e_branch, axis=0, keepdims=True)
        for kb in range(TRUNK):
            e = jnp.exp(s_ref[kb * seg : (kb + 1) * seg, :] - (top - biases[kb]))
            total = total + jnp.sum(e, axis=0, keepdims=True)
            p_ref[kb * seg : (kb + 1) * seg, :] = e.astype(jnp.bfloat16)
        out = mm(v_trunk, p_ref[...])
        out = out + mm(v_ref[there, :].T, e_branch.astype(jnp.bfloat16))
        out = out + mm(v_ref[here, :].T, e_own.astype(jnp.bfloat16))
        out = unstack(out * (1.0 / total), half, seg)
        o_ref[here, :] = out.T.astype(jnp.bfloat16)
        lse_ref[pl.ds(i, 1), :] = top + jnp.log(total)
        return 0

    lax.fori_loop(0, own // seg, one, 0, unroll=True)


def attend_back_kernel(
    own, seg, half, more, info, q_ref, k_ref, v_ref, o_ref, do_ref, lse_ref, *rest
):
    dq_ref, dk_ref, dv_ref, ak, av = rest[3 * more :]
    trunk = TRUNK * seg
    allowed = causal(seg)
    low = jnp.bfloat16
    tk = slice(own, own + trunk)
    k_trunk = k_ref[tk, :].T
    ak[...] = jnp.zeros_like(ak)
    av[...] = jnp.zeros_like(av)

    def one(i, unused):
        count, branch, leaf = info[i, 0], info[i, 1], info[i, 2]
        here = pl.ds(pl.multiple_of(i * seg, seg), seg)
        there = pl.ds(pl.multiple_of(own + branch * seg, seg), seg)
        qs = stacked(q_ref[here, :] * 0.125, half)
        do = do_ref[here, :]
        dos = stacked(do, half)
        prod = (do.astype(jnp.float32) * o_ref[here, :].astype(jnp.float32)).T
        delta = jnp.concatenate(
            [jnp.sum(prod[:half], axis=0, keepdims=True), jnp.sum(prod[half:], axis=0, keepdims=True)],
            axis=1,
        )
        lse = lse_ref[pl.ds(i, 1), :]
        leaf_bias = jnp.where(leaf > 0, 0.0, -1e30)

        def piece(keys, values, shift, mask):
            s = mm(keys, qs, NT)
            if mask:
                s = jnp.where(allowed, s, -1e30)
            if isinstance(shift, list):
                p = jnp.concatenate(
                    [jnp.exp(s[kb * seg : (kb + 1) * seg] - shift[kb]) for kb in range(TRUNK)], axis=0
                )
            else:
                p = jnp.exp(s - shift)
            ds = (p * (mm(values, dos, NT) - delta)).astype(low)
            p = p.astype(low)
            return (mm(p, dos), mm(ds, qs), ds)

        shifts = [lse - jnp.where(kb < count, 0.0, -1e30) for kb in range(TRUNK)]
        dv, dk, ds = piece(k_ref[tk, :], v_ref[tk, :], shifts, False)
        av[tk, :] += dv
        ak[tk, :] += dk
        dq = mm(k_trunk, ds)
        keys = k_ref[there, :]
        dv, dk, ds = piece(keys, v_ref[there, :], lse - leaf_bias, False)
        av[there, :] += dv
        ak[there, :] += dk
        dq = dq + mm(keys.T, ds)
        keys = k_ref[here, :]
        dv, dk, ds = piece(keys, v_ref[here, :], lse, True)
        av[here, :] += dv
        ak[here, :] += dk
        dq = dq + mm(keys.T, ds)
        dq_ref[here, :] = (unstack(dq, half, seg) * 0.125).T.astype(low)
        return 0

    lax.fori_loop(0, own // seg, one, 0, unroll=True)
    dk_ref[...] = ak[...].astype(low)
    dv_ref[...] = av[...].astype(low)


def attend(info, q, kv, seg, begin, count, prev=()):
    own, width = q.shape
    total = kv.shape[0]
    pairs = width // 128
    lane = pl.BlockSpec((own, 128), lambda h: (0, begin + h))
    return pl.pallas_call(
        functools.partial(attend_kernel, own, seg, HEAD_DIM, len(prev) > 0),
        grid=(count,),
        in_specs=[
            pl.BlockSpec(memory_space=pltpu.SMEM),
            lane,
            pl.BlockSpec((total, 128), lambda h: (0, begin + h)),
            pl.BlockSpec((total, 128), lambda h: (0, pairs + begin + h)),
        ]
        + [pl.BlockSpec(memory_space=pl.ANY)] * len(prev),
        out_specs=[lane, pl.BlockSpec((None, 8, 2 * seg), lambda h: (begin + h, 0, 0))],
        out_shape=[
            jax.ShapeDtypeStruct((own, width), jnp.bfloat16),
            jax.ShapeDtypeStruct((pairs, 8, 2 * seg), jnp.float32),
        ],
        input_output_aliases={4 + i: i for i in range(len(prev))},
        scratch_shapes=[
            pltpu.VMEM((TRUNK * seg, 2 * seg), jnp.float32),
            pltpu.VMEM((TRUNK * seg, 2 * seg), jnp.bfloat16),
        ],
        compiler_params=pltpu.CompilerParams(vmem_limit_bytes=60 << 20),
        cost_estimate=pl.CostEstimate(
            flops=1000, bytes_accessed= 1000, transcendentals=0
        ),
        name="attend",
    )(info, q, kv, kv, *prev)


def attend_back(info, q, kv, o, do, lse, seg, begin, count, prev=()):
    own, width = q.shape
    total = kv.shape[0]
    pairs = width // 128
    lane = pl.BlockSpec((own, 128), lambda h: (0, begin + h))
    keys = pl.BlockSpec((total, 128), lambda h: (0, begin + h))
    return pl.pallas_call(
        functools.partial(attend_back_kernel, own, seg, HEAD_DIM, len(prev) > 0),
        grid=(count,),
        in_specs=[
            pl.BlockSpec(memory_space=pltpu.SMEM),
            lane,
            keys,
            pl.BlockSpec((total, 128), lambda h: (0, pairs + begin + h)),
            lane,
            lane,
            pl.BlockSpec((None, 8, 2 * seg), lambda h: (begin + h, 0, 0)),
        ]
        + [pl.BlockSpec(memory_space=pl.ANY)] * len(prev),
        out_specs=[lane, keys, keys],
        out_shape=[
            jax.ShapeDtypeStruct((own, width), jnp.bfloat16),
            jax.ShapeDtypeStruct((total, width), jnp.bfloat16),
            jax.ShapeDtypeStruct((total, width), jnp.bfloat16),
        ],
        input_output_aliases={7 + i: i for i in range(len(prev))},
        scratch_shapes=[
            pltpu.VMEM((total, 128), jnp.float32),
            pltpu.VMEM((total, 128), jnp.float32),
        ],
        compiler_params=pltpu.CompilerParams(vmem_limit_bytes=40 << 20),
        cost_estimate=pl.CostEstimate(
            flops=1000, bytes_accessed= 1000, transcendentals=0
        ),
        name="attend_back",
    )(info, q, kv, kv, o, do, lse, *prev)


def pin(x, *after):
    return lax.optimization_barrier((x,) + after)[0]


def expert_kernel(
    more, capacity, pieces, place, xm_ref, xo_ref, gm_ref, go_ref, w0, w1, w2, w3, *rest
):
    low, full = jnp.bfloat16, jnp.float32
    o_ref, o2_ref, s_ref, s2_ref, dw_ref, x_ref, g_ref, xt, dt, d_ref, oa, sa, wb, gb = rest[more:]
    part = w0.shape[1]
    rows, wide = xm_ref.shape
    padded = rows // pieces
    tail = padded - 16
    here = pl.ds(pl.multiple_of(place[1] * wide, 128), wide)
    there = pl.ds(pl.multiple_of((1 - place[1]) * wide, 128), wide)

    @pl.when(pl.program_id(0) == 0)
    def start():
        x_ref[:, here] = xm_ref[...]
        x_ref[:, there] = xo_ref[...]
        g_ref[:, here] = gm_ref[...]
        g_ref[:, there] = go_ref[...]
        for p in range(pieces):
            mine = slice(p * padded, (p + 1) * padded)
            last = xm_ref[p * padded + tail : (p + 1) * padded, :256].astype(full)
            row = lax.broadcasted_iota(jnp.int32, last.shape, 0) + tail
            inside = (row >= capacity) & (row < capacity + 3)
            gate = jnp.sum(jnp.where(inside, last, 0.0), axis=0, keepdims=True)
            gate = jnp.broadcast_to(gate, (8, 256)).T[:padded, 0:1]
            d_ref[mine, :] = (g_ref[mine, :].astype(full) * gate).astype(low)
        xt[...] = x_ref[...].T
        dt[...] = d_ref[...].T
        oa[...] = jnp.zeros_like(oa)
        sa[...] = jnp.zeros_like(sa)

    def rows_of(r):
        return pl.ds(pl.multiple_of((place[0] ^ r) * part, 64), part)

    for r, w in enumerate((w0, w1, w2, w3)):
        wb[:, rows_of(r), :] = w[...]
    u = mm(x_ref[...], wb[0])
    up = mm(x_ref[...], wb[1])
    sigma = 1.0 / (1.0 + jnp.exp(-u))
    silu = u * sigma
    hidden = (silu * up).astype(low)
    oa[...] += mm(hidden, wb[2], NT)
    dh = mm(d_ref[...], wb[2])
    du = (dh * up * sigma * (1.0 + u * (1.0 - sigma))).astype(low)
    dup = (dh * silu).astype(low)
    sa[...] += mm(du, wb[0], NT) + mm(dup, wb[1], NT)
    gb[0] = mm(xt[...], du).astype(low)
    gb[1] = mm(xt[...], dup).astype(low)
    gb[2] = mm(dt[...], hidden).astype(low)
    for at, r in enumerate(SENT):
        got = gb[:, rows_of(r), :]
        if more:
            got = (got.astype(full) + rest[0][at].astype(full)).astype(low)
        dw_ref[at] = got

    @pl.when(pl.program_id(0) == pl.num_programs(0) - 1)
    def finish():
        o_ref[...] = oa[:, here].astype(low)
        o2_ref[...] = oa[:, there].astype(low)
        s_ref[...] = sa[:, here].astype(low)
        s2_ref[...] = sa[:, there].astype(low)
        for p in range(pieces):
            mine = slice(p * padded, (p + 1) * padded)
            dot = jnp.sum(g_ref[mine, :].astype(full) * oa[mine, :], axis=1, keepdims=True)
            dot = jnp.broadcast_to(dot, (padded, 128)).T[:16, :]
            dot = jnp.concatenate([dot, jnp.zeros((16, wide - padded), full)], axis=1)
            row = lax.broadcasted_iota(jnp.int32, dot.shape, 0) + tail
            kept = jnp.zeros_like(dot)
            for i in range(3):
                piece = dot.astype(low).astype(full)
                kept = jnp.where(row == capacity + i, piece, kept)
                dot = dot - piece
            last = slice(p * padded + tail, (p + 1) * padded)
            row_low = s_ref[last, :].astype(full)
            s_ref[last, :] = jnp.where(row >= capacity, kept, row_low).astype(low)


def expert_pass(place, capacity, pieces, xs, gs, weights, prev):
    rows, half_width = xs[0].shape
    width = 2 * half_width
    three, part, units = weights[0].shape
    low = jnp.bfloat16
    strip = pl.BlockSpec((three, part, PIECE), lambda j, *at: (0, 0, j))
    strips = pl.BlockSpec((4, three, part, PIECE), lambda j, *at: (0, 0, 0, j))
    half = whole(rows, half_width)
    more = prev is not None
    return call(
        functools.partial(expert_kernel, int(more), capacity, pieces),
        "expert_pass",
        [((rows, half_width), low)] * 4 + [((4, three, part, units), low)],
        (place, *xs, *gs, *weights, *([prev] if more else [])),
        [
            pltpu.VMEM((rows, width), low),
            pltpu.VMEM((rows, width), low),
            pltpu.VMEM((width, rows), low),
            pltpu.VMEM((width, rows), low),
            pltpu.VMEM((rows, width), low),
            pltpu.VMEM((rows, width), jnp.float32),
            pltpu.VMEM((rows, width), jnp.float32),
            pltpu.VMEM((three, width, PIECE), low),
            pltpu.VMEM((three, width, PIECE), low),
        ],
        grid=(units // PIECE,),
        in_specs=[half] * 4 + [strip] * 4 + [strips] * more,
        out_specs=[half] * 4 + [strips],
        prefetch=True,
        mib=48,
    )


def spread_kernel(pieces, padded, capacity, gated, place_ref, rows_ref, *rest):
    low = jnp.bfloat16
    outs = rest[1:] if gated else rest
    tokens = rows_ref.shape[0]
    for p in range(pieces):
        slot = lax.broadcasted_iota(jnp.int32, (padded, tokens), 0) + p * padded
        hits = [slot == place_ref[c : c + 1, :] for c in range(2)]
        out = mm(jnp.where(hits[0] | hits[1], 1.0, 0.0).astype(low), rows_ref[...]).astype(low)
        if gated:
            parts = 0.0
            for c in range(2):
                value = rest[0][c : c + 1, :]
                rows3 = []
                for i in range(3):
                    rows3.append(value.astype(low).astype(jnp.float32))
                    value = value - rows3[-1]
                rows3.append(jnp.zeros((13, tokens), jnp.float32))
                three = jnp.concatenate(rows3, axis=0).astype(low)
                parts = parts + mm(three, jnp.where(hits[c], 1.0, 0.0).astype(low), NT)
            parts = parts.astype(low)
            blank = jnp.zeros((parts.shape[0], out.shape[1] - padded), low)
            parts = jnp.concatenate([parts, blank], axis=1)
            row = lax.broadcasted_iota(jnp.int32, out.shape, 0)
            for i in range(3):
                out = jnp.where(row == capacity + i, parts[i : i + 1, :], out)
        outs[p][...] = out


def spread(place, rows, pieces, padded, capacity, parts=None):
    shape = jax.ShapeDtypeStruct((padded, rows.shape[1]), jnp.bfloat16)
    gated = parts is not None
    return pl.pallas_call(
        functools.partial(spread_kernel, pieces, padded, capacity, gated),
        in_specs=[pl.BlockSpec(memory_space=pltpu.VMEM)] * (2 + gated),
        out_specs=[pl.BlockSpec(memory_space=pltpu.VMEM)] * pieces,
        out_shape=[shape] * pieces,
        compiler_params=pltpu.CompilerParams(vmem_limit_bytes=60 << 20),
        cost_estimate=pl.CostEstimate(flops=1000, bytes_accessed= 1000, transcendentals=0),
        name="spread",
    )(place, rows, *([parts] if gated else []))


def expert_of(where_ref, piece):
    upper = jnp.where(where_ref[1] >= 2, 1, 0)
    return (2 * ((piece % 4) ^ where_ref[0]) + ((piece // 4) ^ upper)).astype(jnp.float32)


def spread_gated_kernel(pieces, padded, capacity, gated, where_ref, place_ref, rows_ref, *rest):
    low, full = jnp.bfloat16, jnp.float32
    tokens, width = rows_ref.shape
    if gated:
        gates_ref, outs, wide_ref = rest[0], rest[1:-1], rest[-1]
        lines = []
        for c in range(2):
            value = gates_ref[c : c + 1, :]
            for i in range(3):
                lines.append(value.astype(low).astype(full))
                value = value - lines[-1]
        lines = lines + [gates_ref[4:5, :], jnp.zeros((121, tokens), full)]
        wide_ref[:, :width] = rows_ref[...]
        wide_ref[:, width:] = jnp.concatenate(lines, axis=0).T.astype(low)
    else:
        outs, wide_ref = rest, rows_ref
    for p in range(pieces):
        slot = lax.broadcasted_iota(jnp.int32, (padded, tokens), 0) + p * padded
        hit = (slot == place_ref[0:1, :]) | (slot == place_ref[1:2, :])
        out = mm(jnp.where(hit, 1.0, 0.0).astype(low), wide_ref[...])
        if gated:
            extra = out[:, width:].T
            out = out[:, :width].astype(low)
            row = lax.broadcasted_iota(jnp.int32, out.shape, 0)
            blank = jnp.zeros((1, width - padded), full)
            for i in range(3):
                picked = jnp.where(
                    extra[6:7, :] == expert_of(where_ref, p), extra[i : i + 1, :], extra[3 + i : 4 + i, :]
                )
                picked = jnp.concatenate([picked, blank], axis=1).astype(low)
                out = jnp.where(row == capacity + i, picked, out)
        outs[p][...] = out.astype(low)


def spread_gated(where, place, rows, pieces, padded, capacity, gates=None):
    shape = jax.ShapeDtypeStruct((padded, rows.shape[1]), jnp.bfloat16)
    gated = gates is not None
    return pl.pallas_call(
        functools.partial(spread_gated_kernel, pieces, padded, capacity, gated),
        in_specs=[pl.BlockSpec(memory_space=pltpu.SMEM)]
        + [pl.BlockSpec(memory_space=pltpu.VMEM)] * (2 + gated),
        out_specs=[pl.BlockSpec(memory_space=pltpu.VMEM)] * pieces,
        out_shape=[shape] * pieces,
        scratch_shapes=[pltpu.VMEM((rows.shape[0], rows.shape[1] + 128), jnp.bfloat16)] * gated,
        compiler_params=pltpu.CompilerParams(vmem_limit_bytes=40 << 20),
        cost_estimate=pl.CostEstimate(flops=1000, bytes_accessed=1000, transcendentals=0),
        name="spread",
    )(where, place, rows, *([gates] if gated else []))


def gather_kernel(pieces, padded, capacity, dots, where_ref, place_ref, pair_ref, *rest):
    low, full = jnp.bfloat16, jnp.float32
    if dots:
        ins, (out_ref, out2_ref, dot_ref, dot2_ref) = rest[:pieces], rest[pieces:]
    else:
        ins, (out_ref, out2_ref) = rest[: pieces // 2], rest[pieces // 2 :]
    tokens = place_ref.shape[0]
    total = None
    sums = [0.0, 0.0]
    for p in range(pieces):
        slot = lax.broadcasted_iota(jnp.int32, (tokens, padded), 1) + p * padded
        hits = [slot == place_ref[:, c : c + 1] for c in range(2)]
        if dots:
            source = ins[p][...]
            width = source.shape[1]
            values = ins[p][padded - 16 :, :padded].astype(full)
            values = jnp.concatenate([values, jnp.zeros((112, padded), full)], axis=0).T
            source = jnp.concatenate([source, values.astype(low)], axis=1)
            part = mm(jnp.where(hits[0] | hits[1], 1.0, 0.0).astype(low), source)
            lane = lax.broadcasted_iota(jnp.int32, (tokens, 128), 1)
            lane = lane + (padded - 16 - capacity)
            dot = jnp.where((lane >= 0) & (lane < 3), part[:, width:], 0.0)
            mine = pair_ref[:, 0:1] == expert_of(where_ref, p)
            sums[0] = sums[0] + jnp.where(mine, dot, 0.0)
            sums[1] = sums[1] + jnp.where(mine, 0.0, dot)
            part = part[:, :width]
        else:
            pick = jnp.where(hits[0], pair_ref[:, 0:1], jnp.where(hits[1], pair_ref[:, 1:2], 0.0))
            part = mm(pick.astype(low), ins[p % 4][p // 4])
        total = part if total is None else total + part
    rows = tokens // 2
    out_ref[...] = total[:rows].astype(low)
    out2_ref[...] = total[rows:].astype(low)
    if dots:
        for c in range(2):
            dot_ref[:, c : c + 1] = jnp.sum(sums[c][:rows], axis=1, keepdims=True)
            dot2_ref[:, c : c + 1] = jnp.sum(sums[c][rows:], axis=1, keepdims=True)


def gather(where, place, pair, pieces, capacity, dots):
    padded, width = pieces[0].shape[-2:]
    number = sum(p.size // (padded * width) for p in pieces)
    tokens = place.shape[0]
    shapes = [jax.ShapeDtypeStruct((tokens // 2, width), jnp.bfloat16)] * 2
    if dots:
        shapes = shapes + [jax.ShapeDtypeStruct((tokens // 2, 2), jnp.float32)] * 2
    return pl.pallas_call(
        functools.partial(gather_kernel, number, padded, capacity, dots),
        in_specs=[pl.BlockSpec(memory_space=pltpu.SMEM)]
        + [pl.BlockSpec(memory_space=pltpu.VMEM)] * (len(pieces) + 2),
        out_specs=[pl.BlockSpec(memory_space=pltpu.VMEM)] * len(shapes),
        out_shape=shapes,
        compiler_params=pltpu.CompilerParams(vmem_limit_bytes=60 << 20),
        cost_estimate=pl.CostEstimate(flops=1000, bytes_accessed= 1000, transcendentals=0),
        name="gather",
    )(where, place, pair, *pieces)


def whole(*shape):
    return pl.BlockSpec(shape, lambda *at: (0,) * len(shape))


def by_rows(*shape):
    return pl.BlockSpec(shape, lambda j, *at: (j, 0))


def chosen(number, *shape):
    return pl.BlockSpec((None,) + shape, lambda j, place: (number ^ place[0], 0, 0))


def call(kernel, name, outs, args, scratch=(), grid=(1,), in_specs=None, out_specs=None, prefetch=False, mib=40):
    if out_specs is None:
        out_specs = [whole(*o[0]) for o in outs]
    spec = pltpu.PrefetchScalarGridSpec(
        num_scalar_prefetch=int(prefetch),
        grid=grid,
        in_specs=in_specs,
        out_specs=out_specs,
        scratch_shapes=list(scratch),
    )
    return pl.pallas_call(
        kernel,
        grid_spec=spec,
        out_shape=[jax.ShapeDtypeStruct(*o) for o in outs],
        compiler_params=pltpu.CompilerParams(vmem_limit_bytes=mib << 20),
        cost_estimate=pl.CostEstimate(flops=1000, bytes_accessed=1000, transcendentals=0),
        name=name,
    )(*args)


def unit_rows(x):
    x = x.astype(jnp.float32)
    return x * lax.rsqrt(jnp.mean(x * x, axis=-1, keepdims=True) + eps)


def project_kernel(place, x0, near, mid, farther, gain, wm, wo, q_ref, kv_ref, n_ref, x_ref):
    low = jnp.bfloat16
    shard, ctx = place[0], place[1]
    rows, width = x0.shape
    half = wm.shape[2]

    def project(lo, x):
        here = slice(lo, lo + x.shape[0])
        normed = (unit_rows(x) * gain[...]).astype(low)
        x_ref[here, :] = x
        n_ref[here, :] = normed
        for m in (1, 2):
            for h, w in enumerate((wm, wo)):
                at = (m - 1) * width + h * half
                kv_ref[here, at : at + half] = mm(normed, w[m ^ shard]).astype(low)
        if lo == 0:
            for h, w in enumerate((wm, wo)):
                q_ref[:, h * half : (h + 1) * half] = mm(normed, w[shard]).astype(low)

    edge = x_ref.shape[0] - 3 * rows
    project(0, x0[...])
    later = jnp.where(ctx == 2, mid[...], farther[...])
    project(rows, jnp.where(ctx == 0, x0[...], jnp.where(ctx == 1, near[...], later)))
    later = jnp.where(ctx == 2, near[...], mid[...])
    project(2 * rows, jnp.where(ctx == 1, x0[...], later))
    project(3 * rows, jnp.where(ctx == 2, x0[:edge, :], near[:edge, :]))


def settle_kernel(
    place, o, x, wm, wo, gain, router, res, ids,
    mixed_ref, second_ref, mine_ref, other_ref, probs_ref, stat_ref, gates_ref,
):
    tp = place[2]
    half = wm.shape[1]
    attn = mm(o[:, :half], wm[...], NT) + mm(o[:, half:], wo[...], NT)
    mixed = x[...].astype(jnp.float32) + attn
    mixed_ref[...] = mixed
    inverse = lax.rsqrt(jnp.mean(mixed * mixed, axis=-1, keepdims=True) + eps)
    second = (mixed * inverse * gain[...]).astype(jnp.bfloat16)
    second_ref[...] = second
    mine_ref[...] = second_ref[:, pl.ds(pl.multiple_of(tp * half, 128), half)]
    other_ref[...] = second_ref[:, pl.ds(pl.multiple_of((1 - tp) * half, 128), half)]
    logits = mm(second, router[...], NT) + res[...]
    expo = jnp.exp(logits - jnp.max(logits, axis=-1, keepdims=True))
    probs = expo / jnp.sum(expo, axis=-1, keepdims=True)
    probs_ref[...] = probs
    lane = lax.broadcasted_iota(jnp.int32, probs.shape, 1)
    picked = [
        jnp.sum(jnp.where(lane == ids[:, c : c + 1], probs, 0.0), axis=-1, keepdims=True)
        for c in range(2)
    ]
    total = picked[0] + picked[1]
    wide = lax.broadcasted_iota(jnp.int32, (probs.shape[0], 128), 1)
    stat = jnp.where(wide == 0, picked[0] / total, jnp.where(wide == 1, picked[1] / total, 0.0))
    stat = jnp.where(wide == 2, total, jnp.where(wide == 3, inverse, stat))
    stat = jnp.where(wide == 4, ids[:, 0:1].astype(jnp.float32), stat)
    stat_ref[...] = stat[:, :8]
    gates_ref[...] = stat.T[:8, :]


def settle_back_kernel(
    copy_id, place, dr_mine, dr_came, dg_mine, dg_came, g_ref, mixed, second, probs_ref, stat, ids,
    const, router, gain, wm, wo, dmix_ref, dattn_ref, do_ref, dlog_ref, small_ref, full_ref,
):
    low, full = jnp.bfloat16, jnp.float32
    tp = place[2]
    half = wm.shape[1]
    full_ref[:, pl.ds(pl.multiple_of(tp * half, 128), half)] = dr_mine[...]
    full_ref[:, pl.ds(pl.multiple_of((1 - tp) * half, 128), half)] = dr_came[...]
    g = g_ref[...].astype(full)
    probs = probs_ref[...]
    gates = [stat[:, 0:1], stat[:, 1:2]]
    total, inverse = stat[:, 2:3], stat[:, 3:4]
    ids_c = [ids[:, 0:1], ids[:, 1:2]]
    zero = jnp.zeros_like(total)

    def gate_of(number):
        return sum(jnp.where(ids_c[c] == number, gates[c], zero) for c in range(2))

    copy_gate = gate_of(copy_id)
    const_gate = [gate_of(copy_id + 1 + k) for k in range(2)]
    dots = [jnp.sum(g * second[...].astype(full), axis=-1, keepdims=True)]
    dots = dots + [jnp.sum(g * const[k : k + 1, :], axis=-1, keepdims=True) for k in range(2)]
    d_gates = []
    for c in range(2):
        d = dg_mine[:, c : c + 1] + dg_came[:, c : c + 1]
        for k in range(3):
            d = d + jnp.where(ids_c[c] == copy_id + k, dots[k], zero)
        d_gates.append(d)
    mean = d_gates[0] * gates[0] + d_gates[1] * gates[1]
    lane = lax.broadcasted_iota(jnp.int32, probs.shape, 1)
    d_probs = jnp.zeros_like(probs)
    for c in range(2):
        d_probs = d_probs + jnp.where(lane == ids_c[c], (d_gates[c] - mean) / total, 0.0)
    d_logits = probs * (d_probs - jnp.sum(probs * d_probs, axis=-1, keepdims=True))
    dlog_ref[...] = d_logits
    d_second = copy_gate * g + full_ref[...].astype(full)
    rest = d_logits
    for i in range(3):
        piece = rest.astype(low)
        rest = rest - piece.astype(full)
        d_second = d_second + mm(piece, router[...])
    unit = mixed[...] * inverse
    d_gain = jnp.sum(d_second * unit, axis=0, keepdims=True)
    d_unit = d_second * gain[...]
    d_mixed = g + inverse * (d_unit - unit * jnp.mean(d_unit * unit, axis=-1, keepdims=True))
    dmix_ref[...] = d_mixed
    d_attn = d_mixed.astype(low)
    dattn_ref[...] = d_attn
    do_ref[:, :half] = mm(d_attn, wm[...]).astype(low)
    do_ref[:, half:] = mm(d_attn, wo[...]).astype(low)
    count = probs.shape[1]
    pad = jnp.zeros((probs.shape[0], 128 - count), full)
    wide = lax.broadcasted_iota(jnp.int32, (probs.shape[0], 128), 1)
    table = jnp.concatenate([d_logits, pad], axis=1)
    table = jnp.where(wide == count + 2, const_gate[0], table)
    table = jnp.where(wide == count + 3, const_gate[1], table)
    rest = table.T[: count + 4, :]
    from_second = from_g = 0.0
    for i in range(3):
        piece = rest.astype(low)
        rest = rest - piece.astype(full)
        from_second = from_second + mm(piece, second[...])
        from_g = from_g + mm(piece, g_ref[...])
    row = lax.broadcasted_iota(jnp.int32, from_g.shape, 0)
    small = jnp.where(row < count, from_second, jnp.where(row >= count + 2, from_g, 0.0))
    small_ref[...] = jnp.where(row == count + 1, d_gain, small)


def keys_back_kernel(place, dq, dk, dv, x, wm, wo, own_ref, p0_ref, p1_ref, p2_ref, gain_ref):
    shard = place[0]
    rows, width = own_ref.shape
    half = wm.shape[2]
    gain = jnp.zeros((1, width), jnp.float32)
    lo = 0
    for out in (own_ref, p0_ref, p1_ref, p2_ref):
        here = slice(lo, lo + out.shape[0])
        lo = lo + out.shape[0]
        d = 0.0
        for m, grad in ((0, dq), (1, dk), (2, dv)):
            if m > 0 or out is own_ref:
                d = d + mm(grad[here, :half], wm[m ^ shard], NT)
                d = d + mm(grad[here, half:], wo[m ^ shard], NT)
        out[...] = d.astype(out.dtype)
        gain = gain + jnp.sum(d * unit_rows(x[here, :]), axis=0, keepdims=True)
    gain_ref[...] = gain


def weights_back_kernel(n_ref, dq, dk, dv, da_ref, o, tiny, mine_ref, other_ref, nt, at):
    rows = dq.shape[0]
    step = pl.program_id(0)

    @pl.when(step == 0)
    def start():
        nt[...] = n_ref[...].T
        at[...] = da_ref[...].T

    def put(value):
        value = value.astype(jnp.bfloat16)
        parts, half = mine_ref.shape[0], mine_ref.shape[2]
        part = value.shape[0] // parts
        for z in range(parts):
            mine_ref[z, :part, :] = value[z * part : (z + 1) * part, :half]
            other_ref[z, :part, :] = value[z * part : (z + 1) * part, half:]
            mine_ref[z, part:, :] = tiny[z, :, :half]
            other_ref[z, part:, :] = tiny[z, :, half:]

    pl.when(step == 0)(lambda: put(mm(nt[:, :rows], dq[...])))
    pl.when(step == 1)(lambda: put(mm(nt[...], dk[...])))
    pl.when(step == 2)(lambda: put(mm(nt[...], dv[...])))
    pl.when(step == 3)(lambda: put(mm(at[...], o[...])))


def weights_back(normed, dq, dk, dv, d_attn, o, tiny):
    total, width = normed.shape
    rows, half = dq.shape[0], width // 2
    parts, room = tiny.shape[1], tiny.shape[2]
    low = jnp.bfloat16
    out = pl.BlockSpec((None, parts, width // parts + room, half), lambda j: (j, 0, 0, 0))
    shape = ((4, parts, width // parts + room, half), low)
    return call(
        weights_back_kernel,
        "weights_back",
        [shape, shape],
        (normed, dq, dk, dv, d_attn, o, tiny),
        [pltpu.VMEM((width, total), low), pltpu.VMEM((width, rows), low)],
        grid=(4,),
        in_specs=[whole(total, width), whole(rows, width), whole(total, width), whole(total, width)]
        + [whole(rows, width), whole(rows, width)]
        + [pl.BlockSpec((None, parts, room, width), lambda j: (j, 0, 0, 0))],
        out_specs=[out, out],
        mib=60,
    )


def flip(x, axis, bit, size):
    return lax.ppermute(x, axis, [(i, i ^ bit) for i in range(size)])


def turn_gather(x, size, position):
    out = jnp.zeros((size,) + x.shape, x.dtype)
    out = lax.dynamic_update_index_in_dim(out, x, position, 0)
    for k in range(1, size):
        block = lax.ppermute(x, "ctx", [(i, (i + k) % size) for i in range(size)])
        out = lax.dynamic_update_index_in_dim(out, block, (position - k) % size, 0)
    return out


def turn_sum(x, size, position):
    total = lax.dynamic_index_in_dim(x, position, 0, keepdims=False).astype(jnp.float32)
    for k in range(1, size):
        block = lax.dynamic_index_in_dim(x, (position + k) % size, 0, keepdims=False)
        got = lax.ppermute(block, "ctx", [(i, (i + k) % size) for i in range(size)])
        total = total + got.astype(jnp.float32)
    return total


def far(x, k, shards_n, ctx_n):
    pairs = []
    for s in range(shards_n):
        for z in range(ctx_n):
            pairs.append((s * ctx_n + z, (s ^ k) * ctx_n + (z ^ 2)))
    return lax.ppermute(x, ("shard", "ctx"), pairs)


def three_parts(x):
    one = x.astype(jnp.bfloat16)
    rest = x - one.astype(jnp.float32)
    two = rest.astype(jnp.bfloat16)
    return jnp.stack([one, two, (rest - two.astype(jnp.float32)).astype(jnp.bfloat16)], axis=-2)


def with_rows(slots, values, at):
    extra = three_parts(values)
    after = slots.shape[-2] - at - extra.shape[-2]
    pads = ((0, 0), (at, after), (0, slots.shape[-1] - extra.shape[-1]))
    return slots + jnp.pad(extra, pads)


def row_values(slots, at):
    return jnp.sum(slots[:, at : at + 3, : slots.shape[1]].astype(jnp.float32), axis=1)


def by_core(
    tokens, gate_res, cotangent, parents, expert_ids, priority, w_qkv, w_out, w_router, attn_gain,
    ffn_gain, const_vec, w_gate_up, w_down,
):
    low, full = jnp.bfloat16, jnp.float32
    shard, ctx, tp = lax.axis_index("shard"), lax.axis_index("ctx"), lax.axis_index("tp")
    shards_n, ctx_n = lax.axis_size("shard"), lax.axis_size("ctx")
    trees, rows, width = tokens.shape
    rows_d = w_qkv.shape[0]
    part = width // 2
    seg = rows * ctx_n // parents.shape[1]
    own_segs = rows // seg
    edge = KEY_SEGS * seg - 2 * rows

    def own_tree(x):
        return lax.dynamic_index_in_dim(x, tp, 0, keepdims=False)

    def in_order(x, other, axis=0):
        return jnp.concatenate([jnp.where(tp == 0, x, other), jnp.where(tp == 0, other, x)], axis=axis)

    def both_trees(x, other):
        both = jnp.broadcast_to(x[None], (2,) + x.shape)
        return lax.dynamic_update_index_in_dim(both, other, 1 - tp, 0)

    def unit_of(x):
        x = x.astype(full)
        inverse = lax.rsqrt(jnp.mean(x * x, axis=-1, keepdims=True) + eps)
        return (x * inverse, inverse)

    def swap(x):
        return flip(x, "tp", 1, 2)

    def plus(x, y):
        return (x.astype(full) + y.astype(full)).astype(low)

    def my_half(x, which):
        return lax.dynamic_slice_in_dim(x, which * part, part, x.ndim - 1)

    x_own = lax.optimization_barrier(own_tree(tokens))
    ends = [(i, i + 1) for i in range(ctx_n - 1)]
    near = lax.ppermute(x_own, "ctx", ends)

    mine = jnp.stack([w_qkv[:, 0], w_qkv[:, 1], w_qkv[:, 2], w_out])
    small = jnp.concatenate([w_router.T, attn_gain[None], ffn_gain[None], const_vec.T], axis=0)
    all_experts = w_router.shape[1]
    mine = lax.dynamic_index_in_dim(mine, shard, 0, keepdims=False)
    mine = jnp.concatenate([mine, small.reshape(-1, part)], axis=0)
    turned = turn_gather(mine, ctx_n, ctx)
    matrix = turned[:, :rows_d].reshape(width, -1)
    small = turned[:, rows_d:].reshape(ctx_n, -1, rows_d).transpose(1, 0, 2).reshape(-1, width)
    router_t = small[:all_experts]
    gain_a = small[all_experts].astype(full)
    gain_f = small[all_experts + 1].astype(full)
    const_t = small[all_experts + 2 :].astype(full)

    mid = lax.ppermute(pin(near, matrix), "ctx", ends[1:])
    plane_pieces = [matrix] + [flip(matrix, "shard", k, shards_n) for k in range(1, shards_n)]
    capacity = trees * rows * 2 // all_experts
    experts = shards_n * w_gate_up.shape[1]
    padded = -(-(capacity + 3) // 16) * 16
    count = experts * padded
    flat = expert_ids.reshape(-1)
    order = (2 * priority[0, 0][:, None] + jnp.arange(2, dtype=jnp.int32)[None, :]).reshape(-1)
    earlier = (flat[:, None] == flat[None, :]) & (order[None, :] < order[:, None])
    ranks = jnp.sum(earlier.astype(jnp.int32), axis=1)
    kept = (flat < experts) & (ranks < capacity)
    piece = ((flat % 2) ^ (ctx // 2)) * shards_n + ((flat // 2) ^ shard)
    place = jnp.where(kept, piece * padded + ranks, -1).reshape(trees, rows, 2)
    place = jnp.where(tp == 0, place, place[::-1]).reshape(trees * rows, 2)
    place_t = place.T

    g_own = own_tree(cotangent)
    g_other = lax.dynamic_index_in_dim(cotangent, 1 - tp, 0, keepdims=False)
    g_half = my_half(jnp.concatenate([g_own, g_other], axis=0), tp)
    g_slots = spread(place_t, g_half, experts, padded, capacity)
    ids = own_tree(expert_ids)
    res = own_tree(gate_res)
    ids, res, router_t, gain_a, gain_f, const_t, mid, *g_slots = lax.optimization_barrier(
        (ids, res, router_t, gain_a[None], gain_f[None], const_t, mid, *g_slots)
    )
    farther = lax.ppermute(mid, "ctx", ends[2:])
    plane = jnp.stack(plane_pieces)

    plane_other = swap(plane)
    place3 = jnp.stack([shard, ctx, tp]).astype(jnp.int32)

    capacity = trees * rows * 2 // all_experts
    experts = shards_n * w_gate_up.shape[1]
    padded = -(-(capacity + 3) // 16) * 16
    count = experts * padded
    flat = expert_ids.reshape(-1)
    order = (2 * priority[0, 0][:, None] + jnp.arange(2, dtype=jnp.int32)[None, :]).reshape(-1)
    earlier = (flat[:, None] == flat[None, :]) & (order[None, :] < order[:, None])
    ranks = jnp.sum(earlier.astype(jnp.int32), axis=1)
    kept = (flat < experts) & (ranks < capacity)
    piece = ((flat % 2) ^ (ctx // 2)) * shards_n + ((flat // 2) ^ shard)
    place = jnp.where(kept, piece * padded + ranks, -1).reshape(trees, rows, 2)
    place = jnp.where(tp == 0, place, place[::-1]).reshape(trees * rows, 2)
    place_t = place.T

    g_own = own_tree(cotangent)
    g_other = lax.dynamic_index_in_dim(cotangent, 1 - tp, 0, keepdims=False)
    g_half = my_half(jnp.concatenate([g_own, g_other], axis=0), tp)
    g_slots = spread(place_t, g_half, experts, padded, capacity)
    g_near = jnp.stack(g_slots[:shards_n])
    g_far = flip(pin(jnp.stack(g_slots[shards_n:]), mid), "ctx", 2, ctx_n)
    plane_other = swap(plane)
    place3 = jnp.stack([shard, ctx, tp]).astype(jnp.int32)

    g_near = jnp.stack(g_slots[:shards_n])
    g_far = flip(jnp.stack(g_slots[shards_n:]), "ctx", 2, ctx_n)

    held, gu, dn = lax.optimization_barrier((near, w_gate_up, w_down))
    lower = ctx < 2
    first = jnp.stack([gu[:, 0, 0], gu[:, 0, 1], dn[:, 0]])
    second_e = jnp.stack([gu[:, 1, 0], gu[:, 1, 1], dn[:, 1]])
    rows_own = jnp.where(lower, first, second_e)
    rows_two = flip(pin(jnp.where(lower, second_e, first), farther, g_far), "ctx", 2, ctx_n)
    rows_one = flip(pin(rows_own, farther, g_far), "ctx", 1, ctx_n)

    total = 3 * rows + edge
    q, kv, normed, x_all = call(
        project_kernel,
        "project",
        [((rows, width), low), ((total, 2 * width), low), ((total, width), low), ((total, width), low)],
        (place3, x_own, near, mid, farther, gain_a, plane, plane_other),
        in_specs=[whole(rows, width)] * 4
        + [whole(1, width), whole(4, width, part), whole(4, width, part)],
        prefetch=True,
    )

    seg_id = ctx * own_segs + jnp.arange(own_segs, dtype=jnp.int32)
    parent = jnp.take(own_tree(parents), seg_id)
    leaf = (seg_id >= KEY_SEGS).astype(jnp.int32)
    info = jnp.stack([jnp.minimum(seg_id, TRUNK), jnp.where(leaf > 0, parent, TRUNK), leaf], axis=1)
    half_pairs = width // 256
    ahead = attend(info, q, kv, seg, 0, half_pairs)
    o_low, lse = attend(info, q, kv, seg, half_pairs, half_pairs, ahead)
    g_pairs = jnp.stack([g_near, pin(g_far, ahead[0])], axis=1)
    g_got = [g_pairs[0]] + [flip(g_pairs[k], "shard", k, shards_n) for k in range(1, shards_n)]
    o_low = pin(o_low, rows_one, rows_two, *g_got)
    g_in = jnp.stack(g_got, axis=1).reshape(2, shards_n * padded, part)
    g_out = swap(g_in)

    one_half = ((rows, part), low)
    mixed, second, second_mine, second_other, probs, stat, gates_t = call(
        settle_kernel,
        "settle",
        [
            ((rows, width), full), ((rows, width), low), one_half, one_half,
            ((rows, all_experts), full), ((rows, 8), full), ((8, rows), full),
        ],
        (place3, o_low, x_own, plane, plane_other, gain_f, router_t, res, ids),
        in_specs=[
            whole(rows, width), whole(rows, width), chosen(3, width, part), chosen(3, width, part),
            whole(1, width), whole(all_experts, width), whole(rows, all_experts), whole(rows, 2),
        ],
        prefetch=True,
    )
    second_half = jnp.concatenate([second_mine, swap(second_other)], axis=0)
    gates_both = jnp.concatenate([gates_t, swap(gates_t)], axis=1)

    rows_three = flip(pin(rows_two, o_low), "ctx", 1, ctx_n)
    weights = (rows_own, rows_one, rows_two, rows_three)
    slots = spread_gated(place3, place_t, second_half, experts, padded, capacity, gates_both)
    x_far = [far(slots[shards_n + k], k, shards_n, ctx_n) for k in range(shards_n)]
    x_near = [slots[0]] + [flip(slots[k], "shard", k, shards_n) for k in range(1, shards_n)]

    def experts_on(pieces, gs, prev):
        x = jnp.concatenate(pieces, axis=0)
        return expert_pass(place3[1:], capacity, shards_n, (x, swap(x)), gs, weights, prev)

    def answers(mine, other):
        return plus(mine, swap(other)).reshape(shards_n, padded, part)

    x_near[0] = pin(x_near[0], rows_three)
    on1, ox1, sn1, sx1, dw = experts_on(x_near, (g_in[0], g_out[0]), None)
    x_far = list(lax.optimization_barrier((*x_far, sn1))[:-1])
    on2, ox2, sn2, sx2, dw = experts_on(x_far, (g_in[1], g_out[1]), dw)
    ds_far = answers(sn2, sx2)
    ds_near = answers(sn1, sx1)
    ds_far = [far(ds_far[k], k, shards_n, ctx_n) for k in range(shards_n)]
    ds_near = [ds_near[0]] + [flip(ds_near[k], "shard", k, shards_n) for k in range(1, shards_n)]

    rows_tn = (((0,), (0,)), ((), ()))
    d_routed, d_routed_other, d_pairs, d_pairs_other = gather(
        place3, place, gates_both[4][:, None], ds_near + ds_far, capacity, True
    )
    d_mixed, d_attn, d_o, d_logits, d_small = call(
        functools.partial(settle_back_kernel, experts + 1),
        "settle_back",
        [
            ((rows, width), full), ((rows, width), low), ((rows, width), low),
            ((rows, all_experts), full), ((all_experts + 4, width), full),
        ],
        (
            place3, d_routed, swap(d_routed_other), d_pairs, swap(d_pairs_other), g_own, mixed, second,
            probs, stat, ids, const_t, router_t, gain_f, plane, plane_other,
        ),
        [pltpu.VMEM((rows, width), low)],
        in_specs=[
            whole(rows, part), whole(rows, part), whole(rows, 2), whole(rows, 2), whole(rows, width),
            whole(rows, width), whole(rows, width), whole(rows, all_experts), whole(rows, 8),
            whole(rows, 2), whole(2, width), whole(all_experts, width), whole(1, width),
            chosen(3, width, part), chosen(3, width, part),
        ],
        prefetch=True,
        mib=60,
    )

    ox1, ox2, held = lax.optimization_barrier((ox1, ox2, d_routed))
    out_near = plus(on1, swap(ox1)).reshape(shards_n, padded, part)
    out_far = plus(on2, swap(ox2)).reshape(shards_n, padded, part)

    got = flip(pin(dw[2:], d_routed), "ctx", 1, ctx_n)

    third = width // 384
    back = attend_back(info, q, kv, o_low, d_o, lse, seg, 0, third)
    out_near, out_far, q_later, held = lax.optimization_barrier((out_near, out_far, q, back[0]))
    back = attend_back(info, q_later, kv, o_low, d_o, lse, seg, third, third, back)
    out_near, out_far = (out_near, out_far)
    out_cross = flip(out_far, "ctx", 2, ctx_n)
    q_later = pin(q, back[0])
    dq, dk, dv = attend_back(info, q_later, kv, o_low, d_o, lse, seg, 2 * third, third, back)
    got = pin(got, dq)
    sent_rows = plus(dw[1], got[1])
    came_rows = flip(sent_rows, "ctx", 2, ctx_n)
    out_pairs = jnp.stack([out_near, pin(out_cross, dq)], axis=1)
    out_got = [out_pairs[0]] + [flip(out_pairs[k], "shard", k, shards_n) for k in range(1, shards_n)]
    d_near, part0, part1, part2, d_gain_a = call(
        keys_back_kernel,
        "keys_back",
        [
            ((rows, width), full), ((rows, width), low), ((rows, width), low), ((edge, width), low),
            ((1, width), full),
        ],
        (pin(place3, sent_rows), dq, dk, dv, x_all, plane, plane_other),
        in_specs=[
            whole(rows, width), whole(total, width), whole(total, width), whole(total, width),
            whole(4, width, part), whole(4, width, part),
        ],
        prefetch=True,
        mib=60,
    )

    tiny = jnp.concatenate([d_small[:all_experts], d_gain_a, d_small[all_experts + 1 :]], axis=0)
    tiny = tiny.reshape(4, 2, 2, ctx_n, rows_d).transpose(0, 3, 1, 2, 4).reshape(4, ctx_n, 2, 2 * rows_d)
    tiny = jnp.where(tp == 0, tiny, tiny[:, :, ::-1]).reshape(4, ctx_n, 1, width).astype(low)
    tiny = jnp.pad(tiny, ((0, 0), (0, 0), (0, 15), (0, 0)))
    shared_mine, shared_other = weights_back(normed, dq, dk, dv, d_attn, o_low, tiny)

    def down(x, step):
        return lax.ppermute(x, "ctx", [(i, i - 1) for i in range(ctx_n - step, ctx_n)])

    came = down(part0, 1)
    shared_other = pin(shared_other, came, *out_got, came_rows)
    payload = jnp.where(ctx == 3, part1, plus(part0, came))
    came = down(payload, 2)
    shared = plus(pin(shared_mine, payload), swap(shared_other))

    def numbered(k):
        return lax.dynamic_index_in_dim(shared, shard ^ k, 0, keepdims=False)

    plane_parts = [flip(numbered(k), "shard", k, shards_n) for k in range(1, shards_n)]
    plane_sum = numbered(0).astype(full)
    for got_part in plane_parts:
        plane_sum = plane_sum + got_part.astype(full)
    came = pin(came, plane_parts[0])
    part2 = jnp.pad(part2, ((0, rows - edge), (0, 0)))
    came = down(jnp.where(ctx == 3, part2, jnp.where(ctx == 2, plus(part1, came), plus(part0, came))), 3)
    came_rows = pin(came_rows, plane_parts[0]).astype(full)
    kept_rows = dw[0].astype(full) + got[0].astype(full)
    first = jnp.where(lower, kept_rows, came_rows)
    second_e = jnp.where(lower, came_rows, kept_rows)
    d_gate_up = jnp.stack(
        [jnp.stack([first[0], first[1]], axis=1), jnp.stack([second_e[0], second_e[1]], axis=1)], axis=1
    )
    d_down = jnp.stack([first[2], second_e[2]], axis=1)
    came = pin(came, d_gate_up, d_down)
    base = jnp.where(ctx == 0, part0, jnp.where(ctx == 1, part1, part2)).astype(full)
    extra = jnp.where(ctx == 3, 0.0, base + came.astype(full))
    d_normed = d_near + extra
    unit_own, inv_own = unit_of(x_own)
    gain_a = gain_a[0]
    d_first = d_normed * gain_a
    d_tokens = d_mixed + inv_own * (
        d_first - unit_own * jnp.mean(d_first * unit_own, axis=-1, keepdims=True)
    )

    total = turn_sum(plane_sum.astype(low), ctx_n, ctx).astype(low)
    out_got = [pin(o, plane_parts[0]) for o in out_got]
    gate_columns = jnp.stack([gates_both[0], gates_both[1]], axis=1)
    combined, combined_other = gather(place3, place, gate_columns, out_got, capacity, False)
    combined = in_order(combined, swap(combined_other), 1).astype(full)
    second_f = second.astype(full)

    def gate_of(number):
        return jnp.sum(jnp.where(ids == number, stat[:, :2], 0.0), axis=1, keepdims=True)

    copy_gate = gate_of(experts + 1)
    const_gate = jnp.concatenate([gate_of(experts + 2), gate_of(experts + 3)], axis=1)
    mixed_out = (
        mixed
        + combined
        + copy_gate * second_f
        + const_gate[:, :1] * const_t[0][None]
        + const_gate[:, 1:] * const_t[1][None]
    )
    total = pin(total, mixed_out, d_tokens)
    d_tokens_other = swap(d_tokens)
    four = [total] + [flip(total, "shard", k, shards_n) for k in range(1, shards_n)]
    four = jnp.stack([pin(f, d_tokens_other) for f in four])
    four = jnp.stack(
        [lax.dynamic_index_in_dim(four, m ^ shard, 0, keepdims=False) for m in range(4)]
    )
    d_q, d_k, d_v, d_w_out = [four[m, :rows_d].astype(full) for m in range(4)]
    d_w_qkv = jnp.stack([d_q, d_k, d_v], axis=1)
    tiny = four[:, rows_d]
    tiny = both_trees(tiny, swap(tiny)).transpose(1, 0, 2).reshape(16, rows_d).astype(full)

    return (
        both_trees(mixed_out, swap(mixed_out)),
        both_trees(d_tokens, d_tokens_other),
        both_trees(d_logits, swap(d_logits)),
        d_w_qkv,
        d_w_out,
        tiny[:all_experts].T,
        tiny[all_experts],
        tiny[all_experts + 1],
        tiny[all_experts + 2 :].T,
        d_gate_up,
        d_down,
    )


def program(tokens, gate_res, cotangent, parents, expert_ids, priority, w_qkv, *weights):
    trees, rows, width = tokens.shape
    ctx_n = lax.axis_size("ctx")
    seg = rows * ctx_n // parents.shape[1]
    fits = (
        ctx_n == 4
        and lax.axis_size("shard") == 4
        and lax.axis_size("tp") == 2
        and trees == 2
        and seg == 128
        and rows % seg == 0
        and 2 * rows < KEY_SEGS * seg <= 3 * rows
        and weights[-1].shape[1] == 2
    )
    chosen = by_core if fits else shards
    return chosen(tokens, gate_res, cotangent, parents, expert_ids, priority, w_qkv, *weights)


def solution(mesh):
    return jax.shard_map(
        program,
        mesh=mesh,
        in_specs=(
            P("shard", "ctx", None),
            P("shard", "ctx", None),
            P("shard", "ctx", None),
            P("shard", None),
            P("shard", "ctx", None),
            P("shard", "ctx", None),
            P("ctx", None, "tp"),
            P("ctx", "tp"),
            P("ctx", None),
            P("ctx"),
            P("ctx"),
            P("ctx", None),
            P("ctx", "shard", None, "tp"),
            P("ctx", "shard", "tp"),
        ),
        out_specs=(
            P("shard", "ctx", None),
            P("shard", "ctx", None),
            P("shard", "ctx", None),
            P("ctx", None, "tp"),
            P("ctx", "tp"),
            P("ctx", None),
            P("ctx"),
            P("ctx"),
            P("ctx", None),
            P("ctx", "shard", None, "tp"),
            P("ctx", "shard", "tp"),
        ),
        check_vma=False,
    )
```

```python
import functools
import math

import jax
import jax.numpy as jnp
from jax import lax
from jax.experimental import pallas as pl
from jax.experimental.pallas import tpu as pltpu
from jax.sharding import PartitionSpec as P

HEAD_DIM = 64


eps = 1e-06
score_scale = 0.125


def ancestry(parent_row):
    seg_count = parent_row.shape[0]
    position = jnp.arange(seg_count, dtype=jnp.int32)
    linked = (parent_row[:, None] == position[None, :]) | (position[:, None] == position[None, :])
    reach = linked.astype(jnp.float32)
    for repeat in range(seg_count.bit_length()):
        reach = jnp.minimum(jnp.dot(reach, reach, precision=lax.Precision.HIGHEST), 1.0)
    return reach


def path_rows(positions, seg_len, ancestors):
    onehot = (
        (positions // seg_len)[:, None] == jnp.arange(ancestors.shape[0], dtype=jnp.int32)[None, :]
    ).astype(jnp.float32)
    return jnp.dot(onehot, ancestors)


def allowed_block(query_rows, query_pos, key_start, key_count, seg_len):
    key_pos = key_start + jnp.arange(key_count, dtype=jnp.int32)
    key_onehot = (
        (key_pos // seg_len)[:, None] == jnp.arange(query_rows.shape[1], dtype=jnp.int32)[None, :]
    ).astype(jnp.float32)
    linked = jnp.dot(query_rows, key_onehot.T) > 0.5
    return (linked & (key_pos[None, :] <= query_pos[:, None]))[None]


def slot_table(picked_ids, ranking, experts, capacity):
    count_rows = picked_ids.shape[0]
    flat_ids = picked_ids.reshape(-1)
    rank_key = (2 * ranking[:, None] + jnp.arange(2, dtype=jnp.int32)[None, :]).reshape(-1)
    earlier = (flat_ids[:, None] == flat_ids[None, :]) & (rank_key[None, :] < rank_key[:, None])
    ranks = jnp.sum(earlier.astype(jnp.int32), axis=1)
    kept = (flat_ids < experts) & (ranks < capacity)
    target = jnp.where(kept, flat_ids * capacity + ranks, -1).reshape(count_rows, 2)
    slot_index = jnp.arange(experts * capacity, dtype=jnp.int32)
    return slot_index[None, :, None] == target.T[:, None, :]


def block_scores(queries, keys_blk):
    return (
        jnp.einsum("qhe,khe->hqk", queries, keys_blk, preferred_element_type=jnp.float32)
        * score_scale
    )


def softmax_grads(queries, grads_out, stat_lse, stat_delta, keys_blk, values_blk, mask):
    prob = jnp.where(mask, jnp.exp(block_scores(queries, keys_blk) - stat_lse[:, :, None]), 0.0)
    dprob = jnp.einsum("qhe,khe->hqk", grads_out, values_blk, preferred_element_type=jnp.float32)
    dscore = (prob * (dprob - stat_delta[:, :, None])).astype(jnp.bfloat16)
    return (prob.astype(jnp.bfloat16), dscore)


def shards(
    tokens,
    gate_res,
    cotangent,
    parents,
    expert_ids,
    priority,
    w_qkv,
    w_out,
    w_router,
    attn_gain,
    ffn_gain,
    const_vec,
    w_gate_up,
    w_down,
):
    full_qkv, full_out, full_router, full_again, full_fgain, full_const, full_gu, full_down = (
        lax.all_gather(w_qkv, "ctx", axis=0, tiled=True),
        lax.all_gather(w_out, "ctx", axis=0, tiled=True),
        lax.all_gather(w_router, "ctx", axis=0, tiled=True),
        lax.all_gather(attn_gain, "ctx", axis=0, tiled=True),
        lax.all_gather(ffn_gain, "ctx", axis=0, tiled=True),
        lax.all_gather(const_vec, "ctx", axis=0, tiled=True),
        lax.all_gather(w_gate_up, "ctx", axis=0, tiled=True),
        lax.all_gather(w_down, "ctx", axis=0, tiled=True),
    )
    tree_count, rows, model_width = tokens.shape
    tok_rows = tree_count * rows
    inputs = tokens.reshape(tok_rows, model_width).astype(jnp.float32)
    local_width = full_out.shape[1]
    local_heads = local_width // HEAD_DIM
    ctx_index = lax.axis_index("ctx")
    tree_len = rows * lax.axis_size("ctx")
    ancestors_all = jax.vmap(ancestry)(parents)
    seg_len = tree_len // parents.shape[1]
    key_block = math.gcd(tree_len, 512)
    starts = jnp.arange(tree_len // key_block, dtype=jnp.int32) * key_block
    key_start_own = ctx_index * rows
    query_pos = key_start_own + jnp.arange(rows, dtype=jnp.int32)
    query_rows_all = jax.vmap(lambda anc: path_rows(query_pos, seg_len, anc))(ancestors_all)
    inv_first = lax.rsqrt(jnp.mean(inputs * inputs, axis=-1, keepdims=True) + eps)
    first_unit = inputs * inv_first
    first_gain = full_again.astype(jnp.float32)
    normed = (first_unit * first_gain).astype(jnp.bfloat16)
    projected = jnp.einsum("nd,dke->nke", normed, full_qkv, preferred_element_type=jnp.float32)
    q_low = projected[:, 0].astype(jnp.bfloat16)
    k_low = projected[:, 1].astype(jnp.bfloat16)
    v_low = projected[:, 2].astype(jnp.bfloat16)
    keys_all, values_all = (
        lax.all_gather(k_low.reshape(tree_count, rows, local_width), "ctx", axis=1, tiled=True),
        lax.all_gather(v_low.reshape(tree_count, rows, local_width), "ctx", axis=1, tiled=True),
    )
    q_heads = q_low.reshape(tree_count, rows, local_heads, HEAD_DIM)
    k_heads = keys_all.reshape(tree_count, tree_len, local_heads, HEAD_DIM)
    v_heads = values_all.reshape(tree_count, tree_len, local_heads, HEAD_DIM)

    def tree_forward(q_one, k_one, v_one, rows_one):

        def stat_step(carry, start):
            running_top, running_sum = carry
            keys_blk = lax.dynamic_slice_in_dim(k_one, start, key_block, 0)
            mask = allowed_block(rows_one, query_pos, start, key_block, seg_len)
            masked = jnp.where(mask, block_scores(q_one, keys_blk), -1e30)
            new_top = jnp.maximum(running_top, jnp.max(masked, axis=2))
            expo = jnp.where(mask, jnp.exp(masked - new_top[:, :, None]), 0.0)
            running_sum = running_sum * jnp.exp(running_top - new_top) + jnp.sum(expo, axis=2)
            return ((new_top, running_sum), None)

        start_top = jnp.full((local_heads, rows), -1e30, jnp.float32)
        (final_top, final_sum), unused = lax.scan(
            stat_step, (start_top, jnp.zeros_like(start_top)), starts
        )
        lse_one = final_top + jnp.log(final_sum)

        def out_step(accum, start):
            keys_blk = lax.dynamic_slice_in_dim(k_one, start, key_block, 0)
            values_blk = lax.dynamic_slice_in_dim(v_one, start, key_block, 0)
            mask = allowed_block(rows_one, query_pos, start, key_block, seg_len)
            prob = jnp.where(
                mask, jnp.exp(block_scores(q_one, keys_blk) - lse_one[:, :, None]), 0.0
            ).astype(jnp.bfloat16)
            return (
                accum
                + jnp.einsum("hqk,khe->qhe", prob, values_blk, preferred_element_type=jnp.float32),
                None,
            )

        attended_one, unused = lax.scan(
            out_step, jnp.zeros((rows, local_heads, HEAD_DIM), jnp.float32), starts
        )
        return (attended_one, lse_one)

    attended, lse = jax.vmap(tree_forward)(q_heads, k_heads, v_heads, query_rows_all)
    attended_low = attended.reshape(tok_rows, local_width).astype(jnp.bfloat16)
    attn_part = jnp.einsum("nh,dh->nd", attended_low, full_out, preferred_element_type=jnp.float32)
    attn_sum = lax.psum(attn_part.astype(jnp.bfloat16), "tp").astype(jnp.float32)
    mixed = inputs + attn_sum
    inv_second = lax.rsqrt(jnp.mean(mixed * mixed, axis=-1, keepdims=True) + eps)
    second_unit = mixed * inv_second
    second_gain = full_fgain.astype(jnp.float32)
    second_low = (second_unit * second_gain).astype(jnp.bfloat16)
    second_float = second_low.astype(jnp.float32)
    logits = jnp.dot(
        second_low, full_router, preferred_element_type=jnp.float32
    ) + gate_res.reshape(tok_rows, -1)
    expo_logits = jnp.exp(logits - jnp.max(logits, axis=-1, keepdims=True))
    probs = expo_logits / jnp.sum(expo_logits, axis=-1, keepdims=True)
    experts = lax.axis_size("shard") * w_gate_up.shape[1]
    every_expert = experts + 4
    capacity = tok_rows * 2 // every_expert
    picked_ids = expert_ids.reshape(tok_rows, 2)
    selector = (picked_ids[:, :, None] == jnp.arange(every_expert, dtype=jnp.int32)).astype(
        jnp.float32
    )
    picked = jnp.sum(selector * probs[:, None, :], axis=-1)
    picked_total = jnp.sum(picked, axis=-1, keepdims=True)
    gates = picked / picked_total
    table = slot_table(picked_ids, priority[0, 0], experts, capacity).astype(jnp.bfloat16)
    routed = table[0] + table[1]
    send_slots = jnp.einsum(
        "et,td->ed", routed, second_low, preferred_element_type=jnp.float32
    ).astype(jnp.bfloat16)
    send_slots = send_slots.reshape(experts, 1, capacity, model_width)
    arrived = lax.all_to_all(send_slots, "shard", split_axis=0, concat_axis=1, tiled=True)
    gate_up = jnp.einsum("jsrd,djgf->jsrgf", arrived, full_gu, preferred_element_type=jnp.float32)
    hidden_low = (jax.nn.silu(gate_up[:, :, :, 0]) * gate_up[:, :, :, 1]).astype(jnp.bfloat16)
    partial_out = jnp.einsum(
        "jsrf,djf->jsrd", hidden_low, full_down, preferred_element_type=jnp.float32
    )
    summed = lax.psum(partial_out.astype(jnp.bfloat16), "tp")
    returned = lax.all_to_all(summed, "shard", split_axis=1, concat_axis=0, tiled=True)
    returned, kept_slots = (returned, arrived)
    out_slots = returned.reshape(experts * capacity, model_width)
    ffn_values = jnp.einsum("cet,ed->ctd", table, out_slots, preferred_element_type=jnp.float32)
    copy_flag = selector[:, :, experts + 1]
    const_flags = selector[:, :, experts + 2 :]
    const_float = full_const.astype(jnp.float32)
    fixed_terms = jnp.einsum(
        "nck,dk->cnd", const_flags, const_float, precision=lax.Precision.HIGHEST
    )
    values_pair = ffn_values + copy_flag.T[:, :, None] * second_float[None] + fixed_terms
    mixed_out = mixed + jnp.sum(gates.T[:, :, None] * values_pair, axis=0)
    grad_out = cotangent.reshape(tok_rows, model_width).astype(jnp.float32)
    weighted = gates.T[:, :, None] * grad_out[None]
    d_gates = jnp.einsum("cnd,nd->nc", values_pair, grad_out)
    d_const = jnp.einsum("nck,cnd->dk", const_flags, weighted, precision=lax.Precision.HIGHEST)
    d_out_slots = jnp.einsum(
        "cet,ctd->ed", table.astype(jnp.float32), weighted, precision=lax.Precision.HIGHEST
    )
    d_out_low = d_out_slots.astype(jnp.bfloat16).reshape(experts, 1, capacity, model_width)
    d_picked = (d_gates - jnp.sum(d_gates * gates, axis=-1, keepdims=True)) / picked_total
    d_probs = jnp.einsum("nc,nck->nk", d_picked, selector)
    d_logits = probs * (d_probs - jnp.sum(probs * d_probs, axis=-1, keepdims=True))
    d_router_w = jnp.dot(second_float.T, d_logits, precision=lax.Precision.HIGHEST)
    d_second = jnp.sum(copy_flag.T[:, :, None] * weighted, axis=0)
    d_second = d_second + jnp.dot(
        d_logits, full_router.astype(jnp.float32).T, precision=lax.Precision.HIGHEST
    )
    arrived_grad = lax.all_to_all(d_out_low, "shard", split_axis=0, concat_axis=1, tiled=True)
    gate_up = jnp.einsum(
        "jsrd,djgf->jsrgf", kept_slots, full_gu, preferred_element_type=jnp.float32
    )
    gate_part = gate_up[:, :, :, 0]
    up_part = gate_up[:, :, :, 1]
    sigma = jax.nn.sigmoid(gate_part)
    silu_part = gate_part * sigma
    hidden_low = (silu_part * up_part).astype(jnp.bfloat16)
    d_hidden = jnp.einsum(
        "jsrd,djf->jsrf", arrived_grad, full_down, preferred_element_type=jnp.float32
    )
    d_gate_part = d_hidden * up_part * sigma * (1.0 + gate_part * (1.0 - sigma))
    d_up_part = d_hidden * silu_part
    d_gate_up_low = jnp.stack([d_gate_part, d_up_part], axis=3).astype(jnp.bfloat16)
    d_slot_part = jnp.einsum(
        "jsrgf,djgf->jsrd", d_gate_up_low, full_gu, preferred_element_type=jnp.float32
    )
    d_slot_sum = lax.psum(d_slot_part.astype(jnp.bfloat16), "tp")
    d_slot_back = lax.all_to_all(d_slot_sum, "shard", split_axis=1, concat_axis=0, tiled=True)
    d_gate_up_w = jnp.einsum(
        "jsrd,jsrgf->djgf", kept_slots, d_gate_up_low, preferred_element_type=jnp.float32
    )
    d_down_w = jnp.einsum(
        "jsrd,jsrf->djf", arrived_grad, hidden_low, preferred_element_type=jnp.float32
    )
    d_second = d_second + jnp.einsum(
        "et,ed->td",
        routed,
        d_slot_back.reshape(experts * capacity, model_width),
        preferred_element_type=jnp.float32,
    )
    d_second_gain = jnp.sum(d_second * second_unit, axis=0)
    d_second_unit = d_second * second_gain
    d_mixed = grad_out + inv_second * (
        d_second_unit - second_unit * jnp.mean(d_second_unit * second_unit, axis=-1, keepdims=True)
    )
    d_attn_low = d_mixed.astype(jnp.bfloat16)
    d_out_w = jnp.einsum("nd,nh->dh", d_attn_low, attended_low, preferred_element_type=jnp.float32)
    d_attended = jnp.einsum("nd,dh->nh", d_attn_low, full_out, preferred_element_type=jnp.float32)
    do_low = d_attended.astype(jnp.bfloat16)
    do_heads = do_low.reshape(tree_count, rows, local_heads, HEAD_DIM)
    delta = jnp.einsum("tqhe,tqhe->thq", do_heads.astype(jnp.float32), attended)

    def tree_both(q_one, k_one, v_one, do_one, lse_one, delta_one, rows_one):

        def both_step(dq_accum, start):
            keys_blk = lax.dynamic_slice_in_dim(k_one, start, key_block, 0)
            values_blk = lax.dynamic_slice_in_dim(v_one, start, key_block, 0)
            mask = allowed_block(rows_one, query_pos, start, key_block, seg_len)
            prob_low, dscore = softmax_grads(
                q_one, do_one, lse_one, delta_one, keys_blk, values_blk, mask
            )
            dq_accum = dq_accum + jnp.einsum(
                "hqk,khe->qhe", dscore, keys_blk, preferred_element_type=jnp.float32
            )
            dkey = (
                jnp.einsum("hqk,qhe->khe", dscore, q_one, preferred_element_type=jnp.float32)
                * score_scale
            )
            dval = jnp.einsum("hqk,qhe->khe", prob_low, do_one, preferred_element_type=jnp.float32)
            return (
                dq_accum,
                jnp.stack(
                    [dkey.reshape(key_block, local_width), dval.reshape(key_block, local_width)],
                    axis=1,
                ),
            )

        dq_one, terms_one = lax.scan(
            both_step, jnp.zeros((rows, local_heads, HEAD_DIM), jnp.float32), starts
        )
        return (dq_one, terms_one.reshape(tree_len, 2, local_width))

    dq_total, key_terms = jax.vmap(tree_both)(
        q_heads, k_heads, v_heads, do_heads, lse, delta, query_rows_all
    )
    key_sums = lax.psum_scatter(
        key_terms.astype(jnp.bfloat16), "ctx", scatter_dimension=1, tiled=True
    ).astype(jnp.float32)
    key_grad = key_sums[:, :, 0].reshape(tok_rows, local_width)
    value_grad = key_sums[:, :, 1].reshape(tok_rows, local_width)
    query_grad = (dq_total * score_scale).reshape(tok_rows, local_width)
    d_qkv_low = jnp.stack([query_grad, key_grad, value_grad], axis=1).astype(jnp.bfloat16)
    d_qkv_w = jnp.einsum("nd,nke->dke", normed, d_qkv_low, preferred_element_type=jnp.float32)
    d_normed_part = jnp.einsum(
        "nke,dke->nd", d_qkv_low, full_qkv, preferred_element_type=jnp.float32
    )
    d_normed = lax.psum(d_normed_part.astype(jnp.bfloat16), "tp").astype(jnp.float32)
    d_first_gain = jnp.sum(d_normed * first_unit, axis=0)
    d_first_unit = d_normed * first_gain
    d_inputs = d_mixed + inv_first * (
        d_first_unit - first_unit * jnp.mean(d_first_unit * first_unit, axis=-1, keepdims=True)
    )
    summed_grads = (
        lax.psum_scatter(
            d_qkv_w.astype(jnp.bfloat16), "ctx", scatter_dimension=0, tiled=True
        ).astype(jnp.float32),
        lax.psum_scatter(
            d_out_w.astype(jnp.bfloat16), "ctx", scatter_dimension=0, tiled=True
        ).astype(jnp.float32),
        lax.psum_scatter(
            d_router_w.astype(jnp.bfloat16), "ctx", scatter_dimension=0, tiled=True
        ).astype(jnp.float32),
        lax.psum_scatter(
            d_first_gain.astype(jnp.bfloat16), "ctx", scatter_dimension=0, tiled=True
        ).astype(jnp.float32),
        lax.psum_scatter(
            d_second_gain.astype(jnp.bfloat16), "ctx", scatter_dimension=0, tiled=True
        ).astype(jnp.float32),
        lax.psum_scatter(
            d_const.astype(jnp.bfloat16), "ctx", scatter_dimension=0, tiled=True
        ).astype(jnp.float32),
        lax.psum_scatter(
            d_gate_up_w.astype(jnp.bfloat16), "ctx", scatter_dimension=0, tiled=True
        ).astype(jnp.float32),
        lax.psum_scatter(
            d_down_w.astype(jnp.bfloat16), "ctx", scatter_dimension=0, tiled=True
        ).astype(jnp.float32),
    )
    shared = (
        lax.psum(summed_grads[0].astype(jnp.bfloat16), "shard").astype(jnp.float32),
        lax.psum(summed_grads[1].astype(jnp.bfloat16), "shard").astype(jnp.float32),
        lax.psum(summed_grads[2].astype(jnp.bfloat16), "shard").astype(jnp.float32),
        lax.psum(summed_grads[3].astype(jnp.bfloat16), "shard").astype(jnp.float32),
        lax.psum(summed_grads[4].astype(jnp.bfloat16), "shard").astype(jnp.float32),
        lax.psum(summed_grads[5].astype(jnp.bfloat16), "shard").astype(jnp.float32),
    )
    out_rows = mixed_out.reshape(tree_count, rows, model_width)
    grad_rows = d_inputs.reshape(tree_count, rows, model_width)
    logit_rows = d_logits.reshape(tree_count, rows, every_expert)
    return (
        out_rows,
        grad_rows,
        logit_rows,
        shared[0],
        shared[1],
        shared[2],
        shared[3],
        shared[4],
        shared[5],
        summed_grads[6],
        summed_grads[7],
    )


NT = (((1,), (1,)), ((), ()))
NN = (((1,), (0,)), ((), ()))
TRUNK = 8
KEY_SEGS = 12
PIECE = 256
SENT = (0, 2, 1, 3)


def mm(a, b, dims=NN):
    return lax.dot_general(a, b, dims, preferred_element_type=jnp.float32)


def stacked(rows, half):
    first = lax.broadcasted_iota(jnp.int32, rows.shape, 1) < half
    blank = jnp.zeros_like(rows)
    return jnp.concatenate([jnp.where(first, rows, blank), jnp.where(first, blank, rows)], axis=0)


def unstack(wide, half, seg):
    return jnp.concatenate([wide[:half, :seg], wide[half:, seg:]], axis=0)


def causal(seg):
    row = lax.broadcasted_iota(jnp.int32, (seg, 2 * seg), 0)
    col = lax.broadcasted_iota(jnp.int32, (seg, 2 * seg), 1)
    return row <= jnp.where(col >= seg, col - seg, col)


def attend_kernel(own, seg, half, more, info, q_ref, k_ref, v_ref, *rest):
    o_ref, lse_ref, s_ref, p_ref = rest[2 * more :]
    trunk = TRUNK * seg
    allowed = causal(seg)
    v_trunk = v_ref[own : own + trunk, :].T

    def one(i, unused):
        count, branch, leaf = info[i, 0], info[i, 1], info[i, 2]
        here = pl.ds(pl.multiple_of(i * seg, seg), seg)
        there = pl.ds(pl.multiple_of(own + branch * seg, seg), seg)
        qs = stacked(q_ref[here, :] * 0.125, half)
        s_ref[:trunk, :] = mm(k_ref[own : own + trunk, :], qs, NT)
        s_branch = mm(k_ref[there, :], qs, NT)
        s_own = jnp.where(allowed, mm(k_ref[here, :], qs, NT), -1e30)
        biases = [jnp.where(kb < count, 0.0, -1e30) for kb in range(TRUNK)]
        leaf_bias = jnp.where(leaf > 0, 0.0, -1e30)
        top = jnp.max(s_own, axis=0, keepdims=True)
        top = jnp.maximum(top, jnp.max(s_branch, axis=0, keepdims=True) + leaf_bias)
        for kb in range(TRUNK):
            part = jnp.max(s_ref[kb * seg : (kb + 1) * seg, :], axis=0, keepdims=True)
            top = jnp.maximum(top, part + biases[kb])
        e_own = jnp.exp(s_own - top)
        e_branch = jnp.exp(s_branch - (top - leaf_bias))
        total = jnp.sum(e_own + e_branch, axis=0, keepdims=True)
        for kb in range(TRUNK):
            e = jnp.exp(s_ref[kb * seg : (kb + 1) * seg, :] - (top - biases[kb]))
            total = total + jnp.sum(e, axis=0, keepdims=True)
            p_ref[kb * seg : (kb + 1) * seg, :] = e.astype(jnp.bfloat16)
        out = mm(v_trunk, p_ref[...])
        out = out + mm(v_ref[there, :].T, e_branch.astype(jnp.bfloat16))
        out = out + mm(v_ref[here, :].T, e_own.astype(jnp.bfloat16))
        out = unstack(out * (1.0 / total), half, seg)
        o_ref[here, :] = out.T.astype(jnp.bfloat16)
        lse_ref[pl.ds(i, 1), :] = top + jnp.log(total)
        return 0

    lax.fori_loop(0, own // seg, one, 0, unroll=True)


def attend_back_kernel(
    own, seg, half, more, info, q_ref, k_ref, v_ref, o_ref, do_ref, lse_ref, *rest
):
    dq_ref, dk_ref, dv_ref, ak, av = rest[3 * more :]
    trunk = TRUNK * seg
    allowed = causal(seg)
    low = jnp.bfloat16
    tk = slice(own, own + trunk)
    k_trunk = k_ref[tk, :].T
    ak[...] = jnp.zeros_like(ak)
    av[...] = jnp.zeros_like(av)

    def one(i, unused):
        count, branch, leaf = info[i, 0], info[i, 1], info[i, 2]
        here = pl.ds(pl.multiple_of(i * seg, seg), seg)
        there = pl.ds(pl.multiple_of(own + branch * seg, seg), seg)
        qs = stacked(q_ref[here, :] * 0.125, half)
        do = do_ref[here, :]
        dos = stacked(do, half)
        prod = (do.astype(jnp.float32) * o_ref[here, :].astype(jnp.float32)).T
        delta = jnp.concatenate(
            [jnp.sum(prod[:half], axis=0, keepdims=True), jnp.sum(prod[half:], axis=0, keepdims=True)],
            axis=1,
        )
        lse = lse_ref[pl.ds(i, 1), :]
        leaf_bias = jnp.where(leaf > 0, 0.0, -1e30)

        def piece(keys, values, shift, mask):
            s = mm(keys, qs, NT)
            if mask:
                s = jnp.where(allowed, s, -1e30)
            if isinstance(shift, list):
                p = jnp.concatenate(
                    [jnp.exp(s[kb * seg : (kb + 1) * seg] - shift[kb]) for kb in range(TRUNK)], axis=0
                )
            else:
                p = jnp.exp(s - shift)
            ds = (p * (mm(values, dos, NT) - delta)).astype(low)
            p = p.astype(low)
            return (mm(p, dos), mm(ds, qs), ds)

        shifts = [lse - jnp.where(kb < count, 0.0, -1e30) for kb in range(TRUNK)]
        dv, dk, ds = piece(k_ref[tk, :], v_ref[tk, :], shifts, False)
        av[tk, :] += dv
        ak[tk, :] += dk
        dq = mm(k_trunk, ds)
        keys = k_ref[there, :]
        dv, dk, ds = piece(keys, v_ref[there, :], lse - leaf_bias, False)
        av[there, :] += dv
        ak[there, :] += dk
        dq = dq + mm(keys.T, ds)
        keys = k_ref[here, :]
        dv, dk, ds = piece(keys, v_ref[here, :], lse, True)
        av[here, :] += dv
        ak[here, :] += dk
        dq = dq + mm(keys.T, ds)
        dq_ref[here, :] = (unstack(dq, half, seg) * 0.125).T.astype(low)
        return 0

    lax.fori_loop(0, own // seg, one, 0, unroll=True)
    dk_ref[...] = ak[...].astype(low)
    dv_ref[...] = av[...].astype(low)


def attend(info, q, kv, seg, begin, count, prev=()):
    own, width = q.shape
    total = kv.shape[0]
    pairs = width // 128
    lane = pl.BlockSpec((own, 128), lambda h: (0, begin + h))
    return pl.pallas_call(
        functools.partial(attend_kernel, own, seg, HEAD_DIM, len(prev) > 0),
        grid=(count,),
        in_specs=[
            pl.BlockSpec(memory_space=pltpu.SMEM),
            lane,
            pl.BlockSpec((total, 128), lambda h: (0, begin + h)),
            pl.BlockSpec((total, 128), lambda h: (0, pairs + begin + h)),
        ]
        + [pl.BlockSpec(memory_space=pl.ANY)] * len(prev),
        out_specs=[lane, pl.BlockSpec((None, 8, 2 * seg), lambda h: (begin + h, 0, 0))],
        out_shape=[
            jax.ShapeDtypeStruct((own, width), jnp.bfloat16),
            jax.ShapeDtypeStruct((pairs, 8, 2 * seg), jnp.float32),
        ],
        input_output_aliases={4 + i: i for i in range(len(prev))},
        scratch_shapes=[
            pltpu.VMEM((TRUNK * seg, 2 * seg), jnp.float32),
            pltpu.VMEM((TRUNK * seg, 2 * seg), jnp.bfloat16),
        ],
        compiler_params=pltpu.CompilerParams(vmem_limit_bytes=60 << 20),
        cost_estimate=pl.CostEstimate(
            flops=1000, bytes_accessed= 1000, transcendentals=0
        ),
        name="attend",
    )(info, q, kv, kv, *prev)


def attend_back(info, q, kv, o, do, lse, seg, begin, count, prev=()):
    own, width = q.shape
    total = kv.shape[0]
    pairs = width // 128
    lane = pl.BlockSpec((own, 128), lambda h: (0, begin + h))
    keys = pl.BlockSpec((total, 128), lambda h: (0, begin + h))
    return pl.pallas_call(
        functools.partial(attend_back_kernel, own, seg, HEAD_DIM, len(prev) > 0),
        grid=(count,),
        in_specs=[
            pl.BlockSpec(memory_space=pltpu.SMEM),
            lane,
            keys,
            pl.BlockSpec((total, 128), lambda h: (0, pairs + begin + h)),
            lane,
            lane,
            pl.BlockSpec((None, 8, 2 * seg), lambda h: (begin + h, 0, 0)),
        ]
        + [pl.BlockSpec(memory_space=pl.ANY)] * len(prev),
        out_specs=[lane, keys, keys],
        out_shape=[
            jax.ShapeDtypeStruct((own, width), jnp.bfloat16),
            jax.ShapeDtypeStruct((total, width), jnp.bfloat16),
            jax.ShapeDtypeStruct((total, width), jnp.bfloat16),
        ],
        input_output_aliases={7 + i: i for i in range(len(prev))},
        scratch_shapes=[
            pltpu.VMEM((total, 128), jnp.float32),
            pltpu.VMEM((total, 128), jnp.float32),
        ],
        compiler_params=pltpu.CompilerParams(vmem_limit_bytes=40 << 20),
        cost_estimate=pl.CostEstimate(
            flops=1000, bytes_accessed= 1000, transcendentals=0
        ),
        name="attend_back",
    )(info, q, kv, kv, o, do, lse, *prev)


def pin(x, *after):
    return lax.optimization_barrier((x,) + after)[0]


def expert_kernel(
    more, capacity, pieces, place, xm_ref, xo_ref, gm_ref, go_ref, w0, w1, w2, w3, *rest
):
    low, full = jnp.bfloat16, jnp.float32
    o_ref, o2_ref, s_ref, s2_ref, dw_ref, x_ref, g_ref, xt, dt, d_ref, oa, sa, wb, gb = rest[more:]
    part = w0.shape[1]
    rows, wide = xm_ref.shape
    padded = rows // pieces
    tail = padded - 16
    here = pl.ds(pl.multiple_of(place[1] * wide, 128), wide)
    there = pl.ds(pl.multiple_of((1 - place[1]) * wide, 128), wide)

    @pl.when(pl.program_id(0) == 0)
    def start():
        x_ref[:, here] = xm_ref[...]
        x_ref[:, there] = xo_ref[...]
        g_ref[:, here] = gm_ref[...]
        g_ref[:, there] = go_ref[...]
        for p in range(pieces):
            mine = slice(p * padded, (p + 1) * padded)
            last = xm_ref[p * padded + tail : (p + 1) * padded, :256].astype(full)
            row = lax.broadcasted_iota(jnp.int32, last.shape, 0) + tail
            inside = (row >= capacity) & (row < capacity + 3)
            gate = jnp.sum(jnp.where(inside, last, 0.0), axis=0, keepdims=True)
            gate = jnp.broadcast_to(gate, (8, 256)).T[:padded, 0:1]
            d_ref[mine, :] = (g_ref[mine, :].astype(full) * gate).astype(low)
        xt[...] = x_ref[...].T
        dt[...] = d_ref[...].T
        oa[...] = jnp.zeros_like(oa)
        sa[...] = jnp.zeros_like(sa)

    def rows_of(r):
        return pl.ds(pl.multiple_of((place[0] ^ r) * part, 64), part)

    for r, w in enumerate((w0, w1, w2, w3)):
        for k in range(3):
            wb[rows_of(r), k * PIECE : (k + 1) * PIECE] = w[k]
    pair = mm(x_ref[...], wb[:, : 2 * PIECE])
    u, up = pair[:, :PIECE], pair[:, PIECE:]
    sigma = 1.0 / (1.0 + jnp.exp(-u))
    silu = u * sigma
    hidden = (silu * up).astype(low)
    oa[...] += mm(hidden, wb[:, 2 * PIECE :], NT)
    dh = mm(d_ref[...], wb[:, 2 * PIECE :])
    du = (dh * up * sigma * (1.0 + u * (1.0 - sigma))).astype(low)
    dup = (dh * silu).astype(low)
    d_pair = jnp.concatenate([du, dup], axis=1)
    sa[...] += mm(d_pair, wb[:, : 2 * PIECE], NT)
    gb[:, : 2 * PIECE] = mm(xt[...], d_pair).astype(low)
    gb[:, 2 * PIECE :] = mm(dt[...], hidden).astype(low)
    for at, r in enumerate(SENT):
        for k in range(3):
            got = gb[rows_of(r), k * PIECE : (k + 1) * PIECE]
            if more:
                got = (got.astype(full) + rest[0][at, k].astype(full)).astype(low)
            dw_ref[at, k] = got

    @pl.when(pl.program_id(0) == pl.num_programs(0) - 1)
    def finish():
        o_ref[...] = oa[:, here].astype(low)
        o2_ref[...] = oa[:, there].astype(low)
        s_ref[...] = sa[:, here].astype(low)
        s2_ref[...] = sa[:, there].astype(low)
        for p in range(pieces):
            mine = slice(p * padded, (p + 1) * padded)
            dot = jnp.sum(g_ref[mine, :].astype(full) * oa[mine, :], axis=1, keepdims=True)
            dot = jnp.broadcast_to(dot, (padded, 128)).T[:16, :]
            dot = jnp.concatenate([dot, jnp.zeros((16, wide - padded), full)], axis=1)
            row = lax.broadcasted_iota(jnp.int32, dot.shape, 0) + tail
            kept = jnp.zeros_like(dot)
            for i in range(3):
                piece = dot.astype(low).astype(full)
                kept = jnp.where(row == capacity + i, piece, kept)
                dot = dot - piece
            last = slice(p * padded + tail, (p + 1) * padded)
            row_low = s_ref[last, :].astype(full)
            s_ref[last, :] = jnp.where(row >= capacity, kept, row_low).astype(low)


def expert_pass(place, capacity, pieces, xs, gs, weights, prev):
    rows, half_width = xs[0].shape
    width = 2 * half_width
    three, part, units = weights[0].shape
    low = jnp.bfloat16
    strip = pl.BlockSpec((three, part, PIECE), lambda j, *at: (0, 0, j))
    strips = pl.BlockSpec((4, three, part, PIECE), lambda j, *at: (0, 0, 0, j))
    half = whole(rows, half_width)
    more = prev is not None
    return call(
        functools.partial(expert_kernel, int(more), capacity, pieces),
        "expert_pass",
        [((rows, half_width), low)] * 4 + [((4, three, part, units), low)],
        (place, *xs, *gs, *weights, *([prev] if more else [])),
        [
            pltpu.VMEM((rows, width), low),
            pltpu.VMEM((rows, width), low),
            pltpu.VMEM((width, rows), low),
            pltpu.VMEM((width, rows), low),
            pltpu.VMEM((rows, width), low),
            pltpu.VMEM((rows, width), jnp.float32),
            pltpu.VMEM((rows, width), jnp.float32),
            pltpu.VMEM((width, three * PIECE), low),
            pltpu.VMEM((width, three * PIECE), low),
        ],
        grid=(units // PIECE,),
        in_specs=[half] * 4 + [strip] * 4 + [strips] * more,
        out_specs=[half] * 4 + [strips],
        prefetch=True,
        mib=48,
    )


def spread_kernel(pieces, padded, capacity, gated, place_ref, rows_ref, *rest):
    low = jnp.bfloat16
    outs = rest[1:] if gated else rest
    tokens = rows_ref.shape[0]
    for p in range(pieces):
        slot = lax.broadcasted_iota(jnp.int32, (padded, tokens), 0) + p * padded
        hits = [slot == place_ref[c : c + 1, :] for c in range(2)]
        out = mm(jnp.where(hits[0] | hits[1], 1.0, 0.0).astype(low), rows_ref[...]).astype(low)
        if gated:
            parts = 0.0
            for c in range(2):
                value = rest[0][c : c + 1, :]
                rows3 = []
                for i in range(3):
                    rows3.append(value.astype(low).astype(jnp.float32))
                    value = value - rows3[-1]
                rows3.append(jnp.zeros((13, tokens), jnp.float32))
                three = jnp.concatenate(rows3, axis=0).astype(low)
                parts = parts + mm(three, jnp.where(hits[c], 1.0, 0.0).astype(low), NT)
            parts = parts.astype(low)
            blank = jnp.zeros((parts.shape[0], out.shape[1] - padded), low)
            parts = jnp.concatenate([parts, blank], axis=1)
            row = lax.broadcasted_iota(jnp.int32, out.shape, 0)
            for i in range(3):
                out = jnp.where(row == capacity + i, parts[i : i + 1, :], out)
        outs[p][...] = out


def spread(place, rows, pieces, padded, capacity, parts=None):
    shape = jax.ShapeDtypeStruct((padded, rows.shape[1]), jnp.bfloat16)
    gated = parts is not None
    return pl.pallas_call(
        functools.partial(spread_kernel, pieces, padded, capacity, gated),
        in_specs=[pl.BlockSpec(memory_space=pltpu.VMEM)] * (2 + gated),
        out_specs=[pl.BlockSpec(memory_space=pltpu.VMEM)] * pieces,
        out_shape=[shape] * pieces,
        compiler_params=pltpu.CompilerParams(vmem_limit_bytes=60 << 20),
        cost_estimate=pl.CostEstimate(flops=1000, bytes_accessed= 1000, transcendentals=0),
        name="spread",
    )(place, rows, *([parts] if gated else []))


def expert_of(where_ref, piece):
    upper = jnp.where(where_ref[1] >= 2, 1, 0)
    return (2 * ((piece % 4) ^ where_ref[0]) + ((piece // 4) ^ upper)).astype(jnp.float32)


def spread_gated_kernel(pieces, padded, capacity, gated, where_ref, place_ref, rows_ref, *rest):
    low, full = jnp.bfloat16, jnp.float32
    tokens, width = rows_ref.shape
    if gated:
        gates_ref, outs, wide_ref = rest[0], rest[1:-1], rest[-1]
        lines = []
        for c in range(2):
            value = gates_ref[c : c + 1, :]
            for i in range(3):
                lines.append(value.astype(low).astype(full))
                value = value - lines[-1]
        lines = lines + [gates_ref[4:5, :], jnp.zeros((121, tokens), full)]
        wide_ref[:, :width] = rows_ref[...]
        wide_ref[:, width:] = jnp.concatenate(lines, axis=0).T.astype(low)
    else:
        outs, wide_ref = rest, rows_ref
    for p in range(pieces):
        slot = lax.broadcasted_iota(jnp.int32, (padded, tokens), 0) + p * padded
        hit = (slot == place_ref[0:1, :]) | (slot == place_ref[1:2, :])
        out = mm(jnp.where(hit, 1.0, 0.0).astype(low), wide_ref[...])
        if gated:
            extra = out[:, width:].T
            out = out[:, :width].astype(low)
            row = lax.broadcasted_iota(jnp.int32, out.shape, 0)
            blank = jnp.zeros((1, width - padded), full)
            for i in range(3):
                picked = jnp.where(
                    extra[6:7, :] == expert_of(where_ref, p), extra[i : i + 1, :], extra[3 + i : 4 + i, :]
                )
                picked = jnp.concatenate([picked, blank], axis=1).astype(low)
                out = jnp.where(row == capacity + i, picked, out)
        outs[p][...] = out.astype(low)


def spread_gated(where, place, rows, pieces, padded, capacity, gates=None):
    shape = jax.ShapeDtypeStruct((padded, rows.shape[1]), jnp.bfloat16)
    gated = gates is not None
    return pl.pallas_call(
        functools.partial(spread_gated_kernel, pieces, padded, capacity, gated),
        in_specs=[pl.BlockSpec(memory_space=pltpu.SMEM)]
        + [pl.BlockSpec(memory_space=pltpu.VMEM)] * (2 + gated),
        out_specs=[pl.BlockSpec(memory_space=pltpu.VMEM)] * pieces,
        out_shape=[shape] * pieces,
        scratch_shapes=[pltpu.VMEM((rows.shape[0], rows.shape[1] + 128), jnp.bfloat16)] * gated,
        compiler_params=pltpu.CompilerParams(vmem_limit_bytes=40 << 20),
        cost_estimate=pl.CostEstimate(flops=1000, bytes_accessed=1000, transcendentals=0),
        name="spread",
    )(where, place, rows, *([gates] if gated else []))


def gather_kernel(pieces, padded, capacity, dots, where_ref, place_ref, pair_ref, *rest):
    low, full = jnp.bfloat16, jnp.float32
    if dots:
        ins, (out_ref, out2_ref, dot_ref, dot2_ref) = rest[:pieces], rest[pieces:]
    else:
        ins, (out_ref, out2_ref) = rest[: pieces // 2], rest[pieces // 2 :]
    tokens = place_ref.shape[0]
    total = None
    sums = [0.0, 0.0]
    for p in range(pieces):
        slot = lax.broadcasted_iota(jnp.int32, (tokens, padded), 1) + p * padded
        hits = [slot == place_ref[:, c : c + 1] for c in range(2)]
        if dots:
            source = ins[p][...]
            width = source.shape[1]
            values = ins[p][padded - 16 :, :padded].astype(full)
            values = jnp.concatenate([values, jnp.zeros((112, padded), full)], axis=0).T
            source = jnp.concatenate([source, values.astype(low)], axis=1)
            part = mm(jnp.where(hits[0] | hits[1], 1.0, 0.0).astype(low), source)
            lane = lax.broadcasted_iota(jnp.int32, (tokens, 128), 1)
            lane = lane + (padded - 16 - capacity)
            dot = jnp.where((lane >= 0) & (lane < 3), part[:, width:], 0.0)
            mine = pair_ref[:, 0:1] == expert_of(where_ref, p)
            sums[0] = sums[0] + jnp.where(mine, dot, 0.0)
            sums[1] = sums[1] + jnp.where(mine, 0.0, dot)
            part = part[:, :width]
        else:
            pick = jnp.where(hits[0], pair_ref[:, 0:1], jnp.where(hits[1], pair_ref[:, 1:2], 0.0))
            part = mm(pick.astype(low), ins[p % 4][p // 4])
        total = part if total is None else total + part
    rows = tokens // 2
    out_ref[...] = total[:rows].astype(low)
    out2_ref[...] = total[rows:].astype(low)
    if dots:
        for c in range(2):
            dot_ref[:, c : c + 1] = jnp.sum(sums[c][:rows], axis=1, keepdims=True)
            dot2_ref[:, c : c + 1] = jnp.sum(sums[c][rows:], axis=1, keepdims=True)


def gather(where, place, pair, pieces, capacity, dots):
    padded, width = pieces[0].shape[-2:]
    number = sum(p.size // (padded * width) for p in pieces)
    tokens = place.shape[0]
    shapes = [jax.ShapeDtypeStruct((tokens // 2, width), jnp.bfloat16)] * 2
    if dots:
        shapes = shapes + [jax.ShapeDtypeStruct((tokens // 2, 2), jnp.float32)] * 2
    return pl.pallas_call(
        functools.partial(gather_kernel, number, padded, capacity, dots),
        in_specs=[pl.BlockSpec(memory_space=pltpu.SMEM)]
        + [pl.BlockSpec(memory_space=pltpu.VMEM)] * (len(pieces) + 2),
        out_specs=[pl.BlockSpec(memory_space=pltpu.VMEM)] * len(shapes),
        out_shape=shapes,
        compiler_params=pltpu.CompilerParams(vmem_limit_bytes=60 << 20),
        cost_estimate=pl.CostEstimate(flops=1000, bytes_accessed= 1000, transcendentals=0),
        name="gather",
    )(where, place, pair, *pieces)


def whole(*shape):
    return pl.BlockSpec(shape, lambda *at: (0,) * len(shape))


def by_rows(*shape):
    return pl.BlockSpec(shape, lambda j, *at: (j, 0))


def chosen(number, *shape):
    return pl.BlockSpec((None,) + shape, lambda j, place: (number ^ place[0], 0, 0))


def call(kernel, name, outs, args, scratch=(), grid=(1,), in_specs=None, out_specs=None, prefetch=False, mib=40):
    if out_specs is None:
        out_specs = [whole(*o[0]) for o in outs]
    spec = pltpu.PrefetchScalarGridSpec(
        num_scalar_prefetch=int(prefetch),
        grid=grid,
        in_specs=in_specs,
        out_specs=out_specs,
        scratch_shapes=list(scratch),
    )
    return pl.pallas_call(
        kernel,
        grid_spec=spec,
        out_shape=[jax.ShapeDtypeStruct(*o) for o in outs],
        compiler_params=pltpu.CompilerParams(vmem_limit_bytes=mib << 20),
        cost_estimate=pl.CostEstimate(flops=1000, bytes_accessed=1000, transcendentals=0),
        name=name,
    )(*args)


def unit_rows(x):
    x = x.astype(jnp.float32)
    return x * lax.rsqrt(jnp.mean(x * x, axis=-1, keepdims=True) + eps)


def project_kernel(place, x0, near, mid, farther, gain, wm, wo, q_ref, kv_ref, n_ref, x_ref):
    low = jnp.bfloat16
    shard, ctx = place[0], place[1]
    rows, width = x0.shape
    half = wm.shape[2]

    def project(lo, x):
        here = slice(lo, lo + x.shape[0])
        normed = (unit_rows(x) * gain[...]).astype(low)
        x_ref[here, :] = x
        n_ref[here, :] = normed
        for m in (1, 2):
            for h, w in enumerate((wm, wo)):
                at = (m - 1) * width + h * half
                kv_ref[here, at : at + half] = mm(normed, w[m ^ shard]).astype(low)
        if lo == 0:
            for h, w in enumerate((wm, wo)):
                q_ref[:, h * half : (h + 1) * half] = mm(normed, w[shard]).astype(low)

    edge = x_ref.shape[0] - 3 * rows
    project(0, x0[...])
    later = jnp.where(ctx == 2, mid[...], farther[...])
    project(rows, jnp.where(ctx == 0, x0[...], jnp.where(ctx == 1, near[...], later)))
    later = jnp.where(ctx == 2, near[...], mid[...])
    project(2 * rows, jnp.where(ctx == 1, x0[...], later))
    project(3 * rows, jnp.where(ctx == 2, x0[:edge, :], near[:edge, :]))


def settle_kernel(
    place, o, x, wm, wo, gain, router, res, ids,
    mixed_ref, second_ref, mine_ref, other_ref, probs_ref, stat_ref, gates_ref,
):
    tp = place[2]
    half = wm.shape[1]
    attn = mm(o[:, :half], wm[...], NT) + mm(o[:, half:], wo[...], NT)
    mixed = x[...].astype(jnp.float32) + attn
    mixed_ref[...] = mixed
    inverse = lax.rsqrt(jnp.mean(mixed * mixed, axis=-1, keepdims=True) + eps)
    second = (mixed * inverse * gain[...]).astype(jnp.bfloat16)
    second_ref[...] = second
    mine_ref[...] = second_ref[:, pl.ds(pl.multiple_of(tp * half, 128), half)]
    other_ref[...] = second_ref[:, pl.ds(pl.multiple_of((1 - tp) * half, 128), half)]
    logits = mm(second, router[...], NT) + res[...]
    expo = jnp.exp(logits - jnp.max(logits, axis=-1, keepdims=True))
    probs = expo / jnp.sum(expo, axis=-1, keepdims=True)
    probs_ref[...] = probs
    lane = lax.broadcasted_iota(jnp.int32, probs.shape, 1)
    picked = [
        jnp.sum(jnp.where(lane == ids[:, c : c + 1], probs, 0.0), axis=-1, keepdims=True)
        for c in range(2)
    ]
    total = picked[0] + picked[1]
    wide = lax.broadcasted_iota(jnp.int32, (probs.shape[0], 128), 1)
    stat = jnp.where(wide == 0, picked[0] / total, jnp.where(wide == 1, picked[1] / total, 0.0))
    stat = jnp.where(wide == 2, total, jnp.where(wide == 3, inverse, stat))
    stat = jnp.where(wide == 4, ids[:, 0:1].astype(jnp.float32), stat)
    stat_ref[...] = stat[:, :8]
    gates_ref[...] = stat.T[:8, :]


def settle_back_kernel(
    copy_id, place, dr_mine, dr_came, dg_mine, dg_came, g_ref, mixed, second, probs_ref, stat, ids,
    const, router, gain, wm, wo, dmix_ref, dattn_ref, do_ref, dlog_ref, small_ref, full_ref,
):
    low, full = jnp.bfloat16, jnp.float32
    tp = place[2]
    half = wm.shape[1]
    full_ref[:, pl.ds(pl.multiple_of(tp * half, 128), half)] = dr_mine[...]
    full_ref[:, pl.ds(pl.multiple_of((1 - tp) * half, 128), half)] = dr_came[...]
    g = g_ref[...].astype(full)
    probs = probs_ref[...]
    gates = [stat[:, 0:1], stat[:, 1:2]]
    total, inverse = stat[:, 2:3], stat[:, 3:4]
    ids_c = [ids[:, 0:1], ids[:, 1:2]]
    zero = jnp.zeros_like(total)

    def gate_of(number):
        return sum(jnp.where(ids_c[c] == number, gates[c], zero) for c in range(2))

    copy_gate = gate_of(copy_id)
    const_gate = [gate_of(copy_id + 1 + k) for k in range(2)]
    dots = [jnp.sum(g * second[...].astype(full), axis=-1, keepdims=True)]
    dots = dots + [jnp.sum(g * const[k : k + 1, :], axis=-1, keepdims=True) for k in range(2)]
    d_gates = []
    for c in range(2):
        d = dg_mine[:, c : c + 1] + dg_came[:, c : c + 1]
        for k in range(3):
            d = d + jnp.where(ids_c[c] == copy_id + k, dots[k], zero)
        d_gates.append(d)
    mean = d_gates[0] * gates[0] + d_gates[1] * gates[1]
    lane = lax.broadcasted_iota(jnp.int32, probs.shape, 1)
    d_probs = jnp.zeros_like(probs)
    for c in range(2):
        d_probs = d_probs + jnp.where(lane == ids_c[c], (d_gates[c] - mean) / total, 0.0)
    d_logits = probs * (d_probs - jnp.sum(probs * d_probs, axis=-1, keepdims=True))
    dlog_ref[...] = d_logits
    d_second = copy_gate * g + full_ref[...].astype(full)
    rest = d_logits
    for i in range(3):
        piece = rest.astype(low)
        rest = rest - piece.astype(full)
        d_second = d_second + mm(piece, router[...])
    unit = mixed[...] * inverse
    d_gain = jnp.sum(d_second * unit, axis=0, keepdims=True)
    d_unit = d_second * gain[...]
    d_mixed = g + inverse * (d_unit - unit * jnp.mean(d_unit * unit, axis=-1, keepdims=True))
    dmix_ref[...] = d_mixed
    d_attn = d_mixed.astype(low)
    dattn_ref[...] = d_attn
    do_ref[:, :half] = mm(d_attn, wm[...]).astype(low)
    do_ref[:, half:] = mm(d_attn, wo[...]).astype(low)
    count = probs.shape[1]
    pad = jnp.zeros((probs.shape[0], 128 - count), full)
    wide = lax.broadcasted_iota(jnp.int32, (probs.shape[0], 128), 1)
    table = jnp.concatenate([d_logits, pad], axis=1)
    table = jnp.where(wide == count + 2, const_gate[0], table)
    table = jnp.where(wide == count + 3, const_gate[1], table)
    rest = table.T[: count + 4, :]
    from_second = from_g = 0.0
    for i in range(3):
        piece = rest.astype(low)
        rest = rest - piece.astype(full)
        from_second = from_second + mm(piece, second[...])
        from_g = from_g + mm(piece, g_ref[...])
    row = lax.broadcasted_iota(jnp.int32, from_g.shape, 0)
    small = jnp.where(row < count, from_second, jnp.where(row >= count + 2, from_g, 0.0))
    small_ref[...] = jnp.where(row == count + 1, d_gain, small)


def keys_back_kernel(place, dq, dk, dv, x, wm, wo, own_ref, p0_ref, p1_ref, p2_ref, gain_ref):
    shard = place[0]
    rows, width = own_ref.shape
    half = wm.shape[2]
    gain = jnp.zeros((1, width), jnp.float32)
    lo = 0
    for out in (own_ref, p0_ref, p1_ref, p2_ref):
        here = slice(lo, lo + out.shape[0])
        lo = lo + out.shape[0]
        d = 0.0
        for m, grad in ((0, dq), (1, dk), (2, dv)):
            if m > 0 or out is own_ref:
                d = d + mm(grad[here, :half], wm[m ^ shard], NT)
                d = d + mm(grad[here, half:], wo[m ^ shard], NT)
        out[...] = d.astype(out.dtype)
        gain = gain + jnp.sum(d * unit_rows(x[here, :]), axis=0, keepdims=True)
    gain_ref[...] = gain


def weights_back_kernel(n_ref, dq, dk, dv, da_ref, o, tiny, mine_ref, other_ref, nt, at):
    rows = dq.shape[0]
    step = pl.program_id(0)

    @pl.when(step == 0)
    def start():
        nt[...] = n_ref[...].T
        at[...] = da_ref[...].T

    def put(value):
        value = value.astype(jnp.bfloat16)
        parts, half = mine_ref.shape[0], mine_ref.shape[2]
        part = value.shape[0] // parts
        for z in range(parts):
            mine_ref[z, :part, :] = value[z * part : (z + 1) * part, :half]
            other_ref[z, :part, :] = value[z * part : (z + 1) * part, half:]
            mine_ref[z, part:, :] = tiny[z, :, :half]
            other_ref[z, part:, :] = tiny[z, :, half:]

    pl.when(step == 0)(lambda: put(mm(nt[:, :rows], dq[...])))
    pl.when(step == 1)(lambda: put(mm(nt[...], dk[...])))
    pl.when(step == 2)(lambda: put(mm(nt[...], dv[...])))
    pl.when(step == 3)(lambda: put(mm(at[...], o[...])))


def weights_back(normed, dq, dk, dv, d_attn, o, tiny):
    total, width = normed.shape
    rows, half = dq.shape[0], width // 2
    parts, room = tiny.shape[1], tiny.shape[2]
    low = jnp.bfloat16
    out = pl.BlockSpec((None, parts, width // parts + room, half), lambda j: (j, 0, 0, 0))
    shape = ((4, parts, width // parts + room, half), low)
    return call(
        weights_back_kernel,
        "weights_back",
        [shape, shape],
        (normed, dq, dk, dv, d_attn, o, tiny),
        [pltpu.VMEM((width, total), low), pltpu.VMEM((width, rows), low)],
        grid=(4,),
        in_specs=[whole(total, width), whole(rows, width), whole(total, width), whole(total, width)]
        + [whole(rows, width), whole(rows, width)]
        + [pl.BlockSpec((None, parts, room, width), lambda j: (j, 0, 0, 0))],
        out_specs=[out, out],
        mib=60,
    )


def flip(x, axis, bit, size):
    return lax.ppermute(x, axis, [(i, i ^ bit) for i in range(size)])


def turn_gather(x, size, position):
    out = jnp.zeros((size,) + x.shape, x.dtype)
    out = lax.dynamic_update_index_in_dim(out, x, position, 0)
    for k in range(1, size):
        block = lax.ppermute(x, "ctx", [(i, (i + k) % size) for i in range(size)])
        out = lax.dynamic_update_index_in_dim(out, block, (position - k) % size, 0)
    return out


def turn_sum(x, size, position):
    total = lax.dynamic_index_in_dim(x, position, 0, keepdims=False).astype(jnp.float32)
    for k in range(1, size):
        block = lax.dynamic_index_in_dim(x, (position + k) % size, 0, keepdims=False)
        got = lax.ppermute(block, "ctx", [(i, (i + k) % size) for i in range(size)])
        total = total + got.astype(jnp.float32)
    return total


def far(x, k, shards_n, ctx_n):
    pairs = []
    for s in range(shards_n):
        for z in range(ctx_n):
            pairs.append((s * ctx_n + z, (s ^ k) * ctx_n + (z ^ 2)))
    return lax.ppermute(x, ("shard", "ctx"), pairs)


def three_parts(x):
    one = x.astype(jnp.bfloat16)
    rest = x - one.astype(jnp.float32)
    two = rest.astype(jnp.bfloat16)
    return jnp.stack([one, two, (rest - two.astype(jnp.float32)).astype(jnp.bfloat16)], axis=-2)


def with_rows(slots, values, at):
    extra = three_parts(values)
    after = slots.shape[-2] - at - extra.shape[-2]
    pads = ((0, 0), (at, after), (0, slots.shape[-1] - extra.shape[-1]))
    return slots + jnp.pad(extra, pads)


def row_values(slots, at):
    return jnp.sum(slots[:, at : at + 3, : slots.shape[1]].astype(jnp.float32), axis=1)


def by_core(
    tokens, gate_res, cotangent, parents, expert_ids, priority, w_qkv, w_out, w_router, attn_gain,
    ffn_gain, const_vec, w_gate_up, w_down,
):
    low, full = jnp.bfloat16, jnp.float32
    shard, ctx, tp = lax.axis_index("shard"), lax.axis_index("ctx"), lax.axis_index("tp")
    shards_n, ctx_n = lax.axis_size("shard"), lax.axis_size("ctx")
    trees, rows, width = tokens.shape
    rows_d = w_qkv.shape[0]
    part = width // 2
    seg = rows * ctx_n // parents.shape[1]
    own_segs = rows // seg
    edge = KEY_SEGS * seg - 2 * rows

    def own_tree(x):
        return lax.dynamic_index_in_dim(x, tp, 0, keepdims=False)

    def in_order(x, other, axis=0):
        return jnp.concatenate([jnp.where(tp == 0, x, other), jnp.where(tp == 0, other, x)], axis=axis)

    def both_trees(x, other):
        both = jnp.broadcast_to(x[None], (2,) + x.shape)
        return lax.dynamic_update_index_in_dim(both, other, 1 - tp, 0)

    def unit_of(x):
        x = x.astype(full)
        inverse = lax.rsqrt(jnp.mean(x * x, axis=-1, keepdims=True) + eps)
        return (x * inverse, inverse)

    def swap(x):
        return flip(x, "tp", 1, 2)

    def plus(x, y):
        return (x.astype(full) + y.astype(full)).astype(low)

    def my_half(x, which):
        return lax.dynamic_slice_in_dim(x, which * part, part, x.ndim - 1)

    x_own = lax.optimization_barrier(own_tree(tokens))
    ends = [(i, i + 1) for i in range(ctx_n - 1)]
    near = lax.ppermute(x_own, "ctx", ends)

    mine = jnp.stack([w_qkv[:, 0], w_qkv[:, 1], w_qkv[:, 2], w_out])
    small = jnp.concatenate([w_router.T, attn_gain[None], ffn_gain[None], const_vec.T], axis=0)
    all_experts = w_router.shape[1]
    mine = lax.dynamic_index_in_dim(mine, shard, 0, keepdims=False)
    mine = jnp.concatenate([mine, small.reshape(-1, part)], axis=0)
    turned = turn_gather(mine, ctx_n, ctx)
    matrix = turned[:, :rows_d].reshape(width, -1)
    small = turned[:, rows_d:].reshape(ctx_n, -1, rows_d).transpose(1, 0, 2).reshape(-1, width)
    router_t = small[:all_experts]
    gain_a = small[all_experts].astype(full)
    gain_f = small[all_experts + 1].astype(full)
    const_t = small[all_experts + 2 :].astype(full)

    mid = lax.ppermute(pin(near, matrix), "ctx", ends[1:])
    plane_pieces = [matrix] + [flip(matrix, "shard", k, shards_n) for k in range(1, shards_n)]
    capacity = trees * rows * 2 // all_experts
    experts = shards_n * w_gate_up.shape[1]
    padded = -(-(capacity + 3) // 16) * 16
    count = experts * padded
    flat = expert_ids.reshape(-1)
    order = (2 * priority[0, 0][:, None] + jnp.arange(2, dtype=jnp.int32)[None, :]).reshape(-1)
    earlier = (flat[:, None] == flat[None, :]) & (order[None, :] < order[:, None])
    ranks = jnp.sum(earlier.astype(jnp.int32), axis=1)
    kept = (flat < experts) & (ranks < capacity)
    piece = ((flat % 2) ^ (ctx // 2)) * shards_n + ((flat // 2) ^ shard)
    place = jnp.where(kept, piece * padded + ranks, -1).reshape(trees, rows, 2)
    place = jnp.where(tp == 0, place, place[::-1]).reshape(trees * rows, 2)
    place_t = place.T

    g_own = own_tree(cotangent)
    g_other = lax.dynamic_index_in_dim(cotangent, 1 - tp, 0, keepdims=False)
    g_half = my_half(jnp.concatenate([g_own, g_other], axis=0), tp)
    g_slots = spread(place_t, g_half, experts, padded, capacity)
    ids = own_tree(expert_ids)
    res = own_tree(gate_res)
    ids, res, router_t, gain_a, gain_f, const_t, mid, *g_slots = lax.optimization_barrier(
        (ids, res, router_t, gain_a[None], gain_f[None], const_t, mid, *g_slots)
    )
    farther = lax.ppermute(mid, "ctx", ends[2:])
    plane = jnp.stack(plane_pieces)

    plane_other = swap(plane)
    place3 = jnp.stack([shard, ctx, tp]).astype(jnp.int32)

    capacity = trees * rows * 2 // all_experts
    experts = shards_n * w_gate_up.shape[1]
    padded = -(-(capacity + 3) // 16) * 16
    count = experts * padded
    flat = expert_ids.reshape(-1)
    order = (2 * priority[0, 0][:, None] + jnp.arange(2, dtype=jnp.int32)[None, :]).reshape(-1)
    earlier = (flat[:, None] == flat[None, :]) & (order[None, :] < order[:, None])
    ranks = jnp.sum(earlier.astype(jnp.int32), axis=1)
    kept = (flat < experts) & (ranks < capacity)
    piece = ((flat % 2) ^ (ctx // 2)) * shards_n + ((flat // 2) ^ shard)
    place = jnp.where(kept, piece * padded + ranks, -1).reshape(trees, rows, 2)
    place = jnp.where(tp == 0, place, place[::-1]).reshape(trees * rows, 2)
    place_t = place.T

    g_own = own_tree(cotangent)
    g_other = lax.dynamic_index_in_dim(cotangent, 1 - tp, 0, keepdims=False)
    g_half = my_half(jnp.concatenate([g_own, g_other], axis=0), tp)
    g_slots = spread(place_t, g_half, experts, padded, capacity)
    g_near = jnp.stack(g_slots[:shards_n])
    g_far = flip(pin(jnp.stack(g_slots[shards_n:]), mid), "ctx", 2, ctx_n)
    plane_other = swap(plane)
    place3 = jnp.stack([shard, ctx, tp]).astype(jnp.int32)

    g_near = jnp.stack(g_slots[:shards_n])
    g_far = flip(jnp.stack(g_slots[shards_n:]), "ctx", 2, ctx_n)

    held, gu, dn = lax.optimization_barrier((near, w_gate_up, w_down))
    lower = ctx < 2
    first = jnp.stack([gu[:, 0, 0], gu[:, 0, 1], dn[:, 0]])
    second_e = jnp.stack([gu[:, 1, 0], gu[:, 1, 1], dn[:, 1]])
    rows_own = jnp.where(lower, first, second_e)
    rows_two = flip(pin(jnp.where(lower, second_e, first), farther, g_far), "ctx", 2, ctx_n)
    rows_one = flip(pin(rows_own, farther, g_far), "ctx", 1, ctx_n)

    total = 3 * rows + edge
    q, kv, normed, x_all = call(
        project_kernel,
        "project",
        [((rows, width), low), ((total, 2 * width), low), ((total, width), low), ((total, width), low)],
        (place3, x_own, near, mid, farther, gain_a, plane, plane_other),
        in_specs=[whole(rows, width)] * 4
        + [whole(1, width), whole(4, width, part), whole(4, width, part)],
        prefetch=True,
    )

    seg_id = ctx * own_segs + jnp.arange(own_segs, dtype=jnp.int32)
    parent = jnp.take(own_tree(parents), seg_id)
    leaf = (seg_id >= KEY_SEGS).astype(jnp.int32)
    info = jnp.stack([jnp.minimum(seg_id, TRUNK), jnp.where(leaf > 0, parent, TRUNK), leaf], axis=1)
    half_pairs = width // 256
    ahead = attend(info, q, kv, seg, 0, half_pairs)
    o_low, lse = attend(info, q, kv, seg, half_pairs, half_pairs, ahead)
    g_pairs = jnp.stack([g_near, pin(g_far, ahead[0])], axis=1)
    g_got = [g_pairs[0]] + [flip(g_pairs[k], "shard", k, shards_n) for k in range(1, shards_n)]
    o_low = pin(o_low, rows_one, rows_two, *g_got)
    g_in = jnp.stack(g_got, axis=1).reshape(2, shards_n * padded, part)
    g_out = swap(g_in)

    one_half = ((rows, part), low)
    mixed, second, second_mine, second_other, probs, stat, gates_t = call(
        settle_kernel,
        "settle",
        [
            ((rows, width), full), ((rows, width), low), one_half, one_half,
            ((rows, all_experts), full), ((rows, 8), full), ((8, rows), full),
        ],
        (place3, o_low, x_own, plane, plane_other, gain_f, router_t, res, ids),
        in_specs=[
            whole(rows, width), whole(rows, width), chosen(3, width, part), chosen(3, width, part),
            whole(1, width), whole(all_experts, width), whole(rows, all_experts), whole(rows, 2),
        ],
        prefetch=True,
    )
    second_half = jnp.concatenate([second_mine, swap(second_other)], axis=0)
    gates_both = jnp.concatenate([gates_t, swap(gates_t)], axis=1)

    rows_three = flip(pin(rows_two, o_low), "ctx", 1, ctx_n)
    weights = (rows_own, rows_one, rows_two, rows_three)
    slots = spread_gated(place3, place_t, second_half, experts, padded, capacity, gates_both)
    x_far = [far(slots[shards_n + k], k, shards_n, ctx_n) for k in range(shards_n)]
    x_near = [slots[0]] + [flip(slots[k], "shard", k, shards_n) for k in range(1, shards_n)]

    def experts_on(pieces, gs, prev):
        x = jnp.concatenate(pieces, axis=0)
        return expert_pass(place3[1:], capacity, shards_n, (x, swap(x)), gs, weights, prev)

    def answers(mine, other):
        return plus(mine, swap(other)).reshape(shards_n, padded, part)

    x_near[0] = pin(x_near[0], rows_three)
    on1, ox1, sn1, sx1, dw = experts_on(x_near, (g_in[0], g_out[0]), None)
    x_far = list(lax.optimization_barrier((*x_far, sn1))[:-1])
    on2, ox2, sn2, sx2, dw = experts_on(x_far, (g_in[1], g_out[1]), dw)
    ds_far = answers(sn2, sx2)
    ds_near = answers(sn1, sx1)
    ds_far = [far(ds_far[k], k, shards_n, ctx_n) for k in range(shards_n)]
    ds_near = [ds_near[0]] + [flip(ds_near[k], "shard", k, shards_n) for k in range(1, shards_n)]

    rows_tn = (((0,), (0,)), ((), ()))
    d_routed, d_routed_other, d_pairs, d_pairs_other = gather(
        place3, place, gates_both[4][:, None], ds_near + ds_far, capacity, True
    )
    d_mixed, d_attn, d_o, d_logits, d_small = call(
        functools.partial(settle_back_kernel, experts + 1),
        "settle_back",
        [
            ((rows, width), full), ((rows, width), low), ((rows, width), low),
            ((rows, all_experts), full), ((all_experts + 4, width), full),
        ],
        (
            place3, d_routed, swap(d_routed_other), d_pairs, swap(d_pairs_other), g_own, mixed, second,
            probs, stat, ids, const_t, router_t, gain_f, plane, plane_other,
        ),
        [pltpu.VMEM((rows, width), low)],
        in_specs=[
            whole(rows, part), whole(rows, part), whole(rows, 2), whole(rows, 2), whole(rows, width),
            whole(rows, width), whole(rows, width), whole(rows, all_experts), whole(rows, 8),
            whole(rows, 2), whole(2, width), whole(all_experts, width), whole(1, width),
            chosen(3, width, part), chosen(3, width, part),
        ],
        prefetch=True,
        mib=60,
    )

    ox1, ox2, held = lax.optimization_barrier((ox1, ox2, d_routed))
    out_near = plus(on1, swap(ox1)).reshape(shards_n, padded, part)
    out_far = plus(on2, swap(ox2)).reshape(shards_n, padded, part)

    got = flip(pin(dw[2:], d_routed), "ctx", 1, ctx_n)

    third = width // 384
    back = attend_back(info, q, kv, o_low, d_o, lse, seg, 0, third)
    out_near, out_far, q_later, held = lax.optimization_barrier((out_near, out_far, q, back[0]))
    back = attend_back(info, q_later, kv, o_low, d_o, lse, seg, third, third, back)
    out_near, out_far = (out_near, out_far)
    out_cross = flip(out_far, "ctx", 2, ctx_n)
    q_later = pin(q, back[0])
    dq, dk, dv = attend_back(info, q_later, kv, o_low, d_o, lse, seg, 2 * third, third, back)
    got = pin(got, dq)
    sent_rows = plus(dw[1], got[1])
    came_rows = flip(sent_rows, "ctx", 2, ctx_n)
    out_pairs = jnp.stack([out_near, pin(out_cross, dq)], axis=1)
    out_got = [out_pairs[0]] + [flip(out_pairs[k], "shard", k, shards_n) for k in range(1, shards_n)]
    d_near, part0, part1, part2, d_gain_a = call(
        keys_back_kernel,
        "keys_back",
        [
            ((rows, width), full), ((rows, width), low), ((rows, width), low), ((edge, width), low),
            ((1, width), full),
        ],
        (pin(place3, sent_rows), dq, dk, dv, x_all, plane, plane_other),
        in_specs=[
            whole(rows, width), whole(total, width), whole(total, width), whole(total, width),
            whole(4, width, part), whole(4, width, part),
        ],
        prefetch=True,
        mib=60,
    )

    tiny = jnp.concatenate([d_small[:all_experts], d_gain_a, d_small[all_experts + 1 :]], axis=0)
    tiny = tiny.reshape(4, 2, 2, ctx_n, rows_d).transpose(0, 3, 1, 2, 4).reshape(4, ctx_n, 2, 2 * rows_d)
    tiny = jnp.where(tp == 0, tiny, tiny[:, :, ::-1]).reshape(4, ctx_n, 1, width).astype(low)
    tiny = jnp.pad(tiny, ((0, 0), (0, 0), (0, 15), (0, 0)))
    shared_mine, shared_other = weights_back(normed, dq, dk, dv, d_attn, o_low, tiny)

    def down(x, step):
        return lax.ppermute(x, "ctx", [(i, i - 1) for i in range(ctx_n - step, ctx_n)])

    came = down(part0, 1)
    shared_other = pin(shared_other, came, *out_got, came_rows)
    payload = jnp.where(ctx == 3, part1, plus(part0, came))
    came = down(payload, 2)
    shared = plus(pin(shared_mine, payload), swap(shared_other))

    def numbered(k):
        return lax.dynamic_index_in_dim(shared, shard ^ k, 0, keepdims=False)

    plane_parts = [flip(numbered(k), "shard", k, shards_n) for k in range(1, shards_n)]
    plane_sum = numbered(0).astype(full)
    for got_part in plane_parts:
        plane_sum = plane_sum + got_part.astype(full)
    came = pin(came, plane_parts[0])
    part2 = jnp.pad(part2, ((0, rows - edge), (0, 0)))
    came = down(jnp.where(ctx == 3, part2, jnp.where(ctx == 2, plus(part1, came), plus(part0, came))), 3)
    base = jnp.where(ctx == 0, part0, jnp.where(ctx == 1, part1, part2)).astype(full)
    extra = jnp.where(ctx == 3, 0.0, base + came.astype(full))
    came_rows = pin(came_rows, plane_parts[0]).astype(full)
    kept_rows = dw[0].astype(full) + got[0].astype(full)
    first = jnp.where(lower, kept_rows, came_rows)
    second_e = jnp.where(lower, came_rows, kept_rows)
    d_gate_up = jnp.stack(
        [jnp.stack([first[0], first[1]], axis=1), jnp.stack([second_e[0], second_e[1]], axis=1)], axis=1
    )
    d_down = jnp.stack([first[2], second_e[2]], axis=1)
    d_normed = d_near + extra
    unit_own, inv_own = unit_of(x_own)
    gain_a = gain_a[0]
    d_first = d_normed * gain_a
    d_tokens = d_mixed + inv_own * (
        d_first - unit_own * jnp.mean(d_first * unit_own, axis=-1, keepdims=True)
    )

    total = turn_sum(plane_sum.astype(low), ctx_n, ctx).astype(low)
    out_got = [pin(o, plane_parts[0]) for o in out_got]
    gate_columns = jnp.stack([gates_both[0], gates_both[1]], axis=1)
    combined, combined_other = gather(place3, place, gate_columns, out_got, capacity, False)
    combined = in_order(combined, swap(combined_other), 1).astype(full)
    second_f = second.astype(full)

    def gate_of(number):
        return jnp.sum(jnp.where(ids == number, stat[:, :2], 0.0), axis=1, keepdims=True)

    copy_gate = gate_of(experts + 1)
    const_gate = jnp.concatenate([gate_of(experts + 2), gate_of(experts + 3)], axis=1)
    mixed_out = (
        mixed
        + combined
        + copy_gate * second_f
        + const_gate[:, :1] * const_t[0][None]
        + const_gate[:, 1:] * const_t[1][None]
    )
    total = pin(total, mixed_out, d_tokens)
    d_tokens_other = swap(d_tokens)
    four = [total] + [flip(total, "shard", k, shards_n) for k in range(1, shards_n)]
    four = jnp.stack([pin(f, d_tokens_other) for f in four])
    four = jnp.stack(
        [lax.dynamic_index_in_dim(four, m ^ shard, 0, keepdims=False) for m in range(4)]
    )
    d_q, d_k, d_v, d_w_out = [four[m, :rows_d].astype(full) for m in range(4)]
    d_w_qkv = jnp.stack([d_q, d_k, d_v], axis=1)
    tiny = four[:, rows_d]
    tiny = both_trees(tiny, swap(tiny)).transpose(1, 0, 2).reshape(16, rows_d).astype(full)

    return (
        both_trees(mixed_out, swap(mixed_out)),
        both_trees(d_tokens, d_tokens_other),
        both_trees(d_logits, swap(d_logits)),
        d_w_qkv,
        d_w_out,
        tiny[:all_experts].T,
        tiny[all_experts],
        tiny[all_experts + 1],
        tiny[all_experts + 2 :].T,
        d_gate_up,
        d_down,
    )


def program(tokens, gate_res, cotangent, parents, expert_ids, priority, w_qkv, *weights):
    trees, rows, width = tokens.shape
    ctx_n = lax.axis_size("ctx")
    seg = rows * ctx_n // parents.shape[1]
    fits = (
        ctx_n == 4
        and lax.axis_size("shard") == 4
        and lax.axis_size("tp") == 2
        and trees == 2
        and seg == 128
        and rows % seg == 0
        and 2 * rows < KEY_SEGS * seg <= 3 * rows
        and weights[-1].shape[1] == 2
    )
    chosen = by_core if fits else shards
    return chosen(tokens, gate_res, cotangent, parents, expert_ids, priority, w_qkv, *weights)


def solution(mesh):
    return jax.shard_map(
        program,
        mesh=mesh,
        in_specs=(
            P("shard", "ctx", None),
            P("shard", "ctx", None),
            P("shard", "ctx", None),
            P("shard", None),
            P("shard", "ctx", None),
            P("shard", "ctx", None),
            P("ctx", None, "tp"),
            P("ctx", "tp"),
            P("ctx", None),
            P("ctx"),
            P("ctx"),
            P("ctx", None),
            P("ctx", "shard", None, "tp"),
            P("ctx", "shard", "tp"),
        ),
        out_specs=(
            P("shard", "ctx", None),
            P("shard", "ctx", None),
            P("shard", "ctx", None),
            P("ctx", None, "tp"),
            P("ctx", "tp"),
            P("ctx", None),
            P("ctx"),
            P("ctx"),
            P("ctx", None),
            P("ctx", "shard", None, "tp"),
            P("ctx", "shard", "tp"),
        ),
        check_vma=False,
    )
```
